32 devices in a mesh: seq: 8 (over z, y), ch: 4 (over x, core).
Axes of the slice: x: 2, y: 2, z: 4, core: 2. Of those that a mesh axis runs over, the one named last changes fastest.
Arguments:
- hidden_in: bfloat16 [2, 1024, 2048], P(None, 'seq'), may hold values from -6 to 6
- segments: int32 [2, 1024], P(None, 'seq'), may hold values from 1 to 2048, as said below
- cotangent: bfloat16 [2, 1024, 2048], P(None, 'seq'), may hold values from -6 to 6
- norm_gain: float32 [2, 2048], replicated, may hold values from 0.5 to 1.5
- input_projection_weight: bfloat16 [2, 2048, 2, 4096], P(None, None, None, 'ch'), may hold values from -0.125 to 0.125
- conv_weight: float32 [2, 4, 4096], P(None, None, 'ch'), may hold values from -3 to 3
- conv_bias: float32 [2, 4096], P(None, 'ch'), may hold values from -3 to 3
- proj_weight: bfloat16 [2, 4096, 160], P(None, 'ch'), may hold values from -0.1875 to 0.1875
- step_weight: bfloat16 [2, 128, 4096], P(None, None, 'ch'), may hold values from -0.5 to 0.5
- step_bias: float32 [2, 4096], P(None, 'ch'), may hold values from -4 to -1
- decay_log: float32 [2, 16, 4096], P(None, None, 'ch'), may hold values from -7 to 1.5
- skip_gain: float32 [2, 4096], P(None, 'ch'), may hold values from 0.5 to 1.5
- output_projection_weight: bfloat16 [2, 4096, 2048], P(None, 'ch'), may hold values from -0.09375 to 0.09375
Outputs:
- activations: bfloat16 [2, 1024, 2048], P(None, 'seq', 'ch')
- grad_input: float32 [2, 1024, 2048], P(None, 'seq', 'ch')
- grad_norm_gain: float32 [2, 2048], P(None, 'ch')
- grad_in_weight: float32 [2, 2048, 2, 4096], P(None, 'seq', None, 'ch')
- grad_conv_weight: float32 [2, 4, 4096], P(None, None, 'ch')
- grad_conv_bias: float32 [2, 4096], P(None, 'ch')
- grad_proj_weight: float32 [2, 4096, 160], P(None, 'ch')
- grad_step_weight: float32 [2, 128, 4096], P(None, None, 'ch')
- grad_step_bias: float32 [2, 4096], P(None, 'ch')
- grad_decay_log: float32 [2, 16, 4096], P(None, None, 'ch')
- grad_skip_gain: float32 [2, 4096], P(None, 'ch')
- grad_out_weight: float32 [2, 4096, 2048], P(None, 'ch', 'seq')
The draws below stay inside these ranges and needn't reach their ends.
Inputs may be any that keep to these rules, and one draw needn't show every extreme that they name: `segments`: A token's document id is 1024 times its sequence's number, plus one, plus the position at which its document begins; so ids never fall along a sequence and every id of a later sequence exceeds those of earlier ones. The last token of the last sequence is a document of its own. In one of the sequences a single document begins within its first 128 tokens and lasts into its last 128 tokens.
All inputs are finite; a program needn't handle non-finite values.
Results may differ from the reference program's by a relative error of at most 0.025.
Values may be sent and summed in bfloat16 or wider, within the bound.
A program may use at most 256 MiB of HBM per device.

```python
import jax
import jax.numpy as jnp
from jax import lax

D = 2048
DI = 4096
STATE = 16
RANK = 128
KERN = 4
LAYERS = 2
SEQS = 2
LEN_DEV = 128
LEN = 1024
PROJ = 160


def draw_segments(key, part):
    keys = jax.random.split(key, 5)
    candidates = LEN // 64 + 2
    limits = jax.random.randint(keys[0], (SEQS, candidates), 2, LEN)
    starts = jax.random.randint(keys[1], (SEQS, candidates), 1, limits)
    chosen = jax.random.randint(keys[2], (), 0, SEQS)
    first = jax.random.randint(keys[3], (), 1, LEN_DEV)
    ending = LEN - LEN_DEV + jax.random.randint(keys[4], (), 1, LEN_DEV)
    rows = jnp.arange(SEQS)[:, None]
    inside = (rows == chosen) & (starts > first) & (starts < ending)
    starts = jnp.where(inside, 0, starts)
    extra = jnp.where(rows == chosen, jnp.stack([first, ending])[None, :], 0)
    starts = jnp.concatenate([starts, extra], axis=1)
    flags = jnp.zeros((SEQS, LEN), jnp.int32).at[rows, starts].set(1)
    flags = flags.at[:, 0].set(1)
    flags = flags.at[SEQS - 1, LEN - 1].set(1)
    positions = jnp.arange(LEN, dtype=jnp.int32)[None, :]
    begins = lax.cummax(jnp.where(flags > 0, positions, 0), axis=1)
    return (rows.astype(jnp.int32) * LEN + begins + 1).astype(jnp.int32)


def block_levels(own_key, extent, cuts, smallest, largest):
    loudness, own = 1.0, jax.random.fold_in(own_key, 6)
    for dim, blocks in cuts:
        steps = jnp.exp(jax.random.uniform(jax.random.fold_in(own, dim), (blocks,), jnp.float32, smallest / len(cuts), largest / len(cuts)))
        loudness = loudness * jnp.repeat(steps, extent[dim] // blocks).reshape([-1 if axis == dim else 1 for axis in range(len(extent))])
    return loudness


def bell_draw(own_key, shape, scale, bound, cuts=(), kind=jnp.bfloat16):
    entries = jax.random.normal(own_key, shape, jnp.float32) * scale
    if len(cuts) > 0:
        entries = block_levels(own_key, shape, cuts, -0.22, 0.18) * entries
    return jnp.clip(entries, min=-bound, max=bound).astype(kind)


def setup_inputs(seed: int = 0) -> dict:
    key_list = jax.random.split(jax.random.key(seed), 14)
    return {
        "hidden_in": bell_draw(key_list[0], (SEQS, LEN, D), 1.0, 6.0, ((1, 8),)),
        "segments": draw_segments(jax.random.fold_in(key_list[13], 71), 0),
        "cotangent": bell_draw(key_list[2], (SEQS, LEN, D), 1.0, 6.0, ((1, 8),)),
        "norm_gain": jnp.clip(1.0 + 0.1 * jax.random.normal(key_list[3], (LAYERS, D), jnp.float32), 0.5, 1.5),
        "input_projection_weight": bell_draw(key_list[4], (LAYERS, D, 2, DI), D ** -0.5, 0.125, ((3, 4),)),
        "conv_weight": bell_draw(key_list[5], (LAYERS, KERN, DI), KERN ** -0.5, 3.0, ((2, 4),), jnp.float32),
        "conv_bias": bell_draw(key_list[6], (LAYERS, DI), 0.5, 3.0, ((1, 4),), jnp.float32),
        "proj_weight": bell_draw(key_list[7], (LAYERS, DI, PROJ), (DI // 4) ** -0.5, 0.1875, ((1, 4),)),
        "step_weight": bell_draw(key_list[8], (LAYERS, RANK, DI), RANK ** -0.5, 0.5, ((2, 4),)),
        "step_bias": jnp.clip(-4.0 + 3.0 * jax.random.uniform(key_list[9], (LAYERS, DI), jnp.float32) ** block_levels(key_list[9], (LAYERS, DI), ((1, 4),), -0.2, 0.2), -4.0, -1.0),
        "decay_log": jnp.clip(-7.0 + 8.5 * jax.random.uniform(key_list[10], (LAYERS, STATE, DI), jnp.float32) ** block_levels(key_list[10], (LAYERS, STATE, DI), ((2, 4),), -0.2, 0.2), -7.0, 1.5),
        "skip_gain": jnp.clip(0.5 + 1.0 * jax.random.uniform(key_list[11], (LAYERS, DI), jnp.float32) ** block_levels(key_list[11], (LAYERS, DI), ((1, 4),), -0.2, 0.2), 0.5, 1.5),
        "output_projection_weight": bell_draw(key_list[12], (LAYERS, DI, D), DI ** -0.5, 0.09375, ((1, 4),)),
    }


epsilon = 1e-05

@jax.custom_vjp
def low(v):
    return lax.optimization_barrier(v.astype(jnp.bfloat16)).astype(jnp.float32)

@jax.custom_vjp
def reduced_backward(v):
    return v

def low_keep(v):
    return (low(v), None)

def low_pass(kept, grad):
    return (grad,)

def back_keep(v):
    return (v, None)

def back_low(kept, grad):
    return (low(grad),)
low.defvjp(low_keep, low_pass)
reduced_backward.defvjp(back_keep, back_low)

def gated_product(pattern, left, right):
    return jnp.einsum(pattern, left, right, precision=lax.Precision.HIGHEST)

def rms_norm(hidden_rows, scale):
    mean_sq = lax.optimization_barrier(jnp.mean(hidden_rows * hidden_rows, axis=-1, keepdims=True))
    return hidden_rows * lax.rsqrt(mean_sq + epsilon) * scale

def causal_conv(values, segments, weights, biases):
    length = values.shape[1]
    summed = biases + jnp.zeros_like(values)
    for lag_index in range(KERN):
        lag_size = KERN - 1 - lag_index
        moved = jnp.pad(values, ((0, 0), (lag_size, 0), (0, 0)))[:, :length]
        moved_seg = jnp.pad(segments, ((0, 0), (lag_size, 0)))[:, :length]
        same_doc = (moved_seg == segments).astype(values.dtype)
        summed = summed + weights[lag_index] * moved * same_doc[:, :, None]
    return summed

def token_step(carry, item):
    carried, a_mat = carry
    step_size, values, input_mat, output_mat, keep_mask = item
    decay_now = jnp.exp(step_size[:, :, None] * a_mat)
    carried = keep_mask[:, None, None] * decay_now * carried + (step_size * values)[:, :, None] * input_mat[:, None, :]
    return ((carried, a_mat), lax.optimization_barrier(jnp.sum(carried * output_mat[:, None, :], axis=-1)))

def block_scan(carry, items):
    return lax.scan(token_step, carry, items)

def selective(step_size, values, input_mat, output_mat, keep_mask, a_mat):
    seq_count, length, channels = step_size.shape
    block_count = length // 64

    def arrange(array):
        moved = jnp.moveaxis(array, 1, 0)
        return moved.reshape((block_count, 64) + moved.shape[1:])
    pieces = tuple((arrange(array) for array in (step_size, values, input_mat, output_mat, keep_mask)))
    initial = (jnp.zeros((seq_count, channels, STATE), step_size.dtype), a_mat)
    _, outputs = lax.scan(jax.checkpoint(block_scan), initial, pieces)
    return jnp.moveaxis(outputs.reshape((length, seq_count, channels)), 0, 1)

def forward(hidden_rows, segments, norm_gain, input_projection_weight, conv_weight, conv_bias, proj_weight, step_weight, step_bias, decay_log, skip_gain, output_projection_weight):
    previous = jnp.pad(segments, ((0, 0), (1, 0)))[:, :-1]
    keep_mask = (previous == segments).astype(hidden_rows.dtype)
    for layer_number in range(LAYERS):
        normalized_rows = low(rms_norm(hidden_rows, norm_gain[layer_number]))
        projected_rows = reduced_backward(gated_product('uaz,zfe->uafe', normalized_rows, input_projection_weight[layer_number]))
        values = projected_rows[:, :, 0]
        gate_pre = projected_rows[:, :, 1]
        activated = jax.nn.silu(causal_conv(values, segments, conv_weight[layer_number], conv_bias[layer_number]))
        proj_out = reduced_backward(gated_product('slc,cj->slj', low(activated), proj_weight[layer_number]))
        rank_low = low(proj_out[:, :, :RANK])
        input_mat = proj_out[:, :, RANK:RANK + STATE]
        output_mat = proj_out[:, :, RANK + STATE:]
        step_size = jax.nn.softplus(reduced_backward(gated_product('slr,rc->slc', rank_low, step_weight[layer_number])) + step_bias[layer_number])
        a_mat = -jnp.exp(decay_log[layer_number]).T
        scanned = selective(step_size, activated, input_mat, output_mat, keep_mask, a_mat) + skip_gain[layer_number] * activated
        mixer_output = low(scanned * jax.nn.silu(gate_pre))
        hidden_rows = hidden_rows + reduced_backward(gated_product('uhk,kw->uhw', mixer_output, output_projection_weight[layer_number]))
    return hidden_rows

def reference(hidden_in, segments, cotangent, norm_gain, input_projection_weight, conv_weight, conv_bias, proj_weight, step_weight, step_bias, decay_log, skip_gain, output_projection_weight):
    floats = tuple((array.astype(jnp.float32) for array in (hidden_in, norm_gain, input_projection_weight, conv_weight, conv_bias, proj_weight, step_weight, step_bias, decay_log, skip_gain, output_projection_weight)))

    def apply_all(hidden_rows, *params):
        return forward(hidden_rows, segments, *params)
    output, pull_back = jax.vjp(apply_all, *floats)
    grads = pull_back(cotangent.astype(jnp.float32))
    return (output.astype(jnp.bfloat16), grads[0], grads[1], grads[2], grads[3], grads[4], grads[5], grads[6], grads[7], grads[8], grads[9], grads[10])
```

```python
import functools
from functools import partial

import jax
import jax.numpy as jnp
from jax import lax
from jax.experimental import pallas as pl
from jax.experimental.pallas import tpu as pltpu
from jax.sharding import PartitionSpec as P

STATE = 16
RANK = 128
KERN = 4
LAYERS = 2


epsilon = 1e-05
LANES = 128
BIG = 1e30
LOG2E = 1.4426950408889634

def softplus(v):
    return jnp.maximum(v, 0.0) + jnp.log(1.0 + jnp.exp(-jnp.abs(v)))

def spread_states(bc_ref, wide_ref, pick_ref, rows, unroll=8):
    lane = lax.broadcasted_iota(jnp.int32, (STATE, 2 * STATE), 1)
    row = lax.broadcasted_iota(jnp.int32, (STATE, 2 * STATE), 0)
    mask = (lane % STATE == row).astype(jnp.float32)
    src = lax.broadcasted_iota(jnp.int32, (2 * STATE, 2 * LANES), 0)
    dst = lax.broadcasted_iota(jnp.int32, (2 * STATE, 2 * LANES), 1)
    route = ((src // STATE) == (dst // LANES)).astype(jnp.bfloat16)
    chunk = 32
    def step(i, _):
        t0 = pl.multiple_of(i * chunk, chunk)
        bcv = bc_ref[pl.ds(t0, chunk), :]
        for j in range(chunk):
            pick_ref[pl.ds(j * STATE, STATE), :] = (bcv[j:j + 1] * mask).astype(jnp.bfloat16)
        wide_ref[pl.ds(pl.multiple_of(t0 * STATE, chunk * STATE), chunk * STATE), :] = jnp.dot(pick_ref[...], route, preferred_element_type=jnp.float32)
        return 0
    lax.fori_loop(0, rows // chunk, step, 0)

def prep(step_ref_pre, act_ref, keep_ref, dstep_ref, dx_ref, rows):
    def body(i, _):
        sl = pl.ds(pl.multiple_of(i * 32, 32), 32)
        for g in range(dstep_ref.shape[0]):
            st = softplus(step_ref_pre[sl, lanes(g)])
            dstep_ref[g, sl, :] = jnp.where(keep_ref[sl, :] > 0.0, st, BIG)
            dx_ref[g, sl, :] = st * act_ref[sl, lanes(g)]
        return 0
    lax.fori_loop(0, rows // 32, body, 0)

def lanes(g):
    return pl.ds(g * LANES, LANES)

def group_sets(channels, width):
    n = channels // LANES
    return [list(range(i, min(i + width, n))) for i in range(0, n, width)]

def local_kernel(seqs, pre_ref, act_ref, bc_ref, keep_ref, dl_ref, end_ref, gain_ref, wide, pick, dstep, dx):
    rows, channels = pre_ref.shape
    length = rows // seqs
    spread_states(bc_ref, wide, pick, rows)
    prep(pre_ref, act_ref, keep_ref, dstep, dx, rows)
    for gs in group_sets(channels, 8):
        a2 = [-jnp.exp(dl_ref[:, lanes(g)]) * LOG2E for g in gs]
        for s in range(seqs):
            for k, g in enumerate(gs):
                tot = jnp.sum(dstep[g, pl.ds(s * length, length), :], axis=0, keepdims=True)
                gain_ref[s, :, lanes(g)] = jnp.exp2(a2[k] * tot)
            def blk(i, st):
                st = list(st)
                t0 = pl.multiple_of(s * length + i * 8, 8)
                for j in range(8):
                    b = wide[pl.ds(pl.multiple_of((t0 + j) * STATE, STATE), STATE), pl.ds(0, LANES)]
                    for k, g in enumerate(gs):
                        d = jnp.exp2(a2[k] * dstep[g, pl.ds(t0 + j, 1), :])
                        st[k] = d * st[k] + b * dx[g, pl.ds(t0 + j, 1), :]
                return tuple(st)
            st = lax.fori_loop(0, length // 8, blk, tuple(jnp.zeros((STATE, LANES), jnp.float32) for _ in gs))
            for k, g in enumerate(gs):
                end_ref[s, :, lanes(g)] = st[k]

VM = pl.BlockSpec(memory_space=pltpu.VMEM)

def scan_local(pre, act, bc, keep, dl, seqs):
    rows, channels = pre.shape
    f = jnp.float32
    return pl.pallas_call(
        functools.partial(local_kernel, seqs),
        out_shape=[jax.ShapeDtypeStruct((seqs, STATE, channels), f)] * 2,
        in_specs=[VM] * 5, out_specs=[VM] * 2,
        scratch_shapes=[pltpu.VMEM((rows * STATE, 2 * LANES), f), pltpu.VMEM((32 * STATE, 2 * STATE), jnp.bfloat16),
                        pltpu.VMEM((channels // LANES, rows, LANES), f), pltpu.VMEM((channels // LANES, rows, LANES), f)],
        compiler_params=pltpu.CompilerParams(vmem_limit_bytes=60 * 2**20),
        name="scan_local",
    )(pre, act, bc, keep, dl)

def forward_kernel(seqs, pre_ref, act_ref, bc_ref, keep_ref, dl_ref, in_ref, y_ref, wide, pick, dstep, dx, part):
    rows, channels = pre_ref.shape
    length = rows // seqs
    spread_states(bc_ref, wide, pick, rows)
    prep(pre_ref, act_ref, keep_ref, dstep, dx, rows)
    for gs in group_sets(channels, 4):
        a2 = [-jnp.exp(dl_ref[:, lanes(g)]) * LOG2E for g in gs]
        for s in range(seqs):
            def blk(i, st):
                st = list(st)
                t0 = pl.multiple_of(s * length + i * 8, 8)
                for j in range(8):
                    at = pl.ds(pl.multiple_of((t0 + j) * STATE, STATE), STATE)
                    b = wide[at, pl.ds(0, LANES)]
                    c = wide[at, pl.ds(LANES, LANES)]
                    for k, g in enumerate(gs):
                        d = jnp.exp2(a2[k] * dstep[g, pl.ds(t0 + j, 1), :])
                        st[k] = d * st[k] + b * dx[g, pl.ds(t0 + j, 1), :]
                        v = st[k] * c
                        part[k, pl.ds(pl.multiple_of(i * 64 + j * 8, 8), 8), :] = v[:8] + v[8:]
                return tuple(st)
            lax.fori_loop(0, length // 8, blk, tuple(in_ref[s, :, lanes(g)] for g in gs))
            def red(i, _):
                t0 = pl.multiple_of(s * length + i * 8, 8)
                for k, g in enumerate(gs):
                    acc = part[k, pl.ds(i * 64, 8, stride=8), :]
                    for m in range(1, 8):
                        acc = acc + part[k, pl.ds(i * 64 + m, 8, stride=8), :]
                    y_ref[pl.ds(t0, 8), lanes(g)] = acc
                return 0
            lax.fori_loop(0, length // 8, red, 0)

def scan_forward(pre, act, bc, keep, dl, state_in, seqs):
    rows, channels = pre.shape
    f = jnp.float32
    return pl.pallas_call(
        functools.partial(forward_kernel, seqs),
        out_shape=jax.ShapeDtypeStruct((rows, channels), f),
        in_specs=[VM] * 6, out_specs=VM,
        scratch_shapes=[pltpu.VMEM((rows * STATE, 2 * LANES), f), pltpu.VMEM((32 * STATE, 2 * STATE), jnp.bfloat16),
                        pltpu.VMEM((channels // LANES, rows, LANES), f), pltpu.VMEM((channels // LANES, rows, LANES), f),
                        pltpu.VMEM((4, rows // seqs * 8, LANES), f)],
        compiler_params=pltpu.CompilerParams(vmem_limit_bytes=60 * 2**20),
        name="scan_forward",
    )(pre, act, bc, keep, dl, state_in)

LN2 = 0.6931471805599453

def back_local_kernel(seqs, pre_ref, gs_ref, bc_ref, keep_ref, dl_ref, out_ref, wide, pick, dstep, gsc):
    rows, channels = pre_ref.shape
    length = rows // seqs
    spread_states(bc_ref, wide, pick, rows)
    def body(i, _):
        sl = pl.ds(pl.multiple_of(i * 32, 32), 32)
        for g in range(channels // LANES):
            st = softplus(pre_ref[sl, lanes(g)])
            dstep[g, sl, :] = jnp.where(keep_ref[sl, :] > 0.0, st, BIG)
            gsc[g, sl, :] = gs_ref[sl, lanes(g)]
        return 0
    lax.fori_loop(0, rows // 32, body, 0)
    for gs in group_sets(channels, 8):
        a2 = [-jnp.exp(dl_ref[:, lanes(g)]) * LOG2E for g in gs]
        for s in range(seqs):
            def blk(i, st):
                st = list(st)
                t0 = pl.multiple_of(s * length + (length // 8 - 1 - i) * 8, 8)
                for j in reversed(range(8)):
                    c = wide[pl.ds(pl.multiple_of((t0 + j) * STATE, STATE), STATE), pl.ds(LANES, LANES)]
                    for k, g in enumerate(gs):
                        d = jnp.exp2(a2[k] * dstep[g, pl.ds(t0 + j, 1), :])
                        st[k] = d * (st[k] + c * gsc[g, pl.ds(t0 + j, 1), :])
                return tuple(st)
            st = lax.fori_loop(0, length // 8, blk, tuple(jnp.zeros((STATE, LANES), jnp.float32) for _ in gs))
            for k, g in enumerate(gs):
                out_ref[s, :, lanes(g)] = st[k]

def scan_back_local(pre, gs, bc, keep, dl, seqs):
    rows, channels = pre.shape
    f = jnp.float32
    return pl.pallas_call(
        functools.partial(back_local_kernel, seqs),
        out_shape=jax.ShapeDtypeStruct((seqs, STATE, channels), f),
        in_specs=[VM] * 5, out_specs=VM,
        scratch_shapes=[pltpu.VMEM((rows * STATE, 2 * LANES), f), pltpu.VMEM((32 * STATE, 2 * STATE), jnp.bfloat16),
                        pltpu.VMEM((channels // LANES, rows, LANES), f), pltpu.VMEM((channels // LANES, rows, LANES), f)],
        compiler_params=pltpu.CompilerParams(vmem_limit_bytes=60 * 2**20),
        name="scan_back_local",
    )(pre, gs, bc, keep, dl)

def back_kernel(seqs, pre_ref, act_ref, gs_ref, bc_ref, keep_ref, dl_ref, skip_ref, in_ref, lam_ref,
                gpre_ref, gact_ref, gbc_ref, gdl_ref,
                wide, pick, dstep, dx, stepc, gsc, states, partq, partr, accb, accc, rowsum):
    rows, channels = pre_ref.shape
    length = rows // seqs
    f = jnp.float32
    spread_states(bc_ref, wide, pick, rows)
    def body(i, _):
        sl = pl.ds(pl.multiple_of(i * 32, 32), 32)
        for g in range(channels // LANES):
            st = softplus(pre_ref[sl, lanes(g)])
            stepc[g, sl, :] = st
            dstep[g, sl, :] = jnp.where(keep_ref[sl, :] > 0.0, st, BIG)
            dx[g, sl, :] = st * act_ref[sl, lanes(g)]
            gsc[g, sl, :] = gs_ref[sl, lanes(g)]
        return 0
    lax.fori_loop(0, rows // 32, body, 0)
    sets = group_sets(channels, 4)
    for index, gs in enumerate(sets):
        a2 = [-jnp.exp(dl_ref[:, lanes(g)]) * LOG2E for g in gs]
        gdl = [jnp.zeros((STATE, LANES), f) for _ in gs]
        for s in range(seqs):
            for k, g in enumerate(gs):
                states[k, pl.ds(0, STATE), :] = in_ref[s, :, lanes(g)]
            def fwd(i, st):
                st = list(st)
                t0 = pl.multiple_of(s * length + i * 8, 8)
                for j in range(8):
                    b = wide[pl.ds(pl.multiple_of((t0 + j) * STATE, STATE), STATE), pl.ds(0, LANES)]
                    for k, g in enumerate(gs):
                        d = jnp.exp2(a2[k] * dstep[g, pl.ds(t0 + j, 1), :])
                        st[k] = d * st[k] + b * dx[g, pl.ds(t0 + j, 1), :]
                        states[k, pl.ds(pl.multiple_of((i * 8 + j + 1) * STATE, STATE), STATE), :] = st[k]
                return tuple(st)
            lax.fori_loop(0, length // 8, fwd, tuple(in_ref[s, :, lanes(g)] for g in gs))
            def bwd(i, carry):
                st = list(carry[:len(gs)])
                am = list(carry[len(gs):])
                l0 = (length // 8 - 1 - i) * 8
                t0 = pl.multiple_of(s * length + l0, 8)
                for j in reversed(range(8)):
                    at = pl.ds(pl.multiple_of((t0 + j) * STATE, STATE), STATE)
                    b = wide[at, pl.ds(0, LANES)]
                    c = wide[at, pl.ds(LANES, LANES)]
                    tb = tc = None
                    here = pl.ds(pl.multiple_of((l0 + j) * 8, 8), 8)
                    for k, g in enumerate(gs):
                        row = pl.ds(t0 + j, 1)
                        grow = gsc[g, row, :]
                        d = jnp.exp2(a2[k] * dstep[g, row, :])
                        lam = st[k] + c * grow
                        old = states[k, pl.ds(pl.multiple_of((l0 + j) * STATE, STATE), STATE), :]
                        new = states[k, pl.ds(pl.multiple_of((l0 + j + 1) * STATE, STATE), STATE), :]
                        st[k] = d * lam
                        lp = st[k] * old
                        q = lam * b
                        partq[k, here, :] = q[:8] + q[8:]
                        r = lp * a2[k]
                        partr[k, here, :] = r[:8] + r[8:]
                        am[k] = am[k] + lp * stepc[g, row, :]
                        u = lam * dx[g, row, :]
                        v = new * grow
                        tb = u if tb is None else tb + u
                        tc = v if tc is None else tc + v
                    if index > 0:
                        tb = tb + accb[at, :]
                        tc = tc + accc[at, :]
                    accb[at, :] = tb
                    accc[at, :] = tc
                return tuple(st) + tuple(am)
            out = lax.fori_loop(0, length // 8, bwd, tuple(lam_ref[s, :, lanes(g)] for g in gs) + tuple(gdl))
            gdl = list(out[len(gs):])
            def red(i, _):
                t0 = pl.multiple_of(s * length + i * 8, 8)
                for k, g in enumerate(gs):
                    q = partq[k, pl.ds(i * 64, 8, stride=8), :]
                    r = partr[k, pl.ds(i * 64, 8, stride=8), :]
                    for m in range(1, 8):
                        q = q + partq[k, pl.ds(i * 64 + m, 8, stride=8), :]
                        r = r + partr[k, pl.ds(i * 64 + m, 8, stride=8), :]
                    here = pl.ds(t0, 8)
                    p = pre_ref[here, lanes(g)]
                    gstep = r * LN2 + act_ref[here, lanes(g)] * q
                    gpre_ref[here, lanes(g)] = gstep * (1.0 / (1.0 + jnp.exp(-p)))
                    gact_ref[here, lanes(g)] = stepc[g, here, :] * q + gsc[g, here, :] * skip_ref[:, lanes(g)]
                return 0
            lax.fori_loop(0, length // 8, red, 0)
        for k, g in enumerate(gs):
            gdl_ref[:, lanes(g)] = gdl[k] * (a2[k] * LN2)
    ones = jnp.ones((LANES, LANES), jnp.bfloat16)
    lane = lax.broadcasted_iota(jnp.int32, (32 * STATE, LANES), 1)
    row = lax.broadcasted_iota(jnp.int32, (32 * STATE, LANES), 0) % STATE
    mb = lane == row
    mc = lane == row + STATE
    def fin(i, _):
        sl = pl.ds(pl.multiple_of(i * 32 * STATE, 32 * STATE), 32 * STATE)
        sb = jnp.dot(accb[sl, :].astype(jnp.bfloat16), ones, preferred_element_type=f)
        sc = jnp.dot(accc[sl, :].astype(jnp.bfloat16), ones, preferred_element_type=f)
        rowsum[...] = jnp.where(mb, sb, jnp.where(mc, sc, 0.0))
        acc = rowsum[pl.ds(0, 32, stride=STATE), :]
        for m in range(1, STATE):
            acc = acc + rowsum[pl.ds(m, 32, stride=STATE), :]
        gbc_ref[pl.ds(pl.multiple_of(i * 32, 32), 32), :] = acc
        return 0
    lax.fori_loop(0, rows // 32, fin, 0)

def scan_back(pre, act, gs, bc, keep, dl, skip, state_in, lam_in, seqs):
    rows, channels = pre.shape
    f = jnp.float32
    groups = channels // LANES
    length = rows // seqs
    big = pltpu.VMEM((groups, rows, LANES), f)
    return pl.pallas_call(
        functools.partial(back_kernel, seqs),
        out_shape=[jax.ShapeDtypeStruct((rows, channels), f), jax.ShapeDtypeStruct((rows, channels), f),
                   jax.ShapeDtypeStruct((rows, LANES), f), jax.ShapeDtypeStruct((STATE, channels), f)],
        in_specs=[VM] * 9, out_specs=[VM] * 4,
        scratch_shapes=[pltpu.VMEM((rows * STATE, 2 * LANES), f), pltpu.VMEM((32 * STATE, 2 * STATE), jnp.bfloat16),
                        big, big, big, big,
                        pltpu.VMEM((4, (length + 1) * STATE, LANES), f),
                        pltpu.VMEM((4, length * 8, LANES), f), pltpu.VMEM((4, length * 8, LANES), f),
                        pltpu.VMEM((rows * STATE, LANES), f), pltpu.VMEM((rows * STATE, LANES), f),
                        pltpu.VMEM((32 * STATE, LANES), f)],
        compiler_params=pltpu.CompilerParams(vmem_limit_bytes=60 * 2**20),
        name="scan_back",
    )(pre, act, gs, bc, keep, dl, skip, state_in, lam_in)


def passed_along(block, axis, distance):
    devices = range(lax.axis_size(axis))
    route = [(i - distance, i) for i in devices if i - distance in devices]
    return lax.ppermute(block, axis, route)


def prefix(shard, axis, combine, identity):
    count, here = (lax.axis_size(axis), lax.axis_index(axis))
    everything = jax.tree.map(
        lambda part: lax.all_gather(part.astype(jnp.bfloat16), axis).astype(part.dtype), shard
    )
    start = jax.tree.map(
        lambda part, zero: jnp.broadcast_to(jnp.asarray(zero, part.dtype), part.shape),
        shard,
        identity,
    )

    def prefix_hop(k, before):
        reached = k < here
        new = combine(before, jax.tree.map(lambda part: part[k], everything))
        return jax.tree.map(lambda a, b: jnp.where(reached, a, b), new, before)

    return lax.fori_loop(0, count, prefix_hop, start)


def entering(shard, axis, combine, identity):
    count, here = (lax.axis_size(axis), lax.axis_index(axis))
    everything = jax.tree.map(
        lambda part, kind: lax.all_gather(part.astype(kind), axis),
        shard,
        (jnp.bfloat16, jnp.bfloat16),
    )
    start = jax.tree.map(
        lambda part, zero: jnp.broadcast_to(jnp.asarray(zero, part.dtype), part.shape),
        shard,
        identity,
    )

    def entering_hop(k, before):
        at = count - 1 - k
        reached = at > here
        new = combine(
            before, jax.tree.map(lambda part, own: part[at].astype(own.dtype), everything, shard)
        )
        return jax.tree.map(lambda a, b: jnp.where(reached, a, b), new, before)

    return lax.fori_loop(0, count, entering_hop, start)


def silu_slope(argument):
    logistic = jax.nn.sigmoid(argument)
    return logistic * (1.0 + argument * (1.0 - logistic))


def conv_local(extended, weights, biases, seg_ext):
    length_now = extended.shape[1] - (KERN - 1)
    seg_now = seg_ext[:, KERN - 1 :]
    summed = biases + jnp.zeros((extended.shape[0], length_now, extended.shape[2]), jnp.float32)
    for lag_index in range(KERN):
        same_doc = (seg_ext[:, lag_index : lag_index + length_now] == seg_now).astype(jnp.float32)
        summed = (
            summed
            + weights[lag_index]
            * extended[:, lag_index : lag_index + length_now]
            * same_doc[:, :, None]
        )
    return summed


def compose(earlier, later):
    return (earlier[0] * later[0], later[0] * earlier[1] + later[1])


def local(
    hidden_in,
    segments,
    cotangent,
    norm_gain,
    input_projection_weight,
    conv_weight,
    conv_bias,
    proj_weight,
    step_weight,
    step_bias,
    decay_log,
    skip_gain,
    output_projection_weight,
):
    width = hidden_in.shape[-1]
    share_size = width // lax.axis_size("ch")
    share_start = lax.axis_index("ch") * share_size
    seg_own = segments.astype(jnp.float32)
    hidden_rows = hidden_in.astype(jnp.float32)
    stored = []
    for layer_number in range(LAYERS):
        scale_now = norm_gain[layer_number]
        inv_rms = lax.rsqrt(jnp.mean(hidden_rows * hidden_rows, axis=-1, keepdims=True) + epsilon)
        normalized_rows = (hidden_rows * inv_rms * scale_now).astype(jnp.bfloat16)
        projected_rows = jnp.einsum(
            "uaz,zfe->uafe",
            normalized_rows,
            input_projection_weight[layer_number],
            preferred_element_type=jnp.float32,
        )
        values = projected_rows[:, :, 0]
        gate_pre = projected_rows[:, :, 1]
        edge_rows, seg_edge = passed_along(
            (values[:, -(KERN - 1) :], seg_own[:, -(KERN - 1) :]), "seq", 1
        )
        extended = jnp.concatenate([edge_rows, values], axis=1)
        seg_ext = jnp.concatenate([seg_edge, seg_own], axis=1)
        conv_out, conv_pull = jax.vjp(
            partial(conv_local, seg_ext=seg_ext),
            extended,
            conv_weight[layer_number],
            conv_bias[layer_number],
        )
        activated = jax.nn.silu(conv_out)
        act_low = activated.astype(jnp.bfloat16)
        proj_part = jnp.einsum(
            "slc,cj->slj", act_low, proj_weight[layer_number], preferred_element_type=jnp.float32
        )
        proj_out = lax.psum(proj_part, "ch")
        rank_low = proj_out[:, :, :RANK].astype(jnp.bfloat16)
        step_pre = (
            jnp.einsum(
                "slr,rc->slc",
                rank_low,
                step_weight[layer_number],
                preferred_element_type=jnp.float32,
            )
            + step_bias[layer_number]
        )
        shape = step_pre.shape
        seqs, channels = shape[0], shape[-1]
        flat = lambda v: v.reshape(-1, v.shape[-1])
        rates = decay_log[layer_number]
        mats = flat(proj_out[:, :, RANK:])
        keep = (seg_ext[:, KERN - 2 : -1] == seg_own).astype(jnp.float32).reshape(-1, 1)
        end_state, end_gain = scan_local(
            flat(step_pre), flat(activated), mats, keep, rates, seqs
        )
        identity = (jnp.ones_like(end_gain), jnp.zeros_like(end_state))
        state_in = prefix((end_gain, end_state), "seq", compose, identity)[1]
        y = scan_forward(
            flat(step_pre), flat(activated), mats, keep, rates, state_in, seqs
        ).reshape(shape)
        scanned = y + skip_gain[layer_number] * activated
        gate_act = jax.nn.silu(gate_pre)
        mixer_output_reduced = (scanned * gate_act).astype(jnp.bfloat16)
        out_part = jnp.einsum(
            "uhk,kw->uhw",
            mixer_output_reduced,
            output_projection_weight[layer_number],
            preferred_element_type=jnp.float32,
        )
        branch = lax.psum(out_part, "ch")
        stored.append(
            (
                hidden_rows,
                inv_rms,
                normalized_rows,
                gate_pre,
                conv_out,
                activated,
                act_low,
                conv_pull,
                rank_low,
                step_pre,
                mats,
                keep,
                state_in,
                end_gain,
                scanned,
                gate_act,
                mixer_output_reduced,
            )
        )
        hidden_rows = hidden_rows + branch
    result = lax.dynamic_slice_in_dim(hidden_rows, share_start, share_size, 2).astype(jnp.bfloat16)
    grad_rows = cotangent.astype(jnp.float32)
    collected = [None] * LAYERS
    for layer_number in reversed(range(LAYERS)):
        (
            hidden_rows,
            inv_rms,
            normalized_rows,
            gate_pre,
            conv_out,
            activated,
            act_low,
            conv_pull,
            rank_low,
            step_pre,
            mats,
            keep,
            state_in,
            end_gain,
            scanned,
            gate_act,
            mixer_output_reduced,
        ) = stored[layer_number]
        output_reduced = grad_rows.astype(jnp.bfloat16)
        grad_out_weight = jnp.einsum(
            "okg,okv->gv", output_reduced, mixer_output_reduced, preferred_element_type=jnp.float32
        )
        grad_mixed = jnp.einsum(
            "urp,yp->ury",
            output_reduced,
            output_projection_weight[layer_number],
            preferred_element_type=jnp.float32,
        )
        grad_scan = grad_mixed * gate_act
        grad_gate = grad_mixed * scanned * silu_slope(gate_pre)
        grad_skip = jnp.sum(grad_scan * activated, axis=(0, 1))
        rates = decay_log[layer_number]
        local_gain = scan_back_local(flat(step_pre), flat(grad_scan), mats, keep, rates, seqs)
        identity = (jnp.ones_like(end_gain), jnp.zeros_like(local_gain))
        grad_end = entering((end_gain, local_gain), "seq", compose, identity)[1]
        grad_pre, grad_act, grad_mats, grad_decay_log = scan_back(
            flat(step_pre),
            flat(activated),
            flat(grad_scan),
            mats,
            keep,
            rates,
            skip_gain[layer_number][None],
            state_in,
            grad_end,
            seqs,
        )
        grad_pre = grad_pre.reshape(shape)
        grad_act = grad_act.reshape(shape)
        grad_mats = grad_mats[:, : 2 * STATE].reshape(shape[:2] + (2 * STATE,))
        grad_step_bias = jnp.sum(grad_pre, axis=(0, 1))
        pre_low = grad_pre.astype(jnp.bfloat16)
        grad_step_weight = jnp.einsum(
            "slr,slc->rc", rank_low, pre_low, preferred_element_type=jnp.float32
        )
        rank_part = jnp.einsum(
            "slc,rc->slr", pre_low, step_weight[layer_number], preferred_element_type=jnp.float32
        )
        grad_proj = lax.psum(
            jnp.concatenate([rank_part, grad_mats], axis=-1).astype(jnp.bfloat16), "ch"
        ).astype(jnp.bfloat16)
        grad_proj_weight = jnp.einsum(
            "slc,slj->cj", act_low, grad_proj, preferred_element_type=jnp.float32
        )
        grad_act = grad_act + jnp.einsum(
            "slj,cj->slc", grad_proj, proj_weight[layer_number], preferred_element_type=jnp.float32
        )
        grad_conv_in, grad_conv_weight, grad_conv_bias = conv_pull(grad_act * silu_slope(conv_out))
        returned = passed_along(grad_conv_in[:, : KERN - 1], "seq", -1)
        grad_values = grad_conv_in[:, KERN - 1 :]
        grad_values = jnp.concatenate(
            [grad_values[:, : -(KERN - 1)], grad_values[:, -(KERN - 1) :] + returned], axis=1
        )
        grad_value_gate = jnp.stack([grad_values, grad_gate], axis=2).astype(jnp.bfloat16)
        grad_in_weight = jnp.einsum(
            "xpj,xpze->jze", normalized_rows, grad_value_gate, preferred_element_type=jnp.float32
        )
        grad_part = jnp.einsum(
            "fuva,jva->fuj",
            grad_value_gate,
            input_projection_weight[layer_number],
            preferred_element_type=jnp.float32,
        )
        scale_now = norm_gain[layer_number]
        inv_cubed = inv_rms * inv_rms * inv_rms
        grad_normed = lax.psum(grad_part.astype(jnp.bfloat16), "ch").astype(jnp.float32)
        inner_dot = jnp.sum(grad_normed * scale_now * hidden_rows, axis=-1, keepdims=True)
        grad_hidden = (
            inv_rms * scale_now * grad_normed - hidden_rows * inv_cubed * inner_dot / width
        )
        grad_norm_full = jnp.sum(grad_normed * hidden_rows * inv_rms, axis=(0, 1))
        grad_norm = lax.dynamic_slice_in_dim(grad_norm_full, share_start, share_size, 0)
        grad_rows = grad_rows + grad_hidden
        summed_in, summed_out = (
            lax.psum_scatter(
                grad_in_weight.astype(jnp.bfloat16), "seq", scatter_dimension=0, tiled=True
            ).astype(jnp.float32),
            lax.psum_scatter(
                grad_out_weight.astype(jnp.bfloat16), "seq", scatter_dimension=0, tiled=True
            ).astype(jnp.float32),
        )
        small_grads = (
            lax.psum(grad_norm.astype(jnp.bfloat16), "seq").astype(jnp.float32),
            lax.psum(grad_conv_weight.astype(jnp.bfloat16), "seq").astype(jnp.float32),
            lax.psum(grad_conv_bias.astype(jnp.bfloat16), "seq").astype(jnp.float32),
            lax.psum(grad_proj_weight.astype(jnp.bfloat16), "seq").astype(jnp.float32),
            lax.psum(grad_step_weight.astype(jnp.bfloat16), "seq").astype(jnp.float32),
            lax.psum(grad_step_bias.astype(jnp.bfloat16), "seq").astype(jnp.float32),
            lax.psum(grad_decay_log.astype(jnp.bfloat16), "seq").astype(jnp.float32),
            lax.psum(grad_skip.astype(jnp.bfloat16), "seq").astype(jnp.float32),
        )
        collected[layer_number] = (
            small_grads[0],
            summed_in,
            small_grads[1],
            small_grads[2],
            small_grads[3],
            small_grads[4],
            small_grads[5],
            small_grads[6],
            small_grads[7],
            summed_out.T,
        )
    grad_input = lax.dynamic_slice_in_dim(grad_rows, share_start, share_size, 2)
    stacked = [
        jnp.stack([collected[layer_number][member] for layer_number in range(LAYERS)], axis=0)
        for member in range(10)
    ]
    return (
        result,
        grad_input,
        stacked[0],
        stacked[1],
        stacked[2],
        stacked[3],
        stacked[4],
        stacked[5],
        stacked[6],
        stacked[7],
        stacked[8],
        stacked[9],
    )


def solution(mesh):
    in_specs = (
        P(None, "seq", None),
        P(None, "seq"),
        P(None, "seq", None),
        P(),
        P(None, None, None, "ch"),
        P(None, None, "ch"),
        P(None, "ch"),
        P(None, "ch", None),
        P(None, None, "ch"),
        P(None, "ch"),
        P(None, None, "ch"),
        P(None, "ch"),
        P(None, "ch", None),
    )
    out_specs = (
        P(None, "seq", "ch"),
        P(None, "seq", "ch"),
        P(None, "ch"),
        P(None, "seq", None, "ch"),
        P(None, None, "ch"),
        P(None, "ch"),
        P(None, "ch", None),
        P(None, None, "ch"),
        P(None, "ch"),
        P(None, None, "ch"),
        P(None, "ch"),
        P(None, "ch", "seq"),
    )
    return jax.shard_map(local, mesh=mesh, in_specs=in_specs, out_specs=out_specs, check_vma=False)
```

```python
import functools

import jax
import jax.numpy as jnp
from jax import lax
from jax.experimental import pallas as pl
from jax.experimental.pallas import tpu as pltpu
from jax.sharding import PartitionSpec as P

STATE = 16
RANK = 128
KERN = 4
LAYERS = 2
MESH = pl.DeviceIdType.MESH
ANY = pl.BlockSpec(memory_space=pl.ANY)
f32, bf16 = jnp.float32, jnp.bfloat16
epsilon = 1e-05


def after(kernel, count, pins):
    def run(*refs):
        return kernel(*refs[:count], *refs[count + len(pins) :])
    return run


def cost(us):
    return pl.CostEstimate(flops=int(us * 1.0e9), bytes_accessed=0, transcendentals=0)


LANES = 128
BIG = 1e30
LOG2E = 1.4426950408889634

def softplus(v):
    return jnp.maximum(v, 0.0) + jnp.log(1.0 + jnp.exp(-jnp.abs(v)))

def spread_states(bc_ref, wide_ref, pick_ref, rows, unroll=8):
    lane = lax.broadcasted_iota(jnp.int32, (STATE, 2 * STATE), 1)
    row = lax.broadcasted_iota(jnp.int32, (STATE, 2 * STATE), 0)
    mask = (lane % STATE == row).astype(jnp.float32)
    src = lax.broadcasted_iota(jnp.int32, (2 * STATE, 2 * LANES), 0)
    dst = lax.broadcasted_iota(jnp.int32, (2 * STATE, 2 * LANES), 1)
    route = ((src // STATE) == (dst // LANES)).astype(jnp.bfloat16)
    chunk = 32
    def step(i, _):
        t0 = pl.multiple_of(i * chunk, chunk)
        bcv = bc_ref[pl.ds(t0, chunk), :]
        for j in range(chunk):
            pick_ref[pl.ds(j * STATE, STATE), :] = (bcv[j:j + 1] * mask).astype(jnp.bfloat16)
        wide_ref[pl.ds(pl.multiple_of(t0 * STATE, chunk * STATE), chunk * STATE), :] = jnp.dot(pick_ref[...], route, preferred_element_type=jnp.float32)
        return 0
    lax.fori_loop(0, rows // chunk, step, 0)

def prep(step_ref_pre, act_ref, keep_ref, dstep_ref, dx_ref, rows):
    def body(i, _):
        sl = pl.ds(pl.multiple_of(i * 32, 32), 32)
        for g in range(dstep_ref.shape[0]):
            st = softplus(step_ref_pre[sl, lanes(g)])
            dstep_ref[g, sl, :] = jnp.where(keep_ref[sl, :] > 0.0, st, BIG)
            dx_ref[g, sl, :] = st * act_ref[sl, lanes(g)]
        return 0
    lax.fori_loop(0, rows // 32, body, 0)

def lanes(g):
    return pl.ds(g * LANES, LANES)

def group_sets(channels, width):
    n = channels // LANES
    return [list(range(i, min(i + width, n))) for i in range(0, n, width)]

def local_kernel(seqs, pre_ref, act_ref, bc_ref, keep_ref, dl_ref, end_ref, gain_ref, wide, pick, dstep, dx):
    rows, channels = pre_ref.shape
    length = rows // seqs
    spread_states(bc_ref, wide, pick, rows)
    prep(pre_ref, act_ref, keep_ref, dstep, dx, rows)
    for gs in group_sets(channels, 8):
        a2 = [-jnp.exp(dl_ref[:, lanes(g)]) * LOG2E for g in gs]
        for s in range(seqs):
            for k, g in enumerate(gs):
                tot = jnp.sum(dstep[g, pl.ds(s * length, length), :], axis=0, keepdims=True)
                gain_ref[pl.ds(s, 1), lanes(g)] = tot
            def blk(i, st):
                st = list(st)
                t0 = pl.multiple_of(s * length + i * 8, 8)
                for j in range(8):
                    b = wide[pl.ds(pl.multiple_of((t0 + j) * STATE, STATE), STATE), pl.ds(0, LANES)]
                    for k, g in enumerate(gs):
                        d = jnp.exp2(a2[k] * dstep[g, pl.ds(t0 + j, 1), :])
                        st[k] = d * st[k] + b * dx[g, pl.ds(t0 + j, 1), :]
                return tuple(st)
            st = lax.fori_loop(0, length // 8, blk, tuple(jnp.zeros((STATE, LANES), jnp.float32) for _ in gs))
            for k, g in enumerate(gs):
                end_ref[s, :, lanes(g)] = st[k]

VM = pl.BlockSpec(memory_space=pltpu.VMEM)

def scan_local(pre, act, bc, keep, dl, seqs, pins=()):
    rows, channels = pre.shape
    f = jnp.float32
    return pl.pallas_call(
        after(functools.partial(local_kernel, seqs), 5, pins),
        out_shape=[
            jax.ShapeDtypeStruct((seqs, STATE, channels), f),
            jax.ShapeDtypeStruct((seqs, channels), f),
        ],
        in_specs=[VM] * 5 + [ANY] * len(pins), out_specs=[VM] * 2,
        scratch_shapes=[pltpu.VMEM((rows * STATE, 2 * LANES), f), pltpu.VMEM((32 * STATE, 2 * STATE), jnp.bfloat16),
                        pltpu.VMEM((channels // LANES, rows, LANES), f), pltpu.VMEM((channels // LANES, rows, LANES), f)],
        compiler_params=pltpu.CompilerParams(vmem_limit_bytes=60 * 2**20),
        cost_estimate=cost(8),
        name="scan_local",
    )(pre, act, bc, keep, dl, *pins)

def forward_kernel(seqs, pre_ref, act_ref, bc_ref, keep_ref, dl_ref, in_ref, y_ref, wide, pick, dstep, dx, part):
    rows, channels = pre_ref.shape
    length = rows // seqs
    spread_states(bc_ref, wide, pick, rows)
    prep(pre_ref, act_ref, keep_ref, dstep, dx, rows)
    for gs in group_sets(channels, 4):
        a2 = [-jnp.exp(dl_ref[:, lanes(g)]) * LOG2E for g in gs]
        for s in range(seqs):
            def blk(i, st):
                st = list(st)
                t0 = pl.multiple_of(s * length + i * 8, 8)
                for j in range(8):
                    at = pl.ds(pl.multiple_of((t0 + j) * STATE, STATE), STATE)
                    b = wide[at, pl.ds(0, LANES)]
                    c = wide[at, pl.ds(LANES, LANES)]
                    for k, g in enumerate(gs):
                        d = jnp.exp2(a2[k] * dstep[g, pl.ds(t0 + j, 1), :])
                        st[k] = d * st[k] + b * dx[g, pl.ds(t0 + j, 1), :]
                        v = st[k] * c
                        part[k, pl.ds(pl.multiple_of(i * 64 + j * 8, 8), 8), :] = v[:8] + v[8:]
                return tuple(st)
            lax.fori_loop(0, length // 8, blk, tuple(in_ref[s, :, lanes(g)] for g in gs))
            def red(i, _):
                t0 = pl.multiple_of(s * length + i * 8, 8)
                for k, g in enumerate(gs):
                    acc = part[k, pl.ds(i * 64, 8, stride=8), :]
                    for m in range(1, 8):
                        acc = acc + part[k, pl.ds(i * 64 + m, 8, stride=8), :]
                    y_ref[pl.ds(t0, 8), lanes(g)] = acc
                return 0
            lax.fori_loop(0, length // 8, red, 0)

def scan_forward(pre, act, bc, keep, dl, state_in, seqs, pins=()):
    rows, channels = pre.shape
    f = jnp.float32
    return pl.pallas_call(
        after(functools.partial(forward_kernel, seqs), 6, pins),
        out_shape=jax.ShapeDtypeStruct((rows, channels), f),
        in_specs=[VM] * 6 + [ANY] * len(pins), out_specs=VM,
        scratch_shapes=[pltpu.VMEM((rows * STATE, 2 * LANES), f), pltpu.VMEM((32 * STATE, 2 * STATE), jnp.bfloat16),
                        pltpu.VMEM((channels // LANES, rows, LANES), f), pltpu.VMEM((channels // LANES, rows, LANES), f),
                        pltpu.VMEM((4, rows // seqs * 8, LANES), f)],
        compiler_params=pltpu.CompilerParams(vmem_limit_bytes=60 * 2**20),
        cost_estimate=cost(11),
        name="scan_forward",
    )(pre, act, bc, keep, dl, state_in, *pins)

LN2 = 0.6931471805599453

def back_local_kernel(seqs, pre_ref, gs_ref, bc_ref, keep_ref, dl_ref, out_ref, wide, pick, dstep, gsc):
    rows, channels = pre_ref.shape
    length = rows // seqs
    spread_states(bc_ref, wide, pick, rows)
    def body(i, _):
        sl = pl.ds(pl.multiple_of(i * 32, 32), 32)
        for g in range(channels // LANES):
            st = softplus(pre_ref[sl, lanes(g)])
            dstep[g, sl, :] = jnp.where(keep_ref[sl, :] > 0.0, st, BIG)
            gsc[g, sl, :] = gs_ref[sl, lanes(g)]
        return 0
    lax.fori_loop(0, rows // 32, body, 0)
    for gs in group_sets(channels, 8):
        a2 = [-jnp.exp(dl_ref[:, lanes(g)]) * LOG2E for g in gs]
        for s in range(seqs):
            def blk(i, st):
                st = list(st)
                t0 = pl.multiple_of(s * length + (length // 8 - 1 - i) * 8, 8)
                for j in reversed(range(8)):
                    c = wide[pl.ds(pl.multiple_of((t0 + j) * STATE, STATE), STATE), pl.ds(LANES, LANES)]
                    for k, g in enumerate(gs):
                        d = jnp.exp2(a2[k] * dstep[g, pl.ds(t0 + j, 1), :])
                        st[k] = d * (st[k] + c * gsc[g, pl.ds(t0 + j, 1), :])
                return tuple(st)
            st = lax.fori_loop(0, length // 8, blk, tuple(jnp.zeros((STATE, LANES), jnp.float32) for _ in gs))
            for k, g in enumerate(gs):
                out_ref[s, :, lanes(g)] = st[k]

def scan_back_local(pre, gs, bc, keep, dl, seqs, pins=()):
    rows, channels = pre.shape
    f = jnp.float32
    return pl.pallas_call(
        after(functools.partial(back_local_kernel, seqs), 5, pins),
        out_shape=jax.ShapeDtypeStruct((seqs, STATE, channels), f),
        in_specs=[VM] * 5 + [ANY] * len(pins), out_specs=VM,
        scratch_shapes=[pltpu.VMEM((rows * STATE, 2 * LANES), f), pltpu.VMEM((32 * STATE, 2 * STATE), jnp.bfloat16),
                        pltpu.VMEM((channels // LANES, rows, LANES), f), pltpu.VMEM((channels // LANES, rows, LANES), f)],
        compiler_params=pltpu.CompilerParams(vmem_limit_bytes=60 * 2**20),
        cost_estimate=cost(8),
        name="scan_back_local",
    )(pre, gs, bc, keep, dl, *pins)

def back_kernel(seqs, pre_ref, act_ref, gs_ref, bc_ref, keep_ref, dl_ref, skip_ref, in_ref, lam_ref,
                gpre_ref, gact_ref, gbc_ref, gdl_ref,
                wide, pick, dstep, dx, stepc, gsc, states, partq, partr, accb, accc, rowsum):
    rows, channels = pre_ref.shape
    length = rows // seqs
    f = jnp.float32
    spread_states(bc_ref, wide, pick, rows)
    def body(i, _):
        sl = pl.ds(pl.multiple_of(i * 32, 32), 32)
        for g in range(channels // LANES):
            st = softplus(pre_ref[sl, lanes(g)])
            stepc[g, sl, :] = st
            dstep[g, sl, :] = jnp.where(keep_ref[sl, :] > 0.0, st, BIG)
            dx[g, sl, :] = st * act_ref[sl, lanes(g)]
            gsc[g, sl, :] = gs_ref[sl, lanes(g)]
        return 0
    lax.fori_loop(0, rows // 32, body, 0)
    sets = group_sets(channels, 4)
    for index, gs in enumerate(sets):
        a2 = [-jnp.exp(dl_ref[:, lanes(g)]) * LOG2E for g in gs]
        gdl = [jnp.zeros((STATE, LANES), f) for _ in gs]
        for s in range(seqs):
            for k, g in enumerate(gs):
                states[k, pl.ds(0, STATE), :] = in_ref[s, :, lanes(g)]
            def fwd(i, st):
                st = list(st)
                t0 = pl.multiple_of(s * length + i * 8, 8)
                for j in range(8):
                    b = wide[pl.ds(pl.multiple_of((t0 + j) * STATE, STATE), STATE), pl.ds(0, LANES)]
                    for k, g in enumerate(gs):
                        d = jnp.exp2(a2[k] * dstep[g, pl.ds(t0 + j, 1), :])
                        st[k] = d * st[k] + b * dx[g, pl.ds(t0 + j, 1), :]
                        states[k, pl.ds(pl.multiple_of((i * 8 + j + 1) * STATE, STATE), STATE), :] = st[k]
                return tuple(st)
            lax.fori_loop(0, length // 8, fwd, tuple(in_ref[s, :, lanes(g)] for g in gs))
            def bwd(i, carry):
                st = list(carry[:len(gs)])
                am = list(carry[len(gs):])
                l0 = (length // 8 - 1 - i) * 8
                t0 = pl.multiple_of(s * length + l0, 8)
                for j in reversed(range(8)):
                    at = pl.ds(pl.multiple_of((t0 + j) * STATE, STATE), STATE)
                    b = wide[at, pl.ds(0, LANES)]
                    c = wide[at, pl.ds(LANES, LANES)]
                    tb = tc = None
                    here = pl.ds(pl.multiple_of((l0 + j) * 8, 8), 8)
                    for k, g in enumerate(gs):
                        row = pl.ds(t0 + j, 1)
                        grow = gsc[g, row, :]
                        d = jnp.exp2(a2[k] * dstep[g, row, :])
                        lam = st[k] + c * grow
                        old = states[k, pl.ds(pl.multiple_of((l0 + j) * STATE, STATE), STATE), :]
                        new = states[k, pl.ds(pl.multiple_of((l0 + j + 1) * STATE, STATE), STATE), :]
                        st[k] = d * lam
                        lp = st[k] * old
                        q = lam * b
                        partq[k, here, :] = q[:8] + q[8:]
                        r = lp * a2[k]
                        partr[k, here, :] = r[:8] + r[8:]
                        am[k] = am[k] + lp * stepc[g, row, :]
                        u = lam * dx[g, row, :]
                        v = new * grow
                        tb = u if tb is None else tb + u
                        tc = v if tc is None else tc + v
                    if index > 0:
                        tb = tb + accb[at, :]
                        tc = tc + accc[at, :]
                    accb[at, :] = tb
                    accc[at, :] = tc
                return tuple(st) + tuple(am)
            out = lax.fori_loop(0, length // 8, bwd, tuple(lam_ref[s, :, lanes(g)] for g in gs) + tuple(gdl))
            gdl = list(out[len(gs):])
            def red(i, _):
                t0 = pl.multiple_of(s * length + i * 8, 8)
                for k, g in enumerate(gs):
                    q = partq[k, pl.ds(i * 64, 8, stride=8), :]
                    r = partr[k, pl.ds(i * 64, 8, stride=8), :]
                    for m in range(1, 8):
                        q = q + partq[k, pl.ds(i * 64 + m, 8, stride=8), :]
                        r = r + partr[k, pl.ds(i * 64 + m, 8, stride=8), :]
                    here = pl.ds(t0, 8)
                    p = pre_ref[here, lanes(g)]
                    gstep = r * LN2 + act_ref[here, lanes(g)] * q
                    gpre_ref[here, lanes(g)] = gstep * (1.0 / (1.0 + jnp.exp(-p)))
                    gact_ref[here, lanes(g)] = stepc[g, here, :] * q + gsc[g, here, :] * skip_ref[:, lanes(g)]
                return 0
            lax.fori_loop(0, length // 8, red, 0)
        for k, g in enumerate(gs):
            gdl_ref[:, lanes(g)] = gdl[k] * (a2[k] * LN2)
    ones = jnp.ones((LANES, LANES), jnp.bfloat16)
    lane = lax.broadcasted_iota(jnp.int32, (32 * STATE, LANES), 1)
    row = lax.broadcasted_iota(jnp.int32, (32 * STATE, LANES), 0) % STATE
    mb = lane == row
    mc = lane == row + STATE
    def fin(i, _):
        sl = pl.ds(pl.multiple_of(i * 32 * STATE, 32 * STATE), 32 * STATE)
        sb = jnp.dot(accb[sl, :].astype(jnp.bfloat16), ones, preferred_element_type=f)
        sc = jnp.dot(accc[sl, :].astype(jnp.bfloat16), ones, preferred_element_type=f)
        rowsum[...] = jnp.where(mb, sb, jnp.where(mc, sc, 0.0))
        acc = rowsum[pl.ds(0, 32, stride=STATE), :]
        for m in range(1, STATE):
            acc = acc + rowsum[pl.ds(m, 32, stride=STATE), :]
        gbc_ref[pl.ds(pl.multiple_of(i * 32, 32), 32), :] = acc
        return 0
    lax.fori_loop(0, rows // 32, fin, 0)

def scan_back(pre, act, gs, bc, keep, dl, skip, state_in, lam_in, seqs, pins=()):
    rows, channels = pre.shape
    f = jnp.float32
    groups = channels // LANES
    length = rows // seqs
    big = pltpu.VMEM((groups, rows, LANES), f)
    return pl.pallas_call(
        after(functools.partial(back_kernel, seqs), 9, pins),
        out_shape=[jax.ShapeDtypeStruct((rows, channels), f), jax.ShapeDtypeStruct((rows, channels), f),
                   jax.ShapeDtypeStruct((rows, LANES), f), jax.ShapeDtypeStruct((STATE, channels), f)],
        in_specs=[VM] * 9 + [ANY] * len(pins), out_specs=[VM] * 4,
        scratch_shapes=[pltpu.VMEM((rows * STATE, 2 * LANES), f), pltpu.VMEM((32 * STATE, 2 * STATE), jnp.bfloat16),
                        big, big, big, big,
                        pltpu.VMEM((4, (length + 1) * STATE, LANES), f),
                        pltpu.VMEM((4, length * 8, LANES), f), pltpu.VMEM((4, length * 8, LANES), f),
                        pltpu.VMEM((rows * STATE, LANES), f), pltpu.VMEM((rows * STATE, LANES), f),
                        pltpu.VMEM((32 * STATE, LANES), f)],
        compiler_params=pltpu.CompilerParams(vmem_limit_bytes=60 * 2**20),
        cost_estimate=cost(23),
        name="scan_back",
    )(pre, act, gs, bc, keep, dl, skip, state_in, lam_in, *pins)


def greet(peers):
    barrier = pltpu.get_barrier_semaphore()
    for p in peers:
        pl.semaphore_signal(barrier, inc=1, device_id=p, device_id_type=MESH)
    pl.semaphore_wait(barrier, len(peers))

def ch_sum_kernel(n, x_ref, out_ref, mine, slots, send, recv):
    me = lax.axis_index("ch")
    peers = [{"ch": lax.rem(me + d, n)} for d in range(1, n)]
    greet(peers)
    mine[...] = x_ref[...].astype(bf16)
    copies = []
    for d in range(1, n):
        c = pltpu.make_async_remote_copy(src_ref=mine, dst_ref=slots.at[d - 1], send_sem=send.at[d - 1], recv_sem=recv.at[d - 1], device_id=peers[d - 1], device_id_type=MESH)
        c.start()
        copies.append(c)
    total = x_ref[...].astype(bf16).astype(f32)
    for d, c in zip(range(1, n), copies):
        c.wait()
        total = total + slots[d - 1].astype(f32)
    out_ref[...] = total

def ch_sum(x, n, cid):
    return pl.pallas_call(
        functools.partial(ch_sum_kernel, n),
        out_shape=jax.ShapeDtypeStruct(x.shape, f32), in_specs=[VM], out_specs=VM,
        scratch_shapes=[pltpu.VMEM(x.shape, bf16), pltpu.VMEM((n - 1,) + x.shape, bf16), pltpu.SemaphoreType.DMA((n - 1,)), pltpu.SemaphoreType.DMA((n - 1,))],
        compiler_params=pltpu.CompilerParams(collective_id=cid, has_side_effects=True, vmem_limit_bytes=32 * 2**20), cost_estimate=cost(10), name="ch_sum",
    )(x)

def reduce_kernel(n, parts, gather, x_ref, out_ref, s1, sum1, s2, mine, got, fin, sem1, rem1, sem2, rem2, sem3, rem3, sem4, rem4):
    xs = n // 2
    me = lax.axis_index("ch")
    x, core = me // 2, lax.rem(me, 2)
    peer = {"ch": x * 2 + 1 - core}
    others = [lax.rem(x + d, xs) for d in range(1, xs)]
    greet([peer] + [{"ch": o * 2 + core} for o in others])
    rows, width = x_ref.shape[0] // parts, x_ref.shape[1] // n
    def cols(block):
        return pl.ds(pl.multiple_of(block * width, width), width)
    def stage1(p, k):
        return pltpu.make_async_remote_copy(src_ref=x_ref.at[pl.ds(p * rows, rows), cols(k * 2 + 1 - core)], dst_ref=s1.at[p, k], send_sem=sem1.at[p, k], recv_sem=rem1.at[p, k], device_id=peer, device_id_type=MESH)
    def stage2(p, d):
        o = others[d]
        return pltpu.make_async_remote_copy(src_ref=sum1.at[p, o], dst_ref=s2.at[p, d], send_sem=sem2.at[p, d], recv_sem=rem2.at[p, d], device_id={"ch": o * 2 + core}, device_id_type=MESH)
    def stage3(p, d):
        o = others[d]
        return pltpu.make_async_remote_copy(src_ref=mine.at[p], dst_ref=got.at[p, d], send_sem=sem3.at[p, d], recv_sem=rem3.at[p, d], device_id={"ch": o * 2 + core}, device_id_type=MESH)
    for p in range(parts):
        for k in range(xs):
            stage1(p, k).start()
    for p in range(parts):
        for k in range(xs):
            stage1(p, k).wait_recv()
            sum1[p, k] = (x_ref[pl.ds(p * rows, rows), cols(k * 2 + core)].astype(f32) + s1[p, k].astype(f32)).astype(bf16)
        for d in range(xs - 1):
            stage2(p, d).start()
    for p in range(parts):
        total = sum1[p, x].astype(f32)
        for d in range(xs - 1):
            stage2(p, d).wait_recv()
            total = total + s2[p, d].astype(f32)
        if gather:
            mine[p] = total.astype(bf16)
            for d in range(xs - 1):
                stage3(p, d).start()
        else:
            out_ref[pl.ds(p * rows, rows), :] = total
    if gather:
        def stage4(p, d):
            src = mine.at[p] if d < 0 else got.at[p, d]
            return pltpu.make_async_remote_copy(src_ref=src, dst_ref=fin.at[p, d + 1], send_sem=sem4.at[p, d + 1], recv_sem=rem4.at[p, d + 1], device_id=peer, device_id_type=MESH)
        def chip(d):
            return lax.rem(x + xs - 1 - d, xs)
        for p in range(parts):
            stage4(p, -1).start()
            out_ref[pl.ds(p * rows, rows), cols(me)] = mine[p].astype(out_ref.dtype)
            for d in range(xs - 1):
                stage3(p, d).wait_recv()
                stage4(p, d).start()
                out_ref[pl.ds(p * rows, rows), cols(chip(d) * 2 + core)] = got[p, d].astype(out_ref.dtype)
        for p in range(parts):
            for d in range(-1, xs - 1):
                stage4(p, d).wait_recv()
                out_ref[pl.ds(p * rows, rows), cols(chip(d) * 2 + 1 - core)] = fin[p, d + 1].astype(out_ref.dtype)
    for p in range(parts):
        for k in range(xs):
            stage1(p, k).wait_send()
        for d in range(xs - 1):
            stage2(p, d).wait_send()
            if gather:
                stage3(p, d).wait_send()
        if gather:
            for d in range(-1, xs - 1):
                stage4(p, d).wait_send()

def ch_reduce(x, n, cid, gather, parts=2, out_dtype=f32):
    rows, width = x.shape
    xs, r, w = n // 2, rows // parts, width // n
    sem = pltpu.SemaphoreType.DMA
    return pl.pallas_call(
        functools.partial(reduce_kernel, n, parts, gather),
        out_shape=jax.ShapeDtypeStruct((rows, width if gather else w), out_dtype), in_specs=[VM], out_specs=VM,
        scratch_shapes=[pltpu.VMEM((parts, xs, r, w), bf16), pltpu.VMEM((parts, xs, r, w), bf16), pltpu.VMEM((parts, xs - 1, r, w), bf16),
                        pltpu.VMEM((parts, r, w), bf16), pltpu.VMEM((parts, xs - 1, r, w), bf16), pltpu.VMEM((parts, xs, r, w), bf16),
                        sem((parts, xs)), sem((parts, xs)), sem((parts, xs - 1)), sem((parts, xs - 1)), sem((parts, xs - 1)), sem((parts, xs - 1)), sem((parts, xs)), sem((parts, xs))],
        compiler_params=pltpu.CompilerParams(collective_id=cid, has_side_effects=True, vmem_limit_bytes=48 * 2**20), cost_estimate=cost(18), name="ch_reduce",
    )(x)


def carry_kernel(n, fwd, rev, *refs):
    refs = list(refs)
    tot_ref, dl_ref = refs.pop(0), refs.pop(0)
    k = fwd + rev
    ends = [refs.pop(0) for _ in range(k)]
    outs = [refs.pop(0) for _ in range(k)]
    mine, slots, tots, send, recv, tsend, trecv = refs
    me = lax.axis_index("seq")
    seqs = tot_ref.shape[0]
    greet([{"seq": lax.rem(me + d, n)} for d in range(1, n)])
    a2 = -jnp.exp(dl_ref[...]) * LOG2E
    directions = [False] * fwd + [True] * rev
    def copies(i, d):
        away = -d if directions[i] else d
        to = {"seq": lax.rem(me + away + n, n)}
        return (
            pltpu.make_async_remote_copy(src_ref=mine.at[i], dst_ref=slots.at[i, d - 1], send_sem=send.at[i, d - 1], recv_sem=recv.at[i, d - 1], device_id=to, device_id_type=MESH),
            pltpu.make_async_remote_copy(src_ref=tot_ref, dst_ref=tots.at[i, d - 1], send_sem=tsend.at[i, d - 1], recv_sem=trecv.at[i, d - 1], device_id=to, device_id_type=MESH),
        )
    for i in range(k):
        mine[i] = ends[i][...].astype(bf16)
        outs[i][...] = jnp.zeros_like(outs[i])
    for d in reversed(range(1, n)):
        for i in range(k):
            place = n - 1 - me if directions[i] else me
            @pl.when(place + d < n)
            def _():
                for c in copies(i, d):
                    c.start()
    for d in reversed(range(1, n)):
        for i in range(k):
            place = n - 1 - me if directions[i] else me
            @pl.when(place >= d)
            def _():
                for c in copies(i, d):
                    c.wait_recv()
                for s in range(seqs):
                    gain = jnp.exp2(a2 * tots[i, d - 1, pl.ds(s, 1), :])
                    outs[i][s] = gain * outs[i][s] + slots[i, d - 1, s].astype(f32)
    for d in reversed(range(1, n)):
        for i in range(k):
            place = n - 1 - me if directions[i] else me
            @pl.when(place + d < n)
            def _():
                for c in copies(i, d):
                    c.wait_send()

def carry_over(tot, dl, ends, n, cid, fwd, rev):
    k = len(ends)
    sem = pltpu.SemaphoreType.DMA
    return pl.pallas_call(
        functools.partial(carry_kernel, n, int(fwd), int(rev)),
        out_shape=[jax.ShapeDtypeStruct(ends[0].shape, f32)] * k, in_specs=[VM] * (k + 2), out_specs=[VM] * k,
        scratch_shapes=[pltpu.VMEM((k,) + ends[0].shape, bf16), pltpu.VMEM((k, n - 1) + ends[0].shape, bf16), pltpu.VMEM((k, n - 1) + tot.shape, f32),
                        sem((k, n - 1)), sem((k, n - 1)), sem((k, n - 1)), sem((k, n - 1))],
        compiler_params=pltpu.CompilerParams(collective_id=cid, has_side_effects=True, vmem_limit_bytes=32 * 2**20), cost_estimate=cost(19), name="carry_over",
    )(tot, dl, *ends)


def passed_along(block, axis, distance):
    devices = range(lax.axis_size(axis))
    route = [(i - distance, i) for i in devices if i - distance in devices]
    return lax.ppermute(block, axis, route)


def silu_slope(argument):
    logistic = jax.nn.sigmoid(argument)
    return logistic * (1.0 + argument * (1.0 - logistic))


def conv_local(extended, weights, biases, seg_ext):
    length_now = extended.shape[1] - (KERN - 1)
    seg_now = seg_ext[:, KERN - 1 :]
    summed = biases + jnp.zeros((extended.shape[0], length_now, extended.shape[2]), f32)
    for lag_index in range(KERN):
        same_doc = (seg_ext[:, lag_index : lag_index + length_now] == seg_now).astype(f32)
        summed = (
            summed
            + weights[lag_index]
            * extended[:, lag_index : lag_index + length_now]
            * same_doc[:, :, None]
        )
    return summed


def dot(a, b, contract):
    return lax.dot_general(a, b, ((contract[:1], contract[1:]), ((), ())), preferred_element_type=f32)


def tokens_of_all(rows):
    return lax.all_gather(rows, "seq", tiled=True)


def columns_of_all(rows):
    n = lax.axis_size("seq")
    return lax.all_to_all(rows, "seq", split_axis=1, concat_axis=0, tiled=True)


def local(
    hidden_in,
    segments,
    cotangent,
    norm_gain,
    input_projection_weight,
    conv_weight,
    conv_bias,
    proj_weight,
    step_weight,
    step_bias,
    decay_log,
    skip_gain,
    output_projection_weight,
):
    seqs, length, width = hidden_in.shape
    rows = seqs * length
    nch, nseq = lax.axis_size("ch"), lax.axis_size("seq")
    channels = conv_bias.shape[-1]
    share = width // nch
    share_start = lax.axis_index("ch") * share
    seg_own = segments.astype(f32)
    seg_edge = passed_along(seg_own[:, -(KERN - 1) :], "seq", 1)
    seg_ext = jnp.concatenate([seg_edge, seg_own], axis=1)
    keep = (seg_ext[:, KERN - 2 : -1] == seg_own).astype(f32).reshape(-1, 1)
    hidden = hidden_in.astype(f32).reshape(rows, width)
    grad_rows = cotangent.astype(f32).reshape(rows, width)
    ids = iter(range(100))

    out_cols = {LAYERS - 1: columns_of_all(grad_rows.astype(bf16))}
    stored = []
    result = None
    ready = {(0, "local"): (out_cols[LAYERS - 1],)}
    for layer in range(LAYERS):
        last = layer == LAYERS - 1
        inv_rms = lax.rsqrt(jnp.mean(hidden * hidden, axis=-1, keepdims=True) + epsilon)
        normed = (hidden * inv_rms * norm_gain[layer]).astype(bf16)
        w_in = lax.optimization_barrier(input_projection_weight)[layer]
        both = lax.dot_general(normed, w_in, (((1,), (0,)), ((), ())), preferred_element_type=f32)
        values, gate_pre = both[:, 0], both[:, 1]
        normed_cols = columns_of_all(normed)
        values3 = values.reshape(seqs, length, channels)
        edge = passed_along(values3[:, -(KERN - 1) :], "seq", 1)
        extended = jnp.concatenate([edge, values3], axis=1)
        conv_out, conv_pull = jax.vjp(
            functools.partial(conv_local, seg_ext=seg_ext), extended, conv_weight[layer], conv_bias[layer]
        )
        conv_out = conv_out.reshape(rows, channels)
        activated = jax.nn.silu(conv_out)
        act_low = activated.astype(bf16)
        proj_out = ch_sum(dot(act_low, proj_weight[layer], (1, 0)), nch, next(ids))
        rank_low = proj_out[:, :RANK].astype(bf16)
        mats = proj_out[:, RANK:]
        step_pre = dot(rank_low, step_weight[layer], (1, 0)) + step_bias[layer]
        rates = decay_log[layer]
        end_state, total = scan_local(
            step_pre, activated, mats, keep, rates, seqs, ready.get((layer, "local"), ())
        )
        gate_act = jax.nn.silu(gate_pre)
        if last:
            out_low = grad_rows.astype(bf16)
            grad_mixed = dot(out_low, output_projection_weight[layer], (1, 1))
            grad_scan = grad_mixed * gate_act
            start = scan_back_local(step_pre, grad_scan, mats, keep, rates, seqs)
            state_in, lam_in = carry_over(total, rates, [end_state, start], nseq, next(ids), True, True)
        else:
            (state_in,) = carry_over(total, rates, [end_state], nseq, next(ids), True, False)
        pins = (normed_cols,) if layer == 0 else (normed_cols, stored[0][-2])
        y = scan_forward(step_pre, activated, mats, keep, rates, state_in, seqs, pins)
        scanned = y + skip_gain[layer] * activated
        mixed = (scanned * gate_act).astype(bf16)
        out_part = dot(mixed, output_projection_weight[layer], (1, 0)).astype(bf16)
        mixed_all = tokens_of_all(mixed)
        stored.append(
            (hidden, inv_rms, normed, gate_pre, gate_act, conv_out, activated, act_low, conv_pull, rank_low,
             step_pre, mats, total, state_in, scanned, mixed_all, normed_cols)
        )
        if last:
            branch = ch_reduce(out_part, nch, next(ids), False)
            result = (lax.dynamic_slice_in_dim(hidden, share_start, share, 1) + branch).astype(bf16)
        else:
            hidden = hidden + ch_reduce(out_part, nch, next(ids), True)

    collected = [None] * LAYERS
    for layer in reversed(range(LAYERS)):
        last = layer == LAYERS - 1
        (hidden, inv_rms, normed, gate_pre, gate_act, conv_out, activated, act_low, conv_pull, rank_low,
         step_pre, mats, total, state_in, scanned, mixed_all, normed_cols) = stored[layer]
        rates = decay_log[layer]
        if not last:
            out_low = grad_rows.astype(bf16)
            grad_mixed = dot(out_low, output_projection_weight[layer], (1, 1))
            grad_scan = grad_mixed * gate_act
            start = scan_back_local(step_pre, grad_scan, mats, keep, rates, seqs, (stored[layer + 1][-2],))
            (lam_in,) = carry_over(total, rates, [start], nseq, next(ids), False, True)
            out_cols[layer] = columns_of_all(out_low)
        grad_gate = (grad_mixed * scanned * silu_slope(gate_pre)).astype(bf16)
        gate_all = tokens_of_all(grad_gate)
        grad_skip = jnp.sum(grad_scan * activated, axis=0)
        grad_pre, grad_act, grad_mats, grad_decay = scan_back(
            step_pre, activated, grad_scan, mats, keep, rates, skip_gain[layer][None], state_in, lam_in, seqs,
            () if last else (out_cols[layer], gate_all_last),
        )
        gate_all_last = gate_all
        grad_step_bias = jnp.sum(grad_pre, axis=0)
        pre_low = grad_pre.astype(bf16)
        grad_step_weight = dot(rank_low, pre_low, (0, 0))
        rank_part = dot(pre_low, step_weight[layer], (1, 1))
        grad_proj = ch_sum(
            jnp.concatenate([rank_part, grad_mats[:, : 2 * STATE]], axis=-1), nch, next(ids)
        ).astype(bf16)
        grad_proj_weight = dot(act_low, grad_proj, (0, 0))
        grad_act = grad_act + dot(grad_proj, proj_weight[layer], (1, 1))
        grad_conv = (grad_act * silu_slope(conv_out)).reshape(seqs, length, channels)
        grad_ext, grad_conv_weight, grad_conv_bias = conv_pull(grad_conv)
        returned = passed_along(grad_ext[:, : KERN - 1], "seq", -1)
        grad_values = grad_ext[:, KERN - 1 :]
        grad_values = jnp.concatenate(
            [grad_values[:, : -(KERN - 1)], grad_values[:, -(KERN - 1) :] + returned], axis=1
        ).reshape(rows, channels).astype(bf16)
        values_all = tokens_of_all(grad_values)
        w_in = lax.optimization_barrier(input_projection_weight)[layer]
        grad_both = jnp.stack([grad_values, grad_gate], axis=1)
        grad_part = lax.dot_general(grad_both, w_in, (((1, 2), (1, 2)), ((), ())), preferred_element_type=f32)
        grad_normed = ch_reduce(grad_part.astype(bf16), nch, next(ids), True)
        scale_now = norm_gain[layer]
        inner = jnp.sum(grad_normed * scale_now * hidden, axis=-1, keepdims=True)
        grad_hidden = inv_rms * scale_now * grad_normed - hidden * (inv_rms * inv_rms * inv_rms) * inner / width
        grad_norm = lax.dynamic_slice_in_dim(jnp.sum(grad_normed * hidden * inv_rms, axis=0), share_start, share, 0)
        grad_rows = grad_rows + grad_hidden
        grad_out_weight = dot(mixed_all, out_cols[layer], (0, 0))
        grad_in_gate = dot(normed_cols, gate_all, (0, 0))
        grad_in_values = dot(normed_cols, values_all, (0, 0))
        small = [grad_norm, grad_conv_weight, grad_conv_bias, grad_proj_weight, grad_step_weight, grad_step_bias, grad_decay, grad_skip]
        small = [v.astype(bf16) for v in small]
        if not last:
            small, _ = lax.optimization_barrier((small, collected[LAYERS - 1]))
        small = [lax.psum(v, "seq").astype(f32) for v in small]
        collected[layer] = (
            small[0],
            jnp.stack([grad_in_values, grad_in_gate], axis=1),
            *small[1:],
            grad_out_weight,
        )
    grad_input = lax.dynamic_slice_in_dim(grad_rows, share_start, share, 1).reshape(seqs, length, share)
    stacked = [jnp.stack([collected[layer][member] for layer in range(LAYERS)], axis=0) for member in range(10)]
    return (result.reshape(seqs, length, share), grad_input, *stacked)


def solution(mesh):
    in_specs = (
        P(None, "seq", None),
        P(None, "seq"),
        P(None, "seq", None),
        P(),
        P(None, None, None, "ch"),
        P(None, None, "ch"),
        P(None, "ch"),
        P(None, "ch", None),
        P(None, None, "ch"),
        P(None, "ch"),
        P(None, None, "ch"),
        P(None, "ch"),
        P(None, "ch", None),
    )
    out_specs = (
        P(None, "seq", "ch"),
        P(None, "seq", "ch"),
        P(None, "ch"),
        P(None, "seq", None, "ch"),
        P(None, None, "ch"),
        P(None, "ch"),
        P(None, "ch", None),
        P(None, None, "ch"),
        P(None, "ch"),
        P(None, None, "ch"),
        P(None, "ch"),
        P(None, "ch", "seq"),
    )
    return jax.shard_map(local, mesh=mesh, in_specs=in_specs, out_specs=out_specs, check_vma=False)
```

```python
import functools

import jax
import jax.numpy as jnp
from jax import lax
from jax.experimental import pallas as pl
from jax.experimental.pallas import tpu as pltpu
from jax.sharding import PartitionSpec as P

STATE = 16
RANK = 128
KERN = 4
LAYERS = 2
MESH = pl.DeviceIdType.MESH
ANY = pl.BlockSpec(memory_space=pl.ANY)
f32, bf16 = jnp.float32, jnp.bfloat16
epsilon = 1e-05


def after(kernel, count, pins):
    def run(*refs):
        return kernel(*refs[:count], *refs[count + len(pins) :])
    return run


def cost(us):
    return pl.CostEstimate(flops=int(us * 1.0e9), bytes_accessed=0, transcendentals=0)


LANES = 128
BIG = 1e30
LOG2E = 1.4426950408889634

def softplus(v):
    return jnp.maximum(v, 0.0) + jnp.log(1.0 + jnp.exp(-jnp.abs(v)))

def spread_states(bc_ref, wide_ref, pick_ref, rows, unroll=8):
    lane = lax.broadcasted_iota(jnp.int32, (STATE, 2 * STATE), 1)
    row = lax.broadcasted_iota(jnp.int32, (STATE, 2 * STATE), 0)
    mask = (lane % STATE == row).astype(jnp.float32)
    src = lax.broadcasted_iota(jnp.int32, (2 * STATE, 2 * LANES), 0)
    dst = lax.broadcasted_iota(jnp.int32, (2 * STATE, 2 * LANES), 1)
    route = ((src // STATE) == (dst // LANES)).astype(jnp.bfloat16)
    chunk = 32
    def step(i, _):
        t0 = pl.multiple_of(i * chunk, chunk)
        bcv = bc_ref[pl.ds(t0, chunk), :]
        for j in range(chunk):
            pick_ref[pl.ds(j * STATE, STATE), :] = (bcv[j:j + 1] * mask).astype(jnp.bfloat16)
        wide_ref[pl.ds(pl.multiple_of(t0 * STATE, chunk * STATE), chunk * STATE), :] = jnp.dot(pick_ref[...], route, preferred_element_type=jnp.float32)
        return 0
    lax.fori_loop(0, rows // chunk, step, 0)

def prep(step_ref_pre, act_ref, keep_ref, dstep_ref, dx_ref, rows):
    def body(i, _):
        sl = pl.ds(pl.multiple_of(i * 32, 32), 32)
        for g in range(dstep_ref.shape[0]):
            st = softplus(step_ref_pre[sl, lanes(g)])
            dstep_ref[g, sl, :] = jnp.where(keep_ref[sl, :] > 0.0, st, BIG)
            dx_ref[g, sl, :] = st * act_ref[sl, lanes(g)]
        return 0
    lax.fori_loop(0, rows // 32, body, 0)

def lanes(g):
    return pl.ds(g * LANES, LANES)

def group_sets(channels, width):
    n = channels // LANES
    return [list(range(i, min(i + width, n))) for i in range(0, n, width)]

def local_kernel(seqs, pre_ref, act_ref, bc_ref, keep_ref, dl_ref, end_ref, gain_ref, wide, pick, dstep, dx):
    rows, channels = pre_ref.shape
    length = rows // seqs
    spread_states(bc_ref, wide, pick, rows)
    prep(pre_ref, act_ref, keep_ref, dstep, dx, rows)
    yield
    for gs in group_sets(channels, 8):
        a2 = [-jnp.exp(dl_ref[:, lanes(g)]) * LOG2E for g in gs]
        for s in range(seqs):
            for k, g in enumerate(gs):
                tot = jnp.sum(dstep[g, pl.ds(s * length, length), :], axis=0, keepdims=True)
                gain_ref[pl.ds(s, 1), lanes(g)] = tot
            def blk(i, st):
                st = list(st)
                t0 = pl.multiple_of(s * length + i * 8, 8)
                for j in range(8):
                    b = wide[pl.ds(pl.multiple_of((t0 + j) * STATE, STATE), STATE), pl.ds(0, LANES)]
                    for k, g in enumerate(gs):
                        d = jnp.exp2(a2[k] * dstep[g, pl.ds(t0 + j, 1), :])
                        st[k] = d * st[k] + b * dx[g, pl.ds(t0 + j, 1), :]
                return tuple(st)
            st = lax.fori_loop(0, length // 8, blk, tuple(jnp.zeros((STATE, LANES), jnp.float32) for _ in gs))
            for k, g in enumerate(gs):
                end_ref[s, :, lanes(g)] = st[k]
            yield

VM = pl.BlockSpec(memory_space=pltpu.VMEM)


def played(kernel, counts, plan, places):
    n_in, n_out, n_scratch = counts

    def run(*refs):
        refs = list(refs)

        def take(k):
            head, refs[:] = refs[:k], refs[k:]
            return head

        own = take(n_in)
        sources = take(len(plan))
        own += take(n_out)
        targets = take(len(plan))
        own += take(n_scratch)
        jobs = []
        for (kind, when), src, out in zip(plan, sources, targets):
            jobs.append((kind(*places, src, out, take(kind.semaphores)), when))
        if plan:
            seq, ch = lax.axis_index("seq"), lax.axis_index("ch")
            zs, ys = places
            z, y = seq // ys, lax.rem(seq, ys)
            peers = [{"seq": lax.rem(z + d, zs) * ys + y} for d in range(1, zs)]
            peers += [{"seq": z * ys + lax.rem(y + d, ys)} for d in range(1, ys)]
            xs = lax.axis_size("ch") // 2
            peers += [{"ch": lax.rem(ch // 2 + e, xs) * 2 + lax.rem(ch, 2)} for e in range(1, xs)]
            peers.append({"ch": ch + 1 - 2 * lax.rem(ch, 2)})
            barrier = pltpu.get_barrier_semaphore()
            for peer in peers:
                pl.semaphore_signal(barrier, inc=1, device_id=peer, device_id_type=MESH)
        for at, _ in enumerate(kernel(*own)):
            if at == 0 and plan:
                pl.semaphore_wait(barrier, len(peers))
                for job, _ in jobs:
                    job.begin()
            for job, when in jobs:
                if at in when:
                    job.step(when.index(at))
        for job, when in jobs:
            job.finish()

    return run


def play_call(kernel, counts, plan, places, cid, out_shape, scratch, arrays, us, name, pins=()):
    arrays = list(arrays) + [v for _, _, v in plan]
    kinds = [(kind, when) for kind, when, _ in plan]
    out_shape = list(out_shape) + [kind.result(v, *places) for kind, _, v in plan]
    sems = [spec for kind, _, v in plan for spec in kind.specs(v, *places)]
    extra = dict(collective_id=cid, has_side_effects=True) if plan else {}
    return pl.pallas_call(
        after(played(kernel, counts, kinds, places), len(arrays), pins),
        out_shape=out_shape,
        in_specs=[VM] * len(arrays) + [ANY] * len(pins),
        out_specs=[VM] * len(out_shape),
        scratch_shapes=list(scratch) + sems,
        compiler_params=pltpu.CompilerParams(vmem_limit_bytes=60 * 2**20, **extra),
        cost_estimate=cost(us),
        name=name,
    )(*arrays, *pins)

def scan_local(pre, act, bc, keep, dl, seqs, plan, places, cid):
    rows, channels = pre.shape
    f = jnp.float32
    big = pltpu.VMEM((channels // LANES, rows, LANES), f)
    return play_call(
        functools.partial(local_kernel, seqs), (5, 2, 4), plan, places, cid,
        [jax.ShapeDtypeStruct((seqs, STATE, channels), f), jax.ShapeDtypeStruct((seqs, channels), f)],
        [pltpu.VMEM((rows * STATE, 2 * LANES), f), pltpu.VMEM((32 * STATE, 2 * STATE), jnp.bfloat16), big, big],
        (pre, act, bc, keep, dl), 8, "scan_local",
    )


def forward_kernel(seqs, pre_ref, act_ref, bc_ref, keep_ref, dl_ref, in_ref, y_ref, wide, pick, dstep, dx, part):
    rows, channels = pre_ref.shape
    length = rows // seqs
    spread_states(bc_ref, wide, pick, rows)
    prep(pre_ref, act_ref, keep_ref, dstep, dx, rows)
    yield
    for gs in group_sets(channels, 4):
        a2 = [-jnp.exp(dl_ref[:, lanes(g)]) * LOG2E for g in gs]
        for s in range(seqs):
            def blk(i, st):
                st = list(st)
                t0 = pl.multiple_of(s * length + i * 8, 8)
                for j in range(8):
                    at = pl.ds(pl.multiple_of((t0 + j) * STATE, STATE), STATE)
                    b = wide[at, pl.ds(0, LANES)]
                    c = wide[at, pl.ds(LANES, LANES)]
                    for k, g in enumerate(gs):
                        d = jnp.exp2(a2[k] * dstep[g, pl.ds(t0 + j, 1), :])
                        st[k] = d * st[k] + b * dx[g, pl.ds(t0 + j, 1), :]
                        v = st[k] * c
                        part[k, pl.ds(pl.multiple_of(i * 64 + j * 8, 8), 8), :] = v[:8] + v[8:]
                return tuple(st)
            lax.fori_loop(0, length // 8, blk, tuple(in_ref[s, :, lanes(g)] for g in gs))
            def red(i, _):
                t0 = pl.multiple_of(s * length + i * 8, 8)
                for k, g in enumerate(gs):
                    acc = part[k, pl.ds(i * 64, 8, stride=8), :]
                    for m in range(1, 8):
                        acc = acc + part[k, pl.ds(i * 64 + m, 8, stride=8), :]
                    y_ref[pl.ds(t0, 8), lanes(g)] = acc
                return 0
            lax.fori_loop(0, length // 8, red, 0)
            yield

def scan_forward(pre, act, bc, keep, dl, state_in, seqs, plan, places, cid):
    rows, channels = pre.shape
    f = jnp.float32
    big = pltpu.VMEM((channels // LANES, rows, LANES), f)
    return play_call(
        functools.partial(forward_kernel, seqs), (6, 1, 5), plan, places, cid,
        [jax.ShapeDtypeStruct((rows, channels), f)],
        [pltpu.VMEM((rows * STATE, 2 * LANES), f), pltpu.VMEM((32 * STATE, 2 * STATE), jnp.bfloat16), big, big,
         pltpu.VMEM((4, rows // seqs * 8, LANES), f)],
        (pre, act, bc, keep, dl, state_in), 11, "scan_forward",
    )


LN2 = 0.6931471805599453

def back_local_kernel(seqs, pre_ref, gs_ref, bc_ref, keep_ref, dl_ref, out_ref, wide, pick, dstep, gsc):
    rows, channels = pre_ref.shape
    length = rows // seqs
    spread_states(bc_ref, wide, pick, rows)
    def body(i, _):
        sl = pl.ds(pl.multiple_of(i * 32, 32), 32)
        for g in range(channels // LANES):
            st = softplus(pre_ref[sl, lanes(g)])
            dstep[g, sl, :] = jnp.where(keep_ref[sl, :] > 0.0, st, BIG)
            gsc[g, sl, :] = gs_ref[sl, lanes(g)]
        return 0
    lax.fori_loop(0, rows // 32, body, 0)
    for gs in group_sets(channels, 8):
        a2 = [-jnp.exp(dl_ref[:, lanes(g)]) * LOG2E for g in gs]
        for s in range(seqs):
            def blk(i, st):
                st = list(st)
                t0 = pl.multiple_of(s * length + (length // 8 - 1 - i) * 8, 8)
                for j in reversed(range(8)):
                    c = wide[pl.ds(pl.multiple_of((t0 + j) * STATE, STATE), STATE), pl.ds(LANES, LANES)]
                    for k, g in enumerate(gs):
                        d = jnp.exp2(a2[k] * dstep[g, pl.ds(t0 + j, 1), :])
                        st[k] = d * (st[k] + c * gsc[g, pl.ds(t0 + j, 1), :])
                return tuple(st)
            st = lax.fori_loop(0, length // 8, blk, tuple(jnp.zeros((STATE, LANES), jnp.float32) for _ in gs))
            for k, g in enumerate(gs):
                out_ref[s, :, lanes(g)] = st[k]

def scan_back_local(pre, gs, bc, keep, dl, seqs, pins=()):
    rows, channels = pre.shape
    f = jnp.float32
    return pl.pallas_call(
        after(functools.partial(back_local_kernel, seqs), 5, pins),
        out_shape=jax.ShapeDtypeStruct((seqs, STATE, channels), f),
        in_specs=[VM] * 5 + [ANY] * len(pins), out_specs=VM,
        scratch_shapes=[pltpu.VMEM((rows * STATE, 2 * LANES), f), pltpu.VMEM((32 * STATE, 2 * STATE), jnp.bfloat16),
                        pltpu.VMEM((channels // LANES, rows, LANES), f), pltpu.VMEM((channels // LANES, rows, LANES), f)],
        compiler_params=pltpu.CompilerParams(vmem_limit_bytes=60 * 2**20),
        cost_estimate=cost(8),
        name="scan_back_local",
    )(pre, gs, bc, keep, dl, *pins)

def back_kernel(seqs, with_y, pre_ref, act_ref, gs_ref, bc_ref, keep_ref, dl_ref, skip_ref, in_ref, lam_ref,
                gpre_ref, gact_ref, gbc_ref, gdl_ref, *rest):
    if with_y:
        y_ref, *rest = rest
    (wide, pick, dstep, dx, stepc, gsc, states, partq, partr, accb, accc, rowsum) = rest
    rows, channels = pre_ref.shape
    length = rows // seqs
    f = jnp.float32
    spread_states(bc_ref, wide, pick, rows)
    def body(i, _):
        sl = pl.ds(pl.multiple_of(i * 32, 32), 32)
        for g in range(channels // LANES):
            st = softplus(pre_ref[sl, lanes(g)])
            stepc[g, sl, :] = st
            dstep[g, sl, :] = jnp.where(keep_ref[sl, :] > 0.0, st, BIG)
            dx[g, sl, :] = st * act_ref[sl, lanes(g)]
            gsc[g, sl, :] = gs_ref[sl, lanes(g)]
        return 0
    lax.fori_loop(0, rows // 32, body, 0)
    yield
    sets = group_sets(channels, 4)
    for index, gs in enumerate(sets):
        a2 = [-jnp.exp(dl_ref[:, lanes(g)]) * LOG2E for g in gs]
        gdl = [jnp.zeros((STATE, LANES), f) for _ in gs]
        for s in range(seqs):
            for k, g in enumerate(gs):
                states[k, pl.ds(0, STATE), :] = in_ref[s, :, lanes(g)]
            def fwd(i, st):
                st = list(st)
                t0 = pl.multiple_of(s * length + i * 8, 8)
                for j in range(8):
                    at = pl.ds(pl.multiple_of((t0 + j) * STATE, STATE), STATE)
                    b = wide[at, pl.ds(0, LANES)]
                    if with_y:
                        c = wide[at, pl.ds(LANES, LANES)]
                    for k, g in enumerate(gs):
                        d = jnp.exp2(a2[k] * dstep[g, pl.ds(t0 + j, 1), :])
                        st[k] = d * st[k] + b * dx[g, pl.ds(t0 + j, 1), :]
                        states[k, pl.ds(pl.multiple_of((i * 8 + j + 1) * STATE, STATE), STATE), :] = st[k]
                        if with_y:
                            v = st[k] * c
                            partq[k, pl.ds(pl.multiple_of(i * 64 + j * 8, 8), 8), :] = v[:8] + v[8:]
                return tuple(st)
            lax.fori_loop(0, length // 8, fwd, tuple(in_ref[s, :, lanes(g)] for g in gs))
            if with_y:
                def read(i, _):
                    t0 = pl.multiple_of(s * length + i * 8, 8)
                    for k, g in enumerate(gs):
                        acc = partq[k, pl.ds(i * 64, 8, stride=8), :]
                        for m in range(1, 8):
                            acc = acc + partq[k, pl.ds(i * 64 + m, 8, stride=8), :]
                        y_ref[pl.ds(t0, 8), lanes(g)] = acc
                    return 0
                lax.fori_loop(0, length // 8, read, 0)
            yield
            def bwd(i, carry):
                st = list(carry[:len(gs)])
                am = list(carry[len(gs):])
                l0 = (length // 8 - 1 - i) * 8
                t0 = pl.multiple_of(s * length + l0, 8)
                for j in reversed(range(8)):
                    at = pl.ds(pl.multiple_of((t0 + j) * STATE, STATE), STATE)
                    b = wide[at, pl.ds(0, LANES)]
                    c = wide[at, pl.ds(LANES, LANES)]
                    tb = tc = None
                    here = pl.ds(pl.multiple_of((l0 + j) * 8, 8), 8)
                    for k, g in enumerate(gs):
                        row = pl.ds(t0 + j, 1)
                        grow = gsc[g, row, :]
                        d = jnp.exp2(a2[k] * dstep[g, row, :])
                        lam = st[k] + c * grow
                        old = states[k, pl.ds(pl.multiple_of((l0 + j) * STATE, STATE), STATE), :]
                        new = states[k, pl.ds(pl.multiple_of((l0 + j + 1) * STATE, STATE), STATE), :]
                        st[k] = d * lam
                        lp = st[k] * old
                        q = lam * b
                        partq[k, here, :] = q[:8] + q[8:]
                        r = lp * a2[k]
                        partr[k, here, :] = r[:8] + r[8:]
                        am[k] = am[k] + lp * stepc[g, row, :]
                        u = lam * dx[g, row, :]
                        v = new * grow
                        tb = u if tb is None else tb + u
                        tc = v if tc is None else tc + v
                    if index > 0:
                        tb = tb + accb[at, :]
                        tc = tc + accc[at, :]
                    accb[at, :] = tb
                    accc[at, :] = tc
                return tuple(st) + tuple(am)
            out = lax.fori_loop(0, length // 8, bwd, tuple(lam_ref[s, :, lanes(g)] for g in gs) + tuple(gdl))
            gdl = list(out[len(gs):])
            def red(i, _):
                t0 = pl.multiple_of(s * length + i * 8, 8)
                for k, g in enumerate(gs):
                    q = partq[k, pl.ds(i * 64, 8, stride=8), :]
                    r = partr[k, pl.ds(i * 64, 8, stride=8), :]
                    for m in range(1, 8):
                        q = q + partq[k, pl.ds(i * 64 + m, 8, stride=8), :]
                        r = r + partr[k, pl.ds(i * 64 + m, 8, stride=8), :]
                    here = pl.ds(t0, 8)
                    p = pre_ref[here, lanes(g)]
                    gstep = r * LN2 + act_ref[here, lanes(g)] * q
                    gpre_ref[here, lanes(g)] = gstep * (1.0 / (1.0 + jnp.exp(-p)))
                    gact_ref[here, lanes(g)] = stepc[g, here, :] * q + gsc[g, here, :] * skip_ref[:, lanes(g)]
                return 0
            lax.fori_loop(0, length // 8, red, 0)
            yield
        for k, g in enumerate(gs):
            gdl_ref[:, lanes(g)] = gdl[k] * (a2[k] * LN2)
    ones = jnp.ones((LANES, LANES), jnp.bfloat16)
    lane = lax.broadcasted_iota(jnp.int32, (32 * STATE, LANES), 1)
    row = lax.broadcasted_iota(jnp.int32, (32 * STATE, LANES), 0) % STATE
    mb = lane == row
    mc = lane == row + STATE
    def fin(i, _):
        sl = pl.ds(pl.multiple_of(i * 32 * STATE, 32 * STATE), 32 * STATE)
        sb = jnp.dot(accb[sl, :].astype(jnp.bfloat16), ones, preferred_element_type=f)
        sc = jnp.dot(accc[sl, :].astype(jnp.bfloat16), ones, preferred_element_type=f)
        rowsum[...] = jnp.where(mb, sb, jnp.where(mc, sc, 0.0))
        acc = rowsum[pl.ds(0, 32, stride=STATE), :]
        for m in range(1, STATE):
            acc = acc + rowsum[pl.ds(m, 32, stride=STATE), :]
        gbc_ref[pl.ds(pl.multiple_of(i * 32, 32), 32), :] = acc
        return 0
    lax.fori_loop(0, rows // 32, fin, 0)

def scan_back(pre, act, gs, bc, keep, dl, skip, state_in, lam_in, seqs, with_y, plan, places, cid, pins=()):
    rows, channels = pre.shape
    f = jnp.float32
    groups = channels // LANES
    length = rows // seqs
    big = pltpu.VMEM((groups, rows, LANES), f)
    whole = jax.ShapeDtypeStruct((rows, channels), f)
    return play_call(
        functools.partial(back_kernel, seqs, with_y), (9, 4 + with_y, 12), plan, places, cid,
        [whole, whole, jax.ShapeDtypeStruct((rows, LANES), f), jax.ShapeDtypeStruct((STATE, channels), f)] + [whole] * with_y,
        [pltpu.VMEM((rows * STATE, 2 * LANES), f), pltpu.VMEM((32 * STATE, 2 * STATE), jnp.bfloat16),
         big, big, big, big,
         pltpu.VMEM((4, (length + 1) * STATE, LANES), f),
         pltpu.VMEM((4, length * 8, LANES), f), pltpu.VMEM((4, length * 8, LANES), f),
         pltpu.VMEM((rows * STATE, LANES), f), pltpu.VMEM((rows * STATE, LANES), f),
         pltpu.VMEM((32 * STATE, LANES), f)],
        (pre, act, gs, bc, keep, dl, skip, state_in, lam_in), 23 + 3 * with_y, "scan_back", pins,
    )


def greet(peers):
    barrier = pltpu.get_barrier_semaphore()
    for p in peers:
        pl.semaphore_signal(barrier, inc=1, device_id=p, device_id_type=MESH)
    pl.semaphore_wait(barrier, len(peers))

def ch_sum_kernel(n, x_ref, out_ref, mine, slots, send, recv):
    me = lax.axis_index("ch")
    peers = [{"ch": lax.rem(me + d, n)} for d in range(1, n)]
    greet(peers)
    mine[...] = x_ref[...].astype(bf16)
    copies = []
    for d in range(1, n):
        c = pltpu.make_async_remote_copy(src_ref=mine, dst_ref=slots.at[d - 1], send_sem=send.at[d - 1], recv_sem=recv.at[d - 1], device_id=peers[d - 1], device_id_type=MESH)
        c.start()
        copies.append(c)
    total = x_ref[...].astype(bf16).astype(f32)
    for d, c in zip(range(1, n), copies):
        c.wait()
        total = total + slots[d - 1].astype(f32)
    out_ref[...] = total

def ch_sum(x, n, cid, pins=()):
    return pl.pallas_call(
        after(functools.partial(ch_sum_kernel, n), 1, pins),
        out_shape=jax.ShapeDtypeStruct(x.shape, f32), in_specs=[VM] + [ANY] * len(pins), out_specs=VM,
        scratch_shapes=[pltpu.VMEM(x.shape, bf16), pltpu.VMEM((n - 1,) + x.shape, bf16), pltpu.SemaphoreType.DMA((n - 1,)), pltpu.SemaphoreType.DMA((n - 1,))],
        compiler_params=pltpu.CompilerParams(collective_id=cid, has_side_effects=True, vmem_limit_bytes=32 * 2**20), cost_estimate=cost(10), name="ch_sum",
    )(x, *pins)

def reduce_steps(n, parts, gather, more, x_ref, out_ref, s1, sum1, s2, mine, got, fin, sem1, rem1, sem2, rem2, sem3, rem3, sem4, rem4):
    xs = n // 2
    me = lax.axis_index("ch")
    x, core = me // 2, lax.rem(me, 2)
    peer = {"ch": x * 2 + 1 - core}
    others = [lax.rem(x + d, xs) for d in range(1, xs)]
    greet([peer] + [{"ch": o * 2 + core} for o in others] + more)
    rows, width = x_ref.shape[0] // parts, x_ref.shape[1] // n
    def cols(block):
        return pl.ds(pl.multiple_of(block * width, width), width)
    def stage1(p, k):
        return pltpu.make_async_remote_copy(src_ref=x_ref.at[pl.ds(p * rows, rows), cols(k * 2 + 1 - core)], dst_ref=s1.at[p, k], send_sem=sem1.at[p, k], recv_sem=rem1.at[p, k], device_id=peer, device_id_type=MESH)
    def stage2(p, d):
        o = others[d]
        return pltpu.make_async_remote_copy(src_ref=sum1.at[p, o], dst_ref=s2.at[p, d], send_sem=sem2.at[p, d], recv_sem=rem2.at[p, d], device_id={"ch": o * 2 + core}, device_id_type=MESH)
    def stage3(p, d):
        o = others[d]
        return pltpu.make_async_remote_copy(src_ref=mine.at[p], dst_ref=got.at[p, d], send_sem=sem3.at[p, d], recv_sem=rem3.at[p, d], device_id={"ch": o * 2 + core}, device_id_type=MESH)
    for p in range(parts):
        for k in range(xs):
            stage1(p, k).start()
    yield
    for p in range(parts):
        for k in range(xs):
            stage1(p, k).wait_recv()
            sum1[p, k] = (x_ref[pl.ds(p * rows, rows), cols(k * 2 + core)].astype(f32) + s1[p, k].astype(f32)).astype(bf16)
        for d in range(xs - 1):
            stage2(p, d).start()
    yield
    for p in range(parts):
        total = sum1[p, x].astype(f32)
        for d in range(xs - 1):
            stage2(p, d).wait_recv()
            total = total + s2[p, d].astype(f32)
        if gather:
            mine[p] = total.astype(bf16)
            for d in range(xs - 1):
                stage3(p, d).start()
        else:
            out_ref[pl.ds(p * rows, rows), :] = total
    yield
    if gather:
        def stage4(p, d):
            src = mine.at[p] if d < 0 else got.at[p, d]
            return pltpu.make_async_remote_copy(src_ref=src, dst_ref=fin.at[p, d + 1], send_sem=sem4.at[p, d + 1], recv_sem=rem4.at[p, d + 1], device_id=peer, device_id_type=MESH)
        def chip(d):
            return lax.rem(x + xs - 1 - d, xs)
        for p in range(parts):
            stage4(p, -1).start()
            out_ref[pl.ds(p * rows, rows), cols(me)] = mine[p].astype(out_ref.dtype)
            for d in range(xs - 1):
                stage3(p, d).wait_recv()
                stage4(p, d).start()
                out_ref[pl.ds(p * rows, rows), cols(chip(d) * 2 + core)] = got[p, d].astype(out_ref.dtype)
        yield
        for p in range(parts):
            for d in range(-1, xs - 1):
                stage4(p, d).wait_recv()
                out_ref[pl.ds(p * rows, rows), cols(chip(d) * 2 + 1 - core)] = fin[p, d + 1].astype(out_ref.dtype)
    for p in range(parts):
        for k in range(xs):
            stage1(p, k).wait_send()
        for d in range(xs - 1):
            stage2(p, d).wait_send()
            if gather:
                stage3(p, d).wait_send()
        if gather:
            for d in range(-1, xs - 1):
                stage4(p, d).wait_send()
    yield


class ColumnsLine:
    semaphores = 6

    @staticmethod
    def result(v, zs, ys):
        return jax.ShapeDtypeStruct((zs * v.shape[0], v.shape[1] // zs), v.dtype)

    @staticmethod
    def specs(v, zs, ys):
        sem = pltpu.SemaphoreType.DMA
        xs = lax.axis_size("ch") // 2
        return [sem((zs - 1,))] * 2 + [sem((zs - 1, xs - 1))] * 2 + [sem((zs - 1, xs))] * 2

    def __init__(self, zs, ys, src, out, sems):
        seq, ch = lax.axis_index("seq"), lax.axis_index("ch")
        self.nch = lax.axis_size("ch")
        self.xs = self.nch // 2
        self.zs, self.ys, self.z, self.y, self.ch = zs, ys, seq // ys, lax.rem(seq, ys), ch
        self.x, self.core = ch // 2, lax.rem(ch, 2)
        self.src, self.out, self.sems = src, out, sems
        self.rows, self.width = src.shape[0], src.shape[1] // zs
        self.part = self.rows // self.nch

    def cols(self, z):
        return pl.ds(pl.multiple_of(z * self.width, self.width), self.width)

    def share(self, z, ch):
        return pl.ds(pl.multiple_of(z * self.rows + ch * self.part, self.part), self.part)

    def remote(self, k, at, src, dst, to):
        send, recv = self.sems[2 * k : 2 * k + 2]
        return pltpu.make_async_remote_copy(src_ref=src, dst_ref=dst, send_sem=send.at[at], recv_sem=recv.at[at], device_id=to, device_id_type=MESH)

    def along(self, d):
        to = lax.rem(self.z + d, self.zs)
        src = self.src.at[pl.ds(pl.multiple_of(self.ch * self.part, self.part), self.part), self.cols(to)]
        return self.remote(0, d - 1, src, self.out.at[self.share(self.z, self.ch)], {"seq": to * self.ys + self.y})

    def from_z(self, d):
        return lax.rem(self.z + self.zs - d, self.zs)

    def over(self, d, e):
        rows = self.out.at[self.share(self.from_z(d), self.ch)]
        return self.remote(1, (d - 1, e - 1), rows, rows, {"ch": lax.rem(self.x + e, self.xs) * 2 + self.core})

    def across(self, d, e):
        rows = self.out.at[self.share(self.from_z(d), lax.rem(self.x + self.xs - e, self.xs) * 2 + self.core)]
        return self.remote(2, (d - 1, e), rows, rows, {"ch": self.x * 2 + 1 - self.core})

    def lags(self):
        return range(1, self.zs)

    def begin(self):
        for d in self.lags():
            self.along(d).start()
        here = pl.ds(pl.multiple_of(self.z * self.rows, self.rows), self.rows)
        self.out[here, :] = self.src[:, self.cols(self.z)]

    def step(self, index):
        for d in self.lags():
            if index == 0:
                self.along(d).wait_recv()
                for e in range(1, self.xs):
                    self.over(d, e).start()
                self.across(d, 0).start()
            else:
                for e in range(1, self.xs):
                    self.over(d, e).wait_recv()
                    self.across(d, e).start()

    def finish(self):
        for d in self.lags():
            for e in range(self.xs):
                self.across(d, e).wait_recv()
        for d in self.lags():
            self.along(d).wait_send()
            for e in range(1, self.xs):
                self.over(d, e).wait_send()
            for e in range(self.xs):
                self.across(d, e).wait_send()


def reduce_kernel(n, parts, gather, *refs):
    for _ in reduce_steps(n, parts, gather, [], *refs):
        pass


def reduce_scratch_shapes(shape, n, parts):
    rows, width = shape
    xs, r, w = n // 2, rows // parts, width // n
    sem = pltpu.SemaphoreType.DMA
    return [
        pltpu.VMEM((parts, xs, r, w), bf16), pltpu.VMEM((parts, xs, r, w), bf16), pltpu.VMEM((parts, xs - 1, r, w), bf16),
        pltpu.VMEM((parts, r, w), bf16), pltpu.VMEM((parts, xs - 1, r, w), bf16), pltpu.VMEM((parts, xs, r, w), bf16),
        sem((parts, xs)), sem((parts, xs)), sem((parts, xs - 1)), sem((parts, xs - 1)),
        sem((parts, xs - 1)), sem((parts, xs - 1)), sem((parts, xs)), sem((parts, xs)),
    ]


def ch_reduce(x, n, cid, gather, parts=2):
    rows, width = x.shape
    return pl.pallas_call(
        functools.partial(reduce_kernel, n, parts, gather),
        out_shape=jax.ShapeDtypeStruct((rows, width if gather else width // n), f32),
        in_specs=[VM], out_specs=VM,
        scratch_shapes=reduce_scratch_shapes(x.shape, n, parts),
        compiler_params=pltpu.CompilerParams(collective_id=cid, has_side_effects=True, vmem_limit_bytes=48 * 2**20),
        cost_estimate=cost(18), name="ch_reduce",
    )(x)


def carry_kernel(n, fwd, rev, *refs):
    refs = list(refs)
    tot_ref, dl_ref = refs.pop(0), refs.pop(0)
    k = fwd + rev
    ends = [refs.pop(0) for _ in range(k)]
    outs = [refs.pop(0) for _ in range(k)]
    mine, slots, tots, send, recv, tsend, trecv = refs
    me = lax.axis_index("seq")
    seqs = tot_ref.shape[0]
    greet([{"seq": lax.rem(me + d, n)} for d in range(1, n)])
    a2 = -jnp.exp(dl_ref[...]) * LOG2E
    directions = [False] * fwd + [True] * rev
    def copies(i, d):
        away = -d if directions[i] else d
        to = {"seq": lax.rem(me + away + n, n)}
        return (
            pltpu.make_async_remote_copy(src_ref=mine.at[i], dst_ref=slots.at[i, d - 1], send_sem=send.at[i, d - 1], recv_sem=recv.at[i, d - 1], device_id=to, device_id_type=MESH),
            pltpu.make_async_remote_copy(src_ref=tot_ref, dst_ref=tots.at[i, d - 1], send_sem=tsend.at[i, d - 1], recv_sem=trecv.at[i, d - 1], device_id=to, device_id_type=MESH),
        )
    for i in range(k):
        mine[i] = ends[i][...].astype(bf16)
        outs[i][...] = jnp.zeros_like(outs[i])
    for d in reversed(range(1, n)):
        for i in range(k):
            place = n - 1 - me if directions[i] else me
            @pl.when(place + d < n)
            def _():
                for c in copies(i, d):
                    c.start()
    for d in reversed(range(1, n)):
        for i in range(k):
            place = n - 1 - me if directions[i] else me
            @pl.when(place >= d)
            def _():
                for c in copies(i, d):
                    c.wait_recv()
                for s in range(seqs):
                    gain = jnp.exp2(a2 * tots[i, d - 1, pl.ds(s, 1), :])
                    outs[i][s] = gain * outs[i][s] + slots[i, d - 1, s].astype(f32)
    for d in reversed(range(1, n)):
        for i in range(k):
            place = n - 1 - me if directions[i] else me
            @pl.when(place + d < n)
            def _():
                for c in copies(i, d):
                    c.wait_send()

def carry_over(tot, dl, ends, n, cid, fwd, rev):
    k = len(ends)
    sem = pltpu.SemaphoreType.DMA
    return pl.pallas_call(
        functools.partial(carry_kernel, n, int(fwd), int(rev)),
        out_shape=[jax.ShapeDtypeStruct(ends[0].shape, f32)] * k, in_specs=[VM] * (k + 2), out_specs=[VM] * k,
        scratch_shapes=[pltpu.VMEM((k,) + ends[0].shape, bf16), pltpu.VMEM((k, n - 1) + ends[0].shape, bf16), pltpu.VMEM((k, n - 1) + tot.shape, f32),
                        sem((k, n - 1)), sem((k, n - 1)), sem((k, n - 1)), sem((k, n - 1))],
        compiler_params=pltpu.CompilerParams(collective_id=cid, has_side_effects=True, vmem_limit_bytes=32 * 2**20), cost_estimate=cost(19), name="carry_over",
    )(tot, dl, *ends)


def seq_at(z, y, ys):
    return {"seq": z * ys + y}


class GatherLine:
    semaphores = 2

    @staticmethod
    def result(v, zs, ys):
        return jax.ShapeDtypeStruct((zs * v.shape[0], v.shape[1]), v.dtype)

    @staticmethod
    def specs(v, zs, ys):
        return [pltpu.SemaphoreType.DMA((2, zs - 1))] * 2


    def __init__(self, zs, ys, src, out, sems):
        me = lax.axis_index("seq")
        self.zs, self.ys, self.z, self.y = zs, ys, me // ys, lax.rem(me, ys)
        self.src, self.out = src, out
        self.send, self.recv = sems
        self.rows = src.shape[0]

    def block(self, z):
        return self.out.at[pl.ds(pl.multiple_of(z * self.rows, self.rows), self.rows)]

    def copy(self, way, r):
        z = self.z
        to, b = (lax.rem(z + 1, self.zs), z - r) if way == 0 else (lax.rem(z + self.zs - 1, self.zs), z + r)
        b = lax.rem(b + self.zs, self.zs)
        return pltpu.make_async_remote_copy(
            src_ref=self.src if r == 0 else self.block(b),
            dst_ref=self.block(b),
            send_sem=self.send.at[way, r],
            recv_sem=self.recv.at[way, r],
            device_id=seq_at(to, self.y, self.ys),
            device_id_type=MESH,
        )

    def sends(self, way, r):
        z, last = self.z, self.zs - 1
        return jnp.logical_and(z < last, z >= r) if way == 0 else jnp.logical_and(z > 0, z + r <= last)

    def receives(self, way, r):
        z, last = self.z, self.zs - 1
        return z - 1 - r >= 0 if way == 0 else z + 1 + r <= last

    def begin(self):
        self.start(0)
        self.block(self.z)[...] = self.src[...]

    def step(self, index):
        self.start(index + 1)

    def start(self, r):
        for way in (0, 1):
            if r > 0:
                self.arrive(way, r - 1)
            @pl.when(self.sends(way, r))
            def _():
                self.copy(way, r).start()

    def arrive(self, way, r):
        @pl.when(self.receives(way, r))
        def _():
            self.copy(way, r).wait_recv()

    def finish(self):
        for way in (0, 1):
            self.arrive(way, self.zs - 2)
        for way in (0, 1):
            for r in range(self.zs - 1):
                @pl.when(self.sends(way, r))
                def _():
                    self.copy(way, r).wait_send()


class SumAll:
    def __init__(self, zs, ys, src, out, yslots, ysum, zslots, sems):
        me = lax.axis_index("seq")
        self.zs, self.ys, self.z, self.y = zs, ys, me // ys, lax.rem(me, ys)
        self.src, self.out, self.yslots, self.ysum, self.zslots = src, out, yslots, ysum, zslots
        self.sems = sems
        self.part = src.shape[0] // ys
        self.share = self.part // zs

    def remote(self, k, i, src, dst, to):
        send, recv = self.sems[2 * k : 2 * k + 2]
        return pltpu.make_async_remote_copy(src_ref=src, dst_ref=dst, send_sem=send.at[i], recv_sem=recv.at[i], device_id=to, device_id_type=MESH)

    def rows(self, index, size):
        return pl.ds(pl.multiple_of(index * size, size), size)

    def y1(self, d):
        to = lax.rem(self.y + d, self.ys)
        return self.remote(0, d - 1, self.src.at[self.rows(to, self.part)], self.yslots.at[d - 1], seq_at(self.z, to, self.ys))

    def z1(self, d):
        to = lax.rem(self.z + d, self.zs)
        return self.remote(1, d - 1, self.ysum.at[self.rows(to, self.share)], self.zslots.at[d - 1], seq_at(to, self.y, self.ys))

    def mine(self, z):
        return self.out.at[self.rows(self.y * self.zs + z, self.share)]

    def z2(self, d):
        to = lax.rem(self.z + d, self.zs)
        return self.remote(2, d - 1, self.mine(self.z), self.mine(self.z), seq_at(to, self.y, self.ys))

    def y2(self, d, e):
        to = lax.rem(self.y + d, self.ys)
        share = self.mine(lax.rem(self.z - e + self.zs, self.zs))
        return self.remote(3, (d - 1) * self.zs + e, share, share, seq_at(self.z, to, self.ys))

    def begin(self):
        for d in range(1, self.ys):
            self.y1(d).start()

    def middle(self):
        total = self.src[self.rows(self.y, self.part), :].astype(f32)
        for d in range(1, self.ys):
            self.y1(d).wait_recv()
            total = total + self.yslots[d - 1].astype(f32)
        self.ysum[...] = total.astype(bf16)
        for d in range(1, self.zs):
            self.z1(d).start()

    def gather(self):
        total = self.ysum[self.rows(self.z, self.share), :].astype(f32)
        for d in range(1, self.zs):
            self.z1(d).wait_recv()
            total = total + self.zslots[d - 1].astype(f32)
        self.mine(self.z)[...] = total.astype(bf16)
        for d in range(1, self.zs):
            self.z2(d).start()
        for d in range(1, self.ys):
            self.y2(d, 0).start()

    def spread(self):
        for e in range(1, self.zs):
            self.z2(e).wait_recv()
            for d in range(1, self.ys):
                self.y2(d, e).start()

    def finish(self):
        for d in range(1, self.ys):
            for e in range(self.zs):
                self.y2(d, e).wait_recv()
        for d in range(1, self.ys):
            self.y1(d).wait_send()
            for e in range(self.zs):
                self.y2(d, e).wait_send()
        for d in range(1, self.zs):
            self.z1(d).wait_send()
            self.z2(d).wait_send()


class PartSum:
    semaphores = 3

    @staticmethod
    def result(v, zs, ys):
        return jax.ShapeDtypeStruct(v.shape[1:], f32)

    @staticmethod
    def specs(v, zs, ys):
        sem = pltpu.SemaphoreType.DMA((ys - 1,))
        return [sem, sem, pltpu.VMEM((ys - 1,) + v.shape[1:], v.dtype)]


    def __init__(self, zs, ys, src, out, scratch):
        me = lax.axis_index("seq")
        self.ys, self.z, self.y = ys, me // ys, lax.rem(me, ys)
        self.src, self.out = src, out
        self.send, self.recv, self.slots = scratch

    def copy(self, d):
        to = lax.rem(self.y + d, self.ys)
        return pltpu.make_async_remote_copy(
            src_ref=self.src.at[to],
            dst_ref=self.slots.at[d - 1],
            send_sem=self.send.at[d - 1],
            recv_sem=self.recv.at[d - 1],
            device_id=seq_at(self.z, to, self.ys),
            device_id_type=MESH,
        )

    def begin(self):
        for d in range(1, self.ys):
            self.copy(d).start()

    def finish(self):
        mine = self.src[self.y].astype(f32)
        for d in range(1, self.ys):
            self.copy(d).wait_recv()
            mine = mine + self.slots[d - 1].astype(f32)
        self.out[...] = mine
        for d in range(1, self.ys):
            self.copy(d).wait_send()


def closing_kernel(n, zs, ys, parts, count, pieces, x_ref, v_ref, *refs):
    piece_refs, refs = refs[:pieces], refs[pieces:]
    p_refs, refs = refs[:count], refs[count:]
    out_ref, all_ref, sum_ref, *refs = refs
    part_refs, refs = refs[:count], refs[count:]
    s_ref, *refs = refs
    reduce_scratch, scratch = refs[:14], refs[14:]
    yslots, ysum, zslots, gsend, grecv = scratch[:5]
    seq = lax.axis_index("seq")
    z, y = seq // ys, lax.rem(seq, ys)
    line = GatherLine(zs, ys, v_ref, all_ref, (gsend, grecv))
    total = SumAll(zs, ys, s_ref, sum_ref, yslots, ysum, zslots, scratch[5:13])
    sums = [PartSum(zs, ys, p_refs[k], part_refs[k], scratch[13 + 3 * k : 16 + 3 * k]) for k in range(count)]
    peers = [seq_at(z, lax.rem(y + d, ys), ys) for d in range(1, ys)]
    peers += [seq_at(lax.rem(z + d, zs), y, ys) for d in range(1, zs)]
    steps = reduce_steps(n, parts, False, peers, x_ref, out_ref, *reduce_scratch)
    next(steps)
    offset = 0
    for piece in piece_refs:
        s_ref[pl.ds(offset, piece.shape[0]), :] = piece[...].astype(bf16)
        offset += piece.shape[0]
    if offset < s_ref.shape[0]:
        s_ref[pl.ds(offset, s_ref.shape[0] - offset), :] = jnp.zeros((s_ref.shape[0] - offset, s_ref.shape[1]), bf16)
    line.start(0)
    total.begin()
    for part in sums:
        part.begin()
    all_ref[pl.ds(pl.multiple_of(z * line.rows, line.rows), line.rows), :] = v_ref[...]
    next(steps)
    total.middle()
    next(steps)
    line.start(1)
    for _ in steps:
        pass
    total.gather()
    for r in range(2, zs - 1):
        line.start(r)
    for part in sums[:-1]:
        part.finish()
    total.spread()
    for part in sums[-1:]:
        part.finish()
    line.finish()
    total.finish()


def closing(x, v, pieces, ps, n, zs, ys, cid, parts=2):
    rows, width = x.shape
    sem = pltpu.SemaphoreType.DMA
    height = sum(piece.shape[0] for piece in pieces)
    height += -height % (16 * ys * zs)
    part = height // ys
    w = v.shape[1]
    count = len(ps)
    return pl.pallas_call(
        functools.partial(closing_kernel, n, zs, ys, parts, count, len(pieces)),
        out_shape=[
            jax.ShapeDtypeStruct((rows, width // n), f32),
            jax.ShapeDtypeStruct((zs * v.shape[0], v.shape[1]), bf16),
            jax.ShapeDtypeStruct((height, w), bf16),
        ]
        + [PartSum.result(p, zs, ys) for p in ps],
        in_specs=[VM] * (2 + len(pieces) + count),
        out_specs=[VM] * (3 + count),
        scratch_shapes=[pltpu.VMEM((height, w), bf16)] + reduce_scratch_shapes(x.shape, n, parts)
        + [
            pltpu.VMEM((ys - 1, part, w), bf16),
            pltpu.VMEM((part, w), bf16),
            pltpu.VMEM((zs - 1, part // zs, w), bf16),
        ]
        + [sem((2, zs - 1))] * 2
        + [sem((ys - 1,))] * 2
        + [sem((zs - 1,))] * 4
        + [sem(((ys - 1) * zs,))] * 2
        + [spec for p in ps for spec in PartSum.specs(p, zs, ys)],
        compiler_params=pltpu.CompilerParams(collective_id=cid, has_side_effects=True, vmem_limit_bytes=58 * 2**20),
        cost_estimate=cost(70),
        name="closing",
    )(x, v, *pieces, *ps)


def last_kernel(n, zs, ys, p_ref, t_ref, out_ref, sum_ref, pslots, tslots, psend, precv, tsend, trecv):
    me = lax.axis_index("seq")
    z, y = me // ys, lax.rem(me, ys)
    greet([{"seq": lax.rem(me + d, n)} for d in range(1, n)])
    def part(d):
        to = lax.rem(y + d, ys)
        return pltpu.make_async_remote_copy(src_ref=p_ref.at[to], dst_ref=pslots.at[d - 1], send_sem=psend.at[d - 1], recv_sem=precv.at[d - 1], device_id=seq_at(z, to, ys), device_id_type=MESH)
    def tiny(d):
        return pltpu.make_async_remote_copy(src_ref=t_ref, dst_ref=tslots.at[lax.rem(me, n)], send_sem=tsend.at[d - 1], recv_sem=trecv.at[d - 1], device_id={"seq": lax.rem(me + d, n)}, device_id_type=MESH)
    for d in range(1, n):
        tiny(d).start()
    for d in range(1, ys):
        part(d).start()
    tslots[me] = t_ref[...]
    for d in range(1, n):
        tiny(d).wait_recv()
    total = tslots[0].astype(f32)
    for k in range(1, n):
        total = total + tslots[k].astype(f32)
    sum_ref[...] = total
    mine = p_ref[y].astype(f32)
    for d in range(1, ys):
        part(d).wait_recv()
        mine = mine + pslots[d - 1].astype(f32)
    out_ref[...] = mine
    for d in range(1, n):
        tiny(d).wait_send()
    for d in range(1, ys):
        part(d).wait_send()


def last_sums(p, t, n, zs, ys, cid):
    sem = pltpu.SemaphoreType.DMA
    return pl.pallas_call(
        functools.partial(last_kernel, n, zs, ys),
        out_shape=[jax.ShapeDtypeStruct(p.shape[1:], f32), jax.ShapeDtypeStruct(t.shape, f32)],
        in_specs=[VM] * 2,
        out_specs=[VM] * 2,
        scratch_shapes=[
            pltpu.VMEM((ys - 1,) + p.shape[1:], bf16),
            pltpu.VMEM((n,) + t.shape, bf16),
            sem((ys - 1,)), sem((ys - 1,)), sem((n - 1,)), sem((n - 1,)),
        ],
        compiler_params=pltpu.CompilerParams(collective_id=cid, has_side_effects=True, vmem_limit_bytes=48 * 2**20),
        cost_estimate=cost(25),
        name="last_sums",
    )(p, t)


def passed_along(block, axis, distance):
    devices = range(lax.axis_size(axis))
    route = [(i - distance, i) for i in devices if i - distance in devices]
    return lax.ppermute(block, axis, route)


def silu_slope(argument):
    logistic = jax.nn.sigmoid(argument)
    return logistic * (1.0 + argument * (1.0 - logistic))


def conv_local(extended, weights, biases, seg_ext):
    length_now = extended.shape[1] - (KERN - 1)
    seg_now = seg_ext[:, KERN - 1 :]
    summed = biases + jnp.zeros((extended.shape[0], length_now, extended.shape[2]), f32)
    for lag_index in range(KERN):
        same_doc = (seg_ext[:, lag_index : lag_index + length_now] == seg_now).astype(f32)
        summed = (
            summed
            + weights[lag_index]
            * extended[:, lag_index : lag_index + length_now]
            * same_doc[:, :, None]
        )
    return summed


def dot(a, b, contract):
    return lax.dot_general(a, b, ((contract[:1], contract[1:]), ((), ())), preferred_element_type=f32)


def lines(zs, ys):
    return [[z * ys + y for z in range(zs)] for y in range(ys)]


def tokens_of_line(rows, zs, ys):
    return lax.all_gather(rows, "seq", axis_index_groups=lines(zs, ys), tiled=True)


def local(
    hidden_in,
    segments,
    cotangent,
    norm_gain,
    input_projection_weight,
    conv_weight,
    conv_bias,
    proj_weight,
    step_weight,
    step_bias,
    decay_log,
    skip_gain,
    output_projection_weight,
):
    seqs, length, width = hidden_in.shape
    rows = seqs * length
    nch, nseq = lax.axis_size("ch"), lax.axis_size("seq")
    channels = conv_bias.shape[-1]
    share = width // nch
    share_start = lax.axis_index("ch") * share
    seg_own = segments.astype(f32)
    seg_edge = passed_along(seg_own[:, -(KERN - 1) :], "seq", 1)
    seg_ext = jnp.concatenate([seg_edge, seg_own], axis=1)
    keep = (seg_ext[:, KERN - 2 : -1] == seg_own).astype(f32).reshape(-1, 1)
    hidden = hidden_in.astype(f32).reshape(rows, width)
    grad_rows = cotangent.astype(f32).reshape(rows, width)
    ids = iter(range(100))
    zs = 4 if nseq % 4 == 0 else nseq
    ys = nseq // zs
    fold = width // nseq
    places = (zs, ys)

    out_cols = {}
    stored = []
    for layer in range(LAYERS):
        last = layer == LAYERS - 1
        inv_rms = lax.rsqrt(jnp.mean(hidden * hidden, axis=-1, keepdims=True) + epsilon)
        normed = (hidden * inv_rms * norm_gain[layer]).astype(bf16)
        w_in = lax.optimization_barrier(input_projection_weight)[layer]
        both = lax.dot_general(normed, w_in, (((1,), (0,)), ((), ())), preferred_element_type=f32)
        values, gate_pre = both[:, 0], both[:, 1]
        values3 = values.reshape(seqs, length, channels)
        edge = passed_along(values3[:, -(KERN - 1) :], "seq", 1)
        extended = jnp.concatenate([edge, values3], axis=1)
        conv_out, conv_pull = jax.vjp(
            functools.partial(conv_local, seg_ext=seg_ext), extended, conv_weight[layer], conv_bias[layer]
        )
        conv_out = conv_out.reshape(rows, channels)
        activated = jax.nn.silu(conv_out)
        act_low = activated.astype(bf16)
        proj_out = ch_sum(dot(act_low, proj_weight[layer], (1, 0)), nch, next(ids))
        rank_low = proj_out[:, :RANK].astype(bf16)
        mats = proj_out[:, RANK:]
        step_pre = dot(rank_low, step_weight[layer], (1, 0)) + step_bias[layer]
        rates = decay_log[layer]
        end_state, total = scan_local(step_pre, activated, mats, keep, rates, seqs, [], places, 0)
        gate_act = jax.nn.silu(gate_pre)
        if last:
            out_low = grad_rows.astype(bf16)
            grad_mixed = dot(out_low, output_projection_weight[layer], (1, 1))
            grad_scan = grad_mixed * gate_act
            start = scan_back_local(step_pre, grad_scan, mats, keep, rates, seqs)
            state_in, lam_in = carry_over(total, rates, [end_state, start], nseq, next(ids), True, True)
        else:
            (state_in,) = carry_over(total, rates, [end_state], nseq, next(ids), True, False)
        keeping = (hidden, inv_rms, normed, gate_pre, gate_act, conv_out, activated, act_low, conv_pull, rank_low,
                   step_pre, mats, total, state_in)
        if last:
            stored.append(keeping)
            break
        (y,) = scan_forward(step_pre, activated, mats, keep, rates, state_in, seqs, [], places, 0)
        scanned = y + skip_gain[layer] * activated
        mixed = (scanned * gate_act).astype(bf16)
        out_part = dot(mixed, output_projection_weight[layer], (1, 0)).astype(bf16)
        mixed_all = tokens_of_line(mixed, zs, ys)
        branch = ch_reduce(out_part, nch, next(ids), True)
        hidden = hidden + branch
        stored.append(keeping + (scanned, mixed_all))

    for layer in reversed(range(LAYERS)):
        last = layer == LAYERS - 1
        (hidden, inv_rms, normed, gate_pre, gate_act, conv_out, activated, act_low, conv_pull, rank_low,
         step_pre, mats, total, state_in) = stored[layer][:14]
        rates = decay_log[layer]
        if not last:
            scanned, mixed_all = stored[layer][14:]
            normed_cols = early_cols
            out_low = grad_rows.astype(bf16)
            grad_mixed = dot(out_low, output_projection_weight[layer], (1, 1))
            grad_scan = grad_mixed * gate_act
            grad_gate = (grad_mixed * scanned * silu_slope(gate_pre)).astype(bf16)
            start = scan_back_local(step_pre, grad_scan, mats, keep, rates, seqs)
            (lam_in,) = carry_over(total, rates, [start], nseq, next(ids), False, True)
        grad_skip = jnp.sum(grad_scan * activated, axis=0)
        if last:
            plan = [(ColumnsLine, (4, 6), v) for v in (normed, out_low, stored[0][2])]
        else:
            plan = [
                (ColumnsLine, (2, 4), out_low),
                (GatherLine, (4, 8), grad_gate),
                (PartSum, (), out_parts_last),
                (PartSum, (), gate_parts_last),
            ]
        grad_pre, grad_act, grad_mats, grad_decay, *others = scan_back(
            step_pre, activated, grad_scan, mats, keep, rates, skip_gain[layer][None], state_in, lam_in, seqs, int(last),
            plan, places, next(ids), (stored[0][15],) if last else (),
        )
        if last:
            y, normed_cols, out_cols[layer], early_cols = others
            scanned = y + skip_gain[layer] * activated
            mixed = (scanned * gate_act).astype(bf16)
            mixed_all = tokens_of_line(mixed, zs, ys)
            grad_gate = (grad_mixed * scanned * silu_slope(gate_pre)).astype(bf16)
            gate_all = tokens_of_line(grad_gate, zs, ys)
        else:
            out_cols[layer], gate_all, grad_out_last, grad_gate_last = others
        grad_step_bias = jnp.sum(grad_pre, axis=0)
        pre_low = grad_pre.astype(bf16)
        grad_step_weight = dot(rank_low, pre_low, (0, 0))
        rank_part = dot(pre_low, step_weight[layer], (1, 1))
        grad_proj = ch_sum(
            jnp.concatenate([rank_part, grad_mats[:, : 2 * STATE]], axis=-1), nch, next(ids)
        ).astype(bf16)
        grad_proj_weight = dot(grad_proj, act_low, (0, 0))
        grad_act = grad_act + dot(grad_proj, proj_weight[layer], (1, 1))
        grad_conv = (grad_act * silu_slope(conv_out)).reshape(seqs, length, channels)
        grad_ext, grad_conv_weight, grad_conv_bias = conv_pull(grad_conv)
        returned = passed_along(grad_ext[:, : KERN - 1], "seq", -1)
        grad_values = grad_ext[:, KERN - 1 :]
        grad_values = jnp.concatenate(
            [grad_values[:, : -(KERN - 1)], grad_values[:, -(KERN - 1) :] + returned], axis=1
        ).reshape(rows, channels).astype(bf16)
        w_in = lax.optimization_barrier(input_projection_weight)[layer]
        grad_both = jnp.stack([grad_values, grad_gate], axis=1)
        grad_part = lax.dot_general(grad_both, w_in, (((1, 2), (1, 2)), ((), ())), preferred_element_type=f32)
        scale_now = norm_gain[layer]
        misc = jnp.concatenate([grad_conv_weight, grad_conv_bias[None], grad_step_bias[None], grad_skip[None]], axis=0)
        small = [grad_proj_weight, grad_step_weight, grad_decay, misc]
        if last:
            values_last = tokens_of_line(grad_values, zs, ys)
            values_parts_last = dot(normed_cols, values_last, (0, 0)).astype(bf16).reshape(ys, fold, channels)
            grad_normed = ch_reduce(grad_part.astype(bf16), nch, next(ids), True)
            out_part = dot(mixed, output_projection_weight[layer], (1, 0)).astype(bf16)
            branch = ch_reduce(out_part, nch, next(ids), False)
            result = (lax.dynamic_slice_in_dim(hidden, share_start, share, 1) + branch).astype(bf16)
        columns = [out_cols[layer][:, k * fold : (k + 1) * fold] for k in range(ys)]
        out_parts = jnp.stack([dot(mixed_all, k, (0, 0)).astype(bf16) for k in columns], axis=0)
        gate_parts = dot(normed_cols, gate_all, (0, 0)).astype(bf16).reshape(ys, fold, channels)
        if last:
            out_parts_last, gate_parts_last = out_parts, gate_parts
            inner = jnp.sum(grad_normed * scale_now * hidden, axis=-1, keepdims=True)
            grad_norm = lax.dynamic_slice_in_dim(jnp.sum(grad_normed * hidden * inv_rms, axis=0), share_start, share, 0)
            grad_rows = grad_rows + inv_rms * scale_now * grad_normed - hidden * (inv_rms * inv_rms * inv_rms) * inner / width
            norm_row = jnp.pad(grad_norm[None], ((0, 0), (0, channels - share)))
            small[-1] = jnp.pad(jnp.concatenate([misc, norm_row], axis=0), ((0, 16 - misc.shape[0] - 1), (0, 0)))
            small_last = small
            continue
        inner = jnp.sum(grad_part * scale_now * hidden, axis=-1, keepdims=True)
        inner_high = inner.astype(bf16)
        inner_low = (inner - inner_high.astype(f32)).astype(bf16)
        beside = jnp.pad(jnp.concatenate([inner_high, inner_low], axis=1), ((0, 0), (0, LANES - 2)))
        beside = jnp.broadcast_to(beside[:, None], (rows, nch, LANES))
        send = jnp.concatenate([grad_part.astype(bf16).reshape(rows, nch, share), beside], axis=2)
        small[-1] = jnp.pad(misc, ((0, 16 - misc.shape[0]), (0, 0)))
        got, values_all, sums, grad_gate_now, grad_out_weight, grad_values_last = closing(
            send.reshape(rows, nch * (share + LANES)), grad_values, small + small_last, [gate_parts, out_parts, values_parts_last],
            nch, zs, ys, next(ids),
        )
        grad_share, inner = got[:, :share], got[:, share : share + 1] + got[:, share + 1 : share + 2]
        hidden_share = lax.dynamic_slice_in_dim(hidden, share_start, share, 1)
        scale_share = lax.dynamic_slice_in_dim(scale_now, share_start, share, 0)
        grad_norm = jnp.sum(grad_share * hidden_share * inv_rms, axis=0)
        grad_input = (
            lax.dynamic_slice_in_dim(grad_rows, share_start, share, 1)
            + inv_rms * scale_share * grad_share
            - hidden_share * (inv_rms * inv_rms * inv_rms) * inner / width
        )
        parts = dot(normed_cols, values_all, (0, 0)).astype(bf16).reshape(ys, fold, channels)
        tiny = jnp.pad(grad_norm.astype(bf16)[None], ((0, 15), (0, 0)))
        grad_in_values, tiny = last_sums(parts, tiny, nseq, zs, ys, next(ids))
        total_small = sums.astype(f32)
        heights = [v.shape[0] for v in small_last]
        half = sum(heights)
        pairs, at = [], 0
        for height in heights:
            pairs.append(jnp.stack([total_small[at : at + height], total_small[half + at : half + at + height]], axis=0))
            at += height
        misc = pairs[3]
        norms = jnp.stack([tiny[0], misc[1, KERN + 3, :share]], axis=0)
        in_weight = jnp.stack(
            [jnp.stack(pair, axis=1) for pair in ((grad_in_values, grad_gate_now), (grad_values_last, grad_gate_last))], axis=0
        )
        out_weight = jnp.stack([grad_out_weight, grad_out_last], axis=0)
    shape3 = (seqs, length, share)
    return (
        result.reshape(shape3),
        grad_input.reshape(shape3),
        norms,
        in_weight,
        misc[:, :KERN],
        misc[:, KERN],
        jnp.swapaxes(pairs[0], 1, 2),
        pairs[1],
        misc[:, KERN + 1],
        pairs[2],
        misc[:, KERN + 2],
        out_weight,
    )


def solution(mesh):
    in_specs = (
        P(None, "seq", None),
        P(None, "seq"),
        P(None, "seq", None),
        P(),
        P(None, None, None, "ch"),
        P(None, None, "ch"),
        P(None, "ch"),
        P(None, "ch", None),
        P(None, None, "ch"),
        P(None, "ch"),
        P(None, None, "ch"),
        P(None, "ch"),
        P(None, "ch", None),
    )
    out_specs = (
        P(None, "seq", "ch"),
        P(None, "seq", "ch"),
        P(None, "ch"),
        P(None, "seq", None, "ch"),
        P(None, None, "ch"),
        P(None, "ch"),
        P(None, "ch", None),
        P(None, None, "ch"),
        P(None, "ch"),
        P(None, None, "ch"),
        P(None, "ch"),
        P(None, "ch", "seq"),
    )
    return jax.shard_map(local, mesh=mesh, in_specs=in_specs, out_specs=out_specs, check_vma=False)
```

```python
import functools

import jax
import jax.numpy as jnp
from jax import lax
from jax.experimental import pallas as pl
from jax.experimental.pallas import tpu as pltpu
from jax.sharding import PartitionSpec as P

STATE = 16
RANK = 128
KERN = 4
LAYERS = 2
MESH = pl.DeviceIdType.MESH
ANY = pl.BlockSpec(memory_space=pl.ANY)
f32, bf16 = jnp.float32, jnp.bfloat16
epsilon = 1e-05


def after(kernel, count, pins):
    def run(*refs):
        return kernel(*refs[:count], *refs[count + len(pins) :])
    return run


def cost(us):
    return pl.CostEstimate(flops=int(us * 0.1e9), bytes_accessed=0, transcendentals=0)


LANES = 128
BIG = 1e30
LOG2E = 1.4426950408889634

def softplus(v):
    return jnp.maximum(v, 0.0) + jnp.log(1.0 + jnp.exp(-jnp.abs(v)))

def spread_states(bc_ref, wide_ref, pick_ref, rows, unroll=8):
    lane = lax.broadcasted_iota(jnp.int32, (STATE, 2 * STATE), 1)
    row = lax.broadcasted_iota(jnp.int32, (STATE, 2 * STATE), 0)
    mask = (lane % STATE == row).astype(jnp.float32)
    src = lax.broadcasted_iota(jnp.int32, (2 * STATE, 2 * LANES), 0)
    dst = lax.broadcasted_iota(jnp.int32, (2 * STATE, 2 * LANES), 1)
    route = ((src // STATE) == (dst // LANES)).astype(jnp.bfloat16)
    chunk = 32
    def step(i, _):
        t0 = pl.multiple_of(i * chunk, chunk)
        bcv = bc_ref[pl.ds(t0, chunk), :]
        for j in range(chunk):
            pick_ref[pl.ds(j * STATE, STATE), :] = (bcv[j:j + 1] * mask).astype(jnp.bfloat16)
        wide_ref[pl.ds(pl.multiple_of(t0 * STATE, chunk * STATE), chunk * STATE), :] = jnp.dot(pick_ref[...], route, preferred_element_type=jnp.float32)
        return 0
    lax.fori_loop(0, rows // chunk, step, 0)

def prep(step_ref_pre, act_ref, keep_ref, dstep_ref, dx_ref, rows):
    def body(i, _):
        sl = pl.ds(pl.multiple_of(i * 32, 32), 32)
        for g in range(dstep_ref.shape[0]):
            st = softplus(step_ref_pre[sl, lanes(g)])
            dstep_ref[g, sl, :] = jnp.where(keep_ref[sl, :] > 0.0, st, BIG)
            dx_ref[g, sl, :] = st * act_ref[sl, lanes(g)]
        return 0
    lax.fori_loop(0, rows // 32, body, 0)

def lanes(g):
    return pl.ds(g * LANES, LANES)

def group_sets(channels, width):
    n = channels // LANES
    return [list(range(i, min(i + width, n))) for i in range(0, n, width)]

def local_kernel(seqs, pre_ref, act_ref, bc_ref, keep_ref, dl_ref, end_ref, gain_ref, wide, pick, dstep, dx):
    rows, channels = pre_ref.shape
    length = rows // seqs
    spread_states(bc_ref, wide, pick, rows)
    prep(pre_ref, act_ref, keep_ref, dstep, dx, rows)
    yield
    for gs in group_sets(channels, 8):
        a2 = [-jnp.exp(dl_ref[:, lanes(g)]) * LOG2E for g in gs]
        for s in range(seqs):
            for k, g in enumerate(gs):
                tot = jnp.sum(dstep[g, pl.ds(s * length, length), :], axis=0, keepdims=True)
                gain_ref[pl.ds(s, 1), lanes(g)] = tot
            def blk(i, st):
                st = list(st)
                t0 = pl.multiple_of(s * length + i * 8, 8)
                for j in range(8):
                    b = wide[pl.ds(pl.multiple_of((t0 + j) * STATE, STATE), STATE), pl.ds(0, LANES)]
                    for k, g in enumerate(gs):
                        d = jnp.exp2(a2[k] * dstep[g, pl.ds(t0 + j, 1), :])
                        st[k] = d * st[k] + b * dx[g, pl.ds(t0 + j, 1), :]
                return tuple(st)
            st = lax.fori_loop(0, length // 8, blk, tuple(jnp.zeros((STATE, LANES), jnp.float32) for _ in gs))
            for k, g in enumerate(gs):
                end_ref[s, :, lanes(g)] = st[k]
            yield

VM = pl.BlockSpec(memory_space=pltpu.VMEM)


def played(kernel, counts, plan, places):
    n_in, n_out, n_scratch = counts

    def run(*refs):
        refs = list(refs)

        def take(k):
            head, refs[:] = refs[:k], refs[k:]
            return head

        own = take(n_in)
        sources = take(len(plan))
        own += take(n_out)
        targets = take(len(plan))
        own += take(n_scratch)
        jobs = []
        for (kind, when), src, out in zip(plan, sources, targets):
            jobs.append((kind(*places, src, out, take(kind.semaphores)), when))
        if plan:
            seq, ch = lax.axis_index("seq"), lax.axis_index("ch")
            zs, ys = places
            z, y = seq // ys, lax.rem(seq, ys)
            peers = [{"seq": lax.rem(z + d, zs) * ys + y} for d in range(1, zs)]
            peers += [{"seq": z * ys + lax.rem(y + d, ys)} for d in range(1, ys)]
            xs = lax.axis_size("ch") // 2
            peers += [{"ch": lax.rem(ch // 2 + e, xs) * 2 + lax.rem(ch, 2)} for e in range(1, xs)]
            peers.append({"ch": ch + 1 - 2 * lax.rem(ch, 2)})
            barrier = pltpu.get_barrier_semaphore()
            for peer in peers:
                pl.semaphore_signal(barrier, inc=1, device_id=peer, device_id_type=MESH)
        for at, _ in enumerate(kernel(*own)):
            if at == 0 and plan:
                pl.semaphore_wait(barrier, len(peers))
                for job, _ in jobs:
                    job.begin()
            for job, when in jobs:
                if at in when:
                    job.step(when.index(at))
        for job, when in jobs:
            job.finish()

    return run


def play_call(kernel, counts, plan, places, cid, out_shape, scratch, arrays, us, name, pins=()):
    arrays = list(arrays) + [v for _, _, v in plan]
    kinds = [(kind, when) for kind, when, _ in plan]
    out_shape = list(out_shape) + [kind.result(v, *places) for kind, _, v in plan]
    sems = [spec for kind, _, v in plan for spec in kind.specs(v, *places)]
    extra = dict(collective_id=cid, has_side_effects=True) if plan else {}
    return pl.pallas_call(
        after(played(kernel, counts, kinds, places), len(arrays), pins),
        out_shape=out_shape,
        in_specs=[VM] * len(arrays) + [ANY] * len(pins),
        out_specs=[VM] * len(out_shape),
        scratch_shapes=list(scratch) + sems,
        compiler_params=pltpu.CompilerParams(vmem_limit_bytes=60 * 2**20, **extra),
        cost_estimate=cost(us),
        name=name,
    )(*arrays, *pins)

def scan_local(pre, act, bc, keep, dl, seqs, plan, places, cid):
    rows, channels = pre.shape
    f = jnp.float32
    big = pltpu.VMEM((channels // LANES, rows, LANES), f)
    return play_call(
        functools.partial(local_kernel, seqs), (5, 2, 4), plan, places, cid,
        [jax.ShapeDtypeStruct((seqs, STATE, channels), f), jax.ShapeDtypeStruct((seqs, channels), f)],
        [pltpu.VMEM((rows * STATE, 2 * LANES), f), pltpu.VMEM((32 * STATE, 2 * STATE), jnp.bfloat16), big, big],
        (pre, act, bc, keep, dl), 8, "scan_local",
    )


def forward_kernel(seqs, pre_ref, act_ref, bc_ref, keep_ref, dl_ref, in_ref, y_ref, wide, pick, dstep, dx, part):
    rows, channels = pre_ref.shape
    length = rows // seqs
    spread_states(bc_ref, wide, pick, rows)
    prep(pre_ref, act_ref, keep_ref, dstep, dx, rows)
    yield
    for gs in group_sets(channels, 4):
        a2 = [-jnp.exp(dl_ref[:, lanes(g)]) * LOG2E for g in gs]
        for s in range(seqs):
            def blk(i, st):
                st = list(st)
                t0 = pl.multiple_of(s * length + i * 8, 8)
                for j in range(8):
                    at = pl.ds(pl.multiple_of((t0 + j) * STATE, STATE), STATE)
                    b = wide[at, pl.ds(0, LANES)]
                    c = wide[at, pl.ds(LANES, LANES)]
                    for k, g in enumerate(gs):
                        d = jnp.exp2(a2[k] * dstep[g, pl.ds(t0 + j, 1), :])
                        st[k] = d * st[k] + b * dx[g, pl.ds(t0 + j, 1), :]
                        v = st[k] * c
                        part[k, pl.ds(pl.multiple_of(i * 64 + j * 8, 8), 8), :] = v[:8] + v[8:]
                return tuple(st)
            lax.fori_loop(0, length // 8, blk, tuple(in_ref[s, :, lanes(g)] for g in gs))
            def red(i, _):
                t0 = pl.multiple_of(s * length + i * 8, 8)
                for k, g in enumerate(gs):
                    acc = part[k, pl.ds(i * 64, 8, stride=8), :]
                    for m in range(1, 8):
                        acc = acc + part[k, pl.ds(i * 64 + m, 8, stride=8), :]
                    y_ref[pl.ds(t0, 8), lanes(g)] = acc
                return 0
            lax.fori_loop(0, length // 8, red, 0)
            yield

def scan_forward(pre, act, bc, keep, dl, state_in, seqs, plan, places, cid, pins=()):
    rows, channels = pre.shape
    f = jnp.float32
    big = pltpu.VMEM((channels // LANES, rows, LANES), f)
    return play_call(
        functools.partial(forward_kernel, seqs), (6, 1, 5), plan, places, cid,
        [jax.ShapeDtypeStruct((rows, channels), f)],
        [pltpu.VMEM((rows * STATE, 2 * LANES), f), pltpu.VMEM((32 * STATE, 2 * STATE), jnp.bfloat16), big, big,
         pltpu.VMEM((4, rows // seqs * 8, LANES), f)],
        (pre, act, bc, keep, dl, state_in), 11, "scan_forward", pins,
    )


LN2 = 0.6931471805599453

def back_local_kernel(seqs, pre_ref, gs_ref, bc_ref, keep_ref, dl_ref, out_ref, wide, pick, dstep, gsc):
    rows, channels = pre_ref.shape
    length = rows // seqs
    spread_states(bc_ref, wide, pick, rows)
    def body(i, _):
        sl = pl.ds(pl.multiple_of(i * 32, 32), 32)
        for g in range(channels // LANES):
            st = softplus(pre_ref[sl, lanes(g)])
            dstep[g, sl, :] = jnp.where(keep_ref[sl, :] > 0.0, st, BIG)
            gsc[g, sl, :] = gs_ref[sl, lanes(g)]
        return 0
    lax.fori_loop(0, rows // 32, body, 0)
    for gs in group_sets(channels, 8):
        a2 = [-jnp.exp(dl_ref[:, lanes(g)]) * LOG2E for g in gs]
        for s in range(seqs):
            def blk(i, st):
                st = list(st)
                t0 = pl.multiple_of(s * length + (length // 8 - 1 - i) * 8, 8)
                for j in reversed(range(8)):
                    c = wide[pl.ds(pl.multiple_of((t0 + j) * STATE, STATE), STATE), pl.ds(LANES, LANES)]
                    for k, g in enumerate(gs):
                        d = jnp.exp2(a2[k] * dstep[g, pl.ds(t0 + j, 1), :])
                        st[k] = d * (st[k] + c * gsc[g, pl.ds(t0 + j, 1), :])
                return tuple(st)
            st = lax.fori_loop(0, length // 8, blk, tuple(jnp.zeros((STATE, LANES), jnp.float32) for _ in gs))
            for k, g in enumerate(gs):
                out_ref[s, :, lanes(g)] = st[k]

def scan_back_local(pre, gs, bc, keep, dl, seqs, pins=()):
    rows, channels = pre.shape
    f = jnp.float32
    return pl.pallas_call(
        after(functools.partial(back_local_kernel, seqs), 5, pins),
        out_shape=jax.ShapeDtypeStruct((seqs, STATE, channels), f),
        in_specs=[VM] * 5 + [ANY] * len(pins), out_specs=VM,
        scratch_shapes=[pltpu.VMEM((rows * STATE, 2 * LANES), f), pltpu.VMEM((32 * STATE, 2 * STATE), jnp.bfloat16),
                        pltpu.VMEM((channels // LANES, rows, LANES), f), pltpu.VMEM((channels // LANES, rows, LANES), f)],
        compiler_params=pltpu.CompilerParams(vmem_limit_bytes=60 * 2**20),
        cost_estimate=cost(8),
        name="scan_back_local",
    )(pre, gs, bc, keep, dl, *pins)

def back_kernel(seqs, with_y, pre_ref, act_ref, gs_ref, bc_ref, keep_ref, dl_ref, skip_ref, in_ref, lam_ref,
                gpre_ref, gact_ref, gbc_ref, gdl_ref, *rest):
    if with_y:
        y_ref, *rest = rest
    (wide, pick, dstep, dx, stepc, gsc, states, partq, partr, accb, accc, rowsum) = rest
    rows, channels = pre_ref.shape
    length = rows // seqs
    f = jnp.float32
    spread_states(bc_ref, wide, pick, rows)
    def body(i, _):
        sl = pl.ds(pl.multiple_of(i * 32, 32), 32)
        for g in range(channels // LANES):
            st = softplus(pre_ref[sl, lanes(g)])
            stepc[g, sl, :] = st
            dstep[g, sl, :] = jnp.where(keep_ref[sl, :] > 0.0, st, BIG)
            dx[g, sl, :] = st * act_ref[sl, lanes(g)]
            gsc[g, sl, :] = gs_ref[sl, lanes(g)]
        return 0
    lax.fori_loop(0, rows // 32, body, 0)
    yield
    sets = group_sets(channels, 4)
    for index, gs in enumerate(sets):
        a2 = [-jnp.exp(dl_ref[:, lanes(g)]) * LOG2E for g in gs]
        gdl = [jnp.zeros((STATE, LANES), f) for _ in gs]
        for s in range(seqs):
            for k, g in enumerate(gs):
                states[k, pl.ds(0, STATE), :] = in_ref[s, :, lanes(g)]
            def fwd(i, st):
                st = list(st)
                t0 = pl.multiple_of(s * length + i * 8, 8)
                for j in range(8):
                    at = pl.ds(pl.multiple_of((t0 + j) * STATE, STATE), STATE)
                    b = wide[at, pl.ds(0, LANES)]
                    if with_y:
                        c = wide[at, pl.ds(LANES, LANES)]
                    for k, g in enumerate(gs):
                        d = jnp.exp2(a2[k] * dstep[g, pl.ds(t0 + j, 1), :])
                        st[k] = d * st[k] + b * dx[g, pl.ds(t0 + j, 1), :]
                        states[k, pl.ds(pl.multiple_of((i * 8 + j + 1) * STATE, STATE), STATE), :] = st[k]
                        if with_y:
                            v = st[k] * c
                            partq[k, pl.ds(pl.multiple_of(i * 64 + j * 8, 8), 8), :] = v[:8] + v[8:]
                return tuple(st)
            lax.fori_loop(0, length // 8, fwd, tuple(in_ref[s, :, lanes(g)] for g in gs))
            if with_y:
                def read(i, _):
                    t0 = pl.multiple_of(s * length + i * 8, 8)
                    for k, g in enumerate(gs):
                        acc = partq[k, pl.ds(i * 64, 8, stride=8), :]
                        for m in range(1, 8):
                            acc = acc + partq[k, pl.ds(i * 64 + m, 8, stride=8), :]
                        y_ref[pl.ds(t0, 8), lanes(g)] = acc
                    return 0
                lax.fori_loop(0, length // 8, read, 0)
            yield
            def bwd(i, carry):
                st = list(carry[:len(gs)])
                am = list(carry[len(gs):])
                l0 = (length // 8 - 1 - i) * 8
                t0 = pl.multiple_of(s * length + l0, 8)
                for j in reversed(range(8)):
                    at = pl.ds(pl.multiple_of((t0 + j) * STATE, STATE), STATE)
                    b = wide[at, pl.ds(0, LANES)]
                    c = wide[at, pl.ds(LANES, LANES)]
                    tb = tc = None
                    here = pl.ds(pl.multiple_of((l0 + j) * 8, 8), 8)
                    for k, g in enumerate(gs):
                        row = pl.ds(t0 + j, 1)
                        grow = gsc[g, row, :]
                        d = jnp.exp2(a2[k] * dstep[g, row, :])
                        lam = st[k] + c * grow
                        old = states[k, pl.ds(pl.multiple_of((l0 + j) * STATE, STATE), STATE), :]
                        new = states[k, pl.ds(pl.multiple_of((l0 + j + 1) * STATE, STATE), STATE), :]
                        st[k] = d * lam
                        lp = st[k] * old
                        q = lam * b
                        partq[k, here, :] = q[:8] + q[8:]
                        r = lp * a2[k]
                        partr[k, here, :] = r[:8] + r[8:]
                        am[k] = am[k] + lp * stepc[g, row, :]
                        u = lam * dx[g, row, :]
                        v = new * grow
                        tb = u if tb is None else tb + u
                        tc = v if tc is None else tc + v
                    if index > 0:
                        tb = tb + accb[at, :]
                        tc = tc + accc[at, :]
                    accb[at, :] = tb
                    accc[at, :] = tc
                return tuple(st) + tuple(am)
            out = lax.fori_loop(0, length // 8, bwd, tuple(lam_ref[s, :, lanes(g)] for g in gs) + tuple(gdl))
            gdl = list(out[len(gs):])
            def red(i, _):
                t0 = pl.multiple_of(s * length + i * 8, 8)
                for k, g in enumerate(gs):
                    q = partq[k, pl.ds(i * 64, 8, stride=8), :]
                    r = partr[k, pl.ds(i * 64, 8, stride=8), :]
                    for m in range(1, 8):
                        q = q + partq[k, pl.ds(i * 64 + m, 8, stride=8), :]
                        r = r + partr[k, pl.ds(i * 64 + m, 8, stride=8), :]
                    here = pl.ds(t0, 8)
                    p = pre_ref[here, lanes(g)]
                    gstep = r * LN2 + act_ref[here, lanes(g)] * q
                    gpre_ref[here, lanes(g)] = gstep * (1.0 / (1.0 + jnp.exp(-p)))
                    gact_ref[here, lanes(g)] = stepc[g, here, :] * q + gsc[g, here, :] * skip_ref[:, lanes(g)]
                return 0
            lax.fori_loop(0, length // 8, red, 0)
            yield
        for k, g in enumerate(gs):
            gdl_ref[:, lanes(g)] = gdl[k] * (a2[k] * LN2)
    ones = jnp.ones((LANES, LANES), jnp.bfloat16)
    lane = lax.broadcasted_iota(jnp.int32, (32 * STATE, LANES), 1)
    row = lax.broadcasted_iota(jnp.int32, (32 * STATE, LANES), 0) % STATE
    mb = lane == row
    mc = lane == row + STATE
    def fin(i, _):
        sl = pl.ds(pl.multiple_of(i * 32 * STATE, 32 * STATE), 32 * STATE)
        sb = jnp.dot(accb[sl, :].astype(jnp.bfloat16), ones, preferred_element_type=f)
        sc = jnp.dot(accc[sl, :].astype(jnp.bfloat16), ones, preferred_element_type=f)
        rowsum[...] = jnp.where(mb, sb, jnp.where(mc, sc, 0.0))
        acc = rowsum[pl.ds(0, 32, stride=STATE), :]
        for m in range(1, STATE):
            acc = acc + rowsum[pl.ds(m, 32, stride=STATE), :]
        gbc_ref[pl.ds(pl.multiple_of(i * 32, 32), 32), :] = acc
        return 0
    lax.fori_loop(0, rows // 32, fin, 0)

def scan_back(pre, act, gs, bc, keep, dl, skip, state_in, lam_in, seqs, with_y, plan, places, cid, pins=()):
    rows, channels = pre.shape
    f = jnp.float32
    groups = channels // LANES
    length = rows // seqs
    big = pltpu.VMEM((groups, rows, LANES), f)
    whole = jax.ShapeDtypeStruct((rows, channels), f)
    return play_call(
        functools.partial(back_kernel, seqs, with_y), (9, 4 + with_y, 12), plan, places, cid,
        [whole, whole, jax.ShapeDtypeStruct((rows, LANES), f), jax.ShapeDtypeStruct((STATE, channels), f)] + [whole] * with_y,
        [pltpu.VMEM((rows * STATE, 2 * LANES), f), pltpu.VMEM((32 * STATE, 2 * STATE), jnp.bfloat16),
         big, big, big, big,
         pltpu.VMEM((4, (length + 1) * STATE, LANES), f),
         pltpu.VMEM((4, length * 8, LANES), f), pltpu.VMEM((4, length * 8, LANES), f),
         pltpu.VMEM((rows * STATE, LANES), f), pltpu.VMEM((rows * STATE, LANES), f),
         pltpu.VMEM((32 * STATE, LANES), f)],
        (pre, act, gs, bc, keep, dl, skip, state_in, lam_in), 23 + 3 * with_y, "scan_back", pins,
    )


def greet(peers):
    barrier = pltpu.get_barrier_semaphore()
    for p in peers:
        pl.semaphore_signal(barrier, inc=1, device_id=p, device_id_type=MESH)
    pl.semaphore_wait(barrier, len(peers))

def ch_sum_kernel(n, x_ref, out_ref, mine, slots, send, recv):
    me = lax.axis_index("ch")
    peers = [{"ch": lax.rem(me + d, n)} for d in range(1, n)]
    greet(peers)
    mine[...] = x_ref[...].astype(bf16)
    copies = []
    for d in range(1, n):
        c = pltpu.make_async_remote_copy(src_ref=mine, dst_ref=slots.at[d - 1], send_sem=send.at[d - 1], recv_sem=recv.at[d - 1], device_id=peers[d - 1], device_id_type=MESH)
        c.start()
        copies.append(c)
    total = x_ref[...].astype(bf16).astype(f32)
    for d, c in zip(range(1, n), copies):
        c.wait()
        total = total + slots[d - 1].astype(f32)
    out_ref[...] = total

def ch_sum(x, n, cid, pins=()):
    return pl.pallas_call(
        after(functools.partial(ch_sum_kernel, n), 1, pins),
        out_shape=jax.ShapeDtypeStruct(x.shape, f32), in_specs=[VM] + [ANY] * len(pins), out_specs=VM,
        scratch_shapes=[pltpu.VMEM(x.shape, bf16), pltpu.VMEM((n - 1,) + x.shape, bf16), pltpu.SemaphoreType.DMA((n - 1,)), pltpu.SemaphoreType.DMA((n - 1,))],
        compiler_params=pltpu.CompilerParams(collective_id=cid, has_side_effects=True, vmem_limit_bytes=32 * 2**20), cost_estimate=cost(10), name="ch_sum",
    )(x, *pins)

def reduce_steps(n, parts, gather, more, x_ref, out_ref, s1, sum1, s2, mine, got, fin, sem1, rem1, sem2, rem2, sem3, rem3, sem4, rem4):
    xs = n // 2
    me = lax.axis_index("ch")
    x, core = me // 2, lax.rem(me, 2)
    peer = {"ch": x * 2 + 1 - core}
    others = [lax.rem(x + d, xs) for d in range(1, xs)]
    if more is not None:
        greet([peer] + [{"ch": o * 2 + core} for o in others] + more)
    rows, width = x_ref.shape[0] // parts, x_ref.shape[1] // n
    def cols(block):
        return pl.ds(pl.multiple_of(block * width, width), width)
    def stage1(p, k):
        return pltpu.make_async_remote_copy(src_ref=x_ref.at[pl.ds(p * rows, rows), cols(k * 2 + 1 - core)], dst_ref=s1.at[p, k], send_sem=sem1.at[p, k], recv_sem=rem1.at[p, k], device_id=peer, device_id_type=MESH)
    def stage2(p, d):
        o = others[d]
        return pltpu.make_async_remote_copy(src_ref=sum1.at[p, o], dst_ref=s2.at[p, d], send_sem=sem2.at[p, d], recv_sem=rem2.at[p, d], device_id={"ch": o * 2 + core}, device_id_type=MESH)
    def stage3(p, d):
        o = others[d]
        return pltpu.make_async_remote_copy(src_ref=mine.at[p], dst_ref=got.at[p, d], send_sem=sem3.at[p, d], recv_sem=rem3.at[p, d], device_id={"ch": o * 2 + core}, device_id_type=MESH)
    for p in range(parts):
        for k in range(xs):
            stage1(p, k).start()
    yield
    for p in range(parts):
        for k in range(xs):
            stage1(p, k).wait_recv()
            sum1[p, k] = (x_ref[pl.ds(p * rows, rows), cols(k * 2 + core)].astype(f32) + s1[p, k].astype(f32)).astype(bf16)
        for d in range(xs - 1):
            stage2(p, d).start()
    yield
    for p in range(parts):
        total = sum1[p, x].astype(f32)
        for d in range(xs - 1):
            stage2(p, d).wait_recv()
            total = total + s2[p, d].astype(f32)
        if gather:
            mine[p] = total.astype(bf16)
            for d in range(xs - 1):
                stage3(p, d).start()
        else:
            out_ref[pl.ds(p * rows, rows), :] = total
    yield
    if gather:
        def stage4(p, d):
            src = mine.at[p] if d < 0 else got.at[p, d]
            return pltpu.make_async_remote_copy(src_ref=src, dst_ref=fin.at[p, d + 1], send_sem=sem4.at[p, d + 1], recv_sem=rem4.at[p, d + 1], device_id=peer, device_id_type=MESH)
        def chip(d):
            return lax.rem(x + xs - 1 - d, xs)
        for p in range(parts):
            stage4(p, -1).start()
            out_ref[pl.ds(p * rows, rows), cols(me)] = mine[p].astype(out_ref.dtype)
            for d in range(xs - 1):
                stage3(p, d).wait_recv()
                stage4(p, d).start()
                out_ref[pl.ds(p * rows, rows), cols(chip(d) * 2 + core)] = got[p, d].astype(out_ref.dtype)
        yield
        for p in range(parts):
            for d in range(-1, xs - 1):
                stage4(p, d).wait_recv()
                out_ref[pl.ds(p * rows, rows), cols(chip(d) * 2 + 1 - core)] = fin[p, d + 1].astype(out_ref.dtype)
    for p in range(parts):
        for k in range(xs):
            stage1(p, k).wait_send()
        for d in range(xs - 1):
            stage2(p, d).wait_send()
            if gather:
                stage3(p, d).wait_send()
        if gather:
            for d in range(-1, xs - 1):
                stage4(p, d).wait_send()
    yield


class ColumnsLine:
    semaphores = 6

    @staticmethod
    def result(v, zs, ys):
        return jax.ShapeDtypeStruct((zs * v.shape[0], v.shape[1] // zs), v.dtype)

    @staticmethod
    def specs(v, zs, ys):
        sem = pltpu.SemaphoreType.DMA
        xs = lax.axis_size("ch") // 2
        return [sem((zs - 1,))] * 2 + [sem((zs - 1, xs - 1))] * 2 + [sem((zs - 1, xs))] * 2

    def __init__(self, zs, ys, src, out, sems):
        seq, ch = lax.axis_index("seq"), lax.axis_index("ch")
        self.nch = lax.axis_size("ch")
        self.xs = self.nch // 2
        self.zs, self.ys, self.z, self.y, self.ch = zs, ys, seq // ys, lax.rem(seq, ys), ch
        self.x, self.core = ch // 2, lax.rem(ch, 2)
        self.src, self.out, self.sems = src, out, sems
        self.rows, self.width = src.shape[0], src.shape[1] // zs
        self.part = self.rows // self.nch

    def cols(self, z):
        return pl.ds(pl.multiple_of(z * self.width, self.width), self.width)

    def share(self, z, ch):
        return pl.ds(pl.multiple_of(z * self.rows + ch * self.part, self.part), self.part)

    def remote(self, k, at, src, dst, to):
        send, recv = self.sems[2 * k : 2 * k + 2]
        return pltpu.make_async_remote_copy(src_ref=src, dst_ref=dst, send_sem=send.at[at], recv_sem=recv.at[at], device_id=to, device_id_type=MESH)

    def along(self, d):
        to = lax.rem(self.z + d, self.zs)
        src = self.src.at[pl.ds(pl.multiple_of(self.ch * self.part, self.part), self.part), self.cols(to)]
        return self.remote(0, d - 1, src, self.out.at[self.share(self.z, self.ch)], {"seq": to * self.ys + self.y})

    def from_z(self, d):
        return lax.rem(self.z + self.zs - d, self.zs)

    def over(self, d, e):
        rows = self.out.at[self.share(self.from_z(d), self.ch)]
        return self.remote(1, (d - 1, e - 1), rows, rows, {"ch": lax.rem(self.x + e, self.xs) * 2 + self.core})

    def across(self, d, e):
        rows = self.out.at[self.share(self.from_z(d), lax.rem(self.x + self.xs - e, self.xs) * 2 + self.core)]
        return self.remote(2, (d - 1, e), rows, rows, {"ch": self.x * 2 + 1 - self.core})

    def lags(self):
        return range(1, self.zs)

    def begin(self):
        for d in self.lags():
            self.along(d).start()
        here = pl.ds(pl.multiple_of(self.z * self.rows, self.rows), self.rows)
        self.out[here, :] = self.src[:, self.cols(self.z)]

    def step(self, index):
        for d in self.lags():
            if index == 0:
                self.along(d).wait_recv()
                for e in range(1, self.xs):
                    self.over(d, e).start()
                self.across(d, 0).start()
            else:
                for e in range(1, self.xs):
                    self.over(d, e).wait_recv()
                    self.across(d, e).start()

    def finish(self):
        for d in self.lags():
            for e in range(self.xs):
                self.across(d, e).wait_recv()
        for d in self.lags():
            self.along(d).wait_send()
            for e in range(1, self.xs):
                self.over(d, e).wait_send()
            for e in range(self.xs):
                self.across(d, e).wait_send()


def reduce_kernel(n, parts, gather, *refs):
    for _ in reduce_steps(n, parts, gather, [], *refs):
        pass


def reduce_scratch_shapes(shape, n, parts):
    rows, width = shape
    xs, r, w = n // 2, rows // parts, width // n
    sem = pltpu.SemaphoreType.DMA
    return [
        pltpu.VMEM((parts, xs, r, w), bf16), pltpu.VMEM((parts, xs, r, w), bf16), pltpu.VMEM((parts, xs - 1, r, w), bf16),
        pltpu.VMEM((parts, r, w), bf16), pltpu.VMEM((parts, xs - 1, r, w), bf16), pltpu.VMEM((parts, xs, r, w), bf16),
        sem((parts, xs)), sem((parts, xs)), sem((parts, xs - 1)), sem((parts, xs - 1)),
        sem((parts, xs - 1)), sem((parts, xs - 1)), sem((parts, xs)), sem((parts, xs)),
    ]


def ch_reduce(x, n, cid, gather, parts=2):
    rows, width = x.shape
    return pl.pallas_call(
        functools.partial(reduce_kernel, n, parts, gather),
        out_shape=jax.ShapeDtypeStruct((rows, width if gather else width // n), f32),
        in_specs=[VM], out_specs=VM,
        scratch_shapes=reduce_scratch_shapes(x.shape, n, parts),
        compiler_params=pltpu.CompilerParams(collective_id=cid, has_side_effects=True, vmem_limit_bytes=48 * 2**20),
        cost_estimate=cost(18), name="ch_reduce",
    )(x)


def carry_kernel(n, fwd, rev, count, places, layer, *refs):
    refs = list(refs)
    tot_ref, dl_ref = refs.pop(0), refs.pop(0)
    k = fwd + rev
    ends = [refs.pop(0) for _ in range(k)]
    parts = [refs.pop(0) for _ in range(count)]
    whole = refs.pop(0) if layer is not None else None
    outs = [refs.pop(0) for _ in range(k)]
    sums = [refs.pop(0) for _ in range(count)]
    if layer is not None:
        local = pltpu.make_async_copy(whole.at[layer], refs.pop(0), refs.pop(-1))
        local.start()
    mine, slots, tots, send, recv, tsend, trecv = refs[:7]
    jobs = [PartSum(*places, parts[j], sums[j], refs[7 + 3 * j : 10 + 3 * j]) for j in range(count)]
    me = lax.axis_index("seq")
    seqs = tot_ref.shape[0]
    greet([{"seq": lax.rem(me + d, n)} for d in range(1, n)])
    a2 = -jnp.exp(dl_ref[...]) * LOG2E
    directions = [False] * fwd + [True] * rev
    def copies(i, d):
        away = -d if directions[i] else d
        to = {"seq": lax.rem(me + away + n, n)}
        return (
            pltpu.make_async_remote_copy(src_ref=mine.at[i], dst_ref=slots.at[i, d - 1], send_sem=send.at[i, d - 1], recv_sem=recv.at[i, d - 1], device_id=to, device_id_type=MESH),
            pltpu.make_async_remote_copy(src_ref=tot_ref, dst_ref=tots.at[i, d - 1], send_sem=tsend.at[i, d - 1], recv_sem=trecv.at[i, d - 1], device_id=to, device_id_type=MESH),
        )
    for i in range(k):
        mine[i] = ends[i][...].astype(bf16)
        outs[i][...] = jnp.zeros_like(outs[i])
    for d in reversed(range(1, n)):
        for i in range(k):
            place = n - 1 - me if directions[i] else me
            @pl.when(place + d < n)
            def _():
                for c in copies(i, d):
                    c.start()
    for job in jobs:
        job.begin()
    for d in reversed(range(1, n)):
        for i in range(k):
            place = n - 1 - me if directions[i] else me
            @pl.when(place >= d)
            def _():
                for c in copies(i, d):
                    c.wait_recv()
                for s in range(seqs):
                    gain = jnp.exp2(a2 * tots[i, d - 1, pl.ds(s, 1), :])
                    outs[i][s] = gain * outs[i][s] + slots[i, d - 1, s].astype(f32)
    for d in reversed(range(1, n)):
        for i in range(k):
            place = n - 1 - me if directions[i] else me
            @pl.when(place + d < n)
            def _():
                for c in copies(i, d):
                    c.wait_send()
    for job in jobs:
        job.finish()
    if layer is not None:
        local.wait()


def carry_over(tot, dl, ends, n, cid, fwd, rev, ps=(), places=(), taken=None):
    whole, layer = (None, None) if taken is None else taken
    extra = [] if taken is None else [whole]
    k = len(ends)
    sem = pltpu.SemaphoreType.DMA
    return pl.pallas_call(
        functools.partial(carry_kernel, n, int(fwd), int(rev), len(ps), places, layer),
        out_shape=[jax.ShapeDtypeStruct(ends[0].shape, f32)] * k + [PartSum.result(p, *places) for p in ps]
        + [jax.ShapeDtypeStruct(w.shape[1:], w.dtype) for w in extra],
        in_specs=[VM] * (k + 2 + len(ps)) + [ANY] * len(extra), out_specs=[VM] * (k + len(ps)) + [ANY] * len(extra),
        scratch_shapes=[pltpu.VMEM((k,) + ends[0].shape, bf16), pltpu.VMEM((k, n - 1) + ends[0].shape, bf16), pltpu.VMEM((k, n - 1) + tot.shape, f32),
                        sem((k, n - 1)), sem((k, n - 1)), sem((k, n - 1)), sem((k, n - 1))]
        + [spec for p in ps for spec in PartSum.specs(p, *places)]
        + [pltpu.SemaphoreType.DMA] * len(extra),
        compiler_params=pltpu.CompilerParams(collective_id=cid, has_side_effects=True, vmem_limit_bytes=32 * 2**20), cost_estimate=cost(19), name="carry_over",
    )(tot, dl, *ends, *ps, *extra)


def seq_at(z, y, ys):
    return {"seq": z * ys + y}


class GatherLine:
    semaphores = 2

    @staticmethod
    def result(v, zs, ys):
        return jax.ShapeDtypeStruct((zs * v.shape[0], v.shape[1]), v.dtype)

    @staticmethod
    def specs(v, zs, ys):
        return [pltpu.SemaphoreType.DMA((2, zs - 1))] * 2


    def __init__(self, zs, ys, src, out, sems):
        me = lax.axis_index("seq")
        self.zs, self.ys, self.z, self.y = zs, ys, me // ys, lax.rem(me, ys)
        self.src, self.out = src, out
        self.send, self.recv = sems
        self.rows = src.shape[0]

    def block(self, z):
        return self.out.at[pl.ds(pl.multiple_of(z * self.rows, self.rows), self.rows)]

    def copy(self, way, r):
        z = self.z
        to, b = (lax.rem(z + 1, self.zs), z - r) if way == 0 else (lax.rem(z + self.zs - 1, self.zs), z + r)
        b = lax.rem(b + self.zs, self.zs)
        return pltpu.make_async_remote_copy(
            src_ref=self.src if r == 0 else self.block(b),
            dst_ref=self.block(b),
            send_sem=self.send.at[way, r],
            recv_sem=self.recv.at[way, r],
            device_id=seq_at(to, self.y, self.ys),
            device_id_type=MESH,
        )

    def sends(self, way, r):
        z, last = self.z, self.zs - 1
        return jnp.logical_and(z < last, z >= r) if way == 0 else jnp.logical_and(z > 0, z + r <= last)

    def receives(self, way, r):
        z, last = self.z, self.zs - 1
        return z - 1 - r >= 0 if way == 0 else z + 1 + r <= last

    def begin(self):
        self.start(0)
        self.block(self.z)[...] = self.src[...]

    def step(self, index):
        self.start(index + 1)

    def start(self, r):
        for way in (0, 1):
            if r > 0:
                self.arrive(way, r - 1)
            @pl.when(self.sends(way, r))
            def _():
                self.copy(way, r).start()

    def arrive(self, way, r):
        @pl.when(self.receives(way, r))
        def _():
            self.copy(way, r).wait_recv()

    def finish(self):
        self.arrived()
        self.sent()

    def arrived(self):
        for way in (0, 1):
            self.arrive(way, self.zs - 2)

    def sent(self):
        for way in (0, 1):
            for r in range(self.zs - 1):
                @pl.when(self.sends(way, r))
                def _():
                    self.copy(way, r).wait_send()


class SumAll:
    def __init__(self, zs, ys, src, out, scratch):
        me = lax.axis_index("seq")
        self.zs, self.ys, self.z, self.y = zs, ys, me // ys, lax.rem(me, ys)
        self.src, self.out = src, out
        self.yslots, self.ysum, self.slots, self.running, self.acc = scratch[:5]
        self.y1sems, self.zsems, self.y2sems, gather = scratch[5:7], scratch[7:9], scratch[9:11], scratch[11:13]
        self.part = src.shape[0] // ys
        self.share = self.part // zs
        self.back = GatherLine(zs, ys, self.mine(self.z), out, gather)
        self.back.block = self.mine

    @staticmethod
    def specs(height, w, zs, ys):
        part = height // ys
        share = part // zs
        sem = pltpu.SemaphoreType.DMA
        return [
            pltpu.VMEM((ys - 1, part, w), bf16),
            pltpu.VMEM((part, w), bf16),
            pltpu.VMEM((2, zs, share, w), bf16),
            pltpu.VMEM((2, zs, share, w), bf16),
            pltpu.VMEM((share, w), f32),
            sem((ys - 1,)), sem((ys - 1,)), sem((2, zs)), sem((2, zs)), sem(((ys - 1) * zs,)), sem(((ys - 1) * zs,)),
            sem((2, zs - 1)), sem((2, zs - 1)),
        ]

    def rows(self, index, size):
        return pl.ds(pl.multiple_of(index * size, size), size)

    def mine(self, z):
        return self.out.at[self.rows(self.y * self.zs + z, self.share)]

    def y1(self, d):
        to = lax.rem(self.y + d, self.ys)
        return pltpu.make_async_remote_copy(src_ref=self.src.at[self.rows(to, self.part)], dst_ref=self.yslots.at[d - 1], send_sem=self.y1sems[0].at[d - 1], recv_sem=self.y1sems[1].at[d - 1], device_id=seq_at(self.z, to, self.ys), device_id_type=MESH)

    def run(self, way, k):
        to = lax.rem(self.z + (1 if way == 0 else self.zs - 1), self.zs)
        return pltpu.make_async_remote_copy(src_ref=self.running.at[way, k], dst_ref=self.slots.at[way, k], send_sem=self.zsems[0].at[way, k], recv_sem=self.zsems[1].at[way, k], device_id=seq_at(to, self.y, self.ys), device_id_type=MESH)

    def y2(self, d, b):
        to = lax.rem(self.y + d, self.ys)
        at = (d - 1) * self.zs + b
        return pltpu.make_async_remote_copy(src_ref=self.mine(b), dst_ref=self.mine(b), send_sem=self.y2sems[0].at[at], recv_sem=self.y2sems[1].at[at], device_id=seq_at(self.z, to, self.ys), device_id_type=MESH)

    def begin(self):
        for d in range(1, self.ys):
            self.y1(d).start()

    def middle(self):
        total = self.src[self.rows(self.y, self.part), :].astype(f32)
        for d in range(1, self.ys):
            self.y1(d).wait_recv()
            total = total + self.yslots[d - 1].astype(f32)
        self.ysum[...] = total.astype(bf16)

    def line_sum(self, r):
        for way in (0, 1):
            k = self.zs - 1 - r if way == 0 else r
            z, first = self.z, 0 if way == 0 else self.zs - 1
            own = pl.ds(k * self.share, self.share)
            @pl.when(z == first)
            def _():
                self.running[way, k] = self.ysum[own, :]
                self.run(way, k).start()
            inside = jnp.logical_and(z > 0, z < k) if way == 0 else jnp.logical_and(z < self.zs - 1, z > k)
            @pl.when(inside)
            def _():
                self.run(way, k).wait_recv()
                self.running[way, k] = (self.ysum[own, :].astype(f32) + self.slots[way, k].astype(f32)).astype(bf16)
                self.run(way, k).start()

    def turn(self):
        self.acc[...] = self.ysum[self.rows(self.z, self.share), :].astype(f32)
        for way in (0, 1):
            @pl.when(self.z > 0 if way == 0 else self.z < self.zs - 1)
            def _():
                self.run(way, self.z).wait_recv()
                self.acc[...] = self.acc[...] + self.slots[way, self.z].astype(f32)
        self.mine(self.z)[...] = self.acc[...].astype(bf16)
        self.back.start(0)
        for d in range(1, self.ys):
            self.y2(d, self.z).start()

    def spread(self, r):
        if r < self.zs - 2:
            self.back.start(r + 1)
        else:
            for way in (0, 1):
                self.back.arrive(way, r)
        for way in (0, 1):
            b = self.z - 1 - r if way == 0 else self.z + 1 + r
            b = lax.rem(b + self.zs, self.zs)
            @pl.when(self.back.receives(way, r))
            def _():
                for d in range(1, self.ys):
                    self.y2(d, b).start()

    def finish(self):
        for d in range(1, self.ys):
            for b in range(self.zs):
                self.y2(d, b).wait_recv()
        for d in range(1, self.ys):
            self.y1(d).wait_send()
            for b in range(self.zs):
                self.y2(d, b).wait_send()
        for k in range(self.zs):
            @pl.when(self.z < k)
            def _():
                self.run(0, k).wait_send()
            @pl.when(self.z > k)
            def _():
                self.run(1, k).wait_send()
        self.back.sent()


class PartSum:
    semaphores = 3

    @staticmethod
    def result(v, zs, ys):
        return jax.ShapeDtypeStruct(v.shape[1:], f32)

    @staticmethod
    def specs(v, zs, ys):
        sem = pltpu.SemaphoreType.DMA((ys - 1,))
        return [sem, sem, pltpu.VMEM((ys - 1,) + v.shape[1:], v.dtype)]


    def __init__(self, zs, ys, src, out, scratch):
        me = lax.axis_index("seq")
        self.ys, self.z, self.y = ys, me // ys, lax.rem(me, ys)
        self.src, self.out = src, out
        self.send, self.recv, self.slots = scratch

    def copy(self, d):
        to = lax.rem(self.y + d, self.ys)
        return pltpu.make_async_remote_copy(
            src_ref=self.src.at[to],
            dst_ref=self.slots.at[d - 1],
            send_sem=self.send.at[d - 1],
            recv_sem=self.recv.at[d - 1],
            device_id=seq_at(self.z, to, self.ys),
            device_id_type=MESH,
        )

    def begin(self):
        for d in range(1, self.ys):
            self.copy(d).start()

    def finish(self):
        mine = self.src[self.y].astype(f32)
        for d in range(1, self.ys):
            self.copy(d).wait_recv()
            mine = mine + self.slots[d - 1].astype(f32)
        self.out[...] = mine
        for d in range(1, self.ys):
            self.copy(d).wait_send()


def closing_kernel(n, nseq, zs, ys, parts, count, pieces, x_ref, b_ref, v_ref, cols_ref, h_ref, *refs):
    refs = list(refs)

    def take(k):
        head, refs[:] = refs[:k], refs[k:]
        return head

    piece_refs, p_refs = take(pieces), take(count)
    out_ref, branch_ref, sum_ref, values_ref, norm_ref = take(5)
    part_refs = take(count)
    s_ref, all_ref, mine_ref, mine_slots, t_ref, tslots = take(6)
    reduce_scratch, more_scratch, gather_sems, sum_scratch = take(14), take(14), take(2), take(13)
    part_scratch, (msend, mrecv, tsend, trecv) = take(3 * count), take(4)
    seq = lax.axis_index("seq")
    z = seq // ys
    line = GatherLine(zs, ys, v_ref, all_ref, gather_sems)
    total = SumAll(zs, ys, s_ref, sum_ref, sum_scratch)
    sums = [PartSum(zs, ys, p_refs[k], part_refs[k], part_scratch[3 * k : 3 * k + 3]) for k in range(count)]
    late = PartSum(zs, ys, mine_ref, values_ref, [msend, mrecv, mine_slots])
    steps = reduce_steps(n, parts, False, [{"seq": lax.rem(seq + d, nseq)} for d in range(1, nseq)], x_ref, out_ref, *reduce_scratch)
    more_steps = reduce_steps(n, parts, False, None, b_ref, branch_ref, *more_scratch)

    def tiny(d):
        return pltpu.make_async_remote_copy(src_ref=t_ref, dst_ref=tslots.at[seq], send_sem=tsend.at[d - 1], recv_sem=trecv.at[d - 1], device_id={"seq": lax.rem(seq + d, nseq)}, device_id_type=MESH)

    next(steps)
    next(more_steps)
    line.begin()
    offset = 0
    for piece in piece_refs:
        s_ref[pl.ds(offset, piece.shape[0]), :] = piece[...].astype(bf16)
        offset += piece.shape[0]
    if offset < s_ref.shape[0]:
        s_ref[pl.ds(offset, s_ref.shape[0] - offset), :] = jnp.zeros((s_ref.shape[0] - offset, s_ref.shape[1]), bf16)
    total.begin()
    next(steps)
    next(more_steps)
    line.start(1)
    total.middle()
    total.line_sum(0)
    for part in sums:
        part.begin()
    for _ in steps:
        pass
    w = h_ref.shape[1]
    row = jnp.sum(out_ref[:, pl.ds(0, w)] * h_ref[...], axis=0, keepdims=True)
    t_ref[...] = jnp.broadcast_to(row, t_ref.shape).astype(bf16)
    tslots[seq] = t_ref[...]
    for d in range(1, nseq):
        tiny(d).start()
    total.line_sum(1)
    for r in range(2, zs - 1):
        line.start(r)
        total.line_sum(r)
    total.turn()
    for _ in more_steps:
        pass
    line.arrived()
    fold = mine_ref.shape[1]
    for k in range(ys):
        def chunk(i, _):
            at = pl.ds(pl.multiple_of(i * 256, 256), 256)
            got = jnp.dot(cols_ref[pl.ds(k * fold, fold), :], all_ref[:, at], preferred_element_type=f32)
            mine_ref[k, :, at] = got.astype(bf16)
            return 0
        lax.fori_loop(0, all_ref.shape[1] // 256, chunk, 0)
    late.begin()
    for r in range(zs - 1):
        total.spread(r)
    for part in sums:
        part.finish()
    for d in range(1, nseq):
        tiny(d).wait_recv()
    norm = tslots[0].astype(f32)
    for k in range(1, nseq):
        norm = norm + tslots[k].astype(f32)
    norm_ref[...] = norm
    late.finish()
    total.finish()
    line.sent()
    for d in range(1, nseq):
        tiny(d).wait_send()


def closing(x, branch, v, cols, h, pieces, ps, n, nseq, zs, ys, cid, parts=2):
    rows, width = x.shape
    sem = pltpu.SemaphoreType.DMA
    height = sum(piece.shape[0] for piece in pieces)
    height += -height % (16 * ys * zs)
    w = v.shape[1]
    fold = cols.shape[0] // ys
    count = len(ps)
    tiny = (16, h.shape[1])
    return pl.pallas_call(
        functools.partial(closing_kernel, n, nseq, zs, ys, parts, count, len(pieces)),
        out_shape=[
            jax.ShapeDtypeStruct((rows, width // n), f32),
            jax.ShapeDtypeStruct((rows, branch.shape[1] // n), f32),
            jax.ShapeDtypeStruct((height, w), bf16),
            jax.ShapeDtypeStruct((fold, w), f32),
            jax.ShapeDtypeStruct(tiny, f32),
        ]
        + [PartSum.result(p, zs, ys) for p in ps],
        in_specs=[VM] * (5 + len(pieces) + count),
        out_specs=[VM] * (5 + count),
        scratch_shapes=[
            pltpu.VMEM((height, w), bf16),
            pltpu.VMEM((zs * v.shape[0], w), bf16),
            pltpu.VMEM((ys, fold, w), bf16),
            pltpu.VMEM((ys - 1, fold, w), bf16),
            pltpu.VMEM(tiny, bf16),
            pltpu.VMEM((nseq,) + tiny, bf16),
        ]
        + reduce_scratch_shapes(x.shape, n, parts)
        + reduce_scratch_shapes(branch.shape, n, parts)
        + GatherLine.specs(v, zs, ys)
        + SumAll.specs(height, w, zs, ys)
        + [spec for p in ps for spec in PartSum.specs(p, zs, ys)]
        + [sem((ys - 1,)), sem((ys - 1,)), sem((nseq - 1,)), sem((nseq - 1,))],
        compiler_params=pltpu.CompilerParams(collective_id=cid, has_side_effects=True, vmem_limit_bytes=60 * 2**20),
        cost_estimate=cost(70),
        name="closing",
    )(x, branch, v, cols, h, *pieces, *ps)


def passed_along(block, axis, distance):
    devices = range(lax.axis_size(axis))
    route = [(i - distance, i) for i in devices if i - distance in devices]
    return lax.ppermute(block, axis, route)


def silu_slope(argument):
    logistic = jax.nn.sigmoid(argument)
    return logistic * (1.0 + argument * (1.0 - logistic))


def conv_local(extended, weights, biases, seg_ext):
    length_now = extended.shape[1] - (KERN - 1)
    seg_now = seg_ext[:, KERN - 1 :]
    summed = biases + jnp.zeros((extended.shape[0], length_now, extended.shape[2]), f32)
    for lag_index in range(KERN):
        same_doc = (seg_ext[:, lag_index : lag_index + length_now] == seg_now).astype(f32)
        summed = (
            summed
            + weights[lag_index]
            * extended[:, lag_index : lag_index + length_now]
            * same_doc[:, :, None]
        )
    return summed


def dot(a, b, contract):
    return lax.dot_general(a, b, ((contract[:1], contract[1:]), ((), ())), preferred_element_type=f32)


def lines(zs, ys):
    return [[z * ys + y for z in range(zs)] for y in range(ys)]


def tokens_of_line(rows, zs, ys):
    return lax.all_gather(rows, "seq", axis_index_groups=lines(zs, ys), tiled=True)


def local(
    hidden_in,
    segments,
    cotangent,
    norm_gain,
    input_projection_weight,
    conv_weight,
    conv_bias,
    proj_weight,
    step_weight,
    step_bias,
    decay_log,
    skip_gain,
    output_projection_weight,
):
    seqs, length, width = hidden_in.shape
    rows = seqs * length
    nch, nseq = lax.axis_size("ch"), lax.axis_size("seq")
    channels = conv_bias.shape[-1]
    share = width // nch
    share_start = lax.axis_index("ch") * share
    seg_own = segments.astype(f32)
    seg_edge = passed_along(seg_own[:, -(KERN - 1) :], "seq", 1)
    seg_ext = jnp.concatenate([seg_edge, seg_own], axis=1)
    keep = (seg_ext[:, KERN - 2 : -1] == seg_own).astype(f32).reshape(-1, 1)
    hidden = hidden_in.astype(f32).reshape(rows, width)
    grad_rows = cotangent.astype(f32).reshape(rows, width)
    ids = iter(range(100))
    zs = 4 if nseq % 4 == 0 else nseq
    ys = nseq // zs
    fold = width // nseq
    places = (zs, ys)

    out_cols, w_copy = {}, {}
    stored = []
    out_low = grad_rows.astype(bf16)
    grad_mixed = dot(out_low, output_projection_weight[LAYERS - 1], (1, 1))
    grad_mixed_line = tokens_of_line(grad_mixed.astype(bf16), zs, ys)
    for layer in range(LAYERS):
        last = layer == LAYERS - 1
        inv_rms = lax.rsqrt(jnp.mean(hidden * hidden, axis=-1, keepdims=True) + epsilon)
        normed = (hidden * inv_rms * norm_gain[layer]).astype(bf16)
        w_in = w_copy[1] if layer > 0 else input_projection_weight[0]
        both = lax.dot_general(normed, w_in, (((1,), (0,)), ((), ())), preferred_element_type=f32)
        values, gate_pre = both[:, 0], both[:, 1]
        values3 = values.reshape(seqs, length, channels)
        edge = passed_along(values3[:, -(KERN - 1) :], "seq", 1)
        extended = jnp.concatenate([edge, values3], axis=1)
        conv_out, conv_pull = jax.vjp(
            functools.partial(conv_local, seg_ext=seg_ext), extended, conv_weight[layer], conv_bias[layer]
        )
        conv_out = conv_out.reshape(rows, channels)
        activated = jax.nn.silu(conv_out)
        act_low = activated.astype(bf16)
        proj_out = ch_sum(dot(act_low, proj_weight[layer], (1, 0)), nch, next(ids))
        rank_low = proj_out[:, :RANK].astype(bf16)
        mats = proj_out[:, RANK:]
        step_pre = dot(rank_low, step_weight[layer], (1, 0)) + step_bias[layer]
        rates = decay_log[layer]
        end_state, total = scan_local(step_pre, activated, mats, keep, rates, seqs, [], places, 0)
        gate_act = jax.nn.silu(gate_pre)
        if last:
            gate_line = tokens_of_line(gate_pre.astype(bf16), zs, ys)
            grad_scan = grad_mixed * gate_act
            start = scan_back_local(step_pre, grad_scan, mats, keep, rates, seqs)
            state_in, lam_in, w_copy[0] = carry_over(
                total, rates, [end_state, start], nseq, next(ids), True, True, taken=(input_projection_weight, 0)
            )
        else:
            state_in, w_copy[1] = carry_over(
                total, rates, [end_state], nseq, next(ids), True, False, taken=(input_projection_weight, 1)
            )
        keeping = (hidden, inv_rms, normed, gate_pre, gate_act, conv_out, activated, act_low, conv_pull, rank_low,
                   step_pre, mats, total, state_in)
        if last:
            stored.append(keeping)
            break
        (y,) = scan_forward(
            step_pre, activated, mats, keep, rates, state_in, seqs, [], places, 0, (grad_mixed_line,)
        )
        scanned = y + skip_gain[layer] * activated
        mixed = (scanned * gate_act).astype(bf16)
        out_part = dot(mixed, output_projection_weight[layer], (1, 0)).astype(bf16)
        mixed_all = tokens_of_line(mixed, zs, ys)
        branch = ch_reduce(out_part, nch, next(ids), True)
        hidden = hidden + branch
        stored.append(keeping + (scanned, mixed_all))

    for layer in reversed(range(LAYERS)):
        last = layer == LAYERS - 1
        (hidden, inv_rms, normed, gate_pre, gate_act, conv_out, activated, act_low, conv_pull, rank_low,
         step_pre, mats, total, state_in) = stored[layer][:14]
        rates = decay_log[layer]
        if not last:
            scanned, mixed_all = stored[layer][14:]
            normed_cols = early_cols
            out_low = grad_rows.astype(bf16)
            grad_mixed = dot(out_low, output_projection_weight[layer], (1, 1))
            grad_scan = grad_mixed * gate_act
            grad_gate = (grad_mixed * scanned * silu_slope(gate_pre)).astype(bf16)
            start = scan_back_local(step_pre, grad_scan, mats, keep, rates, seqs)
            gate_all = tokens_of_line(grad_gate, zs, ys)
            lam_in, grad_out_last, grad_gate_last = carry_over(
                total, rates, [start], nseq, next(ids), False, True, [out_parts_last, gate_parts_last], places
            )
        grad_skip = jnp.sum(grad_scan * activated, axis=0)
        if last:
            plan = [
                (ColumnsLine, (3, 5), normed),
                (ColumnsLine, (4, 6), out_low),
                (ColumnsLine, (6, 8), stored[0][2]),
            ]
        else:
            plan = [
                (ColumnsLine, (2, 4), out_low),
                (PartSum, (), values_parts_last),
            ]
        grad_pre, grad_act, grad_mats, grad_decay, *others = scan_back(
            step_pre, activated, grad_scan, mats, keep, rates, skip_gain[layer][None], state_in, lam_in, seqs, int(last),
            plan, places, next(ids), (),
        )
        if last:
            y, normed_cols, out_cols[layer], early_cols = others
            scanned = y + skip_gain[layer] * activated
            mixed = (scanned * gate_act).astype(bf16)
            grad_gate = (grad_mixed * scanned * silu_slope(gate_pre)).astype(bf16)
            scanned_line = tokens_of_line(scanned.astype(bf16), zs, ys).astype(f32)
            gates = gate_line.astype(f32)
            mixed_all = (scanned_line * jax.nn.silu(gates)).astype(bf16)
            gate_all = (grad_mixed_line.astype(f32) * scanned_line * silu_slope(gates)).astype(bf16)
        else:
            out_cols[layer], grad_values_last = others
        grad_step_bias = jnp.sum(grad_pre, axis=0)
        pre_low = grad_pre.astype(bf16)
        grad_step_weight = dot(rank_low, pre_low, (0, 0))
        rank_part = dot(pre_low, step_weight[layer], (1, 1))
        grad_proj = ch_sum(
            jnp.concatenate([rank_part, grad_mats[:, : 2 * STATE]], axis=-1), nch, next(ids),
            (gate_line,) if last else (),
        ).astype(bf16)
        grad_proj_weight = dot(grad_proj, act_low, (0, 0))
        grad_act = grad_act + dot(grad_proj, proj_weight[layer], (1, 1))
        grad_conv = (grad_act * silu_slope(conv_out)).reshape(seqs, length, channels)
        grad_ext, grad_conv_weight, grad_conv_bias = conv_pull(grad_conv)
        returned = passed_along(grad_ext[:, : KERN - 1], "seq", -1)
        grad_values = grad_ext[:, KERN - 1 :]
        grad_values = jnp.concatenate(
            [grad_values[:, : -(KERN - 1)], grad_values[:, -(KERN - 1) :] + returned], axis=1
        ).reshape(rows, channels).astype(bf16)
        w_in = w_copy[layer]
        grad_both = jnp.stack([grad_values, grad_gate], axis=1)
        grad_part = lax.dot_general(grad_both, w_in, (((1, 2), (1, 2)), ((), ())), preferred_element_type=f32)
        scale_now = norm_gain[layer]
        misc = jnp.concatenate([grad_conv_weight, grad_conv_bias[None], grad_step_bias[None], grad_skip[None]], axis=0)
        small = [grad_proj_weight, grad_step_weight, grad_decay, misc]
        if last:
            values_last = tokens_of_line(grad_values, zs, ys)
            values_parts_last = dot(normed_cols, values_last, (0, 0)).astype(bf16).reshape(ys, fold, channels)
            grad_normed = ch_reduce(grad_part.astype(bf16), nch, next(ids), True)
            out_part = dot(mixed, output_projection_weight[layer], (1, 0)).astype(bf16)
            hidden_last = lax.dynamic_slice_in_dim(hidden, share_start, share, 1)
        columns = [out_cols[layer][:, k * fold : (k + 1) * fold] for k in range(ys)]
        out_parts = jnp.stack([dot(mixed_all, k, (0, 0)).astype(bf16) for k in columns], axis=0)
        gate_parts = dot(normed_cols, gate_all, (0, 0)).astype(bf16).reshape(ys, fold, channels)
        if last:
            out_parts_last, gate_parts_last = out_parts, gate_parts
            inner = jnp.sum(grad_normed * scale_now * hidden, axis=-1, keepdims=True)
            grad_norm = lax.dynamic_slice_in_dim(jnp.sum(grad_normed * hidden * inv_rms, axis=0), share_start, share, 0)
            grad_rows = grad_rows + inv_rms * scale_now * grad_normed - hidden * (inv_rms * inv_rms * inv_rms) * inner / width
            norm_row = jnp.pad(grad_norm[None], ((0, 0), (0, channels - share)))
            small[-1] = jnp.pad(jnp.concatenate([misc, norm_row], axis=0), ((0, 16 - misc.shape[0] - 1), (0, 0)))
            small_last = small
            continue
        inner = jnp.sum(grad_part * scale_now * hidden, axis=-1, keepdims=True)
        inner_high = inner.astype(bf16)
        inner_low = (inner - inner_high.astype(f32)).astype(bf16)
        beside = jnp.pad(jnp.concatenate([inner_high, inner_low], axis=1), ((0, 0), (0, LANES - 2)))
        beside = jnp.broadcast_to(beside[:, None], (rows, nch, LANES))
        send = jnp.concatenate([grad_part.astype(bf16).reshape(rows, nch, share), beside], axis=2)
        small[-1] = jnp.pad(misc, ((0, 16 - misc.shape[0]), (0, 0)))
        hidden_share = lax.dynamic_slice_in_dim(hidden, share_start, share, 1)
        scale_share = lax.dynamic_slice_in_dim(scale_now, share_start, share, 0)
        got, branch, sums, grad_in_values, tiny, grad_gate_now, grad_out_weight = closing(
            send.reshape(rows, nch * (share + LANES)), out_part, grad_values, jnp.swapaxes(normed_cols, 0, 1), hidden_share * inv_rms,
            small + small_last, [gate_parts, out_parts], nch, nseq, zs, ys, next(ids),
        )
        grad_share, inner = got[:, :share], got[:, share : share + 1] + got[:, share + 1 : share + 2]
        grad_input = (
            lax.dynamic_slice_in_dim(grad_rows, share_start, share, 1)
            + inv_rms * scale_share * grad_share
            - hidden_share * (inv_rms * inv_rms * inv_rms) * inner / width
        )
        result = (hidden_last + branch).astype(bf16)
        total_small = sums.astype(f32)
        heights = [v.shape[0] for v in small_last]
        half = sum(heights)
        pairs, at = [], 0
        for height in heights:
            pairs.append(jnp.stack([total_small[at : at + height], total_small[half + at : half + at + height]], axis=0))
            at += height
        misc = pairs[3]
        norms = jnp.stack([tiny[0], misc[1, KERN + 3, :share]], axis=0)
        in_weight = jnp.stack(
            [jnp.stack(pair, axis=1) for pair in ((grad_in_values, grad_gate_now), (grad_values_last, grad_gate_last))], axis=0
        )
        out_weight = jnp.stack([grad_out_weight, grad_out_last], axis=0)
    shape3 = (seqs, length, share)
    return (
        result.reshape(shape3),
        grad_input.reshape(shape3),
        norms,
        in_weight,
        misc[:, :KERN],
        misc[:, KERN],
        jnp.swapaxes(pairs[0], 1, 2),
        pairs[1],
        misc[:, KERN + 1],
        pairs[2],
        misc[:, KERN + 2],
        out_weight,
    )


def solution(mesh):
    in_specs = (
        P(None, "seq", None),
        P(None, "seq"),
        P(None, "seq", None),
        P(),
        P(None, None, None, "ch"),
        P(None, None, "ch"),
        P(None, "ch"),
        P(None, "ch", None),
        P(None, None, "ch"),
        P(None, "ch"),
        P(None, None, "ch"),
        P(None, "ch"),
        P(None, "ch", None),
    )
    out_specs = (
        P(None, "seq", "ch"),
        P(None, "seq", "ch"),
        P(None, "ch"),
        P(None, "seq", None, "ch"),
        P(None, None, "ch"),
        P(None, "ch"),
        P(None, "ch", None),
        P(None, None, "ch"),
        P(None, "ch"),
        P(None, None, "ch"),
        P(None, "ch"),
        P(None, "ch", "seq"),
    )
    return jax.shard_map(local, mesh=mesh, in_specs=in_specs, out_specs=out_specs, check_vma=False)
```

```python
import functools

import jax
import jax.numpy as jnp
from jax import lax
from jax.experimental import pallas as pl
from jax.experimental.pallas import tpu as pltpu
from jax.sharding import PartitionSpec as P

STATE = 16
RANK = 128
KERN = 4
LAYERS = 2
MESH = pl.DeviceIdType.MESH
ANY = pl.BlockSpec(memory_space=pl.ANY)
f32, bf16 = jnp.float32, jnp.bfloat16
epsilon = 1e-05


def after(kernel, count, pins):
    def run(*refs):
        return kernel(*refs[:count], *refs[count + len(pins) :])
    return run


def cost(us):
    return pl.CostEstimate(flops=int(us * 0.1e9), bytes_accessed=0, transcendentals=0)


LANES = 128
BIG = 1e30
LOG2E = 1.4426950408889634

def softplus(v):
    return jnp.maximum(v, 0.0) + jnp.log(1.0 + jnp.exp(-jnp.abs(v)))

def spread_states(bc_ref, wide_ref, pick_ref, rows, unroll=8):
    lane = lax.broadcasted_iota(jnp.int32, (STATE, 2 * STATE), 1)
    row = lax.broadcasted_iota(jnp.int32, (STATE, 2 * STATE), 0)
    mask = (lane % STATE == row).astype(jnp.float32)
    src = lax.broadcasted_iota(jnp.int32, (2 * STATE, 2 * LANES), 0)
    dst = lax.broadcasted_iota(jnp.int32, (2 * STATE, 2 * LANES), 1)
    route = ((src // STATE) == (dst // LANES)).astype(jnp.bfloat16)
    chunk = 32
    def step(i, _):
        t0 = pl.multiple_of(i * chunk, chunk)
        bcv = bc_ref[pl.ds(t0, chunk), :]
        for j in range(chunk):
            pick_ref[pl.ds(j * STATE, STATE), :] = (bcv[j:j + 1] * mask).astype(jnp.bfloat16)
        wide_ref[pl.ds(pl.multiple_of(t0 * STATE, chunk * STATE), chunk * STATE), :] = jnp.dot(pick_ref[...], route, preferred_element_type=jnp.float32)
        return 0
    lax.fori_loop(0, rows // chunk, step, 0)

def prep(step_ref_pre, act_ref, keep_ref, dstep_ref, dx_ref, rows):
    def body(i, _):
        sl = pl.ds(pl.multiple_of(i * 32, 32), 32)
        for g in range(dstep_ref.shape[0]):
            st = softplus(step_ref_pre[sl, lanes(g)])
            dstep_ref[g, sl, :] = jnp.where(keep_ref[sl, :] > 0.0, st, BIG)
            dx_ref[g, sl, :] = st * act_ref[sl, lanes(g)]
        return 0
    lax.fori_loop(0, rows // 32, body, 0)

def lanes(g):
    return pl.ds(g * LANES, LANES)

def group_sets(channels, width):
    n = channels // LANES
    return [list(range(i, min(i + width, n))) for i in range(0, n, width)]

def local_kernel(seqs, pre_ref, act_ref, bc_ref, keep_ref, dl_ref, end_ref, gain_ref, wide, pick, dstep, dx):
    rows, channels = pre_ref.shape
    length = rows // seqs
    spread_states(bc_ref, wide, pick, rows)
    prep(pre_ref, act_ref, keep_ref, dstep, dx, rows)
    yield
    for gs in group_sets(channels, 8):
        a2 = [-jnp.exp(dl_ref[:, lanes(g)]) * LOG2E for g in gs]
        for s in range(seqs):
            for k, g in enumerate(gs):
                tot = jnp.sum(dstep[g, pl.ds(s * length, length), :], axis=0, keepdims=True)
                gain_ref[pl.ds(s, 1), lanes(g)] = tot
            def blk(i, st):
                st = list(st)
                t0 = pl.multiple_of(s * length + i * 8, 8)
                for j in range(8):
                    b = wide[pl.ds(pl.multiple_of((t0 + j) * STATE, STATE), STATE), pl.ds(0, LANES)]
                    for k, g in enumerate(gs):
                        d = jnp.exp2(a2[k] * dstep[g, pl.ds(t0 + j, 1), :])
                        st[k] = d * st[k] + b * dx[g, pl.ds(t0 + j, 1), :]
                return tuple(st)
            st = lax.fori_loop(0, length // 8, blk, tuple(jnp.zeros((STATE, LANES), jnp.float32) for _ in gs))
            for k, g in enumerate(gs):
                end_ref[s, :, lanes(g)] = st[k]
            yield

VM = pl.BlockSpec(memory_space=pltpu.VMEM)


def played(kernel, counts, plan, places):
    n_in, n_out, n_scratch = counts

    def run(*refs):
        refs = list(refs)

        def take(k):
            head, refs[:] = refs[:k], refs[k:]
            return head

        own = take(n_in)
        sources = take(len(plan))
        own += take(n_out)
        targets = take(len(plan))
        own += take(n_scratch)
        jobs = []
        for (kind, when), src, out in zip(plan, sources, targets):
            jobs.append((kind(*places, src, out, take(kind.semaphores)), when))
        if plan:
            seq, ch = lax.axis_index("seq"), lax.axis_index("ch")
            zs, ys = places
            z, y = seq // ys, lax.rem(seq, ys)
            peers = [{"seq": lax.rem(z + d, zs) * ys + y} for d in range(1, zs)]
            peers += [{"seq": z * ys + lax.rem(y + d, ys)} for d in range(1, ys)]
            xs = lax.axis_size("ch") // 2
            peers += [{"ch": lax.rem(ch // 2 + e, xs) * 2 + lax.rem(ch, 2)} for e in range(1, xs)]
            peers.append({"ch": ch + 1 - 2 * lax.rem(ch, 2)})
            barrier = pltpu.get_barrier_semaphore()
            for peer in peers:
                pl.semaphore_signal(barrier, inc=1, device_id=peer, device_id_type=MESH)
        for at, _ in enumerate(kernel(*own)):
            if at == 0 and plan:
                pl.semaphore_wait(barrier, len(peers))
                for job, _ in jobs:
                    job.begin()
            for job, when in jobs:
                if at in when:
                    job.step(when.index(at))
        for job, when in jobs:
            job.finish()

    return run


def play_call(kernel, counts, plan, places, cid, out_shape, scratch, arrays, us, name, pins=()):
    arrays = list(arrays) + [v for _, _, v in plan]
    kinds = [(kind, when) for kind, when, _ in plan]
    out_shape = list(out_shape) + [kind.result(v, *places) for kind, _, v in plan]
    sems = [spec for kind, _, v in plan for spec in kind.specs(v, *places)]
    extra = dict(collective_id=cid, has_side_effects=True) if plan else {}
    return pl.pallas_call(
        after(played(kernel, counts, kinds, places), len(arrays), pins),
        out_shape=out_shape,
        in_specs=[VM] * len(arrays) + [ANY] * len(pins),
        out_specs=[VM] * len(out_shape),
        scratch_shapes=list(scratch) + sems,
        compiler_params=pltpu.CompilerParams(vmem_limit_bytes=60 * 2**20, **extra),
        cost_estimate=cost(us),
        name=name,
    )(*arrays, *pins)

def scan_local(pre, act, bc, keep, dl, seqs, plan, places, cid):
    rows, channels = pre.shape
    f = jnp.float32
    big = pltpu.VMEM((channels // LANES, rows, LANES), f)
    return play_call(
        functools.partial(local_kernel, seqs), (5, 2, 4), plan, places, cid,
        [jax.ShapeDtypeStruct((seqs, STATE, channels), f), jax.ShapeDtypeStruct((seqs, channels), f)],
        [pltpu.VMEM((rows * STATE, 2 * LANES), f), pltpu.VMEM((32 * STATE, 2 * STATE), jnp.bfloat16), big, big],
        (pre, act, bc, keep, dl), 8, "scan_local",
    )


def forward_kernel(seqs, pre_ref, act_ref, bc_ref, keep_ref, dl_ref, in_ref, y_ref, wide, pick, dstep, dx, part):
    rows, channels = pre_ref.shape
    length = rows // seqs
    spread_states(bc_ref, wide, pick, rows)
    prep(pre_ref, act_ref, keep_ref, dstep, dx, rows)
    yield
    for gs in group_sets(channels, 4):
        a2 = [-jnp.exp(dl_ref[:, lanes(g)]) * LOG2E for g in gs]
        for s in range(seqs):
            def blk(i, st):
                st = list(st)
                t0 = pl.multiple_of(s * length + i * 8, 8)
                for j in range(8):
                    at = pl.ds(pl.multiple_of((t0 + j) * STATE, STATE), STATE)
                    b = wide[at, pl.ds(0, LANES)]
                    c = wide[at, pl.ds(LANES, LANES)]
                    for k, g in enumerate(gs):
                        d = jnp.exp2(a2[k] * dstep[g, pl.ds(t0 + j, 1), :])
                        st[k] = d * st[k] + b * dx[g, pl.ds(t0 + j, 1), :]
                        v = st[k] * c
                        part[k, pl.ds(pl.multiple_of(i * 64 + j * 8, 8), 8), :] = v[:8] + v[8:]
                return tuple(st)
            lax.fori_loop(0, length // 8, blk, tuple(in_ref[s, :, lanes(g)] for g in gs))
            def red(i, _):
                t0 = pl.multiple_of(s * length + i * 8, 8)
                for k, g in enumerate(gs):
                    acc = part[k, pl.ds(i * 64, 8, stride=8), :]
                    for m in range(1, 8):
                        acc = acc + part[k, pl.ds(i * 64 + m, 8, stride=8), :]
                    y_ref[pl.ds(t0, 8), lanes(g)] = acc
                return 0
            lax.fori_loop(0, length // 8, red, 0)
            yield

def scan_forward(pre, act, bc, keep, dl, state_in, seqs, plan, places, cid, pins=()):
    rows, channels = pre.shape
    f = jnp.float32
    big = pltpu.VMEM((channels // LANES, rows, LANES), f)
    return play_call(
        functools.partial(forward_kernel, seqs), (6, 1, 5), plan, places, cid,
        [jax.ShapeDtypeStruct((rows, channels), f)],
        [pltpu.VMEM((rows * STATE, 2 * LANES), f), pltpu.VMEM((32 * STATE, 2 * STATE), jnp.bfloat16), big, big,
         pltpu.VMEM((4, rows // seqs * 8, LANES), f)],
        (pre, act, bc, keep, dl, state_in), 11, "scan_forward", pins,
    )


LN2 = 0.6931471805599453

def back_local_kernel(seqs, pre_ref, gs_ref, bc_ref, keep_ref, dl_ref, out_ref, wide, pick, dstep, gsc):
    rows, channels = pre_ref.shape
    length = rows // seqs
    spread_states(bc_ref, wide, pick, rows)
    def body(i, _):
        sl = pl.ds(pl.multiple_of(i * 32, 32), 32)
        for g in range(channels // LANES):
            st = softplus(pre_ref[sl, lanes(g)])
            dstep[g, sl, :] = jnp.where(keep_ref[sl, :] > 0.0, st, BIG)
            gsc[g, sl, :] = gs_ref[sl, lanes(g)]
        return 0
    lax.fori_loop(0, rows // 32, body, 0)
    for gs in group_sets(channels, 8):
        a2 = [-jnp.exp(dl_ref[:, lanes(g)]) * LOG2E for g in gs]
        for s in range(seqs):
            def blk(i, st):
                st = list(st)
                t0 = pl.multiple_of(s * length + (length // 8 - 1 - i) * 8, 8)
                for j in reversed(range(8)):
                    c = wide[pl.ds(pl.multiple_of((t0 + j) * STATE, STATE), STATE), pl.ds(LANES, LANES)]
                    for k, g in enumerate(gs):
                        d = jnp.exp2(a2[k] * dstep[g, pl.ds(t0 + j, 1), :])
                        st[k] = d * (st[k] + c * gsc[g, pl.ds(t0 + j, 1), :])
                return tuple(st)
            st = lax.fori_loop(0, length // 8, blk, tuple(jnp.zeros((STATE, LANES), jnp.float32) for _ in gs))
            for k, g in enumerate(gs):
                out_ref[s, :, lanes(g)] = st[k]

def scan_back_local(pre, gs, bc, keep, dl, seqs, pins=()):
    rows, channels = pre.shape
    f = jnp.float32
    return pl.pallas_call(
        after(functools.partial(back_local_kernel, seqs), 5, pins),
        out_shape=jax.ShapeDtypeStruct((seqs, STATE, channels), f),
        in_specs=[VM] * 5 + [ANY] * len(pins), out_specs=VM,
        scratch_shapes=[pltpu.VMEM((rows * STATE, 2 * LANES), f), pltpu.VMEM((32 * STATE, 2 * STATE), jnp.bfloat16),
                        pltpu.VMEM((channels // LANES, rows, LANES), f), pltpu.VMEM((channels // LANES, rows, LANES), f)],
        compiler_params=pltpu.CompilerParams(vmem_limit_bytes=60 * 2**20),
        cost_estimate=cost(8),
        name="scan_back_local",
    )(pre, gs, bc, keep, dl, *pins)

def back_kernel(seqs, with_y, pre_ref, act_ref, gs_ref, bc_ref, keep_ref, dl_ref, skip_ref, in_ref, lam_ref,
                gpre_ref, gact_ref, gbc_ref, gdl_ref, *rest):
    if with_y:
        y_ref, *rest = rest
    (wide, pick, dstep, dx, stepc, gsc, states, partq, partr, accb, accc, rowsum) = rest
    rows, channels = pre_ref.shape
    length = rows // seqs
    f = jnp.float32
    spread_states(bc_ref, wide, pick, rows)
    def body(i, _):
        sl = pl.ds(pl.multiple_of(i * 32, 32), 32)
        for g in range(channels // LANES):
            st = softplus(pre_ref[sl, lanes(g)])
            stepc[g, sl, :] = st
            dstep[g, sl, :] = jnp.where(keep_ref[sl, :] > 0.0, st, BIG)
            dx[g, sl, :] = st * act_ref[sl, lanes(g)]
            gsc[g, sl, :] = gs_ref[sl, lanes(g)]
        return 0
    lax.fori_loop(0, rows // 32, body, 0)
    yield
    sets = group_sets(channels, 4)
    for index, gs in enumerate(sets):
        a2 = [-jnp.exp(dl_ref[:, lanes(g)]) * LOG2E for g in gs]
        gdl = [jnp.zeros((STATE, LANES), f) for _ in gs]
        for s in range(seqs):
            for k, g in enumerate(gs):
                states[k, pl.ds(0, STATE), :] = in_ref[s, :, lanes(g)]
            def fwd(i, st):
                st = list(st)
                t0 = pl.multiple_of(s * length + i * 8, 8)
                for j in range(8):
                    at = pl.ds(pl.multiple_of((t0 + j) * STATE, STATE), STATE)
                    b = wide[at, pl.ds(0, LANES)]
                    if with_y:
                        c = wide[at, pl.ds(LANES, LANES)]
                    for k, g in enumerate(gs):
                        d = jnp.exp2(a2[k] * dstep[g, pl.ds(t0 + j, 1), :])
                        st[k] = d * st[k] + b * dx[g, pl.ds(t0 + j, 1), :]
                        states[k, pl.ds(pl.multiple_of((i * 8 + j + 1) * STATE, STATE), STATE), :] = st[k]
                        if with_y:
                            v = st[k] * c
                            partq[k, pl.ds(pl.multiple_of(i * 64 + j * 8, 8), 8), :] = v[:8] + v[8:]
                return tuple(st)
            lax.fori_loop(0, length // 8, fwd, tuple(in_ref[s, :, lanes(g)] for g in gs))
            if with_y:
                def read(i, _):
                    t0 = pl.multiple_of(s * length + i * 8, 8)
                    for k, g in enumerate(gs):
                        acc = partq[k, pl.ds(i * 64, 8, stride=8), :]
                        for m in range(1, 8):
                            acc = acc + partq[k, pl.ds(i * 64 + m, 8, stride=8), :]
                        y_ref[pl.ds(t0, 8), lanes(g)] = acc
                    return 0
                lax.fori_loop(0, length // 8, read, 0)
            yield
            def bwd(i, carry):
                st = list(carry[:len(gs)])
                am = list(carry[len(gs):])
                l0 = (length // 8 - 1 - i) * 8
                t0 = pl.multiple_of(s * length + l0, 8)
                for j in reversed(range(8)):
                    at = pl.ds(pl.multiple_of((t0 + j) * STATE, STATE), STATE)
                    b = wide[at, pl.ds(0, LANES)]
                    c = wide[at, pl.ds(LANES, LANES)]
                    tb = tc = None
                    here = pl.ds(pl.multiple_of((l0 + j) * 8, 8), 8)
                    for k, g in enumerate(gs):
                        row = pl.ds(t0 + j, 1)
                        grow = gsc[g, row, :]
                        d = jnp.exp2(a2[k] * dstep[g, row, :])
                        lam = st[k] + c * grow
                        old = states[k, pl.ds(pl.multiple_of((l0 + j) * STATE, STATE), STATE), :]
                        new = states[k, pl.ds(pl.multiple_of((l0 + j + 1) * STATE, STATE), STATE), :]
                        st[k] = d * lam
                        lp = st[k] * old
                        q = lam * b
                        partq[k, here, :] = q[:8] + q[8:]
                        r = lp * a2[k]
                        partr[k, here, :] = r[:8] + r[8:]
                        am[k] = am[k] + lp * stepc[g, row, :]
                        u = lam * dx[g, row, :]
                        v = new * grow
                        tb = u if tb is None else tb + u
                        tc = v if tc is None else tc + v
                    if index > 0:
                        tb = tb + accb[at, :]
                        tc = tc + accc[at, :]
                    accb[at, :] = tb
                    accc[at, :] = tc
                return tuple(st) + tuple(am)
            out = lax.fori_loop(0, length // 8, bwd, tuple(lam_ref[s, :, lanes(g)] for g in gs) + tuple(gdl))
            gdl = list(out[len(gs):])
            def red(i, _):
                t0 = pl.multiple_of(s * length + i * 8, 8)
                for k, g in enumerate(gs):
                    q = partq[k, pl.ds(i * 64, 8, stride=8), :]
                    r = partr[k, pl.ds(i * 64, 8, stride=8), :]
                    for m in range(1, 8):
                        q = q + partq[k, pl.ds(i * 64 + m, 8, stride=8), :]
                        r = r + partr[k, pl.ds(i * 64 + m, 8, stride=8), :]
                    here = pl.ds(t0, 8)
                    p = pre_ref[here, lanes(g)]
                    gstep = r * LN2 + act_ref[here, lanes(g)] * q
                    gpre_ref[here, lanes(g)] = gstep * (1.0 / (1.0 + jnp.exp(-p)))
                    gact_ref[here, lanes(g)] = stepc[g, here, :] * q + gsc[g, here, :] * skip_ref[:, lanes(g)]
                return 0
            lax.fori_loop(0, length // 8, red, 0)
            yield
        for k, g in enumerate(gs):
            gdl_ref[:, lanes(g)] = gdl[k] * (a2[k] * LN2)
    ones = jnp.ones((LANES, LANES), jnp.bfloat16)
    lane = lax.broadcasted_iota(jnp.int32, (32 * STATE, LANES), 1)
    row = lax.broadcasted_iota(jnp.int32, (32 * STATE, LANES), 0) % STATE
    mb = lane == row
    mc = lane == row + STATE
    def fin(i, _):
        sl = pl.ds(pl.multiple_of(i * 32 * STATE, 32 * STATE), 32 * STATE)
        sb = jnp.dot(accb[sl, :].astype(jnp.bfloat16), ones, preferred_element_type=f)
        sc = jnp.dot(accc[sl, :].astype(jnp.bfloat16), ones, preferred_element_type=f)
        rowsum[...] = jnp.where(mb, sb, jnp.where(mc, sc, 0.0))
        acc = rowsum[pl.ds(0, 32, stride=STATE), :]
        for m in range(1, STATE):
            acc = acc + rowsum[pl.ds(m, 32, stride=STATE), :]
        gbc_ref[pl.ds(pl.multiple_of(i * 32, 32), 32), :] = acc
        return 0
    lax.fori_loop(0, rows // 32, fin, 0)

def scan_back(pre, act, gs, bc, keep, dl, skip, state_in, lam_in, seqs, with_y, plan, places, cid, pins=()):
    rows, channels = pre.shape
    f = jnp.float32
    groups = channels // LANES
    length = rows // seqs
    big = pltpu.VMEM((groups, rows, LANES), f)
    whole = jax.ShapeDtypeStruct((rows, channels), f)
    return play_call(
        functools.partial(back_kernel, seqs, with_y), (9, 4 + with_y, 12), plan, places, cid,
        [whole, whole, jax.ShapeDtypeStruct((rows, LANES), f), jax.ShapeDtypeStruct((STATE, channels), f)] + [whole] * with_y,
        [pltpu.VMEM((rows * STATE, 2 * LANES), f), pltpu.VMEM((32 * STATE, 2 * STATE), jnp.bfloat16),
         big, big, big, big,
         pltpu.VMEM((4, (length + 1) * STATE, LANES), f),
         pltpu.VMEM((4, length * 8, LANES), f), pltpu.VMEM((4, length * 8, LANES), f),
         pltpu.VMEM((rows * STATE, LANES), f), pltpu.VMEM((rows * STATE, LANES), f),
         pltpu.VMEM((32 * STATE, LANES), f)],
        (pre, act, gs, bc, keep, dl, skip, state_in, lam_in), 23 + 3 * with_y, "scan_back", pins,
    )


def greet(peers):
    barrier = pltpu.get_barrier_semaphore()
    for p in peers:
        pl.semaphore_signal(barrier, inc=1, device_id=p, device_id_type=MESH)
    pl.semaphore_wait(barrier, len(peers))

def ch_sum_kernel(n, x_ref, out_ref, mine, slots, send, recv):
    me = lax.axis_index("ch")
    peers = [{"ch": lax.rem(me + d, n)} for d in range(1, n)]
    greet(peers)
    mine[...] = x_ref[...].astype(bf16)
    copies = []
    for d in range(1, n):
        c = pltpu.make_async_remote_copy(src_ref=mine, dst_ref=slots.at[d - 1], send_sem=send.at[d - 1], recv_sem=recv.at[d - 1], device_id=peers[d - 1], device_id_type=MESH)
        c.start()
        copies.append(c)
    total = x_ref[...].astype(bf16).astype(f32)
    for d, c in zip(range(1, n), copies):
        c.wait()
        total = total + slots[d - 1].astype(f32)
    out_ref[...] = total

def ch_sum(x, n, cid, pins=()):
    return pl.pallas_call(
        after(functools.partial(ch_sum_kernel, n), 1, pins),
        out_shape=jax.ShapeDtypeStruct(x.shape, f32), in_specs=[VM] + [ANY] * len(pins), out_specs=VM,
        scratch_shapes=[pltpu.VMEM(x.shape, bf16), pltpu.VMEM((n - 1,) + x.shape, bf16), pltpu.SemaphoreType.DMA((n - 1,)), pltpu.SemaphoreType.DMA((n - 1,))],
        compiler_params=pltpu.CompilerParams(collective_id=cid, has_side_effects=True, vmem_limit_bytes=32 * 2**20), cost_estimate=cost(10), name="ch_sum",
    )(x, *pins)

def reduce_steps(n, parts, gather, more, x_ref, out_ref, s1, sum1, s2, mine, got, fin, sem1, rem1, sem2, rem2, sem3, rem3, sem4, rem4):
    xs = n // 2
    me = lax.axis_index("ch")
    x, core = me // 2, lax.rem(me, 2)
    peer = {"ch": x * 2 + 1 - core}
    others = [lax.rem(x + d, xs) for d in range(1, xs)]
    if more is not None:
        greet([peer] + [{"ch": o * 2 + core} for o in others] + more)
    rows, width = x_ref.shape[0] // parts, x_ref.shape[1] // n
    def cols(block):
        return pl.ds(pl.multiple_of(block * width, width), width)
    def stage1(p, k):
        return pltpu.make_async_remote_copy(src_ref=x_ref.at[pl.ds(p * rows, rows), cols(k * 2 + 1 - core)], dst_ref=s1.at[p, k], send_sem=sem1.at[p, k], recv_sem=rem1.at[p, k], device_id=peer, device_id_type=MESH)
    def stage2(p, d):
        o = others[d]
        return pltpu.make_async_remote_copy(src_ref=sum1.at[p, o], dst_ref=s2.at[p, d], send_sem=sem2.at[p, d], recv_sem=rem2.at[p, d], device_id={"ch": o * 2 + core}, device_id_type=MESH)
    def stage3(p, d):
        o = others[d]
        return pltpu.make_async_remote_copy(src_ref=mine.at[p], dst_ref=got.at[p, d], send_sem=sem3.at[p, d], recv_sem=rem3.at[p, d], device_id={"ch": o * 2 + core}, device_id_type=MESH)
    for p in range(parts):
        for k in range(xs):
            stage1(p, k).start()
    yield
    for p in range(parts):
        for k in range(xs):
            stage1(p, k).wait_recv()
            sum1[p, k] = (x_ref[pl.ds(p * rows, rows), cols(k * 2 + core)].astype(f32) + s1[p, k].astype(f32)).astype(bf16)
        for d in range(xs - 1):
            stage2(p, d).start()
    yield
    for p in range(parts):
        total = sum1[p, x].astype(f32)
        for d in range(xs - 1):
            stage2(p, d).wait_recv()
            total = total + s2[p, d].astype(f32)
        if gather:
            mine[p] = total.astype(bf16)
            for d in range(xs - 1):
                stage3(p, d).start()
        else:
            out_ref[pl.ds(p * rows, rows), :] = total
    yield
    if gather:
        def stage4(p, d):
            src = mine.at[p] if d < 0 else got.at[p, d]
            return pltpu.make_async_remote_copy(src_ref=src, dst_ref=fin.at[p, d + 1], send_sem=sem4.at[p, d + 1], recv_sem=rem4.at[p, d + 1], device_id=peer, device_id_type=MESH)
        def chip(d):
            return lax.rem(x + xs - 1 - d, xs)
        for p in range(parts):
            stage4(p, -1).start()
            out_ref[pl.ds(p * rows, rows), cols(me)] = mine[p].astype(out_ref.dtype)
            for d in range(xs - 1):
                stage3(p, d).wait_recv()
                stage4(p, d).start()
                out_ref[pl.ds(p * rows, rows), cols(chip(d) * 2 + core)] = got[p, d].astype(out_ref.dtype)
        yield
        for p in range(parts):
            for d in range(-1, xs - 1):
                stage4(p, d).wait_recv()
                out_ref[pl.ds(p * rows, rows), cols(chip(d) * 2 + 1 - core)] = fin[p, d + 1].astype(out_ref.dtype)
    for p in range(parts):
        for k in range(xs):
            stage1(p, k).wait_send()
        for d in range(xs - 1):
            stage2(p, d).wait_send()
            if gather:
                stage3(p, d).wait_send()
        if gather:
            for d in range(-1, xs - 1):
                stage4(p, d).wait_send()
    yield


class ColumnsLine:
    semaphores = 6

    @staticmethod
    def result(v, zs, ys):
        return jax.ShapeDtypeStruct((zs * v.shape[0], v.shape[1] // zs), v.dtype)

    @staticmethod
    def specs(v, zs, ys):
        sem = pltpu.SemaphoreType.DMA
        xs = lax.axis_size("ch") // 2
        return [sem((zs - 1,))] * 2 + [sem((zs - 1, xs - 1))] * 2 + [sem((zs - 1, xs))] * 2

    def __init__(self, zs, ys, src, out, sems):
        seq, ch = lax.axis_index("seq"), lax.axis_index("ch")
        self.nch = lax.axis_size("ch")
        self.xs = self.nch // 2
        self.zs, self.ys, self.z, self.y, self.ch = zs, ys, seq // ys, lax.rem(seq, ys), ch
        self.x, self.core = ch // 2, lax.rem(ch, 2)
        self.src, self.out, self.sems = src, out, sems
        self.rows, self.width = src.shape[0], src.shape[1] // zs
        self.part = self.rows // self.nch

    def cols(self, z):
        return pl.ds(pl.multiple_of(z * self.width, self.width), self.width)

    def share(self, z, ch):
        return pl.ds(pl.multiple_of(z * self.rows + ch * self.part, self.part), self.part)

    def remote(self, k, at, src, dst, to):
        send, recv = self.sems[2 * k : 2 * k + 2]
        return pltpu.make_async_remote_copy(src_ref=src, dst_ref=dst, send_sem=send.at[at], recv_sem=recv.at[at], device_id=to, device_id_type=MESH)

    def along(self, d):
        to = lax.rem(self.z + d, self.zs)
        src = self.src.at[pl.ds(pl.multiple_of(self.ch * self.part, self.part), self.part), self.cols(to)]
        return self.remote(0, d - 1, src, self.out.at[self.share(self.z, self.ch)], {"seq": to * self.ys + self.y})

    def from_z(self, d):
        return lax.rem(self.z + self.zs - d, self.zs)

    def over(self, d, e):
        rows = self.out.at[self.share(self.from_z(d), self.ch)]
        return self.remote(1, (d - 1, e - 1), rows, rows, {"ch": lax.rem(self.x + e, self.xs) * 2 + self.core})

    def across(self, d, e):
        rows = self.out.at[self.share(self.from_z(d), lax.rem(self.x + self.xs - e, self.xs) * 2 + self.core)]
        return self.remote(2, (d - 1, e), rows, rows, {"ch": self.x * 2 + 1 - self.core})

    def lags(self):
        return range(1, self.zs)

    def begin(self):
        for d in self.lags():
            self.along(d).start()
        here = pl.ds(pl.multiple_of(self.z * self.rows, self.rows), self.rows)
        self.out[here, :] = self.src[:, self.cols(self.z)]

    def step(self, index):
        for d in self.lags():
            if index == 0:
                self.along(d).wait_recv()
                for e in range(1, self.xs):
                    self.over(d, e).start()
                self.across(d, 0).start()
            else:
                for e in range(1, self.xs):
                    self.over(d, e).wait_recv()
                    self.across(d, e).start()

    def finish(self):
        for d in self.lags():
            for e in range(self.xs):
                self.across(d, e).wait_recv()
        for d in self.lags():
            self.along(d).wait_send()
            for e in range(1, self.xs):
                self.over(d, e).wait_send()
            for e in range(self.xs):
                self.across(d, e).wait_send()


def reduce_kernel(n, parts, gather, *refs):
    for _ in reduce_steps(n, parts, gather, [], *refs):
        pass


def reduce_scratch_shapes(shape, n, parts):
    rows, width = shape
    xs, r, w = n // 2, rows // parts, width // n
    sem = pltpu.SemaphoreType.DMA
    return [
        pltpu.VMEM((parts, xs, r, w), bf16), pltpu.VMEM((parts, xs, r, w), bf16), pltpu.VMEM((parts, xs - 1, r, w), bf16),
        pltpu.VMEM((parts, r, w), bf16), pltpu.VMEM((parts, xs - 1, r, w), bf16), pltpu.VMEM((parts, xs, r, w), bf16),
        sem((parts, xs)), sem((parts, xs)), sem((parts, xs - 1)), sem((parts, xs - 1)),
        sem((parts, xs - 1)), sem((parts, xs - 1)), sem((parts, xs)), sem((parts, xs)),
    ]


def ch_reduce(x, n, cid, gather, parts=2):
    rows, width = x.shape
    return pl.pallas_call(
        functools.partial(reduce_kernel, n, parts, gather),
        out_shape=jax.ShapeDtypeStruct((rows, width if gather else width // n), f32),
        in_specs=[VM], out_specs=VM,
        scratch_shapes=reduce_scratch_shapes(x.shape, n, parts),
        compiler_params=pltpu.CompilerParams(collective_id=cid, has_side_effects=True, vmem_limit_bytes=48 * 2**20),
        cost_estimate=cost(18), name="ch_reduce",
    )(x)


def carry_kernel(n, fwd, rev, count, places, layer, *refs):
    refs = list(refs)
    tot_ref, dl_ref = refs.pop(0), refs.pop(0)
    k = fwd + rev
    ends = [refs.pop(0) for _ in range(k)]
    parts = [refs.pop(0) for _ in range(count)]
    whole = refs.pop(0) if layer is not None else None
    outs = [refs.pop(0) for _ in range(k)]
    sums = [refs.pop(0) for _ in range(count)]
    if layer is not None:
        local = pltpu.make_async_copy(whole.at[layer], refs.pop(0), refs.pop(-1))
        local.start()
    mine, slots, tots, send, recv, tsend, trecv = refs[:7]
    jobs = [PartSum(*places, parts[j], sums[j], refs[7 + 3 * j : 10 + 3 * j]) for j in range(count)]
    me = lax.axis_index("seq")
    seqs = tot_ref.shape[0]
    greet([{"seq": lax.rem(me + d, n)} for d in range(1, n)])
    a2 = -jnp.exp(dl_ref[...]) * LOG2E
    directions = [False] * fwd + [True] * rev
    def copies(i, d):
        away = -d if directions[i] else d
        to = {"seq": lax.rem(me + away + n, n)}
        return (
            pltpu.make_async_remote_copy(src_ref=mine.at[i], dst_ref=slots.at[i, d - 1], send_sem=send.at[i, d - 1], recv_sem=recv.at[i, d - 1], device_id=to, device_id_type=MESH),
            pltpu.make_async_remote_copy(src_ref=tot_ref, dst_ref=tots.at[i, d - 1], send_sem=tsend.at[i, d - 1], recv_sem=trecv.at[i, d - 1], device_id=to, device_id_type=MESH),
        )
    for i in range(k):
        mine[i] = ends[i][...].astype(bf16)
        outs[i][...] = jnp.zeros_like(outs[i])
    for d in reversed(range(1, n)):
        for i in range(k):
            place = n - 1 - me if directions[i] else me
            @pl.when(place + d < n)
            def _():
                for c in copies(i, d):
                    c.start()
    for job in jobs:
        job.begin()
    for d in reversed(range(1, n)):
        for i in range(k):
            place = n - 1 - me if directions[i] else me
            @pl.when(place >= d)
            def _():
                for c in copies(i, d):
                    c.wait_recv()
                for s in range(seqs):
                    gain = jnp.exp2(a2 * tots[i, d - 1, pl.ds(s, 1), :])
                    outs[i][s] = gain * outs[i][s] + slots[i, d - 1, s].astype(f32)
    for d in reversed(range(1, n)):
        for i in range(k):
            place = n - 1 - me if directions[i] else me
            @pl.when(place + d < n)
            def _():
                for c in copies(i, d):
                    c.wait_send()
    for job in jobs:
        job.finish()
    if layer is not None:
        local.wait()


def carry_over(tot, dl, ends, n, cid, fwd, rev, ps=(), places=(), taken=None):
    whole, layer = (None, None) if taken is None else taken
    extra = [] if taken is None else [whole]
    k = len(ends)
    sem = pltpu.SemaphoreType.DMA
    return pl.pallas_call(
        functools.partial(carry_kernel, n, int(fwd), int(rev), len(ps), places, layer),
        out_shape=[jax.ShapeDtypeStruct(ends[0].shape, f32)] * k + [PartSum.result(p, *places) for p in ps]
        + [jax.ShapeDtypeStruct(w.shape[1:], w.dtype) for w in extra],
        in_specs=[VM] * (k + 2 + len(ps)) + [ANY] * len(extra), out_specs=[VM] * (k + len(ps)) + [ANY] * len(extra),
        scratch_shapes=[pltpu.VMEM((k,) + ends[0].shape, bf16), pltpu.VMEM((k, n - 1) + ends[0].shape, bf16), pltpu.VMEM((k, n - 1) + tot.shape, f32),
                        sem((k, n - 1)), sem((k, n - 1)), sem((k, n - 1)), sem((k, n - 1))]
        + [spec for p in ps for spec in PartSum.specs(p, *places)]
        + [pltpu.SemaphoreType.DMA] * len(extra),
        compiler_params=pltpu.CompilerParams(collective_id=cid, has_side_effects=True, vmem_limit_bytes=32 * 2**20), cost_estimate=cost(19), name="carry_over",
    )(tot, dl, *ends, *ps, *extra)


def seq_at(z, y, ys):
    return {"seq": z * ys + y}


class GatherLine:
    semaphores = 2

    @staticmethod
    def result(v, zs, ys):
        return jax.ShapeDtypeStruct((zs * v.shape[0], v.shape[1]), v.dtype)

    @staticmethod
    def specs(v, zs, ys):
        return [pltpu.SemaphoreType.DMA((2, zs - 1))] * 2


    def __init__(self, zs, ys, src, out, sems):
        me = lax.axis_index("seq")
        self.zs, self.ys, self.z, self.y = zs, ys, me // ys, lax.rem(me, ys)
        self.src, self.out = src, out
        self.send, self.recv = sems
        self.rows = src.shape[0]

    def block(self, z):
        return self.out.at[pl.ds(pl.multiple_of(z * self.rows, self.rows), self.rows)]

    def copy(self, way, r):
        z = self.z
        to, b = (lax.rem(z + 1, self.zs), z - r) if way == 0 else (lax.rem(z + self.zs - 1, self.zs), z + r)
        b = lax.rem(b + self.zs, self.zs)
        return pltpu.make_async_remote_copy(
            src_ref=self.src if r == 0 else self.block(b),
            dst_ref=self.block(b),
            send_sem=self.send.at[way, r],
            recv_sem=self.recv.at[way, r],
            device_id=seq_at(to, self.y, self.ys),
            device_id_type=MESH,
        )

    def sends(self, way, r):
        z, last = self.z, self.zs - 1
        return jnp.logical_and(z < last, z >= r) if way == 0 else jnp.logical_and(z > 0, z + r <= last)

    def receives(self, way, r):
        z, last = self.z, self.zs - 1
        return z - 1 - r >= 0 if way == 0 else z + 1 + r <= last

    def begin(self):
        self.start(0)
        self.block(self.z)[...] = self.src[...]

    def step(self, index):
        self.start(index + 1)

    def start(self, r):
        for way in (0, 1):
            if r > 0:
                self.arrive(way, r - 1)
            @pl.when(self.sends(way, r))
            def _():
                self.copy(way, r).start()

    def arrive(self, way, r):
        @pl.when(self.receives(way, r))
        def _():
            self.copy(way, r).wait_recv()

    def finish(self):
        self.arrived()
        self.sent()

    def arrived(self):
        for way in (0, 1):
            self.arrive(way, self.zs - 2)

    def sent(self):
        for way in (0, 1):
            for r in range(self.zs - 1):
                @pl.when(self.sends(way, r))
                def _():
                    self.copy(way, r).wait_send()


class SumAll:
    def __init__(self, zs, ys, src, out, scratch):
        me = lax.axis_index("seq")
        self.zs, self.ys, self.z, self.y = zs, ys, me // ys, lax.rem(me, ys)
        self.src, self.out = src, out
        self.yslots, self.ysum, self.slots, self.running, self.acc = scratch[:5]
        self.y1sems, self.zsems, self.y2sems, gather = scratch[5:7], scratch[7:9], scratch[9:11], scratch[11:13]
        self.part = src.shape[0] // ys
        self.share = self.part // zs
        self.back = GatherLine(zs, ys, self.mine(self.z), out, gather)
        self.back.block = self.mine

    @staticmethod
    def specs(height, w, zs, ys):
        part = height // ys
        share = part // zs
        sem = pltpu.SemaphoreType.DMA
        return [
            pltpu.VMEM((ys - 1, part, w), bf16),
            pltpu.VMEM((part, w), bf16),
            pltpu.VMEM((2, zs, share, w), bf16),
            pltpu.VMEM((2, zs, share, w), bf16),
            pltpu.VMEM((share, w), f32),
            sem((ys - 1,)), sem((ys - 1,)), sem((2, zs)), sem((2, zs)), sem(((ys - 1) * zs,)), sem(((ys - 1) * zs,)),
            sem((2, zs - 1)), sem((2, zs - 1)),
        ]

    def rows(self, index, size):
        return pl.ds(pl.multiple_of(index * size, size), size)

    def mine(self, z):
        return self.out.at[self.rows(self.y * self.zs + z, self.share)]

    def y1(self, d):
        to = lax.rem(self.y + d, self.ys)
        return pltpu.make_async_remote_copy(src_ref=self.src.at[self.rows(to, self.part)], dst_ref=self.yslots.at[d - 1], send_sem=self.y1sems[0].at[d - 1], recv_sem=self.y1sems[1].at[d - 1], device_id=seq_at(self.z, to, self.ys), device_id_type=MESH)

    def run(self, way, k):
        to = lax.rem(self.z + (1 if way == 0 else self.zs - 1), self.zs)
        return pltpu.make_async_remote_copy(src_ref=self.running.at[way, k], dst_ref=self.slots.at[way, k], send_sem=self.zsems[0].at[way, k], recv_sem=self.zsems[1].at[way, k], device_id=seq_at(to, self.y, self.ys), device_id_type=MESH)

    def y2(self, d, b):
        to = lax.rem(self.y + d, self.ys)
        at = (d - 1) * self.zs + b
        return pltpu.make_async_remote_copy(src_ref=self.mine(b), dst_ref=self.mine(b), send_sem=self.y2sems[0].at[at], recv_sem=self.y2sems[1].at[at], device_id=seq_at(self.z, to, self.ys), device_id_type=MESH)

    def begin(self):
        for d in range(1, self.ys):
            self.y1(d).start()

    def middle(self):
        total = self.src[self.rows(self.y, self.part), :].astype(f32)
        for d in range(1, self.ys):
            self.y1(d).wait_recv()
            total = total + self.yslots[d - 1].astype(f32)
        self.ysum[...] = total.astype(bf16)

    def line_sum(self, r):
        for way in (0, 1):
            k = self.zs - 1 - r if way == 0 else r
            z, first = self.z, 0 if way == 0 else self.zs - 1
            own = pl.ds(k * self.share, self.share)
            @pl.when(z == first)
            def _():
                self.running[way, k] = self.ysum[own, :]
                self.run(way, k).start()
            inside = jnp.logical_and(z > 0, z < k) if way == 0 else jnp.logical_and(z < self.zs - 1, z > k)
            @pl.when(inside)
            def _():
                self.run(way, k).wait_recv()
                self.running[way, k] = (self.ysum[own, :].astype(f32) + self.slots[way, k].astype(f32)).astype(bf16)
                self.run(way, k).start()

    def turn(self):
        self.acc[...] = self.ysum[self.rows(self.z, self.share), :].astype(f32)
        for way in (0, 1):
            @pl.when(self.z > 0 if way == 0 else self.z < self.zs - 1)
            def _():
                self.run(way, self.z).wait_recv()
                self.acc[...] = self.acc[...] + self.slots[way, self.z].astype(f32)
        self.mine(self.z)[...] = self.acc[...].astype(bf16)
        self.back.start(0)
        for d in range(1, self.ys):
            self.y2(d, self.z).start()

    def spread(self, r):
        if r < self.zs - 2:
            self.back.start(r + 1)
        else:
            for way in (0, 1):
                self.back.arrive(way, r)
        for way in (0, 1):
            b = self.z - 1 - r if way == 0 else self.z + 1 + r
            b = lax.rem(b + self.zs, self.zs)
            @pl.when(self.back.receives(way, r))
            def _():
                for d in range(1, self.ys):
                    self.y2(d, b).start()

    def finish(self):
        for d in range(1, self.ys):
            for b in range(self.zs):
                self.y2(d, b).wait_recv()
        for d in range(1, self.ys):
            self.y1(d).wait_send()
            for b in range(self.zs):
                self.y2(d, b).wait_send()
        for k in range(self.zs):
            @pl.when(self.z < k)
            def _():
                self.run(0, k).wait_send()
            @pl.when(self.z > k)
            def _():
                self.run(1, k).wait_send()
        self.back.sent()


class PartSum:
    semaphores = 3

    @staticmethod
    def result(v, zs, ys):
        return jax.ShapeDtypeStruct(v.shape[1:], f32)

    @staticmethod
    def specs(v, zs, ys):
        sem = pltpu.SemaphoreType.DMA((ys - 1,))
        return [sem, sem, pltpu.VMEM((ys - 1,) + v.shape[1:], v.dtype)]


    def __init__(self, zs, ys, src, out, scratch):
        me = lax.axis_index("seq")
        self.ys, self.z, self.y = ys, me // ys, lax.rem(me, ys)
        self.src, self.out = src, out
        self.send, self.recv, self.slots = scratch

    def copy(self, d):
        to = lax.rem(self.y + d, self.ys)
        return pltpu.make_async_remote_copy(
            src_ref=self.src.at[to],
            dst_ref=self.slots.at[d - 1],
            send_sem=self.send.at[d - 1],
            recv_sem=self.recv.at[d - 1],
            device_id=seq_at(self.z, to, self.ys),
            device_id_type=MESH,
        )

    def begin(self):
        for d in range(1, self.ys):
            self.copy(d).start()

    def finish(self):
        mine = self.src[self.y].astype(f32)
        for d in range(1, self.ys):
            self.copy(d).wait_recv()
            mine = mine + self.slots[d - 1].astype(f32)
        self.out[...] = mine
        for d in range(1, self.ys):
            self.copy(d).wait_send()


def closing_kernel(n, nseq, zs, ys, parts, count, pieces, x_ref, b_ref, v_ref, cols_ref, h_ref, *refs):
    refs = list(refs)

    def take(k):
        head, refs[:] = refs[:k], refs[k:]
        return head

    piece_refs, p_refs = take(pieces), take(count)
    out_ref, branch_ref, sum_ref, values_ref, norm_ref = take(5)
    part_refs = take(count)
    s_ref, all_ref, mine_ref, mine_slots, t_ref, tslots = take(6)
    reduce_scratch, more_scratch, gather_sems, sum_scratch = take(14), take(14), take(2), take(13)
    part_scratch, (msend, mrecv, tsend, trecv) = take(3 * count), take(4)
    seq = lax.axis_index("seq")
    z = seq // ys
    line = GatherLine(zs, ys, v_ref, all_ref, gather_sems)
    total = SumAll(zs, ys, s_ref, sum_ref, sum_scratch)
    sums = [PartSum(zs, ys, p_refs[k], part_refs[k], part_scratch[3 * k : 3 * k + 3]) for k in range(count)]
    late = PartSum(zs, ys, mine_ref, values_ref, [msend, mrecv, mine_slots])
    steps = reduce_steps(n, parts, False, [{"seq": lax.rem(seq + d, nseq)} for d in range(1, nseq)], x_ref, out_ref, *reduce_scratch)
    more_steps = reduce_steps(n, parts, False, None, b_ref, branch_ref, *more_scratch)

    def tiny(d):
        return pltpu.make_async_remote_copy(src_ref=t_ref, dst_ref=tslots.at[seq], send_sem=tsend.at[d - 1], recv_sem=trecv.at[d - 1], device_id={"seq": lax.rem(seq + d, nseq)}, device_id_type=MESH)

    next(steps)
    next(more_steps)
    line.begin()
    offset = 0
    for piece in piece_refs:
        s_ref[pl.ds(offset, piece.shape[0]), :] = piece[...].astype(bf16)
        offset += piece.shape[0]
    if offset < s_ref.shape[0]:
        s_ref[pl.ds(offset, s_ref.shape[0] - offset), :] = jnp.zeros((s_ref.shape[0] - offset, s_ref.shape[1]), bf16)
    total.begin()
    next(steps)
    next(more_steps)
    line.start(1)
    total.middle()
    total.line_sum(0)
    for part in sums:
        part.begin()
    for _ in steps:
        pass
    w = h_ref.shape[1]
    row = jnp.sum(out_ref[:, pl.ds(0, w)] * h_ref[...], axis=0, keepdims=True)
    t_ref[...] = jnp.broadcast_to(row, t_ref.shape).astype(bf16)
    tslots[seq] = t_ref[...]
    for d in range(1, nseq):
        tiny(d).start()
    total.line_sum(1)
    for r in range(2, zs - 1):
        line.start(r)
        total.line_sum(r)
    total.turn()
    for _ in more_steps:
        pass
    line.arrived()
    fold = mine_ref.shape[1]
    for k in range(ys):
        def chunk(i, _):
            at = pl.ds(pl.multiple_of(i * 256, 256), 256)
            got = jnp.dot(cols_ref[pl.ds(k * fold, fold), :], all_ref[:, at], preferred_element_type=f32)
            mine_ref[k, :, at] = got.astype(bf16)
            return 0
        lax.fori_loop(0, all_ref.shape[1] // 256, chunk, 0)
    late.begin()
    for r in range(zs - 1):
        total.spread(r)
    for part in sums:
        part.finish()
    for d in range(1, nseq):
        tiny(d).wait_recv()
    norm = tslots[0].astype(f32)
    for k in range(1, nseq):
        norm = norm + tslots[k].astype(f32)
    norm_ref[...] = norm
    late.finish()
    total.finish()
    line.sent()
    for d in range(1, nseq):
        tiny(d).wait_send()


def closing(x, branch, v, cols, h, pieces, ps, n, nseq, zs, ys, cid, parts=2):
    rows, width = x.shape
    sem = pltpu.SemaphoreType.DMA
    height = sum(piece.shape[0] for piece in pieces)
    height += -height % (16 * ys * zs)
    w = v.shape[1]
    fold = cols.shape[0] // ys
    count = len(ps)
    tiny = (16, h.shape[1])
    return pl.pallas_call(
        functools.partial(closing_kernel, n, nseq, zs, ys, parts, count, len(pieces)),
        out_shape=[
            jax.ShapeDtypeStruct((rows, width // n), f32),
            jax.ShapeDtypeStruct((rows, branch.shape[1] // n), f32),
            jax.ShapeDtypeStruct((height, w), bf16),
            jax.ShapeDtypeStruct((fold, w), f32),
            jax.ShapeDtypeStruct(tiny, f32),
        ]
        + [PartSum.result(p, zs, ys) for p in ps],
        in_specs=[VM] * (5 + len(pieces) + count),
        out_specs=[VM] * (5 + count),
        scratch_shapes=[
            pltpu.VMEM((height, w), bf16),
            pltpu.VMEM((zs * v.shape[0], w), bf16),
            pltpu.VMEM((ys, fold, w), bf16),
            pltpu.VMEM((ys - 1, fold, w), bf16),
            pltpu.VMEM(tiny, bf16),
            pltpu.VMEM((nseq,) + tiny, bf16),
        ]
        + reduce_scratch_shapes(x.shape, n, parts)
        + reduce_scratch_shapes(branch.shape, n, parts)
        + GatherLine.specs(v, zs, ys)
        + SumAll.specs(height, w, zs, ys)
        + [spec for p in ps for spec in PartSum.specs(p, zs, ys)]
        + [sem((ys - 1,)), sem((ys - 1,)), sem((nseq - 1,)), sem((nseq - 1,))],
        compiler_params=pltpu.CompilerParams(collective_id=cid, has_side_effects=True, vmem_limit_bytes=60 * 2**20),
        cost_estimate=cost(70),
        name="closing",
    )(x, branch, v, cols, h, *pieces, *ps)


def passed_along(block, axis, distance):
    devices = range(lax.axis_size(axis))
    route = [(i - distance, i) for i in devices if i - distance in devices]
    return lax.ppermute(block, axis, route)


def silu_slope(argument):
    logistic = jax.nn.sigmoid(argument)
    return logistic * (1.0 + argument * (1.0 - logistic))


def conv_local(extended, weights, biases, seg_ext):
    length_now = extended.shape[1] - (KERN - 1)
    seg_now = seg_ext[:, KERN - 1 :]
    summed = biases + jnp.zeros((extended.shape[0], length_now, extended.shape[2]), f32)
    for lag_index in range(KERN):
        same_doc = (seg_ext[:, lag_index : lag_index + length_now] == seg_now).astype(f32)
        summed = (
            summed
            + weights[lag_index]
            * extended[:, lag_index : lag_index + length_now]
            * same_doc[:, :, None]
        )
    return summed


def dot(a, b, contract):
    return lax.dot_general(a, b, ((contract[:1], contract[1:]), ((), ())), preferred_element_type=f32)


def lines(zs, ys):
    return [[z * ys + y for z in range(zs)] for y in range(ys)]


def tokens_of_line(rows, zs, ys):
    return lax.all_gather(rows, "seq", axis_index_groups=lines(zs, ys), tiled=True)


def local(
    hidden_in,
    segments,
    cotangent,
    norm_gain,
    input_projection_weight,
    conv_weight,
    conv_bias,
    proj_weight,
    step_weight,
    step_bias,
    decay_log,
    skip_gain,
    output_projection_weight,
):
    seqs, length, width = hidden_in.shape
    rows = seqs * length
    nch, nseq = lax.axis_size("ch"), lax.axis_size("seq")
    channels = conv_bias.shape[-1]
    share = width // nch
    share_start = lax.axis_index("ch") * share
    seg_own = segments.astype(f32)
    seg_edge = passed_along(seg_own[:, -(KERN - 1) :], "seq", 1)
    seg_ext = jnp.concatenate([seg_edge, seg_own], axis=1)
    keep = (seg_ext[:, KERN - 2 : -1] == seg_own).astype(f32).reshape(-1, 1)
    hidden = hidden_in.astype(f32).reshape(rows, width)
    grad_rows = cotangent.astype(f32).reshape(rows, width)
    ids = iter(range(100))
    zs = 4 if nseq % 4 == 0 else nseq
    ys = nseq // zs
    fold = width // nseq
    places = (zs, ys)

    out_cols, w_copy = {}, {}
    stored = []
    out_low = grad_rows.astype(bf16)
    grad_mixed = dot(out_low, output_projection_weight[LAYERS - 1], (1, 1))
    grad_mixed_line = tokens_of_line(grad_mixed.astype(bf16), zs, ys)
    for layer in range(LAYERS):
        last = layer == LAYERS - 1
        inv_rms = lax.rsqrt(jnp.mean(hidden * hidden, axis=-1, keepdims=True) + epsilon)
        normed = (hidden * inv_rms * norm_gain[layer]).astype(bf16)
        w_in = w_copy[1] if layer > 0 else input_projection_weight[0]
        both = lax.dot_general(normed, w_in, (((1,), (0,)), ((), ())), preferred_element_type=f32)
        values, gate_pre = both[:, 0], both[:, 1]
        values3 = values.reshape(seqs, length, channels)
        edge = passed_along(values3[:, -(KERN - 1) :], "seq", 1)
        extended = jnp.concatenate([edge, values3], axis=1)
        conv_out, conv_pull = jax.vjp(
            functools.partial(conv_local, seg_ext=seg_ext), extended, conv_weight[layer], conv_bias[layer]
        )
        conv_out = conv_out.reshape(rows, channels)
        activated = jax.nn.silu(conv_out)
        act_low = activated.astype(bf16)
        proj_out = ch_sum(dot(act_low, proj_weight[layer], (1, 0)), nch, next(ids))
        rank_low = proj_out[:, :RANK].astype(bf16)
        mats = proj_out[:, RANK:]
        step_pre = dot(rank_low, step_weight[layer], (1, 0)) + step_bias[layer]
        rates = decay_log[layer]
        end_state, total = scan_local(step_pre, activated, mats, keep, rates, seqs, [], places, 0)
        gate_act = jax.nn.silu(gate_pre)
        if last:
            gate_line = tokens_of_line(gate_pre.astype(bf16), zs, ys)
            grad_scan = grad_mixed * gate_act
            start = scan_back_local(step_pre, grad_scan, mats, keep, rates, seqs)
            state_in, lam_in, w_copy[0] = carry_over(
                total, rates, [end_state, start], nseq, next(ids), True, True, taken=(input_projection_weight, 0)
            )
        else:
            state_in, w_copy[1] = carry_over(
                total, rates, [end_state], nseq, next(ids), True, False, taken=(input_projection_weight, 1)
            )
        keeping = (hidden, inv_rms, normed, gate_pre, gate_act, conv_out, activated, act_low, conv_pull, rank_low,
                   step_pre, mats, total, state_in)
        if last:
            stored.append(keeping)
            break
        (y,) = scan_forward(
            step_pre, activated, mats, keep, rates, state_in, seqs, [], places, 0, (grad_mixed_line,)
        )
        scanned = y + skip_gain[layer] * activated
        mixed = (scanned * gate_act).astype(bf16)
        out_part = dot(mixed, output_projection_weight[layer], (1, 0)).astype(bf16)
        mixed_all = tokens_of_line(mixed, zs, ys)
        branch = ch_reduce(out_part, nch, next(ids), True)
        hidden = hidden + branch
        stored.append(keeping + (scanned, mixed_all))

    for layer in reversed(range(LAYERS)):
        last = layer == LAYERS - 1
        (hidden, inv_rms, normed, gate_pre, gate_act, conv_out, activated, act_low, conv_pull, rank_low,
         step_pre, mats, total, state_in) = stored[layer][:14]
        rates = decay_log[layer]
        if not last:
            scanned, mixed_all = stored[layer][14:]
            normed_cols = early_cols
            out_low = grad_rows.astype(bf16)
            grad_mixed = dot(out_low, output_projection_weight[layer], (1, 1))
            grad_scan = grad_mixed * gate_act
            grad_gate = (grad_mixed * scanned * silu_slope(gate_pre)).astype(bf16)
            start = scan_back_local(step_pre, grad_scan, mats, keep, rates, seqs)
            gate_all = tokens_of_line(grad_gate, zs, ys)
            lam_in, grad_out_last = carry_over(
                total, rates, [start], nseq, next(ids), False, True, [out_parts_last], places
            )
        grad_skip = jnp.sum(grad_scan * activated, axis=0)
        if last:
            plan = [
                (ColumnsLine, (3, 5), normed),
                (ColumnsLine, (4, 6), out_low),
                (ColumnsLine, (6, 8), stored[0][2]),
            ]
        else:
            plan = [
                (ColumnsLine, (2, 4), out_low),
                (PartSum, (), values_parts_last),
                (PartSum, (), gate_parts_last),
            ]
        grad_pre, grad_act, grad_mats, grad_decay, *others = scan_back(
            step_pre, activated, grad_scan, mats, keep, rates, skip_gain[layer][None], state_in, lam_in, seqs, int(last),
            plan, places, next(ids), (),
        )
        if last:
            y, normed_cols, out_cols[layer], early_cols = others
            scanned = y + skip_gain[layer] * activated
            mixed = (scanned * gate_act).astype(bf16)
            grad_gate = (grad_mixed * scanned * silu_slope(gate_pre)).astype(bf16)
            scanned_line = tokens_of_line(scanned.astype(bf16), zs, ys).astype(f32)
        else:
            out_cols[layer], grad_values_last, grad_gate_last = others
        grad_step_bias = jnp.sum(grad_pre, axis=0)
        pre_low = grad_pre.astype(bf16)
        grad_step_weight = dot(rank_low, pre_low, (0, 0))
        rank_part = dot(pre_low, step_weight[layer], (1, 1))
        grad_proj = ch_sum(
            jnp.concatenate([rank_part, grad_mats[:, : 2 * STATE]], axis=-1), nch, next(ids),
            (gate_line,) if last else (),
        ).astype(bf16)
        grad_proj_weight = dot(grad_proj, act_low, (0, 0))
        grad_act = grad_act + dot(grad_proj, proj_weight[layer], (1, 1))
        grad_conv = (grad_act * silu_slope(conv_out)).reshape(seqs, length, channels)
        grad_ext, grad_conv_weight, grad_conv_bias = conv_pull(grad_conv)
        returned = passed_along(grad_ext[:, : KERN - 1], "seq", -1)
        grad_values = grad_ext[:, KERN - 1 :]
        grad_values = jnp.concatenate(
            [grad_values[:, : -(KERN - 1)], grad_values[:, -(KERN - 1) :] + returned], axis=1
        ).reshape(rows, channels).astype(bf16)
        w_in = w_copy[layer]
        grad_both = jnp.stack([grad_values, grad_gate], axis=1)
        grad_part = lax.dot_general(grad_both, w_in, (((1, 2), (1, 2)), ((), ())), preferred_element_type=f32)
        scale_now = norm_gain[layer]
        misc = jnp.concatenate([grad_conv_weight, grad_conv_bias[None], grad_step_bias[None], grad_skip[None]], axis=0)
        small = [grad_proj_weight, grad_step_weight, grad_decay, misc]
        if last:
            values_last = tokens_of_line(grad_values, zs, ys)
            values_parts_last = dot(normed_cols, values_last, (0, 0)).astype(bf16).reshape(ys, fold, channels)
            grad_normed = ch_reduce(grad_part.astype(bf16), nch, next(ids), True)
            scanned_line = scanned_line + 0.0 * grad_normed[0, 0]
            gates = gate_line.astype(f32)
            mixed_all = (scanned_line * jax.nn.silu(gates)).astype(bf16)
            gate_all = (grad_mixed_line.astype(f32) * scanned_line * silu_slope(gates)).astype(bf16)
            out_part = dot(mixed, output_projection_weight[layer], (1, 0)).astype(bf16)
            hidden_last = lax.dynamic_slice_in_dim(hidden, share_start, share, 1)
        columns = [out_cols[layer][:, k * fold : (k + 1) * fold] for k in range(ys)]
        out_parts = jnp.stack([dot(mixed_all, k, (0, 0)).astype(bf16) for k in columns], axis=0)
        gate_parts = dot(normed_cols, gate_all, (0, 0)).astype(bf16).reshape(ys, fold, channels)
        if last:
            out_parts_last, gate_parts_last = out_parts, gate_parts
            inner = jnp.sum(grad_normed * scale_now * hidden, axis=-1, keepdims=True)
            grad_norm = lax.dynamic_slice_in_dim(jnp.sum(grad_normed * hidden * inv_rms, axis=0), share_start, share, 0)
            grad_rows = grad_rows + inv_rms * scale_now * grad_normed - hidden * (inv_rms * inv_rms * inv_rms) * inner / width
            norm_row = jnp.pad(grad_norm[None], ((0, 0), (0, channels - share)))
            small[-1] = jnp.pad(jnp.concatenate([misc, norm_row], axis=0), ((0, 16 - misc.shape[0] - 1), (0, 0)))
            small_last = small
            continue
        inner = jnp.sum(grad_part * scale_now * hidden, axis=-1, keepdims=True)
        inner_high = inner.astype(bf16)
        inner_low = (inner - inner_high.astype(f32)).astype(bf16)
        beside = jnp.pad(jnp.concatenate([inner_high, inner_low], axis=1), ((0, 0), (0, LANES - 2)))
        beside = jnp.broadcast_to(beside[:, None], (rows, nch, LANES))
        send = jnp.concatenate([grad_part.astype(bf16).reshape(rows, nch, share), beside], axis=2)
        small[-1] = jnp.pad(misc, ((0, 16 - misc.shape[0]), (0, 0)))
        hidden_share = lax.dynamic_slice_in_dim(hidden, share_start, share, 1)
        scale_share = lax.dynamic_slice_in_dim(scale_now, share_start, share, 0)
        got, branch, sums, grad_in_values, tiny, grad_gate_now, grad_out_weight = closing(
            send.reshape(rows, nch * (share + LANES)), out_part, grad_values, jnp.swapaxes(normed_cols, 0, 1), hidden_share * inv_rms,
            small + small_last, [gate_parts, out_parts], nch, nseq, zs, ys, next(ids),
        )
        grad_share, inner = got[:, :share], got[:, share : share + 1] + got[:, share + 1 : share + 2]
        grad_input = (
            lax.dynamic_slice_in_dim(grad_rows, share_start, share, 1)
            + inv_rms * scale_share * grad_share
            - hidden_share * (inv_rms * inv_rms * inv_rms) * inner / width
        )
        result = (hidden_last + branch).astype(bf16)
        total_small = sums.astype(f32)
        heights = [v.shape[0] for v in small_last]
        half = sum(heights)
        pairs, at = [], 0
        for height in heights:
            pairs.append(jnp.stack([total_small[at : at + height], total_small[half + at : half + at + height]], axis=0))
            at += height
        misc = pairs[3]
        norms = jnp.stack([tiny[0], misc[1, KERN + 3, :share]], axis=0)
        in_weight = jnp.stack(
            [jnp.stack(pair, axis=1) for pair in ((grad_in_values, grad_gate_now), (grad_values_last, grad_gate_last))], axis=0
        )
        out_weight = jnp.stack([grad_out_weight, grad_out_last], axis=0)
    shape3 = (seqs, length, share)
    return (
        result.reshape(shape3),
        grad_input.reshape(shape3),
        norms,
        in_weight,
        misc[:, :KERN],
        misc[:, KERN],
        jnp.swapaxes(pairs[0], 1, 2),
        pairs[1],
        misc[:, KERN + 1],
        pairs[2],
        misc[:, KERN + 2],
        out_weight,
    )


def solution(mesh):
    in_specs = (
        P(None, "seq", None),
        P(None, "seq"),
        P(None, "seq", None),
        P(),
        P(None, None, None, "ch"),
        P(None, None, "ch"),
        P(None, "ch"),
        P(None, "ch", None),
        P(None, None, "ch"),
        P(None, "ch"),
        P(None, None, "ch"),
        P(None, "ch"),
        P(None, "ch", None),
    )
    out_specs = (
        P(None, "seq", "ch"),
        P(None, "seq", "ch"),
        P(None, "ch"),
        P(None, "seq", None, "ch"),
        P(None, None, "ch"),
        P(None, "ch"),
        P(None, "ch", None),
        P(None, None, "ch"),
        P(None, "ch"),
        P(None, None, "ch"),
        P(None, "ch"),
        P(None, "ch", "seq"),
    )
    return jax.shard_map(local, mesh=mesh, in_specs=in_specs, out_specs=out_specs, check_vma=False)
```

```python
import functools

import jax
import jax.numpy as jnp
from jax import lax
from jax.experimental import pallas as pl
from jax.experimental.pallas import tpu as pltpu
from jax.sharding import PartitionSpec as P

STATE = 16
RANK = 128
KERN = 4
LAYERS = 2
MESH = pl.DeviceIdType.MESH
ANY = pl.BlockSpec(memory_space=pl.ANY)
f32, bf16 = jnp.float32, jnp.bfloat16
epsilon = 1e-05


def after(kernel, count, pins):
    def run(*refs):
        return kernel(*refs[:count], *refs[count + len(pins) :])
    return run


def cost(us):
    return pl.CostEstimate(flops=int(us * 0.1e9), bytes_accessed=0, transcendentals=0)


LANES = 128
BIG = 1e30
LOG2E = 1.4426950408889634

def softplus(v):
    return jnp.maximum(v, 0.0) + jnp.log(1.0 + jnp.exp(-jnp.abs(v)))

def spread_states(bc_ref, wide_ref, pick_ref, rows, unroll=8):
    lane = lax.broadcasted_iota(jnp.int32, (STATE, 2 * STATE), 1)
    row = lax.broadcasted_iota(jnp.int32, (STATE, 2 * STATE), 0)
    mask = (lane % STATE == row).astype(jnp.float32)
    src = lax.broadcasted_iota(jnp.int32, (2 * STATE, 2 * LANES), 0)
    dst = lax.broadcasted_iota(jnp.int32, (2 * STATE, 2 * LANES), 1)
    route = ((src // STATE) == (dst // LANES)).astype(jnp.bfloat16)
    chunk = 32
    def step(i, _):
        t0 = pl.multiple_of(i * chunk, chunk)
        bcv = bc_ref[pl.ds(t0, chunk), :]
        for j in range(chunk):
            pick_ref[pl.ds(j * STATE, STATE), :] = (bcv[j:j + 1] * mask).astype(jnp.bfloat16)
        wide_ref[pl.ds(pl.multiple_of(t0 * STATE, chunk * STATE), chunk * STATE), :] = jnp.dot(pick_ref[...], route, preferred_element_type=jnp.float32)
        return 0
    lax.fori_loop(0, rows // chunk, step, 0)

def prep(step_ref_pre, act_ref, keep_ref, dstep_ref, dx_ref, rows):
    def body(i, _):
        sl = pl.ds(pl.multiple_of(i * 32, 32), 32)
        for g in range(dstep_ref.shape[0]):
            st = softplus(step_ref_pre[sl, lanes(g)])
            dstep_ref[g, sl, :] = jnp.where(keep_ref[sl, :] > 0.0, st, BIG)
            dx_ref[g, sl, :] = st * act_ref[sl, lanes(g)]
        return 0
    lax.fori_loop(0, rows // 32, body, 0)

def lanes(g):
    return pl.ds(g * LANES, LANES)

def group_sets(channels, width):
    n = channels // LANES
    return [list(range(i, min(i + width, n))) for i in range(0, n, width)]

def local_kernel(seqs, pre_ref, act_ref, bc_ref, keep_ref, dl_ref, end_ref, gain_ref, wide, pick, dstep, dx):
    rows, channels = pre_ref.shape
    length = rows // seqs
    spread_states(bc_ref, wide, pick, rows)
    prep(pre_ref, act_ref, keep_ref, dstep, dx, rows)
    yield
    for gs in group_sets(channels, 8):
        a2 = [-jnp.exp(dl_ref[:, lanes(g)]) * LOG2E for g in gs]
        for s in range(seqs):
            for k, g in enumerate(gs):
                tot = jnp.sum(dstep[g, pl.ds(s * length, length), :], axis=0, keepdims=True)
                gain_ref[pl.ds(s, 1), lanes(g)] = tot
            def blk(i, st):
                st = list(st)
                t0 = pl.multiple_of(s * length + i * 8, 8)
                for j in range(8):
                    b = wide[pl.ds(pl.multiple_of((t0 + j) * STATE, STATE), STATE), pl.ds(0, LANES)]
                    for k, g in enumerate(gs):
                        d = jnp.exp2(a2[k] * dstep[g, pl.ds(t0 + j, 1), :])
                        st[k] = d * st[k] + b * dx[g, pl.ds(t0 + j, 1), :]
                return tuple(st)
            st = lax.fori_loop(0, length // 8, blk, tuple(jnp.zeros((STATE, LANES), jnp.float32) for _ in gs))
            for k, g in enumerate(gs):
                end_ref[s, :, lanes(g)] = st[k]
            yield

VM = pl.BlockSpec(memory_space=pltpu.VMEM)


def played(kernel, counts, plan, places):
    n_in, n_out, n_scratch = counts

    def run(*refs):
        refs = list(refs)

        def take(k):
            head, refs[:] = refs[:k], refs[k:]
            return head

        own = take(n_in)
        sources = take(len(plan))
        own += take(n_out)
        targets = take(len(plan))
        own += take(n_scratch)
        jobs = []
        for (kind, when), src, out in zip(plan, sources, targets):
            jobs.append((kind(*places, src, out, take(kind.semaphores)), when))
        if plan:
            seq, ch = lax.axis_index("seq"), lax.axis_index("ch")
            zs, ys = places
            z, y = seq // ys, lax.rem(seq, ys)
            peers = [{"seq": lax.rem(z + d, zs) * ys + y} for d in range(1, zs)]
            peers += [{"seq": z * ys + lax.rem(y + d, ys)} for d in range(1, ys)]
            xs = lax.axis_size("ch") // 2
            peers += [{"ch": lax.rem(ch // 2 + e, xs) * 2 + lax.rem(ch, 2)} for e in range(1, xs)]
            peers.append({"ch": ch + 1 - 2 * lax.rem(ch, 2)})
            barrier = pltpu.get_barrier_semaphore()
            for peer in peers:
                pl.semaphore_signal(barrier, inc=1, device_id=peer, device_id_type=MESH)
        for at, _ in enumerate(kernel(*own)):
            if at == 0 and plan:
                pl.semaphore_wait(barrier, len(peers))
                for job, _ in jobs:
                    job.begin()
            for job, when in jobs:
                if at in when:
                    job.step(when.index(at))
        for job, when in jobs:
            job.finish()

    return run


def play_call(kernel, counts, plan, places, cid, out_shape, scratch, arrays, us, name, pins=()):
    arrays = list(arrays) + [v for _, _, v in plan]
    kinds = [(kind, when) for kind, when, _ in plan]
    out_shape = list(out_shape) + [kind.result(v, *places) for kind, _, v in plan]
    sems = [spec for kind, _, v in plan for spec in kind.specs(v, *places)]
    extra = dict(collective_id=cid, has_side_effects=True) if plan else {}
    return pl.pallas_call(
        after(played(kernel, counts, kinds, places), len(arrays), pins),
        out_shape=out_shape,
        in_specs=[VM] * len(arrays) + [ANY] * len(pins),
        out_specs=[VM] * len(out_shape),
        scratch_shapes=list(scratch) + sems,
        compiler_params=pltpu.CompilerParams(vmem_limit_bytes=60 * 2**20, **extra),
        cost_estimate=cost(us),
        name=name,
    )(*arrays, *pins)

def scan_local(pre, act, bc, keep, dl, seqs, plan, places, cid):
    rows, channels = pre.shape
    f = jnp.float32
    big = pltpu.VMEM((channels // LANES, rows, LANES), f)
    return play_call(
        functools.partial(local_kernel, seqs), (5, 2, 4), plan, places, cid,
        [jax.ShapeDtypeStruct((seqs, STATE, channels), f), jax.ShapeDtypeStruct((seqs, channels), f)],
        [pltpu.VMEM((rows * STATE, 2 * LANES), f), pltpu.VMEM((32 * STATE, 2 * STATE), jnp.bfloat16), big, big],
        (pre, act, bc, keep, dl), 8, "scan_local",
    )


def forward_kernel(seqs, pre_ref, act_ref, bc_ref, keep_ref, dl_ref, in_ref, y_ref, wide, pick, dstep, dx, part):
    rows, channels = pre_ref.shape
    length = rows // seqs
    spread_states(bc_ref, wide, pick, rows)
    prep(pre_ref, act_ref, keep_ref, dstep, dx, rows)
    yield
    for gs in group_sets(channels, 4):
        a2 = [-jnp.exp(dl_ref[:, lanes(g)]) * LOG2E for g in gs]
        for s in range(seqs):
            def blk(i, st):
                st = list(st)
                t0 = pl.multiple_of(s * length + i * 8, 8)
                for j in range(8):
                    at = pl.ds(pl.multiple_of((t0 + j) * STATE, STATE), STATE)
                    b = wide[at, pl.ds(0, LANES)]
                    c = wide[at, pl.ds(LANES, LANES)]
                    for k, g in enumerate(gs):
                        d = jnp.exp2(a2[k] * dstep[g, pl.ds(t0 + j, 1), :])
                        st[k] = d * st[k] + b * dx[g, pl.ds(t0 + j, 1), :]
                        v = st[k] * c
                        part[k, pl.ds(pl.multiple_of(i * 64 + j * 8, 8), 8), :] = v[:8] + v[8:]
                return tuple(st)
            lax.fori_loop(0, length // 8, blk, tuple(in_ref[s, :, lanes(g)] for g in gs))
            def red(i, _):
                t0 = pl.multiple_of(s * length + i * 8, 8)
                for k, g in enumerate(gs):
                    acc = part[k, pl.ds(i * 64, 8, stride=8), :]
                    for m in range(1, 8):
                        acc = acc + part[k, pl.ds(i * 64 + m, 8, stride=8), :]
                    y_ref[pl.ds(t0, 8), lanes(g)] = acc
                return 0
            lax.fori_loop(0, length // 8, red, 0)
            yield

def scan_forward(pre, act, bc, keep, dl, state_in, seqs, plan, places, cid, pins=()):
    rows, channels = pre.shape
    f = jnp.float32
    big = pltpu.VMEM((channels // LANES, rows, LANES), f)
    return play_call(
        functools.partial(forward_kernel, seqs), (6, 1, 5), plan, places, cid,
        [jax.ShapeDtypeStruct((rows, channels), f)],
        [pltpu.VMEM((rows * STATE, 2 * LANES), f), pltpu.VMEM((32 * STATE, 2 * STATE), jnp.bfloat16), big, big,
         pltpu.VMEM((4, rows // seqs * 8, LANES), f)],
        (pre, act, bc, keep, dl, state_in), 11, "scan_forward", pins,
    )


LN2 = 0.6931471805599453

def back_local_kernel(seqs, pre_ref, gs_ref, bc_ref, keep_ref, dl_ref, out_ref, wide, pick, dstep, gsc):
    rows, channels = pre_ref.shape
    length = rows // seqs
    spread_states(bc_ref, wide, pick, rows)
    def body(i, _):
        sl = pl.ds(pl.multiple_of(i * 32, 32), 32)
        for g in range(channels // LANES):
            st = softplus(pre_ref[sl, lanes(g)])
            dstep[g, sl, :] = jnp.where(keep_ref[sl, :] > 0.0, st, BIG)
            gsc[g, sl, :] = gs_ref[sl, lanes(g)]
        return 0
    lax.fori_loop(0, rows // 32, body, 0)
    for gs in group_sets(channels, 8):
        a2 = [-jnp.exp(dl_ref[:, lanes(g)]) * LOG2E for g in gs]
        for s in range(seqs):
            def blk(i, st):
                st = list(st)
                t0 = pl.multiple_of(s * length + (length // 8 - 1 - i) * 8, 8)
                for j in reversed(range(8)):
                    c = wide[pl.ds(pl.multiple_of((t0 + j) * STATE, STATE), STATE), pl.ds(LANES, LANES)]
                    for k, g in enumerate(gs):
                        d = jnp.exp2(a2[k] * dstep[g, pl.ds(t0 + j, 1), :])
                        st[k] = d * (st[k] + c * gsc[g, pl.ds(t0 + j, 1), :])
                return tuple(st)
            st = lax.fori_loop(0, length // 8, blk, tuple(jnp.zeros((STATE, LANES), jnp.float32) for _ in gs))
            for k, g in enumerate(gs):
                out_ref[s, :, lanes(g)] = st[k]

def scan_back_local(pre, gs, bc, keep, dl, seqs, pins=()):
    rows, channels = pre.shape
    f = jnp.float32
    return pl.pallas_call(
        after(functools.partial(back_local_kernel, seqs), 5, pins),
        out_shape=jax.ShapeDtypeStruct((seqs, STATE, channels), f),
        in_specs=[VM] * 5 + [ANY] * len(pins), out_specs=VM,
        scratch_shapes=[pltpu.VMEM((rows * STATE, 2 * LANES), f), pltpu.VMEM((32 * STATE, 2 * STATE), jnp.bfloat16),
                        pltpu.VMEM((channels // LANES, rows, LANES), f), pltpu.VMEM((channels // LANES, rows, LANES), f)],
        compiler_params=pltpu.CompilerParams(vmem_limit_bytes=60 * 2**20),
        cost_estimate=cost(8),
        name="scan_back_local",
    )(pre, gs, bc, keep, dl, *pins)

def back_kernel(seqs, with_y, pre_ref, act_ref, gs_ref, bc_ref, keep_ref, dl_ref, skip_ref, in_ref, lam_ref,
                gpre_ref, gact_ref, gbc_ref, gdl_ref, *rest):
    if with_y:
        y_ref, *rest = rest
    (wide, pick, dstep, dx, stepc, gsc, states, partq, partr, accb, accc, rowsum) = rest
    rows, channels = pre_ref.shape
    length = rows // seqs
    f = jnp.float32
    spread_states(bc_ref, wide, pick, rows)
    def body(i, _):
        sl = pl.ds(pl.multiple_of(i * 32, 32), 32)
        for g in range(channels // LANES):
            st = softplus(pre_ref[sl, lanes(g)])
            stepc[g, sl, :] = st
            dstep[g, sl, :] = jnp.where(keep_ref[sl, :] > 0.0, st, BIG)
            dx[g, sl, :] = st * act_ref[sl, lanes(g)]
            gsc[g, sl, :] = gs_ref[sl, lanes(g)]
        return 0
    lax.fori_loop(0, rows // 32, body, 0)
    yield
    sets = group_sets(channels, 4)
    for index, gs in enumerate(sets):
        a2 = [-jnp.exp(dl_ref[:, lanes(g)]) * LOG2E for g in gs]
        gdl = [jnp.zeros((STATE, LANES), f) for _ in gs]
        for s in range(seqs):
            for k, g in enumerate(gs):
                states[k, pl.ds(0, STATE), :] = in_ref[s, :, lanes(g)]
            def fwd(i, st):
                st = list(st)
                t0 = pl.multiple_of(s * length + i * 8, 8)
                for j in range(8):
                    at = pl.ds(pl.multiple_of((t0 + j) * STATE, STATE), STATE)
                    b = wide[at, pl.ds(0, LANES)]
                    if with_y:
                        c = wide[at, pl.ds(LANES, LANES)]
                    for k, g in enumerate(gs):
                        d = jnp.exp2(a2[k] * dstep[g, pl.ds(t0 + j, 1), :])
                        st[k] = d * st[k] + b * dx[g, pl.ds(t0 + j, 1), :]
                        states[k, pl.ds(pl.multiple_of((i * 8 + j + 1) * STATE, STATE), STATE), :] = st[k]
                        if with_y:
                            v = st[k] * c
                            partq[k, pl.ds(pl.multiple_of(i * 64 + j * 8, 8), 8), :] = v[:8] + v[8:]
                return tuple(st)
            lax.fori_loop(0, length // 8, fwd, tuple(in_ref[s, :, lanes(g)] for g in gs))
            if with_y:
                def read(i, _):
                    t0 = pl.multiple_of(s * length + i * 8, 8)
                    for k, g in enumerate(gs):
                        acc = partq[k, pl.ds(i * 64, 8, stride=8), :]
                        for m in range(1, 8):
                            acc = acc + partq[k, pl.ds(i * 64 + m, 8, stride=8), :]
                        y_ref[pl.ds(t0, 8), lanes(g)] = acc
                    return 0
                lax.fori_loop(0, length // 8, read, 0)
            yield
            def bwd(i, carry):
                st = list(carry[:len(gs)])
                am = list(carry[len(gs):])
                l0 = (length // 8 - 1 - i) * 8
                t0 = pl.multiple_of(s * length + l0, 8)
                for j in reversed(range(8)):
                    at = pl.ds(pl.multiple_of((t0 + j) * STATE, STATE), STATE)
                    b = wide[at, pl.ds(0, LANES)]
                    c = wide[at, pl.ds(LANES, LANES)]
                    tb = tc = None
                    here = pl.ds(pl.multiple_of((l0 + j) * 8, 8), 8)
                    for k, g in enumerate(gs):
                        row = pl.ds(t0 + j, 1)
                        grow = gsc[g, row, :]
                        d = jnp.exp2(a2[k] * dstep[g, row, :])
                        lam = st[k] + c * grow
                        old = states[k, pl.ds(pl.multiple_of((l0 + j) * STATE, STATE), STATE), :]
                        new = states[k, pl.ds(pl.multiple_of((l0 + j + 1) * STATE, STATE), STATE), :]
                        st[k] = d * lam
                        lp = st[k] * old
                        q = lam * b
                        partq[k, here, :] = q[:8] + q[8:]
                        r = lp * a2[k]
                        partr[k, here, :] = r[:8] + r[8:]
                        am[k] = am[k] + lp * stepc[g, row, :]
                        u = lam * dx[g, row, :]
                        v = new * grow
                        tb = u if tb is None else tb + u
                        tc = v if tc is None else tc + v
                    if index > 0:
                        tb = tb + accb[at, :]
                        tc = tc + accc[at, :]
                    accb[at, :] = tb
                    accc[at, :] = tc
                return tuple(st) + tuple(am)
            out = lax.fori_loop(0, length // 8, bwd, tuple(lam_ref[s, :, lanes(g)] for g in gs) + tuple(gdl))
            gdl = list(out[len(gs):])
            def red(i, _):
                t0 = pl.multiple_of(s * length + i * 8, 8)
                for k, g in enumerate(gs):
                    q = partq[k, pl.ds(i * 64, 8, stride=8), :]
                    r = partr[k, pl.ds(i * 64, 8, stride=8), :]
                    for m in range(1, 8):
                        q = q + partq[k, pl.ds(i * 64 + m, 8, stride=8), :]
                        r = r + partr[k, pl.ds(i * 64 + m, 8, stride=8), :]
                    here = pl.ds(t0, 8)
                    p = pre_ref[here, lanes(g)]
                    gstep = r * LN2 + act_ref[here, lanes(g)] * q
                    gpre_ref[here, lanes(g)] = gstep * (1.0 / (1.0 + jnp.exp(-p)))
                    gact_ref[here, lanes(g)] = stepc[g, here, :] * q + gsc[g, here, :] * skip_ref[:, lanes(g)]
                return 0
            lax.fori_loop(0, length // 8, red, 0)
            yield
        for k, g in enumerate(gs):
            gdl_ref[:, lanes(g)] = gdl[k] * (a2[k] * LN2)
    ones = jnp.ones((LANES, LANES), jnp.bfloat16)
    lane = lax.broadcasted_iota(jnp.int32, (32 * STATE, LANES), 1)
    row = lax.broadcasted_iota(jnp.int32, (32 * STATE, LANES), 0) % STATE
    mb = lane == row
    mc = lane == row + STATE
    def fin(i, _):
        sl = pl.ds(pl.multiple_of(i * 32 * STATE, 32 * STATE), 32 * STATE)
        sb = jnp.dot(accb[sl, :].astype(jnp.bfloat16), ones, preferred_element_type=f)
        sc = jnp.dot(accc[sl, :].astype(jnp.bfloat16), ones, preferred_element_type=f)
        rowsum[...] = jnp.where(mb, sb, jnp.where(mc, sc, 0.0))
        acc = rowsum[pl.ds(0, 32, stride=STATE), :]
        for m in range(1, STATE):
            acc = acc + rowsum[pl.ds(m, 32, stride=STATE), :]
        gbc_ref[pl.ds(pl.multiple_of(i * 32, 32), 32), :] = acc
        return 0
    lax.fori_loop(0, rows // 32, fin, 0)

def scan_back(pre, act, gs, bc, keep, dl, skip, state_in, lam_in, seqs, with_y, plan, places, cid, pins=()):
    rows, channels = pre.shape
    f = jnp.float32
    groups = channels // LANES
    length = rows // seqs
    big = pltpu.VMEM((groups, rows, LANES), f)
    whole = jax.ShapeDtypeStruct((rows, channels), f)
    return play_call(
        functools.partial(back_kernel, seqs, with_y), (9, 4 + with_y, 12), plan, places, cid,
        [whole, whole, jax.ShapeDtypeStruct((rows, LANES), f), jax.ShapeDtypeStruct((STATE, channels), f)] + [whole] * with_y,
        [pltpu.VMEM((rows * STATE, 2 * LANES), f), pltpu.VMEM((32 * STATE, 2 * STATE), jnp.bfloat16),
         big, big, big, big,
         pltpu.VMEM((4, (length + 1) * STATE, LANES), f),
         pltpu.VMEM((4, length * 8, LANES), f), pltpu.VMEM((4, length * 8, LANES), f),
         pltpu.VMEM((rows * STATE, LANES), f), pltpu.VMEM((rows * STATE, LANES), f),
         pltpu.VMEM((32 * STATE, LANES), f)],
        (pre, act, gs, bc, keep, dl, skip, state_in, lam_in), 23 + 3 * with_y, "scan_back", pins,
    )


def greet(peers):
    barrier = pltpu.get_barrier_semaphore()
    for p in peers:
        pl.semaphore_signal(barrier, inc=1, device_id=p, device_id_type=MESH)
    pl.semaphore_wait(barrier, len(peers))

def ch_sum_kernel(n, x_ref, out_ref, mine, slots, send, recv):
    me = lax.axis_index("ch")
    peers = [{"ch": lax.rem(me + d, n)} for d in range(1, n)]
    greet(peers)
    mine[...] = x_ref[...].astype(bf16)
    copies = []
    for d in range(1, n):
        c = pltpu.make_async_remote_copy(src_ref=mine, dst_ref=slots.at[d - 1], send_sem=send.at[d - 1], recv_sem=recv.at[d - 1], device_id=peers[d - 1], device_id_type=MESH)
        c.start()
        copies.append(c)
    total = x_ref[...].astype(bf16).astype(f32)
    for d, c in zip(range(1, n), copies):
        c.wait()
        total = total + slots[d - 1].astype(f32)
    out_ref[...] = total

def ch_sum(x, n, cid, pins=()):
    return pl.pallas_call(
        after(functools.partial(ch_sum_kernel, n), 1, pins),
        out_shape=jax.ShapeDtypeStruct(x.shape, f32), in_specs=[VM] + [ANY] * len(pins), out_specs=VM,
        scratch_shapes=[pltpu.VMEM(x.shape, bf16), pltpu.VMEM((n - 1,) + x.shape, bf16), pltpu.SemaphoreType.DMA((n - 1,)), pltpu.SemaphoreType.DMA((n - 1,))],
        compiler_params=pltpu.CompilerParams(collective_id=cid, has_side_effects=True, vmem_limit_bytes=32 * 2**20), cost_estimate=cost(10), name="ch_sum",
    )(x, *pins)

def reduce_steps(n, parts, gather, more, x_ref, out_ref, s1, sum1, s2, mine, got, fin, sem1, rem1, sem2, rem2, sem3, rem3, sem4, rem4):
    xs = n // 2
    me = lax.axis_index("ch")
    x, core = me // 2, lax.rem(me, 2)
    peer = {"ch": x * 2 + 1 - core}
    others = [lax.rem(x + d, xs) for d in range(1, xs)]
    if more is not None:
        greet([peer] + [{"ch": o * 2 + core} for o in others] + more)
    rows, width = x_ref.shape[0] // parts, x_ref.shape[1] // n
    def cols(block):
        return pl.ds(pl.multiple_of(block * width, width), width)
    def stage1(p, k):
        return pltpu.make_async_remote_copy(src_ref=x_ref.at[pl.ds(p * rows, rows), cols(k * 2 + 1 - core)], dst_ref=s1.at[p, k], send_sem=sem1.at[p, k], recv_sem=rem1.at[p, k], device_id=peer, device_id_type=MESH)
    def stage2(p, d):
        o = others[d]
        return pltpu.make_async_remote_copy(src_ref=sum1.at[p, o], dst_ref=s2.at[p, d], send_sem=sem2.at[p, d], recv_sem=rem2.at[p, d], device_id={"ch": o * 2 + core}, device_id_type=MESH)
    def stage3(p, d):
        o = others[d]
        return pltpu.make_async_remote_copy(src_ref=mine.at[p], dst_ref=got.at[p, d], send_sem=sem3.at[p, d], recv_sem=rem3.at[p, d], device_id={"ch": o * 2 + core}, device_id_type=MESH)
    for p in range(parts):
        for k in range(xs):
            stage1(p, k).start()
    yield
    for p in range(parts):
        for k in range(xs):
            stage1(p, k).wait_recv()
            sum1[p, k] = (x_ref[pl.ds(p * rows, rows), cols(k * 2 + core)].astype(f32) + s1[p, k].astype(f32)).astype(bf16)
        for d in range(xs - 1):
            stage2(p, d).start()
    yield
    for p in range(parts):
        total = sum1[p, x].astype(f32)
        for d in range(xs - 1):
            stage2(p, d).wait_recv()
            total = total + s2[p, d].astype(f32)
        if gather:
            mine[p] = total.astype(bf16)
            for d in range(xs - 1):
                stage3(p, d).start()
        else:
            out_ref[pl.ds(p * rows, rows), :] = total
    yield
    if gather:
        def stage4(p, d):
            src = mine.at[p] if d < 0 else got.at[p, d]
            return pltpu.make_async_remote_copy(src_ref=src, dst_ref=fin.at[p, d + 1], send_sem=sem4.at[p, d + 1], recv_sem=rem4.at[p, d + 1], device_id=peer, device_id_type=MESH)
        def chip(d):
            return lax.rem(x + xs - 1 - d, xs)
        for p in range(parts):
            stage4(p, -1).start()
            out_ref[pl.ds(p * rows, rows), cols(me)] = mine[p].astype(out_ref.dtype)
            for d in range(xs - 1):
                stage3(p, d).wait_recv()
                stage4(p, d).start()
                out_ref[pl.ds(p * rows, rows), cols(chip(d) * 2 + core)] = got[p, d].astype(out_ref.dtype)
        yield
        for p in range(parts):
            for d in range(-1, xs - 1):
                stage4(p, d).wait_recv()
                out_ref[pl.ds(p * rows, rows), cols(chip(d) * 2 + 1 - core)] = fin[p, d + 1].astype(out_ref.dtype)
    for p in range(parts):
        for k in range(xs):
            stage1(p, k).wait_send()
        for d in range(xs - 1):
            stage2(p, d).wait_send()
            if gather:
                stage3(p, d).wait_send()
        if gather:
            for d in range(-1, xs - 1):
                stage4(p, d).wait_send()
    yield


class ColumnsLine:
    semaphores = 6

    @staticmethod
    def result(v, zs, ys):
        return jax.ShapeDtypeStruct((zs * v.shape[0], v.shape[1] // zs), v.dtype)

    @staticmethod
    def specs(v, zs, ys):
        sem = pltpu.SemaphoreType.DMA
        xs = lax.axis_size("ch") // 2
        return [sem((zs - 1,))] * 2 + [sem((zs - 1, xs - 1))] * 2 + [sem((zs - 1, xs))] * 2

    def __init__(self, zs, ys, src, out, sems):
        seq, ch = lax.axis_index("seq"), lax.axis_index("ch")
        self.nch = lax.axis_size("ch")
        self.xs = self.nch // 2
        self.zs, self.ys, self.z, self.y, self.ch = zs, ys, seq // ys, lax.rem(seq, ys), ch
        self.x, self.core = ch // 2, lax.rem(ch, 2)
        self.src, self.out, self.sems = src, out, sems
        self.rows, self.width = src.shape[0], src.shape[1] // zs
        self.part = self.rows // self.nch

    def cols(self, z):
        return pl.ds(pl.multiple_of(z * self.width, self.width), self.width)

    def share(self, z, ch):
        return pl.ds(pl.multiple_of(z * self.rows + ch * self.part, self.part), self.part)

    def remote(self, k, at, src, dst, to):
        send, recv = self.sems[2 * k : 2 * k + 2]
        return pltpu.make_async_remote_copy(src_ref=src, dst_ref=dst, send_sem=send.at[at], recv_sem=recv.at[at], device_id=to, device_id_type=MESH)

    def along(self, d):
        to = lax.rem(self.z + d, self.zs)
        src = self.src.at[pl.ds(pl.multiple_of(self.ch * self.part, self.part), self.part), self.cols(to)]
        return self.remote(0, d - 1, src, self.out.at[self.share(self.z, self.ch)], {"seq": to * self.ys + self.y})

    def from_z(self, d):
        return lax.rem(self.z + self.zs - d, self.zs)

    def over(self, d, e):
        rows = self.out.at[self.share(self.from_z(d), self.ch)]
        return self.remote(1, (d - 1, e - 1), rows, rows, {"ch": lax.rem(self.x + e, self.xs) * 2 + self.core})

    def across(self, d, e):
        rows = self.out.at[self.share(self.from_z(d), lax.rem(self.x + self.xs - e, self.xs) * 2 + self.core)]
        return self.remote(2, (d - 1, e), rows, rows, {"ch": self.x * 2 + 1 - self.core})

    def lags(self):
        return range(1, self.zs)

    def begin(self):
        for d in self.lags():
            self.along(d).start()
        here = pl.ds(pl.multiple_of(self.z * self.rows, self.rows), self.rows)
        self.out[here, :] = self.src[:, self.cols(self.z)]

    def step(self, index):
        for d in self.lags():
            if index == 0:
                self.along(d).wait_recv()
                for e in range(1, self.xs):
                    self.over(d, e).start()
                self.across(d, 0).start()
            else:
                for e in range(1, self.xs):
                    self.over(d, e).wait_recv()
                    self.across(d, e).start()

    def finish(self):
        for d in self.lags():
            for e in range(self.xs):
                self.across(d, e).wait_recv()
        for d in self.lags():
            self.along(d).wait_send()
            for e in range(1, self.xs):
                self.over(d, e).wait_send()
            for e in range(self.xs):
                self.across(d, e).wait_send()


def reduce_kernel(n, parts, gather, *refs):
    for _ in reduce_steps(n, parts, gather, [], *refs):
        pass


def reduce_scratch_shapes(shape, n, parts):
    rows, width = shape
    xs, r, w = n // 2, rows // parts, width // n
    sem = pltpu.SemaphoreType.DMA
    return [
        pltpu.VMEM((parts, xs, r, w), bf16), pltpu.VMEM((parts, xs, r, w), bf16), pltpu.VMEM((parts, xs - 1, r, w), bf16),
        pltpu.VMEM((parts, r, w), bf16), pltpu.VMEM((parts, xs - 1, r, w), bf16), pltpu.VMEM((parts, xs, r, w), bf16),
        sem((parts, xs)), sem((parts, xs)), sem((parts, xs - 1)), sem((parts, xs - 1)),
        sem((parts, xs - 1)), sem((parts, xs - 1)), sem((parts, xs)), sem((parts, xs)),
    ]


def ch_reduce(x, n, cid, gather, parts=2):
    rows, width = x.shape
    return pl.pallas_call(
        functools.partial(reduce_kernel, n, parts, gather),
        out_shape=jax.ShapeDtypeStruct((rows, width if gather else width // n), f32),
        in_specs=[VM], out_specs=VM,
        scratch_shapes=reduce_scratch_shapes(x.shape, n, parts),
        compiler_params=pltpu.CompilerParams(collective_id=cid, has_side_effects=True, vmem_limit_bytes=48 * 2**20),
        cost_estimate=cost(18), name="ch_reduce",
    )(x)


def carry_kernel(n, fwd, rev, count, places, layer, *refs):
    refs = list(refs)
    tot_ref, dl_ref = refs.pop(0), refs.pop(0)
    k = fwd + rev
    ends = [refs.pop(0) for _ in range(k)]
    parts = [refs.pop(0) for _ in range(count)]
    whole = refs.pop(0) if layer is not None else None
    outs = [refs.pop(0) for _ in range(k)]
    sums = [refs.pop(0) for _ in range(count)]
    if layer is not None:
        local = pltpu.make_async_copy(whole.at[layer], refs.pop(0), refs.pop(-1))
        local.start()
    mine, slots, tots, send, recv, tsend, trecv = refs[:7]
    jobs = [PartSum(*places, parts[j], sums[j], refs[7 + 3 * j : 10 + 3 * j]) for j in range(count)]
    me = lax.axis_index("seq")
    seqs = tot_ref.shape[0]
    greet([{"seq": lax.rem(me + d, n)} for d in range(1, n)])
    a2 = -jnp.exp(dl_ref[...]) * LOG2E
    directions = [False] * fwd + [True] * rev
    def copies(i, d):
        away = -d if directions[i] else d
        to = {"seq": lax.rem(me + away + n, n)}
        return (
            pltpu.make_async_remote_copy(src_ref=mine.at[i], dst_ref=slots.at[i, d - 1], send_sem=send.at[i, d - 1], recv_sem=recv.at[i, d - 1], device_id=to, device_id_type=MESH),
            pltpu.make_async_remote_copy(src_ref=tot_ref, dst_ref=tots.at[i, d - 1], send_sem=tsend.at[i, d - 1], recv_sem=trecv.at[i, d - 1], device_id=to, device_id_type=MESH),
        )
    for i in range(k):
        mine[i] = ends[i][...].astype(bf16)
        outs[i][...] = jnp.zeros_like(outs[i])
    for d in reversed(range(1, n)):
        for i in range(k):
            place = n - 1 - me if directions[i] else me
            @pl.when(place + d < n)
            def _():
                for c in copies(i, d):
                    c.start()
    for job in jobs:
        job.begin()
    for d in reversed(range(1, n)):
        for i in range(k):
            place = n - 1 - me if directions[i] else me
            @pl.when(place >= d)
            def _():
                for c in copies(i, d):
                    c.wait_recv()
                for s in range(seqs):
                    gain = jnp.exp2(a2 * tots[i, d - 1, pl.ds(s, 1), :])
                    outs[i][s] = gain * outs[i][s] + slots[i, d - 1, s].astype(f32)
    for d in reversed(range(1, n)):
        for i in range(k):
            place = n - 1 - me if directions[i] else me
            @pl.when(place + d < n)
            def _():
                for c in copies(i, d):
                    c.wait_send()
    for job in jobs:
        job.finish()
    if layer is not None:
        local.wait()


def carry_over(tot, dl, ends, n, cid, fwd, rev, ps=(), places=(), taken=None):
    whole, layer = (None, None) if taken is None else taken
    extra = [] if taken is None else [whole]
    k = len(ends)
    sem = pltpu.SemaphoreType.DMA
    return pl.pallas_call(
        functools.partial(carry_kernel, n, int(fwd), int(rev), len(ps), places, layer),
        out_shape=[jax.ShapeDtypeStruct(ends[0].shape, f32)] * k + [PartSum.result(p, *places) for p in ps]
        + [jax.ShapeDtypeStruct(w.shape[1:], w.dtype) for w in extra],
        in_specs=[VM] * (k + 2 + len(ps)) + [ANY] * len(extra), out_specs=[VM] * (k + len(ps)) + [pl.BlockSpec(memory_space=pltpu.HBM)] * len(extra),
        scratch_shapes=[pltpu.VMEM((k,) + ends[0].shape, bf16), pltpu.VMEM((k, n - 1) + ends[0].shape, bf16), pltpu.VMEM((k, n - 1) + tot.shape, f32),
                        sem((k, n - 1)), sem((k, n - 1)), sem((k, n - 1)), sem((k, n - 1))]
        + [spec for p in ps for spec in PartSum.specs(p, *places)]
        + [pltpu.SemaphoreType.DMA] * len(extra),
        compiler_params=pltpu.CompilerParams(collective_id=cid, has_side_effects=True, vmem_limit_bytes=32 * 2**20), cost_estimate=cost(19), name="carry_over",
    )(tot, dl, *ends, *ps, *extra)


def seq_at(z, y, ys):
    return {"seq": z * ys + y}


class GatherLine:
    semaphores = 2

    @staticmethod
    def result(v, zs, ys):
        return jax.ShapeDtypeStruct((zs * v.shape[0], v.shape[1]), v.dtype)

    @staticmethod
    def specs(v, zs, ys):
        return [pltpu.SemaphoreType.DMA((2, zs - 1))] * 2


    def __init__(self, zs, ys, src, out, sems):
        me = lax.axis_index("seq")
        self.zs, self.ys, self.z, self.y = zs, ys, me // ys, lax.rem(me, ys)
        self.src, self.out = src, out
        self.send, self.recv = sems
        self.rows = src.shape[0]

    def block(self, z):
        return self.out.at[pl.ds(pl.multiple_of(z * self.rows, self.rows), self.rows)]

    def copy(self, way, r):
        z = self.z
        to, b = (lax.rem(z + 1, self.zs), z - r) if way == 0 else (lax.rem(z + self.zs - 1, self.zs), z + r)
        b = lax.rem(b + self.zs, self.zs)
        return pltpu.make_async_remote_copy(
            src_ref=self.src if r == 0 else self.block(b),
            dst_ref=self.block(b),
            send_sem=self.send.at[way, r],
            recv_sem=self.recv.at[way, r],
            device_id=seq_at(to, self.y, self.ys),
            device_id_type=MESH,
        )

    def sends(self, way, r):
        z, last = self.z, self.zs - 1
        return jnp.logical_and(z < last, z >= r) if way == 0 else jnp.logical_and(z > 0, z + r <= last)

    def receives(self, way, r):
        z, last = self.z, self.zs - 1
        return z - 1 - r >= 0 if way == 0 else z + 1 + r <= last

    def begin(self):
        self.start(0)
        self.block(self.z)[...] = self.src[...]

    def step(self, index):
        self.start(index + 1)

    def start(self, r):
        for way in (0, 1):
            if r > 0:
                self.arrive(way, r - 1)
            @pl.when(self.sends(way, r))
            def _():
                self.copy(way, r).start()

    def arrive(self, way, r):
        @pl.when(self.receives(way, r))
        def _():
            self.copy(way, r).wait_recv()

    def finish(self):
        self.arrived()
        self.sent()

    def arrived(self):
        for way in (0, 1):
            self.arrive(way, self.zs - 2)

    def sent(self):
        for way in (0, 1):
            for r in range(self.zs - 1):
                @pl.when(self.sends(way, r))
                def _():
                    self.copy(way, r).wait_send()


class SumAll:
    def __init__(self, zs, ys, src, out, scratch):
        me = lax.axis_index("seq")
        self.zs, self.ys, self.z, self.y = zs, ys, me // ys, lax.rem(me, ys)
        self.src, self.out = src, out
        self.yslots, self.ysum, self.slots, self.running, self.acc = scratch[:5]
        self.y1sems, self.zsems, self.y2sems, gather = scratch[5:7], scratch[7:9], scratch[9:11], scratch[11:13]
        self.part = src.shape[0] // ys
        self.share = self.part // zs
        self.back = GatherLine(zs, ys, self.mine(self.z), out, gather)
        self.back.block = self.mine

    @staticmethod
    def specs(height, w, zs, ys):
        part = height // ys
        share = part // zs
        sem = pltpu.SemaphoreType.DMA
        return [
            pltpu.VMEM((ys - 1, part, w), bf16),
            pltpu.VMEM((part, w), bf16),
            pltpu.VMEM((2, zs, share, w), bf16),
            pltpu.VMEM((2, zs, share, w), bf16),
            pltpu.VMEM((share, w), f32),
            sem((ys - 1,)), sem((ys - 1,)), sem((2, zs)), sem((2, zs)), sem(((ys - 1) * zs,)), sem(((ys - 1) * zs,)),
            sem((2, zs - 1)), sem((2, zs - 1)),
        ]

    def rows(self, index, size):
        return pl.ds(pl.multiple_of(index * size, size), size)

    def mine(self, z):
        return self.out.at[self.rows(self.y * self.zs + z, self.share)]

    def y1(self, d):
        to = lax.rem(self.y + d, self.ys)
        return pltpu.make_async_remote_copy(src_ref=self.src.at[self.rows(to, self.part)], dst_ref=self.yslots.at[d - 1], send_sem=self.y1sems[0].at[d - 1], recv_sem=self.y1sems[1].at[d - 1], device_id=seq_at(self.z, to, self.ys), device_id_type=MESH)

    def run(self, way, k):
        to = lax.rem(self.z + (1 if way == 0 else self.zs - 1), self.zs)
        return pltpu.make_async_remote_copy(src_ref=self.running.at[way, k], dst_ref=self.slots.at[way, k], send_sem=self.zsems[0].at[way, k], recv_sem=self.zsems[1].at[way, k], device_id=seq_at(to, self.y, self.ys), device_id_type=MESH)

    def y2(self, d, b):
        to = lax.rem(self.y + d, self.ys)
        at = (d - 1) * self.zs + b
        return pltpu.make_async_remote_copy(src_ref=self.mine(b), dst_ref=self.mine(b), send_sem=self.y2sems[0].at[at], recv_sem=self.y2sems[1].at[at], device_id=seq_at(self.z, to, self.ys), device_id_type=MESH)

    def begin(self):
        for d in range(1, self.ys):
            self.y1(d).start()

    def middle(self):
        total = self.src[self.rows(self.y, self.part), :].astype(f32)
        for d in range(1, self.ys):
            self.y1(d).wait_recv()
            total = total + self.yslots[d - 1].astype(f32)
        self.ysum[...] = total.astype(bf16)

    def line_sum(self, r):
        for way in (0, 1):
            k = self.zs - 1 - r if way == 0 else r
            z, first = self.z, 0 if way == 0 else self.zs - 1
            own = pl.ds(k * self.share, self.share)
            @pl.when(z == first)
            def _():
                self.running[way, k] = self.ysum[own, :]
                self.run(way, k).start()
            inside = jnp.logical_and(z > 0, z < k) if way == 0 else jnp.logical_and(z < self.zs - 1, z > k)
            @pl.when(inside)
            def _():
                self.run(way, k).wait_recv()
                self.running[way, k] = (self.ysum[own, :].astype(f32) + self.slots[way, k].astype(f32)).astype(bf16)
                self.run(way, k).start()

    def turn(self):
        self.acc[...] = self.ysum[self.rows(self.z, self.share), :].astype(f32)
        for way in (0, 1):
            @pl.when(self.z > 0 if way == 0 else self.z < self.zs - 1)
            def _():
                self.run(way, self.z).wait_recv()
                self.acc[...] = self.acc[...] + self.slots[way, self.z].astype(f32)
        self.mine(self.z)[...] = self.acc[...].astype(bf16)
        self.back.start(0)
        for d in range(1, self.ys):
            self.y2(d, self.z).start()

    def spread(self, r):
        if r < self.zs - 2:
            self.back.start(r + 1)
        else:
            for way in (0, 1):
                self.back.arrive(way, r)
        for way in (0, 1):
            b = self.z - 1 - r if way == 0 else self.z + 1 + r
            b = lax.rem(b + self.zs, self.zs)
            @pl.when(self.back.receives(way, r))
            def _():
                for d in range(1, self.ys):
                    self.y2(d, b).start()

    def finish(self):
        for d in range(1, self.ys):
            for b in range(self.zs):
                self.y2(d, b).wait_recv()
        for d in range(1, self.ys):
            self.y1(d).wait_send()
            for b in range(self.zs):
                self.y2(d, b).wait_send()
        for k in range(self.zs):
            @pl.when(self.z < k)
            def _():
                self.run(0, k).wait_send()
            @pl.when(self.z > k)
            def _():
                self.run(1, k).wait_send()
        self.back.sent()


class PartSum:
    semaphores = 3

    @staticmethod
    def result(v, zs, ys):
        return jax.ShapeDtypeStruct(v.shape[1:], f32)

    @staticmethod
    def specs(v, zs, ys):
        sem = pltpu.SemaphoreType.DMA((ys - 1,))
        return [sem, sem, pltpu.VMEM((ys - 1,) + v.shape[1:], v.dtype)]


    def __init__(self, zs, ys, src, out, scratch):
        me = lax.axis_index("seq")
        self.ys, self.z, self.y = ys, me // ys, lax.rem(me, ys)
        self.src, self.out = src, out
        self.send, self.recv, self.slots = scratch

    def copy(self, d):
        to = lax.rem(self.y + d, self.ys)
        return pltpu.make_async_remote_copy(
            src_ref=self.src.at[to],
            dst_ref=self.slots.at[d - 1],
            send_sem=self.send.at[d - 1],
            recv_sem=self.recv.at[d - 1],
            device_id=seq_at(self.z, to, self.ys),
            device_id_type=MESH,
        )

    def begin(self):
        for d in range(1, self.ys):
            self.copy(d).start()

    def finish(self):
        mine = self.src[self.y].astype(f32)
        for d in range(1, self.ys):
            self.copy(d).wait_recv()
            mine = mine + self.slots[d - 1].astype(f32)
        self.out[...] = mine
        for d in range(1, self.ys):
            self.copy(d).wait_send()


def closing_kernel(n, nseq, zs, ys, parts, count, pieces, x_ref, b_ref, v_ref, cols_ref, h_ref, *refs):
    refs = list(refs)

    def take(k):
        head, refs[:] = refs[:k], refs[k:]
        return head

    piece_refs, p_refs = take(pieces), take(count)
    out_ref, branch_ref, sum_ref, values_ref, norm_ref = take(5)
    part_refs = take(count)
    s_ref, all_ref, mine_ref, mine_slots, t_ref, tslots = take(6)
    reduce_scratch, more_scratch, gather_sems, sum_scratch = take(14), take(14), take(2), take(13)
    part_scratch, (msend, mrecv, tsend, trecv) = take(3 * count), take(4)
    seq = lax.axis_index("seq")
    z = seq // ys
    line = GatherLine(zs, ys, v_ref, all_ref, gather_sems)
    total = SumAll(zs, ys, s_ref, sum_ref, sum_scratch)
    sums = [PartSum(zs, ys, p_refs[k], part_refs[k], part_scratch[3 * k : 3 * k + 3]) for k in range(count)]
    late = PartSum(zs, ys, mine_ref, values_ref, [msend, mrecv, mine_slots])
    steps = reduce_steps(n, parts, False, [{"seq": lax.rem(seq + d, nseq)} for d in range(1, nseq)], x_ref, out_ref, *reduce_scratch)
    more_steps = reduce_steps(n, parts, False, None, b_ref, branch_ref, *more_scratch)

    def tiny(d):
        return pltpu.make_async_remote_copy(src_ref=t_ref, dst_ref=tslots.at[seq], send_sem=tsend.at[d - 1], recv_sem=trecv.at[d - 1], device_id={"seq": lax.rem(seq + d, nseq)}, device_id_type=MESH)

    next(steps)
    next(more_steps)
    line.begin()
    offset = 0
    for piece in piece_refs:
        s_ref[pl.ds(offset, piece.shape[0]), :] = piece[...].astype(bf16)
        offset += piece.shape[0]
    if offset < s_ref.shape[0]:
        s_ref[pl.ds(offset, s_ref.shape[0] - offset), :] = jnp.zeros((s_ref.shape[0] - offset, s_ref.shape[1]), bf16)
    total.begin()
    next(steps)
    next(more_steps)
    line.start(1)
    total.middle()
    total.line_sum(0)
    for part in sums:
        part.begin()
    for _ in steps:
        pass
    w = h_ref.shape[1]
    row = jnp.sum(out_ref[:, pl.ds(0, w)] * h_ref[...], axis=0, keepdims=True)
    t_ref[...] = jnp.broadcast_to(row, t_ref.shape).astype(bf16)
    tslots[seq] = t_ref[...]
    for d in range(1, nseq):
        tiny(d).start()
    total.line_sum(1)
    for r in range(2, zs - 1):
        line.start(r)
        total.line_sum(r)
    total.turn()
    for _ in more_steps:
        pass
    line.arrived()
    fold = mine_ref.shape[1]
    for k in range(ys):
        def chunk(i, _):
            at = pl.ds(pl.multiple_of(i * 256, 256), 256)
            got = jnp.dot(cols_ref[pl.ds(k * fold, fold), :], all_ref[:, at], preferred_element_type=f32)
            mine_ref[k, :, at] = got.astype(bf16)
            return 0
        lax.fori_loop(0, all_ref.shape[1] // 256, chunk, 0)
    late.begin()
    for r in range(zs - 1):
        total.spread(r)
    for part in sums:
        part.finish()
    for d in range(1, nseq):
        tiny(d).wait_recv()
    norm = tslots[0].astype(f32)
    for k in range(1, nseq):
        norm = norm + tslots[k].astype(f32)
    norm_ref[...] = norm
    late.finish()
    total.finish()
    line.sent()
    for d in range(1, nseq):
        tiny(d).wait_send()


def closing(x, branch, v, cols, h, pieces, ps, n, nseq, zs, ys, cid, parts=2):
    rows, width = x.shape
    sem = pltpu.SemaphoreType.DMA
    height = sum(piece.shape[0] for piece in pieces)
    height += -height % (16 * ys * zs)
    w = v.shape[1]
    fold = cols.shape[0] // ys
    count = len(ps)
    tiny = (16, h.shape[1])
    return pl.pallas_call(
        functools.partial(closing_kernel, n, nseq, zs, ys, parts, count, len(pieces)),
        out_shape=[
            jax.ShapeDtypeStruct((rows, width // n), f32),
            jax.ShapeDtypeStruct((rows, branch.shape[1] // n), f32),
            jax.ShapeDtypeStruct((height, w), bf16),
            jax.ShapeDtypeStruct((fold, w), f32),
            jax.ShapeDtypeStruct(tiny, f32),
        ]
        + [PartSum.result(p, zs, ys) for p in ps],
        in_specs=[VM] * (5 + len(pieces) + count),
        out_specs=[VM] * (5 + count),
        scratch_shapes=[
            pltpu.VMEM((height, w), bf16),
            pltpu.VMEM((zs * v.shape[0], w), bf16),
            pltpu.VMEM((ys, fold, w), bf16),
            pltpu.VMEM((ys - 1, fold, w), bf16),
            pltpu.VMEM(tiny, bf16),
            pltpu.VMEM((nseq,) + tiny, bf16),
        ]
        + reduce_scratch_shapes(x.shape, n, parts)
        + reduce_scratch_shapes(branch.shape, n, parts)
        + GatherLine.specs(v, zs, ys)
        + SumAll.specs(height, w, zs, ys)
        + [spec for p in ps for spec in PartSum.specs(p, zs, ys)]
        + [sem((ys - 1,)), sem((ys - 1,)), sem((nseq - 1,)), sem((nseq - 1,))],
        compiler_params=pltpu.CompilerParams(collective_id=cid, has_side_effects=True, vmem_limit_bytes=60 * 2**20),
        cost_estimate=cost(70),
        name="closing",
    )(x, branch, v, cols, h, *pieces, *ps)


def passed_along(block, axis, distance):
    devices = range(lax.axis_size(axis))
    route = [(i - distance, i) for i in devices if i - distance in devices]
    return lax.ppermute(block, axis, route)


def silu_slope(argument):
    logistic = jax.nn.sigmoid(argument)
    return logistic * (1.0 + argument * (1.0 - logistic))


def conv_local(extended, weights, biases, seg_ext):
    length_now = extended.shape[1] - (KERN - 1)
    seg_now = seg_ext[:, KERN - 1 :]
    summed = biases + jnp.zeros((extended.shape[0], length_now, extended.shape[2]), f32)
    for lag_index in range(KERN):
        same_doc = (seg_ext[:, lag_index : lag_index + length_now] == seg_now).astype(f32)
        summed = (
            summed
            + weights[lag_index]
            * extended[:, lag_index : lag_index + length_now]
            * same_doc[:, :, None]
        )
    return summed


def dot(a, b, contract):
    return lax.dot_general(a, b, ((contract[:1], contract[1:]), ((), ())), preferred_element_type=f32)


def lines(zs, ys):
    return [[z * ys + y for z in range(zs)] for y in range(ys)]


def tokens_of_line(rows, zs, ys):
    return lax.all_gather(rows, "seq", axis_index_groups=lines(zs, ys), tiled=True)


def local(
    hidden_in,
    segments,
    cotangent,
    norm_gain,
    input_projection_weight,
    conv_weight,
    conv_bias,
    proj_weight,
    step_weight,
    step_bias,
    decay_log,
    skip_gain,
    output_projection_weight,
):
    seqs, length, width = hidden_in.shape
    rows = seqs * length
    nch, nseq = lax.axis_size("ch"), lax.axis_size("seq")
    channels = conv_bias.shape[-1]
    share = width // nch
    share_start = lax.axis_index("ch") * share
    seg_own = segments.astype(f32)
    seg_ext = None
    hidden = hidden_in.astype(f32).reshape(rows, width)
    grad_rows = cotangent.astype(f32).reshape(rows, width)
    ids = iter(range(100))
    zs = 4 if nseq % 4 == 0 else nseq
    ys = nseq // zs
    fold = width // nseq
    places = (zs, ys)

    out_cols, w_copy = {}, {}
    stored = []
    out_low = grad_rows.astype(bf16)
    grad_mixed = dot(out_low, output_projection_weight[LAYERS - 1], (1, 1))
    grad_mixed_line = tokens_of_line(grad_mixed.astype(bf16), zs, ys)
    for layer in range(LAYERS):
        last = layer == LAYERS - 1
        inv_rms = lax.rsqrt(jnp.mean(hidden * hidden, axis=-1, keepdims=True) + epsilon)
        normed = (hidden * inv_rms * norm_gain[layer]).astype(bf16)
        w_in = w_copy[1] if layer > 0 else input_projection_weight[0]
        both = lax.dot_general(normed, w_in, (((1,), (0,)), ((), ())), preferred_element_type=f32)
        values, gate_pre = both[:, 0], both[:, 1]
        values3 = values.reshape(seqs, length, channels)
        edge = values3[:, -(KERN - 1) :]
        if seg_ext is None:
            ids_edge = jnp.broadcast_to(seg_own[:, -(KERN - 1) :, None], (seqs, KERN - 1, LANES))
            edge = passed_along(jnp.concatenate([edge, ids_edge], axis=2), "seq", 1)
            seg_ext = jnp.concatenate([edge[:, :, channels], seg_own], axis=1)
            keep = (seg_ext[:, KERN - 2 : -1] == seg_own).astype(f32).reshape(-1, 1)
            edge = edge[:, :, :channels]
        else:
            edge = passed_along(edge, "seq", 1)
        extended = jnp.concatenate([edge, values3], axis=1)
        conv_out, conv_pull = jax.vjp(
            functools.partial(conv_local, seg_ext=seg_ext), extended, conv_weight[layer], conv_bias[layer]
        )
        conv_out = conv_out.reshape(rows, channels)
        activated = jax.nn.silu(conv_out)
        act_low = activated.astype(bf16)
        proj_out = ch_sum(dot(act_low, proj_weight[layer], (1, 0)), nch, next(ids))
        rank_low = proj_out[:, :RANK].astype(bf16)
        mats = proj_out[:, RANK:]
        step_pre = dot(rank_low, step_weight[layer], (1, 0)) + step_bias[layer]
        rates = decay_log[layer]
        end_state, total = scan_local(step_pre, activated, mats, keep, rates, seqs, [], places, 0)
        gate_act = jax.nn.silu(gate_pre)
        if last:
            gate_line = tokens_of_line(gate_pre.astype(bf16), zs, ys)
            grad_scan = grad_mixed * gate_act
            start = scan_back_local(step_pre, grad_scan, mats, keep, rates, seqs)
            state_in, lam_in, w_copy[0] = carry_over(
                total, rates, [end_state, start], nseq, next(ids), True, True, taken=(input_projection_weight, 0)
            )
        else:
            state_in, w_copy[1] = carry_over(
                total, rates, [end_state], nseq, next(ids), True, False, taken=(input_projection_weight, 1)
            )
        keeping = (hidden, inv_rms, normed, gate_pre, gate_act, conv_out, activated, act_low, conv_pull, rank_low,
                   step_pre, mats, total, state_in)
        if last:
            stored.append(keeping)
            break
        (y,) = scan_forward(
            step_pre, activated, mats, keep, rates, state_in, seqs, [], places, 0, (grad_mixed_line,)
        )
        scanned = y + skip_gain[layer] * activated
        mixed = (scanned * gate_act).astype(bf16)
        out_part = dot(mixed, output_projection_weight[layer], (1, 0)).astype(bf16)
        mixed_all = tokens_of_line(mixed, zs, ys)
        branch = ch_reduce(out_part, nch, next(ids), True)
        hidden = hidden + branch
        stored.append(keeping + (scanned, mixed_all))

    for layer in reversed(range(LAYERS)):
        last = layer == LAYERS - 1
        (hidden, inv_rms, normed, gate_pre, gate_act, conv_out, activated, act_low, conv_pull, rank_low,
         step_pre, mats, total, state_in) = stored[layer][:14]
        rates = decay_log[layer]
        if not last:
            scanned, mixed_all = stored[layer][14:]
            normed_cols = early_cols
            out_low = grad_rows.astype(bf16)
            grad_mixed = dot(out_low, output_projection_weight[layer], (1, 1))
            grad_scan = grad_mixed * gate_act
            grad_gate = (grad_mixed * scanned * silu_slope(gate_pre)).astype(bf16)
            start = scan_back_local(step_pre, grad_scan, mats, keep, rates, seqs)
            gate_all = tokens_of_line(grad_gate, zs, ys)
            lam_in, grad_out_last = carry_over(
                total, rates, [start], nseq, next(ids), False, True, [out_parts_last], places
            )
        grad_skip = jnp.sum(grad_scan * activated, axis=0)
        if last:
            plan = [
                (ColumnsLine, (3, 5), normed),
                (ColumnsLine, (4, 6), out_low),
                (ColumnsLine, (6, 8), stored[0][2]),
            ]
        else:
            plan = [
                (ColumnsLine, (2, 4), out_low),
                (PartSum, (), values_parts_last),
                (PartSum, (), gate_parts_last),
            ]
        grad_pre, grad_act, grad_mats, grad_decay, *others = scan_back(
            step_pre, activated, grad_scan, mats, keep, rates, skip_gain[layer][None], state_in, lam_in, seqs, int(last),
            plan, places, next(ids), (),
        )
        if last:
            y, normed_cols, out_cols[layer], early_cols = others
            scanned = y + skip_gain[layer] * activated
            mixed = (scanned * gate_act).astype(bf16)
            grad_gate = (grad_mixed * scanned * silu_slope(gate_pre)).astype(bf16)
            scanned_line = tokens_of_line(scanned.astype(bf16), zs, ys).astype(f32)
        else:
            out_cols[layer], grad_values_last, grad_gate_last = others
        grad_step_bias = jnp.sum(grad_pre, axis=0)
        pre_low = grad_pre.astype(bf16)
        grad_step_weight = dot(rank_low, pre_low, (0, 0))
        rank_part = dot(pre_low, step_weight[layer], (1, 1))
        grad_proj = ch_sum(
            jnp.concatenate([rank_part, grad_mats[:, : 2 * STATE]], axis=-1), nch, next(ids),
            (gate_line,) if last else (),
        ).astype(bf16)
        grad_proj_weight = dot(grad_proj, act_low, (0, 0))
        grad_act = grad_act + dot(grad_proj, proj_weight[layer], (1, 1))
        grad_conv = (grad_act * silu_slope(conv_out)).reshape(seqs, length, channels)
        grad_ext, grad_conv_weight, grad_conv_bias = conv_pull(grad_conv)
        returned = passed_along(grad_ext[:, : KERN - 1], "seq", -1)
        grad_values = grad_ext[:, KERN - 1 :]
        grad_values = jnp.concatenate(
            [grad_values[:, : -(KERN - 1)], grad_values[:, -(KERN - 1) :] + returned], axis=1
        ).reshape(rows, channels).astype(bf16)
        w_in = w_copy[layer]
        grad_both = jnp.stack([grad_values, grad_gate], axis=1)
        grad_part = lax.dot_general(grad_both, w_in, (((1, 2), (1, 2)), ((), ())), preferred_element_type=f32)
        scale_now = norm_gain[layer]
        misc = jnp.concatenate([grad_conv_weight, grad_conv_bias[None], grad_step_bias[None], grad_skip[None]], axis=0)
        small = [grad_proj_weight, grad_step_weight, grad_decay, misc]
        if last:
            values_last = tokens_of_line(grad_values, zs, ys)
            values_parts_last = dot(normed_cols, values_last, (0, 0)).astype(bf16).reshape(ys, fold, channels)
            grad_normed = ch_reduce(grad_part.astype(bf16), nch, next(ids), True)
            scanned_line = scanned_line + 0.0 * grad_normed[0, 0]
            gates = gate_line.astype(f32)
            mixed_all = (scanned_line * jax.nn.silu(gates)).astype(bf16)
            gate_all = (grad_mixed_line.astype(f32) * scanned_line * silu_slope(gates)).astype(bf16)
            out_part = dot(mixed, output_projection_weight[layer], (1, 0)).astype(bf16)
            hidden_last = lax.dynamic_slice_in_dim(hidden, share_start, share, 1)
        columns = [out_cols[layer][:, k * fold : (k + 1) * fold] for k in range(ys)]
        out_parts = jnp.stack([dot(mixed_all, k, (0, 0)).astype(bf16) for k in columns], axis=0)
        gate_parts = dot(normed_cols, gate_all, (0, 0)).astype(bf16).reshape(ys, fold, channels)
        if last:
            out_parts_last, gate_parts_last = out_parts, gate_parts
            inner = jnp.sum(grad_normed * scale_now * hidden, axis=-1, keepdims=True)
            grad_norm = lax.dynamic_slice_in_dim(jnp.sum(grad_normed * hidden * inv_rms, axis=0), share_start, share, 0)
            grad_rows = grad_rows + inv_rms * scale_now * grad_normed - hidden * (inv_rms * inv_rms * inv_rms) * inner / width
            norm_row = jnp.pad(grad_norm[None], ((0, 0), (0, channels - share)))
            small[-1] = jnp.pad(jnp.concatenate([misc, norm_row], axis=0), ((0, 16 - misc.shape[0] - 1), (0, 0)))
            small_last = small
            continue
        inner = jnp.sum(grad_part * scale_now * hidden, axis=-1, keepdims=True)
        inner_high = inner.astype(bf16)
        inner_low = (inner - inner_high.astype(f32)).astype(bf16)
        beside = jnp.pad(jnp.concatenate([inner_high, inner_low], axis=1), ((0, 0), (0, LANES - 2)))
        beside = jnp.broadcast_to(beside[:, None], (rows, nch, LANES))
        send = jnp.concatenate([grad_part.astype(bf16).reshape(rows, nch, share), beside], axis=2)
        small[-1] = jnp.pad(misc, ((0, 16 - misc.shape[0]), (0, 0)))
        hidden_share = lax.dynamic_slice_in_dim(hidden, share_start, share, 1)
        scale_share = lax.dynamic_slice_in_dim(scale_now, share_start, share, 0)
        got, branch, sums, grad_in_values, tiny, grad_gate_now, grad_out_weight = closing(
            send.reshape(rows, nch * (share + LANES)), out_part, grad_values, jnp.swapaxes(normed_cols, 0, 1), hidden_share * inv_rms,
            small + small_last, [gate_parts, out_parts], nch, nseq, zs, ys, next(ids),
        )
        grad_share, inner = got[:, :share], got[:, share : share + 1] + got[:, share + 1 : share + 2]
        grad_input = (
            lax.dynamic_slice_in_dim(grad_rows, share_start, share, 1)
            + inv_rms * scale_share * grad_share
            - hidden_share * (inv_rms * inv_rms * inv_rms) * inner / width
        )
        result = (hidden_last + branch).astype(bf16)
        total_small = sums.astype(f32)
        heights = [v.shape[0] for v in small_last]
        half = sum(heights)
        pairs, at = [], 0
        for height in heights:
            pairs.append(jnp.stack([total_small[at : at + height], total_small[half + at : half + at + height]], axis=0))
            at += height
        misc = pairs[3]
        norms = jnp.stack([tiny[0], misc[1, KERN + 3, :share]], axis=0)
        in_weight = jnp.stack(
            [jnp.stack(pair, axis=1) for pair in ((grad_in_values, grad_gate_now), (grad_values_last, grad_gate_last))], axis=0
        )
        out_weight = jnp.stack([grad_out_weight, grad_out_last], axis=0)
    shape3 = (seqs, length, share)
    return (
        result.reshape(shape3),
        grad_input.reshape(shape3),
        norms,
        in_weight,
        misc[:, :KERN],
        misc[:, KERN],
        jnp.swapaxes(pairs[0], 1, 2),
        pairs[1],
        misc[:, KERN + 1],
        pairs[2],
        misc[:, KERN + 2],
        out_weight,
    )


def solution(mesh):
    in_specs = (
        P(None, "seq", None),
        P(None, "seq"),
        P(None, "seq", None),
        P(),
        P(None, None, None, "ch"),
        P(None, None, "ch"),
        P(None, "ch"),
        P(None, "ch", None),
        P(None, None, "ch"),
        P(None, "ch"),
        P(None, None, "ch"),
        P(None, "ch"),
        P(None, "ch", None),
    )
    out_specs = (
        P(None, "seq", "ch"),
        P(None, "seq", "ch"),
        P(None, "ch"),
        P(None, "seq", None, "ch"),
        P(None, None, "ch"),
        P(None, "ch"),
        P(None, "ch", None),
        P(None, None, "ch"),
        P(None, "ch"),
        P(None, None, "ch"),
        P(None, "ch"),
        P(None, "ch", "seq"),
    )
    return jax.shard_map(local, mesh=mesh, in_specs=in_specs, out_specs=out_specs, check_vma=False)
```

```python
import functools

import jax
import jax.numpy as jnp
from jax import lax
from jax.experimental import pallas as pl
from jax.experimental.pallas import tpu as pltpu
from jax.sharding import PartitionSpec as P

STATE = 16
RANK = 128
KERN = 4
LAYERS = 2
MESH = pl.DeviceIdType.MESH
ANY = pl.BlockSpec(memory_space=pl.ANY)
f32, bf16 = jnp.float32, jnp.bfloat16
epsilon = 1e-05


def after(kernel, count, pins):
    def run(*refs):
        return kernel(*refs[:count], *refs[count + len(pins) :])
    return run


def cost(us):
    return pl.CostEstimate(flops=int(us * 0.1e9), bytes_accessed=0, transcendentals=0)


LANES = 128
BIG = 1e30
LOG2E = 1.4426950408889634

def softplus(v):
    return jnp.maximum(v, 0.0) + jnp.log(1.0 + jnp.exp(-jnp.abs(v)))

def spread_states(bc_ref, wide_ref, pick_ref, rows, unroll=8):
    lane = lax.broadcasted_iota(jnp.int32, (STATE, 2 * STATE), 1)
    row = lax.broadcasted_iota(jnp.int32, (STATE, 2 * STATE), 0)
    mask = (lane % STATE == row).astype(jnp.float32)
    src = lax.broadcasted_iota(jnp.int32, (2 * STATE, 2 * LANES), 0)
    dst = lax.broadcasted_iota(jnp.int32, (2 * STATE, 2 * LANES), 1)
    route = ((src // STATE) == (dst // LANES)).astype(jnp.bfloat16)
    chunk = 32
    def step(i, _):
        t0 = pl.multiple_of(i * chunk, chunk)
        bcv = bc_ref[pl.ds(t0, chunk), :]
        for j in range(chunk):
            pick_ref[pl.ds(j * STATE, STATE), :] = (bcv[j:j + 1] * mask).astype(jnp.bfloat16)
        wide_ref[pl.ds(pl.multiple_of(t0 * STATE, chunk * STATE), chunk * STATE), :] = jnp.dot(pick_ref[...], route, preferred_element_type=jnp.float32)
        return 0
    lax.fori_loop(0, rows // chunk, step, 0)

def prep(step_ref_pre, act_ref, keep_ref, dstep_ref, dx_ref, rows):
    def body(i, _):
        sl = pl.ds(pl.multiple_of(i * 32, 32), 32)
        for g in range(dstep_ref.shape[0]):
            st = softplus(step_ref_pre[sl, lanes(g)])
            dstep_ref[g, sl, :] = jnp.where(keep_ref[sl, :] > 0.0, st, BIG)
            dx_ref[g, sl, :] = st * act_ref[sl, lanes(g)]
        return 0
    lax.fori_loop(0, rows // 32, body, 0)

def lanes(g):
    return pl.ds(g * LANES, LANES)

def group_sets(channels, width):
    n = channels // LANES
    return [list(range(i, min(i + width, n))) for i in range(0, n, width)]

def local_kernel(seqs, pre_ref, act_ref, bc_ref, keep_ref, dl_ref, end_ref, gain_ref, wide, pick, dstep, dx):
    rows, channels = pre_ref.shape
    length = rows // seqs
    spread_states(bc_ref, wide, pick, rows)
    prep(pre_ref, act_ref, keep_ref, dstep, dx, rows)
    yield
    for gs in group_sets(channels, 8):
        a2 = [-jnp.exp(dl_ref[:, lanes(g)]) * LOG2E for g in gs]
        for s in range(seqs):
            for k, g in enumerate(gs):
                tot = jnp.sum(dstep[g, pl.ds(s * length, length), :], axis=0, keepdims=True)
                gain_ref[pl.ds(s, 1), lanes(g)] = tot
            def blk(i, st):
                st = list(st)
                t0 = pl.multiple_of(s * length + i * 8, 8)
                for j in range(8):
                    b = wide[pl.ds(pl.multiple_of((t0 + j) * STATE, STATE), STATE), pl.ds(0, LANES)]
                    for k, g in enumerate(gs):
                        d = jnp.exp2(a2[k] * dstep[g, pl.ds(t0 + j, 1), :])
                        st[k] = d * st[k] + b * dx[g, pl.ds(t0 + j, 1), :]
                return tuple(st)
            st = lax.fori_loop(0, length // 8, blk, tuple(jnp.zeros((STATE, LANES), jnp.float32) for _ in gs))
            for k, g in enumerate(gs):
                end_ref[s, :, lanes(g)] = st[k]
            yield

VM = pl.BlockSpec(memory_space=pltpu.VMEM)


def played(kernel, counts, plan, places):
    n_in, n_out, n_scratch = counts

    def run(*refs):
        refs = list(refs)

        def take(k):
            head, refs[:] = refs[:k], refs[k:]
            return head

        own = take(n_in)
        sources = take(len(plan))
        own += take(n_out)
        targets = take(len(plan))
        own += take(n_scratch)
        jobs = []
        for (kind, when), src, out in zip(plan, sources, targets):
            jobs.append((kind(*places, src, out, take(kind.semaphores)), when))
        if plan:
            seq, ch = lax.axis_index("seq"), lax.axis_index("ch")
            zs, ys = places
            z, y = seq // ys, lax.rem(seq, ys)
            peers = [{"seq": lax.rem(z + d, zs) * ys + y} for d in range(1, zs)]
            peers += [{"seq": z * ys + lax.rem(y + d, ys)} for d in range(1, ys)]
            xs = lax.axis_size("ch") // 2
            peers += [{"ch": lax.rem(ch // 2 + e, xs) * 2 + lax.rem(ch, 2)} for e in range(1, xs)]
            peers.append({"ch": ch + 1 - 2 * lax.rem(ch, 2)})
            barrier = pltpu.get_barrier_semaphore()
            for peer in peers:
                pl.semaphore_signal(barrier, inc=1, device_id=peer, device_id_type=MESH)
        for at, _ in enumerate(kernel(*own)):
            if at == 0 and plan:
                pl.semaphore_wait(barrier, len(peers))
                for job, _ in jobs:
                    job.begin()
            for job, when in jobs:
                if at in when:
                    job.step(when.index(at))
        for job, when in jobs:
            job.finish()

    return run


def play_call(kernel, counts, plan, places, cid, out_shape, scratch, arrays, us, name, pins=()):
    arrays = list(arrays) + [v for _, _, v in plan]
    kinds = [(kind, when) for kind, when, _ in plan]
    out_shape = list(out_shape) + [kind.result(v, *places) for kind, _, v in plan]
    sems = [spec for kind, _, v in plan for spec in kind.specs(v, *places)]
    extra = dict(collective_id=cid, has_side_effects=True) if plan else {}
    return pl.pallas_call(
        after(played(kernel, counts, kinds, places), len(arrays), pins),
        out_shape=out_shape,
        in_specs=[VM] * len(arrays) + [ANY] * len(pins),
        out_specs=[VM] * len(out_shape),
        scratch_shapes=list(scratch) + sems,
        compiler_params=pltpu.CompilerParams(vmem_limit_bytes=60 * 2**20, **extra),
        cost_estimate=cost(us),
        name=name,
    )(*arrays, *pins)

def scan_local(pre, act, bc, keep, dl, seqs, plan, places, cid):
    rows, channels = pre.shape
    f = jnp.float32
    big = pltpu.VMEM((channels // LANES, rows, LANES), f)
    return play_call(
        functools.partial(local_kernel, seqs), (5, 2, 4), plan, places, cid,
        [jax.ShapeDtypeStruct((seqs, STATE, channels), f), jax.ShapeDtypeStruct((seqs, channels), f)],
        [pltpu.VMEM((rows * STATE, 2 * LANES), f), pltpu.VMEM((32 * STATE, 2 * STATE), jnp.bfloat16), big, big],
        (pre, act, bc, keep, dl), 8, "scan_local",
    )


def forward_kernel(seqs, pre_ref, act_ref, bc_ref, keep_ref, dl_ref, in_ref, y_ref, wide, pick, dstep, dx, part):
    rows, channels = pre_ref.shape
    length = rows // seqs
    spread_states(bc_ref, wide, pick, rows)
    prep(pre_ref, act_ref, keep_ref, dstep, dx, rows)
    yield
    for gs in group_sets(channels, 4):
        a2 = [-jnp.exp(dl_ref[:, lanes(g)]) * LOG2E for g in gs]
        for s in range(seqs):
            def blk(i, st):
                st = list(st)
                t0 = pl.multiple_of(s * length + i * 8, 8)
                for j in range(8):
                    at = pl.ds(pl.multiple_of((t0 + j) * STATE, STATE), STATE)
                    b = wide[at, pl.ds(0, LANES)]
                    c = wide[at, pl.ds(LANES, LANES)]
                    for k, g in enumerate(gs):
                        d = jnp.exp2(a2[k] * dstep[g, pl.ds(t0 + j, 1), :])
                        st[k] = d * st[k] + b * dx[g, pl.ds(t0 + j, 1), :]
                        v = st[k] * c
                        part[k, pl.ds(pl.multiple_of(i * 64 + j * 8, 8), 8), :] = v[:8] + v[8:]
                return tuple(st)
            lax.fori_loop(0, length // 8, blk, tuple(in_ref[s, :, lanes(g)] for g in gs))
            def red(i, _):
                t0 = pl.multiple_of(s * length + i * 8, 8)
                for k, g in enumerate(gs):
                    acc = part[k, pl.ds(i * 64, 8, stride=8), :]
                    for m in range(1, 8):
                        acc = acc + part[k, pl.ds(i * 64 + m, 8, stride=8), :]
                    y_ref[pl.ds(t0, 8), lanes(g)] = acc
                return 0
            lax.fori_loop(0, length // 8, red, 0)
            yield

def scan_forward(pre, act, bc, keep, dl, state_in, seqs, plan, places, cid, pins=()):
    rows, channels = pre.shape
    f = jnp.float32
    big = pltpu.VMEM((channels // LANES, rows, LANES), f)
    return play_call(
        functools.partial(forward_kernel, seqs), (6, 1, 5), plan, places, cid,
        [jax.ShapeDtypeStruct((rows, channels), f)],
        [pltpu.VMEM((rows * STATE, 2 * LANES), f), pltpu.VMEM((32 * STATE, 2 * STATE), jnp.bfloat16), big, big,
         pltpu.VMEM((4, rows // seqs * 8, LANES), f)],
        (pre, act, bc, keep, dl, state_in), 11, "scan_forward", pins,
    )


LN2 = 0.6931471805599453

def back_local_kernel(seqs, pre_ref, gs_ref, bc_ref, keep_ref, dl_ref, out_ref, wide, pick, dstep, gsc):
    rows, channels = pre_ref.shape
    length = rows // seqs
    spread_states(bc_ref, wide, pick, rows)
    def body(i, _):
        sl = pl.ds(pl.multiple_of(i * 32, 32), 32)
        for g in range(channels // LANES):
            st = softplus(pre_ref[sl, lanes(g)])
            dstep[g, sl, :] = jnp.where(keep_ref[sl, :] > 0.0, st, BIG)
            gsc[g, sl, :] = gs_ref[sl, lanes(g)]
        return 0
    lax.fori_loop(0, rows // 32, body, 0)
    for gs in group_sets(channels, 8):
        a2 = [-jnp.exp(dl_ref[:, lanes(g)]) * LOG2E for g in gs]
        for s in range(seqs):
            def blk(i, st):
                st = list(st)
                t0 = pl.multiple_of(s * length + (length // 8 - 1 - i) * 8, 8)
                for j in reversed(range(8)):
                    c = wide[pl.ds(pl.multiple_of((t0 + j) * STATE, STATE), STATE), pl.ds(LANES, LANES)]
                    for k, g in enumerate(gs):
                        d = jnp.exp2(a2[k] * dstep[g, pl.ds(t0 + j, 1), :])
                        st[k] = d * (st[k] + c * gsc[g, pl.ds(t0 + j, 1), :])
                return tuple(st)
            st = lax.fori_loop(0, length // 8, blk, tuple(jnp.zeros((STATE, LANES), jnp.float32) for _ in gs))
            for k, g in enumerate(gs):
                out_ref[s, :, lanes(g)] = st[k]

def scan_back_local(pre, gs, bc, keep, dl, seqs, pins=()):
    rows, channels = pre.shape
    f = jnp.float32
    return pl.pallas_call(
        after(functools.partial(back_local_kernel, seqs), 5, pins),
        out_shape=jax.ShapeDtypeStruct((seqs, STATE, channels), f),
        in_specs=[VM] * 5 + [ANY] * len(pins), out_specs=VM,
        scratch_shapes=[pltpu.VMEM((rows * STATE, 2 * LANES), f), pltpu.VMEM((32 * STATE, 2 * STATE), jnp.bfloat16),
                        pltpu.VMEM((channels // LANES, rows, LANES), f), pltpu.VMEM((channels // LANES, rows, LANES), f)],
        compiler_params=pltpu.CompilerParams(vmem_limit_bytes=60 * 2**20),
        cost_estimate=cost(8),
        name="scan_back_local",
    )(pre, gs, bc, keep, dl, *pins)

def back_kernel(seqs, with_y, pre_ref, act_ref, gs_ref, bc_ref, keep_ref, dl_ref, skip_ref, in_ref, lam_ref,
                gpre_ref, gact_ref, gbc_ref, gdl_ref, *rest):
    if with_y:
        y_ref, *rest = rest
    (wide, pick, dstep, dx, stepc, gsc, states, partq, partr, accb, accc, rowsum) = rest
    rows, channels = pre_ref.shape
    length = rows // seqs
    f = jnp.float32
    spread_states(bc_ref, wide, pick, rows)
    def body(i, _):
        sl = pl.ds(pl.multiple_of(i * 32, 32), 32)
        for g in range(channels // LANES):
            st = softplus(pre_ref[sl, lanes(g)])
            stepc[g, sl, :] = st
            dstep[g, sl, :] = jnp.where(keep_ref[sl, :] > 0.0, st, BIG)
            dx[g, sl, :] = st * act_ref[sl, lanes(g)]
            gsc[g, sl, :] = gs_ref[sl, lanes(g)]
        return 0
    lax.fori_loop(0, rows // 32, body, 0)
    yield
    sets = group_sets(channels, 4)
    for index, gs in enumerate(sets):
        a2 = [-jnp.exp(dl_ref[:, lanes(g)]) * LOG2E for g in gs]
        gdl = [jnp.zeros((STATE, LANES), f) for _ in gs]
        for s in range(seqs):
            for k, g in enumerate(gs):
                states[k, pl.ds(0, STATE), :] = in_ref[s, :, lanes(g)]
            def fwd(i, st):
                st = list(st)
                t0 = pl.multiple_of(s * length + i * 8, 8)
                for j in range(8):
                    at = pl.ds(pl.multiple_of((t0 + j) * STATE, STATE), STATE)
                    b = wide[at, pl.ds(0, LANES)]
                    if with_y:
                        c = wide[at, pl.ds(LANES, LANES)]
                    for k, g in enumerate(gs):
                        d = jnp.exp2(a2[k] * dstep[g, pl.ds(t0 + j, 1), :])
                        st[k] = d * st[k] + b * dx[g, pl.ds(t0 + j, 1), :]
                        states[k, pl.ds(pl.multiple_of((i * 8 + j + 1) * STATE, STATE), STATE), :] = st[k]
                        if with_y:
                            v = st[k] * c
                            partq[k, pl.ds(pl.multiple_of(i * 64 + j * 8, 8), 8), :] = v[:8] + v[8:]
                return tuple(st)
            lax.fori_loop(0, length // 8, fwd, tuple(in_ref[s, :, lanes(g)] for g in gs))
            if with_y:
                def read(i, _):
                    t0 = pl.multiple_of(s * length + i * 8, 8)
                    for k, g in enumerate(gs):
                        acc = partq[k, pl.ds(i * 64, 8, stride=8), :]
                        for m in range(1, 8):
                            acc = acc + partq[k, pl.ds(i * 64 + m, 8, stride=8), :]
                        y_ref[pl.ds(t0, 8), lanes(g)] = acc
                    return 0
                lax.fori_loop(0, length // 8, read, 0)
            yield
            def bwd(i, carry):
                st = list(carry[:len(gs)])
                am = list(carry[len(gs):])
                l0 = (length // 8 - 1 - i) * 8
                t0 = pl.multiple_of(s * length + l0, 8)
                for j in reversed(range(8)):
                    at = pl.ds(pl.multiple_of((t0 + j) * STATE, STATE), STATE)
                    b = wide[at, pl.ds(0, LANES)]
                    c = wide[at, pl.ds(LANES, LANES)]
                    tb = tc = None
                    here = pl.ds(pl.multiple_of((l0 + j) * 8, 8), 8)
                    for k, g in enumerate(gs):
                        row = pl.ds(t0 + j, 1)
                        grow = gsc[g, row, :]
                        d = jnp.exp2(a2[k] * dstep[g, row, :])
                        lam = st[k] + c * grow
                        old = states[k, pl.ds(pl.multiple_of((l0 + j) * STATE, STATE), STATE), :]
                        new = states[k, pl.ds(pl.multiple_of((l0 + j + 1) * STATE, STATE), STATE), :]
                        st[k] = d * lam
                        lp = st[k] * old
                        q = lam * b
                        partq[k, here, :] = q[:8] + q[8:]
                        r = lp * a2[k]
                        partr[k, here, :] = r[:8] + r[8:]
                        am[k] = am[k] + lp * stepc[g, row, :]
                        u = lam * dx[g, row, :]
                        v = new * grow
                        tb = u if tb is None else tb + u
                        tc = v if tc is None else tc + v
                    if index > 0:
                        tb = tb + accb[at, :]
                        tc = tc + accc[at, :]
                    accb[at, :] = tb
                    accc[at, :] = tc
                return tuple(st) + tuple(am)
            out = lax.fori_loop(0, length // 8, bwd, tuple(lam_ref[s, :, lanes(g)] for g in gs) + tuple(gdl))
            gdl = list(out[len(gs):])
            def red(i, _):
                t0 = pl.multiple_of(s * length + i * 8, 8)
                for k, g in enumerate(gs):
                    q = partq[k, pl.ds(i * 64, 8, stride=8), :]
                    r = partr[k, pl.ds(i * 64, 8, stride=8), :]
                    for m in range(1, 8):
                        q = q + partq[k, pl.ds(i * 64 + m, 8, stride=8), :]
                        r = r + partr[k, pl.ds(i * 64 + m, 8, stride=8), :]
                    here = pl.ds(t0, 8)
                    p = pre_ref[here, lanes(g)]
                    gstep = r * LN2 + act_ref[here, lanes(g)] * q
                    gpre_ref[here, lanes(g)] = gstep * (1.0 / (1.0 + jnp.exp(-p)))
                    gact_ref[here, lanes(g)] = stepc[g, here, :] * q + gsc[g, here, :] * skip_ref[:, lanes(g)]
                return 0
            lax.fori_loop(0, length // 8, red, 0)
            yield
        for k, g in enumerate(gs):
            gdl_ref[:, lanes(g)] = gdl[k] * (a2[k] * LN2)
    ones = jnp.ones((LANES, LANES), jnp.bfloat16)
    lane = lax.broadcasted_iota(jnp.int32, (32 * STATE, LANES), 1)
    row = lax.broadcasted_iota(jnp.int32, (32 * STATE, LANES), 0) % STATE
    mb = lane == row
    mc = lane == row + STATE
    def fin(i, _):
        sl = pl.ds(pl.multiple_of(i * 32 * STATE, 32 * STATE), 32 * STATE)
        sb = jnp.dot(accb[sl, :].astype(jnp.bfloat16), ones, preferred_element_type=f)
        sc = jnp.dot(accc[sl, :].astype(jnp.bfloat16), ones, preferred_element_type=f)
        rowsum[...] = jnp.where(mb, sb, jnp.where(mc, sc, 0.0))
        acc = rowsum[pl.ds(0, 32, stride=STATE), :]
        for m in range(1, STATE):
            acc = acc + rowsum[pl.ds(m, 32, stride=STATE), :]
        gbc_ref[pl.ds(pl.multiple_of(i * 32, 32), 32), :] = acc
        return 0
    lax.fori_loop(0, rows // 32, fin, 0)

def scan_back(pre, act, gs, bc, keep, dl, skip, state_in, lam_in, seqs, with_y, plan, places, cid, pins=()):
    rows, channels = pre.shape
    f = jnp.float32
    groups = channels // LANES
    length = rows // seqs
    big = pltpu.VMEM((groups, rows, LANES), f)
    whole = jax.ShapeDtypeStruct((rows, channels), f)
    return play_call(
        functools.partial(back_kernel, seqs, with_y), (9, 4 + with_y, 12), plan, places, cid,
        [whole, whole, jax.ShapeDtypeStruct((rows, LANES), f), jax.ShapeDtypeStruct((STATE, channels), f)] + [whole] * with_y,
        [pltpu.VMEM((rows * STATE, 2 * LANES), f), pltpu.VMEM((32 * STATE, 2 * STATE), jnp.bfloat16),
         big, big, big, big,
         pltpu.VMEM((4, (length + 1) * STATE, LANES), f),
         pltpu.VMEM((4, length * 8, LANES), f), pltpu.VMEM((4, length * 8, LANES), f),
         pltpu.VMEM((rows * STATE, LANES), f), pltpu.VMEM((rows * STATE, LANES), f),
         pltpu.VMEM((32 * STATE, LANES), f)],
        (pre, act, gs, bc, keep, dl, skip, state_in, lam_in), 23 + 3 * with_y, "scan_back", pins,
    )


def greet(peers):
    barrier = pltpu.get_barrier_semaphore()
    for p in peers:
        pl.semaphore_signal(barrier, inc=1, device_id=p, device_id_type=MESH)
    pl.semaphore_wait(barrier, len(peers))

def ch_sum_kernel(n, x_ref, out_ref, mine, slots, send, recv):
    me = lax.axis_index("ch")
    peers = [{"ch": lax.rem(me + d, n)} for d in range(1, n)]
    greet(peers)
    mine[...] = x_ref[...].astype(bf16)
    copies = []
    for d in range(1, n):
        c = pltpu.make_async_remote_copy(src_ref=mine, dst_ref=slots.at[d - 1], send_sem=send.at[d - 1], recv_sem=recv.at[d - 1], device_id=peers[d - 1], device_id_type=MESH)
        c.start()
        copies.append(c)
    total = x_ref[...].astype(bf16).astype(f32)
    for d, c in zip(range(1, n), copies):
        c.wait()
        total = total + slots[d - 1].astype(f32)
    out_ref[...] = total

def ch_sum(x, n, cid, pins=()):
    return pl.pallas_call(
        after(functools.partial(ch_sum_kernel, n), 1, pins),
        out_shape=jax.ShapeDtypeStruct(x.shape, f32), in_specs=[VM] + [ANY] * len(pins), out_specs=VM,
        scratch_shapes=[pltpu.VMEM(x.shape, bf16), pltpu.VMEM((n - 1,) + x.shape, bf16), pltpu.SemaphoreType.DMA((n - 1,)), pltpu.SemaphoreType.DMA((n - 1,))],
        compiler_params=pltpu.CompilerParams(collective_id=cid, has_side_effects=True, vmem_limit_bytes=32 * 2**20), cost_estimate=cost(10), name="ch_sum",
    )(x, *pins)

def reduce_steps(n, parts, gather, more, x_ref, out_ref, s1, sum1, s2, mine, got, fin, sem1, rem1, sem2, rem2, sem3, rem3, sem4, rem4):
    xs = n // 2
    me = lax.axis_index("ch")
    x, core = me // 2, lax.rem(me, 2)
    peer = {"ch": x * 2 + 1 - core}
    others = [lax.rem(x + d, xs) for d in range(1, xs)]
    if more is not None:
        greet([peer] + [{"ch": o * 2 + core} for o in others] + more)
    rows, width = x_ref.shape[0] // parts, x_ref.shape[1] // n
    def cols(block):
        return pl.ds(pl.multiple_of(block * width, width), width)
    def stage1(p, k):
        return pltpu.make_async_remote_copy(src_ref=x_ref.at[pl.ds(p * rows, rows), cols(k * 2 + 1 - core)], dst_ref=s1.at[p, k], send_sem=sem1.at[p, k], recv_sem=rem1.at[p, k], device_id=peer, device_id_type=MESH)
    def stage2(p, d):
        o = others[d]
        return pltpu.make_async_remote_copy(src_ref=sum1.at[p, o], dst_ref=s2.at[p, d], send_sem=sem2.at[p, d], recv_sem=rem2.at[p, d], device_id={"ch": o * 2 + core}, device_id_type=MESH)
    def stage3(p, d):
        o = others[d]
        return pltpu.make_async_remote_copy(src_ref=mine.at[p], dst_ref=got.at[p, d], send_sem=sem3.at[p, d], recv_sem=rem3.at[p, d], device_id={"ch": o * 2 + core}, device_id_type=MESH)
    for p in range(parts):
        for k in range(xs):
            stage1(p, k).start()
    yield
    for p in range(parts):
        for k in range(xs):
            stage1(p, k).wait_recv()
            sum1[p, k] = (x_ref[pl.ds(p * rows, rows), cols(k * 2 + core)].astype(f32) + s1[p, k].astype(f32)).astype(bf16)
        for d in range(xs - 1):
            stage2(p, d).start()
    yield
    for p in range(parts):
        total = sum1[p, x].astype(f32)
        for d in range(xs - 1):
            stage2(p, d).wait_recv()
            total = total + s2[p, d].astype(f32)
        if gather:
            mine[p] = total.astype(bf16)
            for d in range(xs - 1):
                stage3(p, d).start()
        else:
            out_ref[pl.ds(p * rows, rows), :] = total
    yield
    if gather:
        def stage4(p, d):
            src = mine.at[p] if d < 0 else got.at[p, d]
            return pltpu.make_async_remote_copy(src_ref=src, dst_ref=fin.at[p, d + 1], send_sem=sem4.at[p, d + 1], recv_sem=rem4.at[p, d + 1], device_id=peer, device_id_type=MESH)
        def chip(d):
            return lax.rem(x + xs - 1 - d, xs)
        for p in range(parts):
            stage4(p, -1).start()
            out_ref[pl.ds(p * rows, rows), cols(me)] = mine[p].astype(out_ref.dtype)
            for d in range(xs - 1):
                stage3(p, d).wait_recv()
                stage4(p, d).start()
                out_ref[pl.ds(p * rows, rows), cols(chip(d) * 2 + core)] = got[p, d].astype(out_ref.dtype)
        yield
        for p in range(parts):
            for d in range(-1, xs - 1):
                stage4(p, d).wait_recv()
                out_ref[pl.ds(p * rows, rows), cols(chip(d) * 2 + 1 - core)] = fin[p, d + 1].astype(out_ref.dtype)
    for p in range(parts):
        for k in range(xs):
            stage1(p, k).wait_send()
        for d in range(xs - 1):
            stage2(p, d).wait_send()
            if gather:
                stage3(p, d).wait_send()
        if gather:
            for d in range(-1, xs - 1):
                stage4(p, d).wait_send()
    yield


class ColumnsLine:
    semaphores = 6

    @staticmethod
    def result(v, zs, ys):
        return jax.ShapeDtypeStruct((zs * v.shape[0], v.shape[1] // zs), v.dtype)

    @staticmethod
    def specs(v, zs, ys):
        sem = pltpu.SemaphoreType.DMA
        xs = lax.axis_size("ch") // 2
        return [sem((zs - 1,))] * 2 + [sem((zs - 1, xs - 1))] * 2 + [sem((zs - 1, xs))] * 2

    def __init__(self, zs, ys, src, out, sems):
        seq, ch = lax.axis_index("seq"), lax.axis_index("ch")
        self.nch = lax.axis_size("ch")
        self.xs = self.nch // 2
        self.zs, self.ys, self.z, self.y, self.ch = zs, ys, seq // ys, lax.rem(seq, ys), ch
        self.x, self.core = ch // 2, lax.rem(ch, 2)
        self.src, self.out, self.sems = src, out, sems
        self.rows, self.width = src.shape[0], src.shape[1] // zs
        self.part = self.rows // self.nch

    def cols(self, z):
        return pl.ds(pl.multiple_of(z * self.width, self.width), self.width)

    def share(self, z, ch):
        return pl.ds(pl.multiple_of(z * self.rows + ch * self.part, self.part), self.part)

    def remote(self, k, at, src, dst, to):
        send, recv = self.sems[2 * k : 2 * k + 2]
        return pltpu.make_async_remote_copy(src_ref=src, dst_ref=dst, send_sem=send.at[at], recv_sem=recv.at[at], device_id=to, device_id_type=MESH)

    def along(self, d):
        to = lax.rem(self.z + d, self.zs)
        src = self.src.at[pl.ds(pl.multiple_of(self.ch * self.part, self.part), self.part), self.cols(to)]
        return self.remote(0, d - 1, src, self.out.at[self.share(self.z, self.ch)], {"seq": to * self.ys + self.y})

    def from_z(self, d):
        return lax.rem(self.z + self.zs - d, self.zs)

    def over(self, d, e):
        rows = self.out.at[self.share(self.from_z(d), self.ch)]
        return self.remote(1, (d - 1, e - 1), rows, rows, {"ch": lax.rem(self.x + e, self.xs) * 2 + self.core})

    def across(self, d, e):
        rows = self.out.at[self.share(self.from_z(d), lax.rem(self.x + self.xs - e, self.xs) * 2 + self.core)]
        return self.remote(2, (d - 1, e), rows, rows, {"ch": self.x * 2 + 1 - self.core})

    def lags(self):
        return range(1, self.zs)

    def begin(self):
        for d in self.lags():
            self.along(d).start()
        here = pl.ds(pl.multiple_of(self.z * self.rows, self.rows), self.rows)
        self.out[here, :] = self.src[:, self.cols(self.z)]

    def step(self, index):
        for d in self.lags():
            if index == 0:
                self.along(d).wait_recv()
                for e in range(1, self.xs):
                    self.over(d, e).start()
                self.across(d, 0).start()
            else:
                for e in range(1, self.xs):
                    self.over(d, e).wait_recv()
                    self.across(d, e).start()

    def finish(self):
        for d in self.lags():
            for e in range(self.xs):
                self.across(d, e).wait_recv()
        for d in self.lags():
            self.along(d).wait_send()
            for e in range(1, self.xs):
                self.over(d, e).wait_send()
            for e in range(self.xs):
                self.across(d, e).wait_send()


def reduce_kernel(n, parts, gather, *refs):
    for _ in reduce_steps(n, parts, gather, [], *refs):
        pass


def reduce_scratch_shapes(shape, n, parts):
    rows, width = shape
    xs, r, w = n // 2, rows // parts, width // n
    sem = pltpu.SemaphoreType.DMA
    return [
        pltpu.VMEM((parts, xs, r, w), bf16), pltpu.VMEM((parts, xs, r, w), bf16), pltpu.VMEM((parts, xs - 1, r, w), bf16),
        pltpu.VMEM((parts, r, w), bf16), pltpu.VMEM((parts, xs - 1, r, w), bf16), pltpu.VMEM((parts, xs, r, w), bf16),
        sem((parts, xs)), sem((parts, xs)), sem((parts, xs - 1)), sem((parts, xs - 1)),
        sem((parts, xs - 1)), sem((parts, xs - 1)), sem((parts, xs)), sem((parts, xs)),
    ]


def ch_reduce(x, n, cid, gather, parts=2):
    rows, width = x.shape
    return pl.pallas_call(
        functools.partial(reduce_kernel, n, parts, gather),
        out_shape=jax.ShapeDtypeStruct((rows, width if gather else width // n), f32),
        in_specs=[VM], out_specs=VM,
        scratch_shapes=reduce_scratch_shapes(x.shape, n, parts),
        compiler_params=pltpu.CompilerParams(collective_id=cid, has_side_effects=True, vmem_limit_bytes=48 * 2**20),
        cost_estimate=cost(18), name="ch_reduce",
    )(x)


def carry_kernel(n, fwd, rev, count, places, layer, *refs):
    refs = list(refs)
    tot_ref, dl_ref = refs.pop(0), refs.pop(0)
    k = fwd + rev
    ends = [refs.pop(0) for _ in range(k)]
    parts = [refs.pop(0) for _ in range(count)]
    whole = refs.pop(0) if layer is not None else None
    outs = [refs.pop(0) for _ in range(k)]
    sums = [refs.pop(0) for _ in range(count)]
    if layer is not None:
        local = pltpu.make_async_copy(whole.at[layer], refs.pop(0), refs.pop(-1))
        local.start()
    mine, slots, tots, send, recv, tsend, trecv = refs[:7]
    jobs = [PartSum(*places, parts[j], sums[j], refs[7 + 3 * j : 10 + 3 * j]) for j in range(count)]
    me = lax.axis_index("seq")
    seqs = tot_ref.shape[0]
    greet([{"seq": lax.rem(me + d, n)} for d in range(1, n)])
    a2 = -jnp.exp(dl_ref[...]) * LOG2E
    directions = [False] * fwd + [True] * rev
    def copies(i, d):
        away = -d if directions[i] else d
        to = {"seq": lax.rem(me + away + n, n)}
        return (
            pltpu.make_async_remote_copy(src_ref=mine.at[i], dst_ref=slots.at[i, d - 1], send_sem=send.at[i, d - 1], recv_sem=recv.at[i, d - 1], device_id=to, device_id_type=MESH),
            pltpu.make_async_remote_copy(src_ref=tot_ref, dst_ref=tots.at[i, d - 1], send_sem=tsend.at[i, d - 1], recv_sem=trecv.at[i, d - 1], device_id=to, device_id_type=MESH),
        )
    for i in range(k):
        mine[i] = ends[i][...].astype(bf16)
        outs[i][...] = jnp.zeros_like(outs[i])
    for d in reversed(range(1, n)):
        for i in range(k):
            place = n - 1 - me if directions[i] else me
            @pl.when(place + d < n)
            def _():
                for c in copies(i, d):
                    c.start()
    for job in jobs:
        job.begin()
    for d in reversed(range(1, n)):
        for i in range(k):
            place = n - 1 - me if directions[i] else me
            @pl.when(place >= d)
            def _():
                for c in copies(i, d):
                    c.wait_recv()
                for s in range(seqs):
                    gain = jnp.exp2(a2 * tots[i, d - 1, pl.ds(s, 1), :])
                    outs[i][s] = gain * outs[i][s] + slots[i, d - 1, s].astype(f32)
    for d in reversed(range(1, n)):
        for i in range(k):
            place = n - 1 - me if directions[i] else me
            @pl.when(place + d < n)
            def _():
                for c in copies(i, d):
                    c.wait_send()
    for job in jobs:
        job.finish()
    if layer is not None:
        local.wait()


def carry_over(tot, dl, ends, n, cid, fwd, rev, ps=(), places=(), taken=None):
    whole, layer = (None, None) if taken is None else taken
    extra = [] if taken is None else [whole]
    k = len(ends)
    sem = pltpu.SemaphoreType.DMA
    return pl.pallas_call(
        functools.partial(carry_kernel, n, int(fwd), int(rev), len(ps), places, layer),
        out_shape=[jax.ShapeDtypeStruct(ends[0].shape, f32)] * k + [PartSum.result(p, *places) for p in ps]
        + [jax.ShapeDtypeStruct(w.shape[1:], w.dtype) for w in extra],
        in_specs=[VM] * (k + 2 + len(ps)) + [ANY] * len(extra), out_specs=[VM] * (k + len(ps)) + [pl.BlockSpec(memory_space=pltpu.HBM)] * len(extra),
        scratch_shapes=[pltpu.VMEM((k,) + ends[0].shape, bf16), pltpu.VMEM((k, n - 1) + ends[0].shape, bf16), pltpu.VMEM((k, n - 1) + tot.shape, f32),
                        sem((k, n - 1)), sem((k, n - 1)), sem((k, n - 1)), sem((k, n - 1))]
        + [spec for p in ps for spec in PartSum.specs(p, *places)]
        + [pltpu.SemaphoreType.DMA] * len(extra),
        compiler_params=pltpu.CompilerParams(collective_id=cid, has_side_effects=True, vmem_limit_bytes=32 * 2**20), cost_estimate=cost(19), name="carry_over",
    )(tot, dl, *ends, *ps, *extra)


def seq_at(z, y, ys):
    return {"seq": z * ys + y}


class GatherLine:
    semaphores = 2

    @staticmethod
    def result(v, zs, ys):
        return jax.ShapeDtypeStruct((zs * v.shape[0], v.shape[1]), v.dtype)

    @staticmethod
    def specs(v, zs, ys):
        return [pltpu.SemaphoreType.DMA((2, zs - 1))] * 2


    def __init__(self, zs, ys, src, out, sems):
        me = lax.axis_index("seq")
        self.zs, self.ys, self.z, self.y = zs, ys, me // ys, lax.rem(me, ys)
        self.src, self.out = src, out
        self.send, self.recv = sems
        self.rows = src.shape[0]

    def block(self, z):
        return self.out.at[pl.ds(pl.multiple_of(z * self.rows, self.rows), self.rows)]

    def copy(self, way, r):
        z = self.z
        to, b = (lax.rem(z + 1, self.zs), z - r) if way == 0 else (lax.rem(z + self.zs - 1, self.zs), z + r)
        b = lax.rem(b + self.zs, self.zs)
        return pltpu.make_async_remote_copy(
            src_ref=self.src if r == 0 else self.block(b),
            dst_ref=self.block(b),
            send_sem=self.send.at[way, r],
            recv_sem=self.recv.at[way, r],
            device_id=seq_at(to, self.y, self.ys),
            device_id_type=MESH,
        )

    def sends(self, way, r):
        z, last = self.z, self.zs - 1
        return jnp.logical_and(z < last, z >= r) if way == 0 else jnp.logical_and(z > 0, z + r <= last)

    def receives(self, way, r):
        z, last = self.z, self.zs - 1
        return z - 1 - r >= 0 if way == 0 else z + 1 + r <= last

    def begin(self):
        self.start(0)
        self.block(self.z)[...] = self.src[...]

    def step(self, index):
        self.start(index + 1)

    def start(self, r):
        for way in (0, 1):
            if r > 0:
                self.arrive(way, r - 1)
            @pl.when(self.sends(way, r))
            def _():
                self.copy(way, r).start()

    def arrive(self, way, r):
        @pl.when(self.receives(way, r))
        def _():
            self.copy(way, r).wait_recv()

    def finish(self):
        self.arrived()
        self.sent()

    def arrived(self):
        for way in (0, 1):
            self.arrive(way, self.zs - 2)

    def sent(self):
        for way in (0, 1):
            for r in range(self.zs - 1):
                @pl.when(self.sends(way, r))
                def _():
                    self.copy(way, r).wait_send()


class SumAll:
    def __init__(self, zs, ys, src, out, scratch):
        me = lax.axis_index("seq")
        self.zs, self.ys, self.z, self.y = zs, ys, me // ys, lax.rem(me, ys)
        self.src, self.out = src, out
        self.yslots, self.ysum, self.slots, self.running, self.acc = scratch[:5]
        self.y1sems, self.zsems, self.y2sems, gather = scratch[5:7], scratch[7:9], scratch[9:11], scratch[11:13]
        self.part = src.shape[0] // ys
        self.share = self.part // zs
        self.back = GatherLine(zs, ys, self.mine(self.z), out, gather)
        self.back.block = self.mine

    @staticmethod
    def specs(height, w, zs, ys):
        part = height // ys
        share = part // zs
        sem = pltpu.SemaphoreType.DMA
        return [
            pltpu.VMEM((ys - 1, part, w), bf16),
            pltpu.VMEM((part, w), bf16),
            pltpu.VMEM((2, zs, share, w), bf16),
            pltpu.VMEM((2, zs, share, w), bf16),
            pltpu.VMEM((share, w), f32),
            sem((ys - 1,)), sem((ys - 1,)), sem((2, zs)), sem((2, zs)), sem(((ys - 1) * zs,)), sem(((ys - 1) * zs,)),
            sem((2, zs - 1)), sem((2, zs - 1)),
        ]

    def rows(self, index, size):
        return pl.ds(pl.multiple_of(index * size, size), size)

    def mine(self, z):
        return self.out.at[self.rows(self.y * self.zs + z, self.share)]

    def y1(self, d):
        to = lax.rem(self.y + d, self.ys)
        return pltpu.make_async_remote_copy(src_ref=self.src.at[self.rows(to, self.part)], dst_ref=self.yslots.at[d - 1], send_sem=self.y1sems[0].at[d - 1], recv_sem=self.y1sems[1].at[d - 1], device_id=seq_at(self.z, to, self.ys), device_id_type=MESH)

    def run(self, way, k):
        to = lax.rem(self.z + (1 if way == 0 else self.zs - 1), self.zs)
        return pltpu.make_async_remote_copy(src_ref=self.running.at[way, k], dst_ref=self.slots.at[way, k], send_sem=self.zsems[0].at[way, k], recv_sem=self.zsems[1].at[way, k], device_id=seq_at(to, self.y, self.ys), device_id_type=MESH)

    def y2(self, d, b):
        to = lax.rem(self.y + d, self.ys)
        at = (d - 1) * self.zs + b
        return pltpu.make_async_remote_copy(src_ref=self.mine(b), dst_ref=self.mine(b), send_sem=self.y2sems[0].at[at], recv_sem=self.y2sems[1].at[at], device_id=seq_at(self.z, to, self.ys), device_id_type=MESH)

    def begin(self):
        for d in range(1, self.ys):
            self.y1(d).start()

    def middle(self):
        total = self.src[self.rows(self.y, self.part), :].astype(f32)
        for d in range(1, self.ys):
            self.y1(d).wait_recv()
            total = total + self.yslots[d - 1].astype(f32)
        self.ysum[...] = total.astype(bf16)

    def line_sum(self, r):
        for way in (0, 1):
            k = self.zs - 1 - r if way == 0 else r
            z, first = self.z, 0 if way == 0 else self.zs - 1
            own = pl.ds(k * self.share, self.share)
            @pl.when(z == first)
            def _():
                self.running[way, k] = self.ysum[own, :]
                self.run(way, k).start()
            inside = jnp.logical_and(z > 0, z < k) if way == 0 else jnp.logical_and(z < self.zs - 1, z > k)
            @pl.when(inside)
            def _():
                self.run(way, k).wait_recv()
                self.running[way, k] = (self.ysum[own, :].astype(f32) + self.slots[way, k].astype(f32)).astype(bf16)
                self.run(way, k).start()

    def turn(self):
        self.acc[...] = self.ysum[self.rows(self.z, self.share), :].astype(f32)
        for way in (0, 1):
            @pl.when(self.z > 0 if way == 0 else self.z < self.zs - 1)
            def _():
                self.run(way, self.z).wait_recv()
                self.acc[...] = self.acc[...] + self.slots[way, self.z].astype(f32)
        self.mine(self.z)[...] = self.acc[...].astype(bf16)
        self.back.start(0)
        for d in range(1, self.ys):
            self.y2(d, self.z).start()

    def spread(self, r):
        if r < self.zs - 2:
            self.back.start(r + 1)
        else:
            for way in (0, 1):
                self.back.arrive(way, r)
        for way in (0, 1):
            b = self.z - 1 - r if way == 0 else self.z + 1 + r
            b = lax.rem(b + self.zs, self.zs)
            @pl.when(self.back.receives(way, r))
            def _():
                for d in range(1, self.ys):
                    self.y2(d, b).start()

    def finish(self):
        for d in range(1, self.ys):
            for b in range(self.zs):
                self.y2(d, b).wait_recv()
        for d in range(1, self.ys):
            self.y1(d).wait_send()
            for b in range(self.zs):
                self.y2(d, b).wait_send()
        for k in range(self.zs):
            @pl.when(self.z < k)
            def _():
                self.run(0, k).wait_send()
            @pl.when(self.z > k)
            def _():
                self.run(1, k).wait_send()
        self.back.sent()


class PartSum:
    semaphores = 3

    @staticmethod
    def result(v, zs, ys):
        return jax.ShapeDtypeStruct(v.shape[1:], f32)

    @staticmethod
    def specs(v, zs, ys):
        sem = pltpu.SemaphoreType.DMA((ys - 1,))
        return [sem, sem, pltpu.VMEM((ys - 1,) + v.shape[1:], v.dtype)]


    def __init__(self, zs, ys, src, out, scratch):
        me = lax.axis_index("seq")
        self.ys, self.z, self.y = ys, me // ys, lax.rem(me, ys)
        self.src, self.out = src, out
        self.send, self.recv, self.slots = scratch

    def copy(self, d):
        to = lax.rem(self.y + d, self.ys)
        return pltpu.make_async_remote_copy(
            src_ref=self.src.at[to],
            dst_ref=self.slots.at[d - 1],
            send_sem=self.send.at[d - 1],
            recv_sem=self.recv.at[d - 1],
            device_id=seq_at(self.z, to, self.ys),
            device_id_type=MESH,
        )

    def begin(self):
        for d in range(1, self.ys):
            self.copy(d).start()

    def finish(self):
        mine = self.src[self.y].astype(f32)
        for d in range(1, self.ys):
            self.copy(d).wait_recv()
            mine = mine + self.slots[d - 1].astype(f32)
        self.out[...] = mine
        for d in range(1, self.ys):
            self.copy(d).wait_send()


def closing_kernel(n, nseq, zs, ys, parts, count, pieces, x_ref, b_ref, v_ref, cols_ref, h_ref, *refs):
    refs = list(refs)

    def take(k):
        head, refs[:] = refs[:k], refs[k:]
        return head

    piece_refs, p_refs = take(pieces), take(count)
    out_ref, branch_ref, sum_ref, values_ref, norm_ref = take(5)
    part_refs = take(count)
    s_ref, all_ref, mine_ref, mine_slots, t_ref, tslots = take(6)
    reduce_scratch, more_scratch, gather_sems, sum_scratch = take(14), take(14), take(2), take(13)
    part_scratch, (msend, mrecv, tsend, trecv) = take(3 * count), take(4)
    seq = lax.axis_index("seq")
    z = seq // ys
    line = GatherLine(zs, ys, v_ref, all_ref, gather_sems)
    total = SumAll(zs, ys, s_ref, sum_ref, sum_scratch)
    sums = [PartSum(zs, ys, p_refs[k], part_refs[k], part_scratch[3 * k : 3 * k + 3]) for k in range(count)]
    late = PartSum(zs, ys, mine_ref, values_ref, [msend, mrecv, mine_slots])
    steps = reduce_steps(n, parts, False, [{"seq": lax.rem(seq + d, nseq)} for d in range(1, nseq)], x_ref, out_ref, *reduce_scratch)
    more_steps = reduce_steps(n, parts, False, None, b_ref, branch_ref, *more_scratch)

    def tiny(d):
        return pltpu.make_async_remote_copy(src_ref=t_ref, dst_ref=tslots.at[seq], send_sem=tsend.at[d - 1], recv_sem=trecv.at[d - 1], device_id={"seq": lax.rem(seq + d, nseq)}, device_id_type=MESH)

    next(steps)
    next(more_steps)
    line.begin()
    offset = 0
    for piece in piece_refs:
        s_ref[pl.ds(offset, piece.shape[0]), :] = piece[...].astype(bf16)
        offset += piece.shape[0]
    if offset < s_ref.shape[0]:
        s_ref[pl.ds(offset, s_ref.shape[0] - offset), :] = jnp.zeros((s_ref.shape[0] - offset, s_ref.shape[1]), bf16)
    total.begin()
    next(steps)
    next(more_steps)
    line.start(1)
    total.middle()
    total.line_sum(0)
    for part in sums:
        part.begin()
    for _ in steps:
        pass
    w = h_ref.shape[1]
    row = jnp.sum(out_ref[:, pl.ds(0, w)] * h_ref[...], axis=0, keepdims=True)
    t_ref[...] = jnp.broadcast_to(row, t_ref.shape).astype(bf16)
    tslots[seq] = t_ref[...]
    for d in range(1, nseq):
        tiny(d).start()
    total.line_sum(1)
    for r in range(2, zs - 1):
        line.start(r)
        total.line_sum(r)
    total.turn()
    for _ in more_steps:
        pass
    line.arrived()
    fold = mine_ref.shape[1]
    for k in range(ys):
        def chunk(i, _):
            at = pl.ds(pl.multiple_of(i * 256, 256), 256)
            got = jnp.dot(cols_ref[pl.ds(k * fold, fold), :], all_ref[:, at], preferred_element_type=f32)
            mine_ref[k, :, at] = got.astype(bf16)
            return 0
        lax.fori_loop(0, all_ref.shape[1] // 256, chunk, 0)
    late.begin()
    for r in range(zs - 1):
        total.spread(r)
    for part in sums:
        part.finish()
    for d in range(1, nseq):
        tiny(d).wait_recv()
    norm = tslots[0].astype(f32)
    for k in range(1, nseq):
        norm = norm + tslots[k].astype(f32)
    norm_ref[...] = norm
    late.finish()
    total.finish()
    line.sent()
    for d in range(1, nseq):
        tiny(d).wait_send()


def closing(x, branch, v, cols, h, pieces, ps, n, nseq, zs, ys, cid, parts=2):
    rows, width = x.shape
    sem = pltpu.SemaphoreType.DMA
    height = sum(piece.shape[0] for piece in pieces)
    height += -height % (16 * ys * zs)
    w = v.shape[1]
    fold = cols.shape[0] // ys
    count = len(ps)
    tiny = (16, h.shape[1])
    return pl.pallas_call(
        functools.partial(closing_kernel, n, nseq, zs, ys, parts, count, len(pieces)),
        out_shape=[
            jax.ShapeDtypeStruct((rows, width // n), f32),
            jax.ShapeDtypeStruct((rows, branch.shape[1] // n), f32),
            jax.ShapeDtypeStruct((height, w), bf16),
            jax.ShapeDtypeStruct((fold, w), f32),
            jax.ShapeDtypeStruct(tiny, f32),
        ]
        + [PartSum.result(p, zs, ys) for p in ps],
        in_specs=[VM] * (5 + len(pieces) + count),
        out_specs=[VM] * (5 + count),
        scratch_shapes=[
            pltpu.VMEM((height, w), bf16),
            pltpu.VMEM((zs * v.shape[0], w), bf16),
            pltpu.VMEM((ys, fold, w), bf16),
            pltpu.VMEM((ys - 1, fold, w), bf16),
            pltpu.VMEM(tiny, bf16),
            pltpu.VMEM((nseq,) + tiny, bf16),
        ]
        + reduce_scratch_shapes(x.shape, n, parts)
        + reduce_scratch_shapes(branch.shape, n, parts)
        + GatherLine.specs(v, zs, ys)
        + SumAll.specs(height, w, zs, ys)
        + [spec for p in ps for spec in PartSum.specs(p, zs, ys)]
        + [sem((ys - 1,)), sem((ys - 1,)), sem((nseq - 1,)), sem((nseq - 1,))],
        compiler_params=pltpu.CompilerParams(collective_id=cid, has_side_effects=True, vmem_limit_bytes=60 * 2**20),
        cost_estimate=cost(70),
        name="closing",
    )(x, branch, v, cols, h, *pieces, *ps)


def passed_along(block, axis, distance):
    devices = range(lax.axis_size(axis))
    route = [(i - distance, i) for i in devices if i - distance in devices]
    return lax.ppermute(block, axis, route)


def silu_slope(argument):
    logistic = jax.nn.sigmoid(argument)
    return logistic * (1.0 + argument * (1.0 - logistic))


def conv_local(extended, weights, biases, seg_ext):
    length_now = extended.shape[1] - (KERN - 1)
    seg_now = seg_ext[:, KERN - 1 :]
    summed = biases + jnp.zeros((extended.shape[0], length_now, extended.shape[2]), f32)
    for lag_index in range(KERN):
        same_doc = (seg_ext[:, lag_index : lag_index + length_now] == seg_now).astype(f32)
        summed = (
            summed
            + weights[lag_index]
            * extended[:, lag_index : lag_index + length_now]
            * same_doc[:, :, None]
        )
    return summed


def dot(a, b, contract):
    return lax.dot_general(a, b, ((contract[:1], contract[1:]), ((), ())), preferred_element_type=f32)


def lines(zs, ys):
    return [[z * ys + y for z in range(zs)] for y in range(ys)]


def tokens_of_line(rows, zs, ys):
    return lax.all_gather(rows, "seq", axis_index_groups=lines(zs, ys), tiled=True)


def local(
    hidden_in,
    segments,
    cotangent,
    norm_gain,
    input_projection_weight,
    conv_weight,
    conv_bias,
    proj_weight,
    step_weight,
    step_bias,
    decay_log,
    skip_gain,
    output_projection_weight,
):
    seqs, length, width = hidden_in.shape
    rows = seqs * length
    nch, nseq = lax.axis_size("ch"), lax.axis_size("seq")
    channels = conv_bias.shape[-1]
    share = width // nch
    share_start = lax.axis_index("ch") * share
    seg_own = segments.astype(f32)
    seg_ext = None
    hidden = hidden_in.astype(f32).reshape(rows, width)
    grad_rows = cotangent.astype(f32).reshape(rows, width)
    ids = iter(range(100))
    zs = 4 if nseq % 4 == 0 else nseq
    ys = nseq // zs
    fold = width // nseq
    places = (zs, ys)

    out_cols, w_copy = {}, {}
    stored = []
    out_low = grad_rows.astype(bf16)
    grad_mixed = dot(out_low, output_projection_weight[LAYERS - 1], (1, 1))
    grad_mixed_line = tokens_of_line(grad_mixed.astype(bf16), zs, ys)
    for layer in range(LAYERS):
        last = layer == LAYERS - 1
        inv_rms = lax.rsqrt(jnp.mean(hidden * hidden, axis=-1, keepdims=True) + epsilon)
        normed = (hidden * inv_rms * norm_gain[layer]).astype(bf16)
        w_in = w_copy[1] if layer > 0 else input_projection_weight[0]
        both = lax.dot_general(normed, w_in, (((1,), (0,)), ((), ())), preferred_element_type=f32)
        values, gate_pre = both[:, 0], both[:, 1]
        values3 = values.reshape(seqs, length, channels)
        edge = values3[:, -(KERN - 1) :]
        if seg_ext is None:
            ids_edge = jnp.broadcast_to(seg_own[:, -(KERN - 1) :, None], (seqs, KERN - 1, LANES))
            edge = passed_along(jnp.concatenate([edge, ids_edge], axis=2), "seq", 1)
            seg_ext = jnp.concatenate([edge[:, :, channels], seg_own], axis=1)
            keep = (seg_ext[:, KERN - 2 : -1] == seg_own).astype(f32).reshape(-1, 1)
            edge = edge[:, :, :channels]
        else:
            edge = passed_along(edge, "seq", 1)
        extended = jnp.concatenate([edge, values3], axis=1)
        conv_out, conv_pull = jax.vjp(
            functools.partial(conv_local, seg_ext=seg_ext), extended, conv_weight[layer], conv_bias[layer]
        )
        conv_out = conv_out.reshape(rows, channels)
        activated = jax.nn.silu(conv_out)
        act_low = activated.astype(bf16)
        proj_out = ch_sum(dot(act_low, proj_weight[layer], (1, 0)), nch, next(ids))
        rank_low = proj_out[:, :RANK].astype(bf16)
        mats = proj_out[:, RANK:]
        step_pre = dot(rank_low, step_weight[layer], (1, 0)) + step_bias[layer]
        rates = decay_log[layer]
        end_state, total = scan_local(step_pre, activated, mats, keep, rates, seqs, [], places, 0)
        gate_act = jax.nn.silu(gate_pre)
        if last:
            gate_line = tokens_of_line(gate_pre.astype(bf16), zs, ys)
            grad_scan = grad_mixed * gate_act
            start = scan_back_local(step_pre, grad_scan, mats, keep, rates, seqs)
            state_in, lam_in, w_copy[0] = carry_over(
                total, rates, [end_state, start], nseq, next(ids), True, True, taken=(input_projection_weight, 0)
            )
        else:
            state_in, w_copy[1] = carry_over(
                total, rates, [end_state], nseq, next(ids), True, False, taken=(input_projection_weight, 1)
            )
        keeping = (hidden, inv_rms, normed, gate_pre, gate_act, conv_out, activated, act_low, conv_pull, rank_low,
                   step_pre, mats, total, state_in)
        if last:
            stored.append(keeping)
            break
        (y,) = scan_forward(
            step_pre, activated, mats, keep, rates, state_in, seqs, [], places, 0, (grad_mixed_line,)
        )
        scanned = y + skip_gain[layer] * activated
        mixed = (scanned * gate_act).astype(bf16)
        out_part = dot(mixed, output_projection_weight[layer], (1, 0)).astype(bf16)
        mixed_all = tokens_of_line(mixed, zs, ys)
        branch = ch_reduce(out_part, nch, next(ids), True)
        hidden = hidden + branch
        stored.append(keeping + (scanned, mixed_all))

    for layer in reversed(range(LAYERS)):
        last = layer == LAYERS - 1
        (hidden, inv_rms, normed, gate_pre, gate_act, conv_out, activated, act_low, conv_pull, rank_low,
         step_pre, mats, total, state_in) = stored[layer][:14]
        rates = decay_log[layer]
        if not last:
            scanned, mixed_all = stored[layer][14:]
            normed_cols = early_cols
            out_low = grad_rows.astype(bf16)
            grad_mixed = dot(out_low, output_projection_weight[layer], (1, 1))
            grad_scan = grad_mixed * gate_act
            grad_gate = (grad_mixed * scanned * silu_slope(gate_pre)).astype(bf16)
            start = scan_back_local(step_pre, grad_scan, mats, keep, rates, seqs)
            gate_all = tokens_of_line(grad_gate, zs, ys)
            lam_in, grad_out_last = carry_over(
                total, rates, [start], nseq, next(ids), False, True, [out_parts_last], places
            )
        grad_skip = jnp.sum(grad_scan * activated, axis=0)
        if last:
            plan = [
                (ColumnsLine, (4, 6), normed),
                (ColumnsLine, (5, 7), out_low),
                (ColumnsLine, (6, 8), stored[0][2]),
            ]
        else:
            plan = [
                (ColumnsLine, (2, 4), out_low),
                (PartSum, (), values_parts_last),
                (PartSum, (), gate_parts_last),
            ]
        grad_pre, grad_act, grad_mats, grad_decay, *others = scan_back(
            step_pre, activated, grad_scan, mats, keep, rates, skip_gain[layer][None], state_in, lam_in, seqs, int(last),
            plan, places, next(ids), (),
        )
        if last:
            y, normed_cols, out_cols[layer], early_cols = others
            scanned = y + skip_gain[layer] * activated
            mixed = (scanned * gate_act).astype(bf16)
            grad_gate = (grad_mixed * scanned * silu_slope(gate_pre)).astype(bf16)
            scanned_line = tokens_of_line(scanned.astype(bf16), zs, ys).astype(f32)
        else:
            out_cols[layer], grad_values_last, grad_gate_last = others
        grad_step_bias = jnp.sum(grad_pre, axis=0)
        pre_low = grad_pre.astype(bf16)
        grad_step_weight = dot(rank_low, pre_low, (0, 0))
        rank_part = dot(pre_low, step_weight[layer], (1, 1))
        grad_proj = ch_sum(
            jnp.concatenate([rank_part, grad_mats[:, : 2 * STATE]], axis=-1), nch, next(ids),
            (gate_line,) if last else (),
        ).astype(bf16)
        grad_proj_weight = dot(grad_proj, act_low, (0, 0))
        grad_act = grad_act + dot(grad_proj, proj_weight[layer], (1, 1))
        grad_conv = (grad_act * silu_slope(conv_out)).reshape(seqs, length, channels)
        grad_ext, grad_conv_weight, grad_conv_bias = conv_pull(grad_conv)
        returned = passed_along(grad_ext[:, : KERN - 1], "seq", -1)
        grad_values = grad_ext[:, KERN - 1 :]
        grad_values = jnp.concatenate(
            [grad_values[:, : -(KERN - 1)], grad_values[:, -(KERN - 1) :] + returned], axis=1
        ).reshape(rows, channels).astype(bf16)
        w_in = w_copy[layer]
        grad_both = jnp.stack([grad_values, grad_gate], axis=1)
        grad_part = lax.dot_general(grad_both, w_in, (((1, 2), (1, 2)), ((), ())), preferred_element_type=f32)
        scale_now = norm_gain[layer]
        misc = jnp.concatenate([grad_conv_weight, grad_conv_bias[None], grad_step_bias[None], grad_skip[None]], axis=0)
        small = [grad_proj_weight, grad_step_weight, grad_decay, misc]
        if last:
            values_last = tokens_of_line(grad_values, zs, ys)
            values_parts_last = dot(normed_cols, values_last, (0, 0)).astype(bf16).reshape(ys, fold, channels)
            grad_normed = ch_reduce(grad_part.astype(bf16), nch, next(ids), True)
            scanned_line = scanned_line + 0.0 * grad_normed[0, 0]
            gates = gate_line.astype(f32)
            mixed_all = (scanned_line * jax.nn.silu(gates)).astype(bf16)
            gate_all = (grad_mixed_line.astype(f32) * scanned_line * silu_slope(gates)).astype(bf16)
            out_part = dot(mixed, output_projection_weight[layer], (1, 0)).astype(bf16)
            hidden_last = lax.dynamic_slice_in_dim(hidden, share_start, share, 1)
        columns = [out_cols[layer][:, k * fold : (k + 1) * fold] for k in range(ys)]
        out_parts = jnp.stack([dot(mixed_all, k, (0, 0)).astype(bf16) for k in columns], axis=0)
        gate_parts = dot(normed_cols, gate_all, (0, 0)).astype(bf16).reshape(ys, fold, channels)
        if last:
            out_parts_last, gate_parts_last = out_parts, gate_parts
            inner = jnp.sum(grad_normed * scale_now * hidden, axis=-1, keepdims=True)
            grad_norm = lax.dynamic_slice_in_dim(jnp.sum(grad_normed * hidden * inv_rms, axis=0), share_start, share, 0)
            grad_rows = grad_rows + inv_rms * scale_now * grad_normed - hidden * (inv_rms * inv_rms * inv_rms) * inner / width
            norm_row = jnp.pad(grad_norm[None], ((0, 0), (0, channels - share)))
            small[-1] = jnp.pad(jnp.concatenate([misc, norm_row], axis=0), ((0, 16 - misc.shape[0] - 1), (0, 0)))
            small_last = small
            continue
        inner = jnp.sum(grad_part * scale_now * hidden, axis=-1, keepdims=True)
        inner_high = inner.astype(bf16)
        inner_low = (inner - inner_high.astype(f32)).astype(bf16)
        beside = jnp.pad(jnp.concatenate([inner_high, inner_low], axis=1), ((0, 0), (0, LANES - 2)))
        beside = jnp.broadcast_to(beside[:, None], (rows, nch, LANES))
        send = jnp.concatenate([grad_part.astype(bf16).reshape(rows, nch, share), beside], axis=2)
        small[-1] = jnp.pad(misc, ((0, 16 - misc.shape[0]), (0, 0)))
        hidden_share = lax.dynamic_slice_in_dim(hidden, share_start, share, 1)
        scale_share = lax.dynamic_slice_in_dim(scale_now, share_start, share, 0)
        got, branch, sums, grad_in_values, tiny, grad_gate_now, grad_out_weight = closing(
            send.reshape(rows, nch * (share + LANES)), out_part, grad_values, jnp.swapaxes(normed_cols, 0, 1), hidden_share * inv_rms,
            small + small_last, [gate_parts, out_parts], nch, nseq, zs, ys, next(ids),
        )
        grad_share, inner = got[:, :share], got[:, share : share + 1] + got[:, share + 1 : share + 2]
        grad_input = (
            lax.dynamic_slice_in_dim(grad_rows, share_start, share, 1)
            + inv_rms * scale_share * grad_share
            - hidden_share * (inv_rms * inv_rms * inv_rms) * inner / width
        )
        result = (hidden_last + branch).astype(bf16)
        total_small = sums.astype(f32)
        heights = [v.shape[0] for v in small_last]
        half = sum(heights)
        pairs, at = [], 0
        for height in heights:
            pairs.append(jnp.stack([total_small[at : at + height], total_small[half + at : half + at + height]], axis=0))
            at += height
        misc = pairs[3]
        norms = jnp.stack([tiny[0], misc[1, KERN + 3, :share]], axis=0)
        in_weight = jnp.stack(
            [jnp.stack(pair, axis=1) for pair in ((grad_in_values, grad_gate_now), (grad_values_last, grad_gate_last))], axis=0
        )
        out_weight = jnp.stack([grad_out_weight, grad_out_last], axis=0)
    shape3 = (seqs, length, share)
    return (
        result.reshape(shape3),
        grad_input.reshape(shape3),
        norms,
        in_weight,
        misc[:, :KERN],
        misc[:, KERN],
        jnp.swapaxes(pairs[0], 1, 2),
        pairs[1],
        misc[:, KERN + 1],
        pairs[2],
        misc[:, KERN + 2],
        out_weight,
    )


def solution(mesh):
    in_specs = (
        P(None, "seq", None),
        P(None, "seq"),
        P(None, "seq", None),
        P(),
        P(None, None, None, "ch"),
        P(None, None, "ch"),
        P(None, "ch"),
        P(None, "ch", None),
        P(None, None, "ch"),
        P(None, "ch"),
        P(None, None, "ch"),
        P(None, "ch"),
        P(None, "ch", None),
    )
    out_specs = (
        P(None, "seq", "ch"),
        P(None, "seq", "ch"),
        P(None, "ch"),
        P(None, "seq", None, "ch"),
        P(None, None, "ch"),
        P(None, "ch"),
        P(None, "ch", None),
        P(None, None, "ch"),
        P(None, "ch"),
        P(None, None, "ch"),
        P(None, "ch"),
        P(None, "ch", "seq"),
    )
    return jax.shard_map(local, mesh=mesh, in_specs=in_specs, out_specs=out_specs, check_vma=False)
```
